32 devices in a mesh: page: 4 (over z), blk: 8 (over y, x, core).
Axes of the slice: x: 2, y: 2, z: 4, core: 2. Of those that a mesh axis runs over, the one named last changes fastest.
Arguments:
- visual: bfloat16 [4, 96, 24, 768], P('page', 'blk'), may hold values from -6 to 6
- query_tokens: bfloat16 [4, 1024, 768], P('page', 'blk'), may hold values from -6 to 6
- answer_len: int32 [4], P('page'), may hold values from 5 to 1024, as said below
- attn_swin: float32 [2359296], P(('page', 'blk')), may hold values from -16 to 16
- attn_self: float32 [2359296], P(('page', 'blk')), may hold values from -16 to 16
- attn_qv: float32 [2359296], P(('page', 'blk')), may hold values from -16 to 16
- attn_vq: float32 [2359296], P(('page', 'blk')), may hold values from -16 to 16
- mlp_up: float32 [2359296], P(('page', 'blk')), may hold values from -0.21875 to 0.21875
- mlp_down: float32 [2359296], P(('page', 'blk')), may hold values from -0.15625 to 0.15625
- norm_gains: float32 [6144], P(('page', 'blk')), may hold values from 0.5 to 1.5
- visual_cot: bfloat16 [4, 96, 24, 768], P('page', 'blk'), may hold values from -6 to 6
- query_cot: bfloat16 [4, 1024, 768], P('page', 'blk'), may hold values from -6 to 6
Outputs:
- visual_out: bfloat16 [4, 96, 24, 768], P('page', 'blk')
- query_out: bfloat16 [4, 1024, 768], P('page', 'blk')
- visual_grad: float32 [4, 96, 24, 768], P('page', 'blk')
- query_grad: float32 [4, 1024, 768], P('page', 'blk')
- swin_grad: float32 [2359296], P(('page', 'blk'))
- self_grad: float32 [2359296], P(('page', 'blk'))
- cross_qv_grad: float32 [2359296], P(('page', 'blk'))
- cross_vq_grad: float32 [2359296], P(('page', 'blk'))
- mlp_up_grad: float32 [2359296], P(('page', 'blk'))
- mlp_down_grad: float32 [2359296], P(('page', 'blk'))
- gains_grad: float32 [6144], P(('page', 'blk'))
The draws below stay inside these ranges and needn't reach their ends.
Inputs may be any that keep to these rules, and one draw needn't show every extreme that they name: `answer_len`: some page has all 1024 slots live.
All inputs are finite; a program needn't handle non-finite values.
Results may differ from the reference program's by a relative error of at most 0.02.
The reference program's roundings to bfloat16 on the way count: a program that leaves them out, or rounds other values in their place, can miss the bound.
Values may be sent and summed in bfloat16 or wider, within the bound.
No kernel may reach another device: no remote copies, remote signals or barrier semaphores. Data moves between devices by JAX's collectives and lax.ppermute only.
A program may use at most 256 MiB of HBM per device.

```python
import jax
import jax.numpy as jnp
from jax import lax

D = 768
HEADS = 12
HD = 64
FF = 3072
WIN = 12
COLS = 24
QSLOTS = 1024
PAGES = 4
PATCH_ROWS = 96
PATCHES = 2304
N_BLK = 8


def block_scaled(base, key_count):
    mats = base.reshape(4, D, D)
    scale = jnp.array([1.25 * D ** (-0.5), 1.25 * D ** (-0.5), D ** (-0.5), (key_count / (8.0 * D)) ** 0.5], jnp.float32)
    return (mats * scale[:, None, None]).reshape(-1)


def draw_attn_swin(key, part):
    key = jax.random.fold_in(key, 11)
    base = jnp.clip(jax.random.normal(key, (4 * D * D,), jnp.float32), -3.0, 3.0)
    return block_scaled(base, WIN * WIN)


def draw_attn_self(key, part):
    key = jax.random.fold_in(key, 12)
    base = jnp.clip(jax.random.normal(key, (4 * D * D,), jnp.float32), -3.0, 3.0)
    return block_scaled(base, QSLOTS // 4)


def draw_attn_qv(key, part):
    key = jax.random.fold_in(key, 13)
    base = jnp.clip(jax.random.normal(key, (4 * D * D,), jnp.float32), -3.0, 3.0)
    return block_scaled(base, PATCHES)


def draw_attn_vq(key, part):
    key = jax.random.fold_in(key, 14)
    base = jnp.clip(jax.random.normal(key, (4 * D * D,), jnp.float32), -3.0, 3.0)
    return block_scaled(base, QSLOTS // 2)


def draw_answer_len(key, part):
    key = jax.random.fold_in(key, 15)
    first_key, second_key = jax.random.split(key)
    lengths = jax.random.randint(first_key, (PAGES,), 5, QSLOTS + 1)
    chosen = jax.random.randint(second_key, (), 0, PAGES)
    return jnp.where(jnp.arange(PAGES) == chosen, QSLOTS, lengths).astype(jnp.int32)


def shard_levels(stream_key, dims, shards, least, high):
    gain = 1.0
    for axis_at, shards_of in shards:
        steps = jax.random.uniform(jax.random.fold_in(jax.random.fold_in(stream_key, 6), axis_at), (shards_of,), jnp.float32, least / len(shards), high / len(shards))
        gain = gain * jnp.repeat(jnp.exp(steps), dims[axis_at] // shards_of).reshape((-1,) + (1,) * (len(dims) - 1 - axis_at))
    return gain


def gaussian(stream_key, extent, width, bound, shards=(), kind=jnp.bfloat16):
    entries = width * jax.random.normal(stream_key, extent, jnp.float32)
    if shards:
        entries = entries * shard_levels(stream_key, extent, shards, -0.22, 0.18)
    return jnp.clip(entries, -bound, bound).astype(kind)


def setup_inputs(seed: int = 0) -> dict:
    splits = jax.random.split(jax.random.key(seed), 13)
    return {
        "visual": gaussian(splits[0], (PAGES, PATCH_ROWS, COLS, D), 1.0, 6.0, ((0, 4), (1, 8))),
        "query_tokens": gaussian(splits[1], (PAGES, QSLOTS, D), 1.0, 6.0, ((0, 4), (1, 8))),
        "answer_len": draw_answer_len(jax.random.fold_in(splits[12], 71), 0),
        "attn_swin": draw_attn_swin(jax.random.fold_in(splits[12], 71), 0),
        "attn_self": draw_attn_self(jax.random.fold_in(splits[12], 71), 0),
        "attn_qv": draw_attn_qv(jax.random.fold_in(splits[12], 71), 0),
        "attn_vq": draw_attn_vq(jax.random.fold_in(splits[12], 71), 0),
        "mlp_up": gaussian(splits[7], (D * FF,), D ** -0.5, 0.21875, ((0, 32),), jnp.float32),
        "mlp_down": gaussian(splits[8], (FF * D,), (FF // 2) ** -0.5, 0.15625, ((0, 32),), jnp.float32),
        "norm_gains": jnp.clip(1.0 + 0.1 * jax.random.normal(splits[9], (8 * D,), jnp.float32), 0.5, 1.5),
        "visual_cot": gaussian(splits[10], (PAGES, PATCH_ROWS, COLS, D), 1.0, 6.0, ((0, 4), (1, 8))),
        "query_cot": gaussian(splits[11], (PAGES, QSLOTS, D), 1.0, 6.0, ((0, 4), (1, 8))),
    }


EPS = 1e-05
NEG = -1e+30
HIGH = lax.Precision.HIGHEST

@jax.custom_vjp
def low(v):
    return lax.optimization_barrier(v.astype(jnp.bfloat16)).astype(jnp.float32)

@jax.custom_vjp
def low_back(v):
    return v

def low_keep(v):
    return (low(v), None)

def low_pass(kept, grad):
    return (grad,)

def back_keep(v):
    return (v, None)

def back_low(kept, grad):
    return (low(grad),)
low.defvjp(low_keep, low_pass)
low_back.defvjp(back_keep, back_low)

def both_ways(values):
    return low_back(low(values))

def layer_norm(rows_in, gain_row):
    centre = lax.optimization_barrier(jnp.mean(rows_in, axis=-1, keepdims=True))
    centred = rows_in - centre
    spread = lax.optimization_barrier(jnp.mean(centred * centred, axis=-1, keepdims=True))
    return centred * lax.rsqrt(spread + EPS) * gain_row

def matmul(left, right):
    return jnp.dot(left, right, precision=HIGH)

def split_block(flat):
    mats = flat.reshape(4, D, D)
    return (jnp.concatenate([mats[0], mats[1], mats[2]], axis=1), mats[3])

def attend(queries, key_rows, value_rows, allowed):
    heads_q = queries.reshape(queries.shape[:-1] + (HEADS, HD))
    heads_k = key_rows.reshape(key_rows.shape[:-1] + (HEADS, HD))
    heads_v = value_rows.reshape(value_rows.shape[:-1] + (HEADS, HD))
    products = jnp.einsum('wqhd,wkhd->whqk', heads_q, heads_k, precision=HIGH) * HD ** (-0.5)
    scores = low_back(jnp.where(allowed[:, None], products, NEG))
    chances = low(jax.nn.softmax(scores, axis=-1))
    mixed = jnp.einsum('whqk,wkhd->wqhd', chances, heads_v, precision=HIGH)
    return both_ways(mixed.reshape(queries.shape))

def window_attention(q_grid, kv_grid, tag_grid):
    half_rows = WIN // 2

    def arrange(grid_rows):
        rolled = jnp.roll(grid_rows, (-half_rows, -half_rows), (0, 1))
        channels = rolled.shape[-1]
        shaped = rolled.reshape(PATCH_ROWS // WIN, WIN, COLS // WIN, WIN, channels)
        return shaped.transpose(0, 2, 1, 3, 4).reshape(PATCH_ROWS // WIN, COLS // WIN, WIN * WIN, channels)
    q_win = arrange(q_grid)
    kv_win = arrange(kv_grid)
    tag_win = arrange(tag_grid[..., None])[..., 0]

    def band_rows(pieces):
        q_band, kv_band, tag_band = pieces
        allowed = tag_band[:, :, None] == tag_band[:, None, :]
        return attend(q_band, kv_band[..., :D], kv_band[..., D:], allowed)
    mixed = lax.map(jax.checkpoint(band_rows), (q_win, kv_win, tag_win))
    shaped = mixed.reshape(PATCH_ROWS // WIN, COLS // WIN, WIN, WIN, D).transpose(0, 2, 1, 3, 4)
    return jnp.roll(shaped.reshape(PATCH_ROWS, COLS, D), (half_rows, half_rows), (0, 1))

def forward(visual_page, query_page, length, attn_swin, attn_self, attn_qv, attn_vq, mlp_up, mlp_down, norm_gains):
    swin_in, swin_out = split_block(low(attn_swin))
    self_in, self_out = split_block(low(attn_self))
    qv_in, qv_out = split_block(low(attn_qv))
    vq_in, vq_out = split_block(low(attn_vq))
    w_up = low(mlp_up).reshape(D, FF)
    w_down = low(mlp_down).reshape(FF, D)
    gain_rows = low(norm_gains).reshape(8, D)
    flat_vis = visual_page.reshape(PATCHES, D)
    normed = low(layer_norm(flat_vis, gain_rows[0]))
    q_swin = both_ways(matmul(normed, swin_in[:, :D]))
    kv_swin = both_ways(matmul(normed, swin_in[:, D:]))
    row_index = jnp.arange(PATCH_ROWS, dtype=jnp.int32)[:, None]
    col_index = jnp.arange(COLS, dtype=jnp.int32)[None, :]
    tags = 2 * (row_index < WIN // 2).astype(jnp.int32) + (col_index < WIN // 2).astype(jnp.int32)
    swin_mixed = window_attention(q_swin.reshape(PATCH_ROWS, COLS, D), kv_swin.reshape(PATCH_ROWS, COLS, 2 * D), tags)
    visual_one = flat_vis + low_back(matmul(swin_mixed.reshape(PATCHES, D), swin_out))
    q_normed = low(layer_norm(query_page, gain_rows[1]))
    self_q = both_ways(matmul(q_normed, self_in[:, :D]))
    self_kv = both_ways(matmul(q_normed, self_in[:, D:]))
    slots = jnp.arange(QSLOTS, dtype=jnp.int32)
    self_allowed = ((slots[None, :] <= slots[:, None]) & (slots[None, :] < length))[None]
    self_mixed = jax.checkpoint(attend)(self_q[None], self_kv[None, :, :D], self_kv[None, :, D:], self_allowed)[0]
    query_one = query_page + low_back(matmul(self_mixed, self_out))
    vis_low = low(layer_norm(visual_one, gain_rows[2]))
    qry_low = low(layer_norm(query_one, gain_rows[3]))
    q_cross_a = both_ways(matmul(qry_low, qv_in[:, :D]))
    kv_cross_a = both_ways(matmul(vis_low, qv_in[:, D:]))
    q_cross_b = both_ways(matmul(vis_low, vq_in[:, :D]))
    kv_cross_b = both_ways(matmul(qry_low, vq_in[:, D:]))
    everything = jnp.ones((1, 1, 1), dtype=jnp.bool_)

    def qv_block(block_rows):
        return attend(block_rows[None], kv_cross_a[None, :, :D], kv_cross_a[None, :, D:], everything)[0]
    qv_mixed = lax.map(jax.checkpoint(qv_block), q_cross_a.reshape(N_BLK, QSLOTS // N_BLK, D)).reshape(QSLOTS, D)
    query_two = query_one + low_back(matmul(qv_mixed, qv_out))
    key_live = (slots < length)[None, None, :]

    def vq_block(block_rows):
        return attend(block_rows[None], kv_cross_b[None, :, :D], kv_cross_b[None, :, D:], key_live)[0]
    vq_mixed = lax.map(jax.checkpoint(vq_block), q_cross_b.reshape(N_BLK, PATCHES // N_BLK, D)).reshape(PATCHES, D)
    visual_two = visual_one + low_back(matmul(vq_mixed, vq_out))
    mlp_low = low(layer_norm(visual_two, gain_rows[4]))
    hidden_pre = low_back(matmul(mlp_low, w_up))
    hidden_act = low(jax.nn.gelu(hidden_pre))
    visual_three = visual_two + low_back(matmul(hidden_act, w_down))
    return (visual_three.reshape(PATCH_ROWS, COLS, D), query_two)

def reference(visual, query_tokens, answer_len, attn_swin, attn_self, attn_qv, attn_vq, mlp_up, mlp_down, norm_gains, visual_cot, query_cot):
    weights = (attn_swin.astype(jnp.float32), attn_self.astype(jnp.float32), attn_qv.astype(jnp.float32), attn_vq.astype(jnp.float32), mlp_up.astype(jnp.float32), mlp_down.astype(jnp.float32), norm_gains.astype(jnp.float32))
    zero_grads = tuple((jnp.zeros_like(member) for member in weights))

    def page_step(carry, page_items):
        vis_page, qry_page, length, vis_cot, qry_cot = page_items

        def run_page(vis_in, qry_in, *params):
            return forward(vis_in, qry_in, length, *params)
        outputs, back_fn = jax.vjp(run_page, vis_page.astype(jnp.float32), qry_page.astype(jnp.float32), *weights)
        grads = back_fn((vis_cot.astype(jnp.float32), qry_cot.astype(jnp.float32)))
        carry = tuple((total + grad for total, grad in zip(carry, grads[2:])))
        return (carry, (outputs[0].astype(jnp.bfloat16), outputs[1].astype(jnp.bfloat16), grads[0], grads[1]))
    sums, stacked = lax.scan(page_step, zero_grads, (visual, query_tokens, answer_len, visual_cot, query_cot))
    return (stacked[0], stacked[1], stacked[2], stacked[3], sums[0], sums[1], sums[2], sums[3], sums[4], sums[5], sums[6])
```

```python
import jax
import jax.numpy as jnp
from jax import lax
from jax.experimental import pallas as pl
from jax.experimental.pallas import tpu as pltpu
from jax.sharding import PartitionSpec as P

D = 768
HEADS = 12
HD = 64
FF = 3072
PAIRS = HEADS // 2
PW = 2 * HD
SCALE = HD ** (-0.5)

EPS = 1e-05
NEG = -1e30

bf16 = jnp.bfloat16
f32 = jnp.float32
VMEM_LIMIT = 56 * 1024 * 1024


def nn(left, right):
    return lax.dot_general(left, right, (((1,), (0,)), ((), ())), preferred_element_type=f32)


def nt(left, right):
    return lax.dot_general(left, right, (((1,), (1,)), ((), ())), preferred_element_type=f32)


def tn(left, right):
    return lax.dot_general(left, right, (((0,), (0,)), ((), ())), preferred_element_type=f32)


def norm_parts(rows):
    centre = jnp.mean(rows, axis=-1, keepdims=True)
    centred = rows - centre
    spread = jnp.mean(centred * centred, axis=-1, keepdims=True)
    inverse = lax.rsqrt(spread + EPS)
    return centred * inverse, inverse


def norm(rows, gain):
    return norm_parts(rows)[0] * gain


def norm_back(rows, gain, grad):
    unit, inverse = norm_parts(rows)
    grad_gain = jnp.sum(grad * unit, axis=0, keepdims=True)
    scaled = grad * gain
    first = jnp.mean(scaled, axis=-1, keepdims=True)
    second = jnp.mean(scaled * unit, axis=-1, keepdims=True)
    return inverse * (scaled - first - unit * second), grad_gain


def mat(ref, index):
    count, rows, _ = ref.shape
    if count >= 4:
        each = count // 4
        return ref[index * each : (index + 1) * each].reshape(D, D)
    return ref[0, index * D : (index + 1) * D]


def lane_half(half, value, dtype):
    lanes = lax.broadcasted_iota(jnp.int32, (1, PW), 1)
    return jnp.where((lanes // HD) == half, value, 0.0).astype(dtype)


def low_half(rows):
    return lax.broadcasted_iota(jnp.int32, (rows, PW), 1) < HD


def column(table, index):
    lanes = lax.broadcasted_iota(jnp.int32, table.shape, 1)
    return jnp.sum(jnp.where(lanes == index, table, 0.0), axis=-1, keepdims=True)


def pair_cols(pair, base=0):
    return pl.ds(pl.multiple_of(base + pair * PW, PW), PW)


def softmax_rows(scores):
    highest = jnp.max(scores, axis=-1, keepdims=True)
    raised = jnp.exp(scores - highest)
    totals = jnp.sum(raised, axis=-1, keepdims=True)
    return raised * (1.0 / totals), highest + jnp.log(totals)


def call(kernel, outs, ins, scratch=(), smem=0, blocks=None, flops=0, name=None):
    def whole(value):
        zeros = (0,) * len(value.shape)
        return pl.BlockSpec(value.shape, lambda i: zeros, pipeline_mode=pl.Buffered(1))

    specs = []
    for index, value in enumerate(ins):
        if index < smem:
            specs.append(pl.BlockSpec(memory_space=pltpu.SMEM))
        elif blocks and index in blocks:
            specs.append(blocks[index])
        else:
            specs.append(whole(value))
    single = not isinstance(outs, list)
    shapes = [outs] if single else outs
    moved = sum(v.size * v.dtype.itemsize for v in list(ins) + shapes)
    result = pl.pallas_call(
        kernel,
        grid=(1,),
        out_shape=shapes,
        in_specs=specs,
        out_specs=[whole(value) for value in shapes],
        scratch_shapes=list(scratch),
        compiler_params=pltpu.CompilerParams(
            vmem_limit_bytes=VMEM_LIMIT, dimension_semantics=("arbitrary",)
        ),
        cost_estimate=pl.CostEstimate(flops=int(flops), bytes_accessed=int(moved), transcendentals=0),
        name=name,
    )(*ins)
    return result[0] if single else result


def sds(shape, dtype):
    return jax.ShapeDtypeStruct(shape, dtype)


def self_bias(bias_ref, first_row, live):
    rows, slots = bias_ref.shape
    keys = lax.broadcasted_iota(jnp.int32, (rows, slots), 1)
    places = lax.broadcasted_iota(jnp.int32, (rows, slots), 0) + first_row
    bias_ref[...] = jnp.where((keys <= places) & (keys < live), 0.0, NEG)


def self_forward_kernel(
    where_ref, y_ref, g_ref, w_ref, b_ref, q_ref, kv_ref, lse_ref, o_ref, y1_ref, c_ref, bias_ref
):
    first_row, live = where_ref[0], where_ref[1]
    slots, own = y_ref.shape[0], q_ref.shape[0]
    tile = 256

    def project(i, carry):
        rows = pl.ds(pl.multiple_of(i * tile, tile), tile)
        normed = norm(y_ref[rows, :].astype(f32), g_ref[1:2, :]).astype(bf16)
        b_ref[rows, :] = normed
        kv_ref[rows, 0:D] = nn(normed, mat(w_ref, 1)).astype(bf16)
        kv_ref[rows, D : 2 * D] = nn(normed, mat(w_ref, 2)).astype(bf16)
        return carry

    lax.fori_loop(0, slots // tile, project, 0)
    mine = pl.ds(pl.multiple_of(first_row, 16), own)
    q_ref[...] = nn(b_ref[mine, :], mat(w_ref, 0)).astype(bf16)
    self_bias(bias_ref, first_row, live)
    lse_ref[...] = jnp.zeros_like(lse_ref)
    lanes = lax.broadcasted_iota(jnp.int32, lse_ref.shape, 1)
    low = low_half(own)

    def attend(pair, carry):
        queries = q_ref[:, pair_cols(pair)]
        keys = kv_ref[:, pair_cols(pair)]
        values = kv_ref[:, pair_cols(pair, D)]
        mixed = []
        table = lse_ref[...]
        for half in range(2):
            scores = nt(queries * lane_half(half, SCALE, bf16), keys) + bias_ref[...]
            chances, log_totals = softmax_rows(scores)
            mixed.append(nn(chances.astype(bf16), values))
            table = jnp.where(lanes == 2 * pair + half, log_totals, table)
        lse_ref[...] = table
        o_ref[:, pair_cols(pair)] = jnp.where(low, mixed[0], mixed[1]).astype(bf16)
        return carry

    lax.fori_loop(0, PAIRS, attend, 0)
    y1 = y_ref[mine, :].astype(f32) + nn(o_ref[...], mat(w_ref, 3))
    y1_ref[...] = y1
    c_ref[...] = norm(y1, g_ref[3:4, :]).astype(bf16)


def window_bias(rows, side, row_split, col_split):
    def flags(shape, dim):
        token = lax.broadcasted_iota(jnp.int32, shape, dim)
        row, col = token // side, token % side
        return jnp.where(row >= side // 2, row_split, 0) + jnp.where(
            col >= side // 2, 2 * col_split, 0
        )

    return jnp.where(flags((rows, rows), 0) == flags((rows, rows), 1), 0.0, NEG)


def swin_forward_kernel(
    side, where_ref, x_ref, g_ref, w_ref, a_ref, qkv_ref, lse_ref, o_ref, v1_ref, e_ref, bias_ref
):
    is_last = where_ref[2]
    tokens = x_ref.shape[0]
    rows = side * side
    windows = tokens // rows
    x = x_ref[...].astype(f32)
    normed = norm(x, g_ref[0:1, :]).astype(bf16)
    a_ref[...] = normed
    for k in range(3):
        qkv_ref[:, k * D : (k + 1) * D] = nn(normed, mat(w_ref, k)).astype(bf16)
    for w in range(windows):
        bias_ref[w] = window_bias(rows, side, is_last, 1 if w == windows - 1 else 0)
    lse_ref[...] = jnp.zeros_like(lse_ref)
    lanes = lax.broadcasted_iota(jnp.int32, (rows, lse_ref.shape[1]), 1)
    low = low_half(rows)

    def attend(pair, carry):
        for w in range(windows):
            at = slice(w * rows, (w + 1) * rows)
            queries = qkv_ref[at, pair_cols(pair)]
            keys = qkv_ref[at, pair_cols(pair, D)]
            values = qkv_ref[at, pair_cols(pair, 2 * D)]
            mixed = []
            table = lse_ref[at, :]
            for half in range(2):
                scores = nt(queries * lane_half(half, SCALE, bf16), keys) + bias_ref[w]
                chances, log_totals = softmax_rows(scores)
                mixed.append(nn(chances.astype(bf16), values))
                table = jnp.where(lanes == 2 * pair + half, log_totals, table)
            lse_ref[at, :] = table
            o_ref[at, pair_cols(pair)] = jnp.where(low, mixed[0], mixed[1]).astype(bf16)
        return carry

    lax.fori_loop(0, PAIRS, attend, 0)
    v1 = x + nn(o_ref[...], mat(w_ref, 3))
    v1_ref[...] = v1
    e_ref[...] = norm(v1, g_ref[2:3, :]).astype(bf16)


def cross_forward_kernel(
    where_ref,
    c_ref,
    cot_ref,
    e_ref,
    wqv_ref,
    wvq_ref,
    qa_ref,
    kvb_ref,
    doa_ref,
    kva_ref,
    qb_ref,
    stats_ref,
    lse_ref,
    ob_ref,
):
    live = where_ref[1]
    slots, tokens = c_ref.shape[0], e_ref.shape[0]
    tile = 256
    normed = e_ref[...]
    for k in range(2):
        kva_ref[:, k * D : (k + 1) * D] = nn(normed, mat(wqv_ref, 1 + k)).astype(bf16)
    qb_ref[...] = nn(normed, mat(wvq_ref, 0)).astype(bf16)

    def project(i, carry):
        rows = pl.ds(pl.multiple_of(i * tile, tile), tile)
        part = c_ref[rows, :]
        qa_ref[rows, :] = nn(part, mat(wqv_ref, 0)).astype(bf16)
        for k in range(2):
            kvb_ref[rows, k * D : (k + 1) * D] = nn(part, mat(wvq_ref, 1 + k)).astype(bf16)
        doa_ref[rows, :] = nt(cot_ref[rows, :], mat(wqv_ref, 3)).astype(bf16)
        return carry

    lax.fori_loop(0, slots // tile, project, 0)
    stats_ref[...] = jnp.zeros_like(stats_ref)

    def page_stats(pair, carry):
        keys = kva_ref[:, pair_cols(pair)]
        values = kva_ref[:, pair_cols(pair, D)]
        for half in range(2):
            head = 2 * pair + half
            keys_h = keys * lane_half(half, SCALE, bf16)
            values_h = values * lane_half(half, 1.0, bf16)
            for i in range(slots // tile):
                rows = slice(i * tile, (i + 1) * tile)
                scores = nt(keys_h, qa_ref[rows, pair_cols(pair)])
                highest = jnp.max(scores, axis=0, keepdims=True)
                raised = jnp.exp(scores - highest)
                grads = nt(values_h, doa_ref[rows, pair_cols(pair)])
                stats_ref[0, pl.ds(head, 1), rows] = highest
                stats_ref[1, pl.ds(head, 1), rows] = jnp.sum(raised, axis=0, keepdims=True)
                stats_ref[2, pl.ds(head, 1), rows] = jnp.sum(raised * grads, axis=0, keepdims=True)
        return carry

    lax.fori_loop(0, PAIRS, page_stats, 0)
    lse_ref[...] = jnp.zeros_like(lse_ref)
    lanes = lax.broadcasted_iota(jnp.int32, lse_ref.shape, 1)
    low = low_half(tokens)
    bias = jnp.where(lax.broadcasted_iota(jnp.int32, (1, slots), 1) < live, 0.0, NEG)

    def attend(pair, carry):
        queries = qb_ref[:, pair_cols(pair)]
        keys = kvb_ref[:, pair_cols(pair)]
        values = kvb_ref[:, pair_cols(pair, D)]
        mixed = []
        table = lse_ref[...]
        for half in range(2):
            scores = nt(queries * lane_half(half, SCALE, bf16), keys) + bias
            chances, log_totals = softmax_rows(scores)
            mixed.append(nn(chances.astype(bf16), values))
            table = jnp.where(lanes == 2 * pair + half, log_totals, table)
        lse_ref[...] = table
        ob_ref[:, pair_cols(pair)] = jnp.where(low, mixed[0], mixed[1]).astype(bf16)
        return carry

    lax.fori_loop(0, PAIRS, attend, 0)


GELU_A = 0.7978845608028654
GELU_B = 0.044715


def mlp_kernel(
    steps,
    v1_ref,
    ob_ref,
    cot_ref,
    g_ref,
    wvq_ref,
    up_ref,
    down_ref,
    v3_ref,
    h_ref,
    act_ref,
    du_ref,
    g2_ref,
    dz_ref,
    dob_ref,
    dg_ref,
    v2_ref,
    sum_ref,
    dh_ref,
):
    step = pl.program_id(0)

    @pl.when(step == 0)
    def _():
        v2 = v1_ref[...] + nn(ob_ref[...], mat(wvq_ref, 3))
        v2_ref[...] = v2
        sum_ref[...] = v2
        h_ref[...] = norm(v2, g_ref[4:5, :]).astype(bf16)
        dh_ref[...] = jnp.zeros_like(dh_ref)

    up, down = up_ref[0], down_ref[0]
    u = nn(h_ref[...], up)
    squared = u * u
    bend = jnp.tanh(GELU_A * (u + GELU_B * u * squared))
    act = (0.5 * u * (1.0 + bend)).astype(bf16)
    act_ref[...] = act
    slope = 0.5 * (1.0 + bend) + 0.5 * u * (1.0 - bend * bend) * GELU_A * (
        1.0 + 3.0 * GELU_B * squared
    )
    du = (nt(cot_ref[...], down) * slope).astype(bf16)
    du_ref[...] = du
    sum_ref[...] += nn(act, down)
    dh_ref[...] += nt(du, up)

    @pl.when(step == steps - 1)
    def _():
        v3_ref[...] = sum_ref[...].astype(bf16)
        part, dg = norm_back(v2_ref[...], g_ref[4:5, :], dh_ref[...])
        dg_ref[...] = dg
        g2 = cot_ref[...].astype(f32) + part
        g2_ref[...] = g2
        dz = g2.astype(bf16)
        dz_ref[...] = dz
        dob_ref[...] = nt(dz, mat(wvq_ref, 3)).astype(bf16)


def mlp(v1, ob, cot, gains, wvq, wvq_spec, up, down):
    tokens = v1.shape[0]
    steps = FF // D
    whole = lambda shape: pl.BlockSpec(shape, lambda i: (0,) * len(shape))
    cols = pl.BlockSpec((tokens, D), lambda i: (0, i))
    weight = pl.BlockSpec((1, D, D), lambda i: (i, 0, 0))
    row = whole((tokens, D))

    def kernel(*refs):
        mlp_kernel(steps, *refs)

    return pl.pallas_call(
        kernel,
        grid=(steps,),
        out_shape=[
            sds((tokens, D), bf16),
            sds((tokens, D), bf16),
            sds((tokens, FF), bf16),
            sds((tokens, FF), bf16),
            sds((tokens, D), f32),
            sds((tokens, D), bf16),
            sds((tokens, D), bf16),
            sds((1, D), f32),
        ],
        in_specs=[
            row,
            row,
            row,
            whole(gains.shape),
            wvq_spec,
            weight,
            weight,
        ],
        out_specs=[row, row, cols, cols, row, row, row, whole((1, D))],
        scratch_shapes=[pltpu.VMEM((tokens, D), f32)] * 3,
        compiler_params=pltpu.CompilerParams(
            vmem_limit_bytes=VMEM_LIMIT, dimension_semantics=("arbitrary",)
        ),
        cost_estimate=pl.CostEstimate(
            flops=2 * tokens * D * D * 18, bytes_accessed=24 * 1024 * 1024, transcendentals=0
        ),
        name="mlp",
    )(v1, ob, cot, gains, wvq, up, down)


def vq_backward_kernel(
    where_ref, qb_ref, kvb_ref, dob_ref, lse_ref, dqb_ref, dkvbt_ref
):
    live = where_ref[1]
    tokens, slots = qb_ref.shape[0], kvb_ref.shape[0]
    bias = jnp.where(lax.broadcasted_iota(jnp.int32, (1, slots), 1) < live, 0.0, NEG)
    low = low_half(tokens)

    def back(pair, carry):
        queries = qb_ref[:, pair_cols(pair)]
        keys = kvb_ref[:, pair_cols(pair)]
        values = kvb_ref[:, pair_cols(pair, D)]
        grads = dob_ref[:, pair_cols(pair)]
        queries_t = (queries * SCALE).astype(f32).T.astype(bf16)
        grads_t = grads.astype(f32).T.astype(bf16)
        parts = []
        for half in range(2):
            own = slice(half * HD, (half + 1) * HD)
            scores = nt(queries * lane_half(half, SCALE, bf16), keys) + bias
            chances = jnp.exp(scores - column(lse_ref[...], 2 * pair + half))
            slopes = nt(grads * lane_half(half, 1.0, bf16), values)
            centre = jnp.sum(chances * slopes, axis=-1, keepdims=True)
            ds = (chances * (slopes - centre)).astype(bf16)
            parts.append(nn(ds, keys))
            at = pair * PW + half * HD
            dkvbt_ref[pl.ds(pl.multiple_of(at, HD), HD), :] = nn(queries_t[own], ds).astype(bf16)
            dkvbt_ref[pl.ds(pl.multiple_of(D + at, HD), HD), :] = nn(
                grads_t[own], chances.astype(bf16)
            ).astype(bf16)
        dqb_ref[:, pair_cols(pair)] = (jnp.where(low, parts[0], parts[1]) * SCALE).astype(bf16)
        return carry

    lax.fori_loop(0, PAIRS, back, 0)


def qv_backward_kernel(qa_ref, kva_ref, doa_ref, lse_ref, centre_ref, oa_ref, dqat_ref, dkva_ref):
    slots, tokens = qa_ref.shape[0], kva_ref.shape[0]
    low = low_half(tokens)
    tile = 512

    def back(pair, carry):
        keys = kva_ref[:, pair_cols(pair)]
        values = kva_ref[:, pair_cols(pair, D)]
        keys_t = (keys * SCALE).astype(f32).T.astype(bf16)
        values_t = values.astype(f32).T.astype(bf16)
        for i in range(slots // tile):
            rows = slice(i * tile, (i + 1) * tile)
            queries = qa_ref[rows, pair_cols(pair)]
            grads = doa_ref[rows, pair_cols(pair)]
            dk, dv, mixed = [], [], []
            for half in range(2):
                head = 2 * pair + half
                own = slice(half * HD, (half + 1) * HD)
                scores = nt(keys * lane_half(half, SCALE, bf16), queries)
                chances = jnp.exp(scores - lse_ref[pl.ds(head, 1), rows])
                slopes = nt(values * lane_half(half, 1.0, bf16), grads)
                ds = (chances * (slopes - centre_ref[pl.ds(head, 1), rows])).astype(bf16)
                rounded = chances.astype(bf16)
                mixed.append(nn(values_t[own], rounded))
                dqat_ref[pl.ds(pl.multiple_of(head * HD, HD), HD), rows] = nn(
                    keys_t[own], ds
                ).astype(bf16)
                dk.append(nn(ds, queries))
                dv.append(nn(rounded, grads))
            oa_ref[rows, pair_cols(pair)] = jnp.concatenate(mixed, axis=0).T.astype(bf16)
            dk_now = jnp.where(low, dk[0], dk[1]) * SCALE
            dv_now = jnp.where(low, dv[0], dv[1])
            if i == 0:
                dk_sum, dv_sum = dk_now, dv_now
            else:
                dk_sum, dv_sum = dk_sum + dk_now, dv_sum + dv_now
        dkva_ref[:, pair_cols(pair)] = dk_sum.astype(bf16)
        dkva_ref[:, pair_cols(pair, D)] = dv_sum.astype(bf16)
        return carry

    lax.fori_loop(0, PAIRS, back, 0)


def slots_back_kernel(dqat_ref, dkvbt_ref, wqv_ref, wvq_ref, dc_ref):
    slots = dqat_ref.shape[1]
    tile = 256
    for i in range(slots // tile):
        cols = slice(i * tile, (i + 1) * tile)
        total = nn(mat(wqv_ref, 0), dqat_ref[:, cols])
        total += nn(mat(wvq_ref, 1), dkvbt_ref[0:D, cols])
        total += nn(mat(wvq_ref, 2), dkvbt_ref[D : 2 * D, cols])
        dc_ref[cols, :] = total.T.astype(bf16)


def swin_backward_kernel(
    side,
    where_ref,
    x_ref,
    v1_ref,
    g2_ref,
    g_ref,
    dkva_ref,
    dqb_ref,
    wqv_ref,
    wvq_ref,
    wsw_ref,
    qkv_ref,
    lse_ref,
    dz_ref,
    dqkv_ref,
    grad_ref,
    dg_ref,
    bias_ref,
    do_ref,
):
    is_last = where_ref[2]
    tokens = x_ref.shape[0]
    rows = side * side
    windows = tokens // rows
    de = nt(dkva_ref[:, 0:D], mat(wqv_ref, 1))
    de += nt(dkva_ref[:, D : 2 * D], mat(wqv_ref, 2))
    de += nt(dqb_ref[...], mat(wvq_ref, 0))
    part, dg3 = norm_back(v1_ref[...], g_ref[2:3, :], de)
    g1 = g2_ref[...] + part
    grad_ref[...] = g1
    dz = g1.astype(bf16)
    dz_ref[...] = dz
    do_ref[...] = nt(dz, mat(wsw_ref, 3)).astype(bf16)
    for w in range(windows):
        bias_ref[w] = window_bias(rows, side, is_last, 1 if w == windows - 1 else 0)
    low = low_half(rows)

    def back(pair, carry):
        for w in range(windows):
            at = slice(w * rows, (w + 1) * rows)
            queries = qkv_ref[at, pair_cols(pair)]
            keys = qkv_ref[at, pair_cols(pair, D)]
            values = qkv_ref[at, pair_cols(pair, 2 * D)]
            grads = do_ref[at, pair_cols(pair)]
            dq, dk, dv = [], [], []
            for half in range(2):
                scores = nt(queries * lane_half(half, SCALE, bf16), keys) + bias_ref[w]
                chances = jnp.exp(scores - column(lse_ref[at, :], 2 * pair + half))
                slopes = nt(grads * lane_half(half, 1.0, bf16), values)
                centre = jnp.sum(chances * slopes, axis=-1, keepdims=True)
                ds = (chances * (slopes - centre)).astype(bf16)
                dq.append(nn(ds, keys))
                dk.append(tn(ds, queries))
                dv.append(tn(chances.astype(bf16), grads))
            for k, (pieces, factor) in enumerate(((dq, SCALE), (dk, SCALE), (dv, 1.0))):
                dqkv_ref[at, pair_cols(pair, k * D)] = (
                    jnp.where(low, pieces[0], pieces[1]) * factor
                ).astype(bf16)
        return carry

    lax.fori_loop(0, PAIRS, back, 0)
    da = nt(dqkv_ref[:, 0:D], mat(wsw_ref, 0))
    da += nt(dqkv_ref[:, D : 2 * D], mat(wsw_ref, 1))
    da += nt(dqkv_ref[:, 2 * D : 3 * D], mat(wsw_ref, 2))
    part, dg1 = norm_back(x_ref[...].astype(f32), g_ref[0:1, :], da)
    grad_ref[...] += part
    dg_ref[...] = jnp.concatenate([dg1, dg3], axis=0)


def self_backward_kernel(
    where_ref,
    dc_ref,
    y1_ref,
    cot_ref,
    g_ref,
    w_ref,
    q_ref,
    kv_ref,
    lse_ref,
    gy1_ref,
    dz_ref,
    dq_ref,
    dkvt_ref,
    db_ref,
    dbq_ref,
    dg_ref,
    bias_ref,
    do_ref,
):
    first_row, live = where_ref[0], where_ref[1]
    own_rows, slots = q_ref.shape[0], kv_ref.shape[0]
    part, dg = norm_back(y1_ref[...], g_ref[3:4, :], dc_ref[...].astype(f32))
    dg_ref[...] = dg
    gy1 = cot_ref[...].astype(f32) + part
    gy1_ref[...] = gy1
    dz = gy1.astype(bf16)
    dz_ref[...] = dz
    do_ref[...] = nt(dz, mat(w_ref, 3)).astype(bf16)
    self_bias(bias_ref, first_row, live)
    low = low_half(own_rows)

    def back(pair, carry):
        queries = q_ref[:, pair_cols(pair)]
        keys = kv_ref[:, pair_cols(pair)]
        values = kv_ref[:, pair_cols(pair, D)]
        grads = do_ref[:, pair_cols(pair)]
        queries_t = (queries * SCALE).astype(f32).T.astype(bf16)
        grads_t = grads.astype(f32).T.astype(bf16)
        parts = []
        for half in range(2):
            own = slice(half * HD, (half + 1) * HD)
            scores = nt(queries * lane_half(half, SCALE, bf16), keys) + bias_ref[...]
            chances = jnp.exp(scores - column(lse_ref[...], 2 * pair + half))
            slopes = nt(grads * lane_half(half, 1.0, bf16), values)
            centre = jnp.sum(chances * slopes, axis=-1, keepdims=True)
            ds = (chances * (slopes - centre)).astype(bf16)
            parts.append(nn(ds, keys))
            at = pair * PW + half * HD
            dkvt_ref[pl.ds(pl.multiple_of(at, HD), HD), :] = nn(queries_t[own], ds).astype(bf16)
            dkvt_ref[pl.ds(pl.multiple_of(D + at, HD), HD), :] = nn(
                grads_t[own], chances.astype(bf16)
            ).astype(bf16)
        dq_ref[:, pair_cols(pair)] = (jnp.where(low, parts[0], parts[1]) * SCALE).astype(bf16)
        return carry

    lax.fori_loop(0, PAIRS, back, 0)
    dbq_ref[...] = nt(dq_ref[...], mat(w_ref, 0))
    tile = 256
    for i in range(slots // tile):
        cols = slice(i * tile, (i + 1) * tile)
        total = nn(mat(w_ref, 1), dkvt_ref[0:D, cols])
        total += nn(mat(w_ref, 2), dkvt_ref[D : 2 * D, cols])
        db_ref[cols, :] = total.T.astype(bf16)


def query_end_kernel(db_ref, dbq_ref, y_ref, gy1_ref, g_ref, grad_ref, dg_ref):
    part, dg = norm_back(
        y_ref[...].astype(f32), g_ref[1:2, :], db_ref[...].astype(f32) + dbq_ref[...]
    )
    grad_ref[...] = gy1_ref[...] + part
    dg_ref[...] = dg


def window_order(grid_rows, half):
    rows, cols, _ = grid_rows.shape
    rolled = jnp.roll(grid_rows, -half, axis=1)
    shaped = rolled.reshape(rows, cols // rows, rows, D).transpose(1, 0, 2, 3)
    return shaped.reshape(rows * cols, D)


def grid_order(tokens_in, rows, cols, half):
    shaped = tokens_in.reshape(cols // rows, rows, rows, D).transpose(1, 0, 2, 3)
    return jnp.roll(shaped.reshape(rows, cols, D), half, axis=1)


def on_device(
    visual,
    query_tokens,
    answer_len,
    attn_swin,
    attn_self,
    attn_qv,
    attn_vq,
    mlp_up,
    mlp_down,
    norm_gains,
    visual_cot,
    query_cot,
):
    everyone = ("page", "blk")
    blk_count = lax.axis_size("blk")
    blk_here = lax.axis_index("blk")
    shards = lax.axis_size("page") * blk_count
    rows_here, cols_all = visual.shape[1], visual.shape[2]
    half = rows_here // 2
    tokens = rows_here * cols_all
    q_rows = query_tokens.shape[1]
    slots = q_rows * blk_count
    share = attn_swin.shape[0] // D
    aligned = share % 16 == 0
    gain_width = norm_gains.shape[0]

    def flat_share(value):
        return value.astype(bf16).reshape(share, D)

    up_share = (
        mlp_up.astype(bf16).reshape(share // 4, 4, D).transpose(1, 0, 2).reshape(share, D)
    )
    gain_row = jnp.pad(norm_gains.astype(bf16)[None], ((0, 15), (0, D - gain_width)))

    def gather(parts):
        joined = lax.all_gather(jnp.concatenate(parts, axis=0), everyone, axis=0, tiled=True)
        return joined.reshape(shards, -1, D)

    first = gather([flat_share(attn_self), flat_share(attn_swin), gain_row])
    second = gather([flat_share(attn_qv), flat_share(attn_vq)])
    third = gather([up_share, flat_share(mlp_down)])
    gains = first[:, 2 * share, :gain_width].reshape(8, D).astype(f32)

    def weight(joined, index):
        if aligned:
            return joined, pl.BlockSpec((shards, share, D), lambda i: (0, index, 0), pipeline_mode=pl.Buffered(1))
        taken = joined[:, index * share : (index + 1) * share].reshape(1, 4 * D, D)
        return taken, pl.BlockSpec((1, 4 * D, D), lambda i: (0, 0, 0), pipeline_mode=pl.Buffered(1))

    w_self, s_self = weight(first, 0)
    w_swin, s_swin = weight(first, 1)
    w_qv, s_qv = weight(second, 0)
    w_vq, s_vq = weight(second, 1)
    w_up = (
        third[:, :share].reshape(shards, 4, share // 4, D).transpose(1, 0, 2, 3).reshape(4, D, D)
    )
    w_down = third[:, share : 2 * share].reshape(4, D, D)

    query_all = lax.all_gather(query_tokens[0], "blk", axis=0, tiled=True)
    cot_all = lax.all_gather(query_cot[0], "blk", axis=0, tiled=True)
    down_one = [(i, (i - 1) % blk_count) for i in range(blk_count)]
    up_one = [(i, (i + 1) % blk_count) for i in range(blk_count)]
    both = jnp.concatenate([visual, visual_cot], axis=0)
    lent = lax.ppermute(both[:, :half], "blk", down_one)
    both = jnp.concatenate([both[:, half:], lent], axis=1)
    vis_in = window_order(both[0], half)
    vis_cot = window_order(both[1], half)

    where = jnp.stack(
        [blk_here * q_rows, answer_len[0], (blk_here == blk_count - 1).astype(jnp.int32)]
    ).astype(jnp.int32)

    b_all, q_self, kv_self, lse_self, o_self, y1, c_own = call(
        self_forward_kernel,
        [
            sds((slots, D), bf16),
            sds((q_rows, D), bf16),
            sds((slots, 2 * D), bf16),
            sds((q_rows, 128), f32),
            sds((q_rows, D), bf16),
            sds((q_rows, D), f32),
            sds((q_rows, D), bf16),
        ],
        [where, query_all, gains, w_self],
        scratch=[pltpu.VMEM((q_rows, slots), f32)],
        smem=1,
        blocks={3: s_self},
        flops=2 * slots * D * 2 * D,
        name="self_forward",
    )
    c_all = lax.all_gather(c_own, "blk", axis=0, tiled=True)

    def swin_forward(*refs):
        swin_forward_kernel(rows_here, *refs)

    a_low, qkv_swin, lse_swin, o_swin, v1, e_low = call(
        swin_forward,
        [
            sds((tokens, D), bf16),
            sds((tokens, 3 * D), bf16),
            sds((tokens, 128), f32),
            sds((tokens, D), bf16),
            sds((tokens, D), f32),
            sds((tokens, D), bf16),
        ],
        [where, vis_in, gains, w_swin],
        scratch=[pltpu.VMEM((cols_all // rows_here, rows_here**2, rows_here**2), f32)],
        smem=1,
        blocks={3: s_swin},
        flops=2 * tokens * D * 4 * D,
        name="swin_forward",
    )

    qa, kvb, doa, kva, qb, stats, lse_vq, o_vq = call(
        cross_forward_kernel,
        [
            sds((slots, D), bf16),
            sds((slots, 2 * D), bf16),
            sds((slots, D), bf16),
            sds((tokens, 2 * D), bf16),
            sds((tokens, D), bf16),
            sds((3, 16, slots), f32),
            sds((tokens, 128), f32),
            sds((tokens, D), bf16),
        ],
        [where, c_all, cot_all, e_low, w_qv, w_vq],
        smem=1,
        blocks={4: s_qv, 5: s_vq},
        flops=2 * slots * D * 4 * D + 2 * tokens * slots * D * 4,
        name="cross_forward",
    )

    all_stats = lax.all_gather(stats, "blk", axis=0)
    peaks = jnp.max(all_stats[:, 0], axis=0)
    weights = jnp.exp(all_stats[:, 0] - peaks[None])
    totals = jnp.sum(all_stats[:, 1] * weights, axis=0)
    lse_qv = peaks + jnp.log(totals)
    centre_qv = jnp.sum(all_stats[:, 2] * weights, axis=0) / totals

    v3, h_low, act_low, du_low, g2, dz_vq, dob, dg5 = mlp(
        v1, o_vq, vis_cot, gains, w_vq, s_vq, w_up, w_down
    )

    dqb, dkvbt = call(
        vq_backward_kernel,
        [sds((tokens, D), bf16), sds((2 * D, slots), bf16)],
        [where, qb, kvb, dob, lse_vq],
        smem=1,
        flops=2 * tokens * slots * D * 5,
        name="vq_backward",
    )
    oa_part, dqat, dkva = call(
        qv_backward_kernel,
        [sds((slots, D), bf16), sds((D, slots), bf16), sds((tokens, 2 * D), bf16)],
        [qa, kva, doa, lse_qv, centre_qv],
        flops=2 * tokens * slots * D * 6,
        name="qv_backward",
    )
    dc_part = call(
        slots_back_kernel,
        sds((slots, D), bf16),
        [dqat, dkvbt, w_qv, w_vq],
        blocks={2: s_qv, 3: s_vq},
        flops=2 * slots * D * D * 3,
        name="slots_back",
    )
    merged = lax.psum_scatter(
        jnp.concatenate([oa_part, dc_part], axis=1), "blk", scatter_dimension=0, tiled=True
    )
    oa_low, dc_low = merged[:, :D], merged[:, D:]

    def swin_backward(*refs):
        swin_backward_kernel(rows_here, *refs)

    dz_swin, dqkv_swin, visual_grad, dg_visual = call(
        swin_backward,
        [
            sds((tokens, D), bf16),
            sds((tokens, 3 * D), bf16),
            sds((tokens, D), f32),
            sds((2, D), f32),
        ],
        [where, vis_in, v1, g2, gains, dkva, dqb, w_qv, w_vq, w_swin, qkv_swin, lse_swin],
        scratch=[
            pltpu.VMEM((cols_all // rows_here, rows_here**2, rows_here**2), f32),
            pltpu.VMEM((tokens, D), bf16),
        ],
        smem=1,
        blocks={7: s_qv, 8: s_vq, 9: s_swin},
        flops=2 * tokens * D * 7 * D,
        name="swin_backward",
    )

    gy1, dz_self, dq_self, dkvt_self, db_part, dbq, dg4 = call(
        self_backward_kernel,
        [
            sds((q_rows, D), f32),
            sds((q_rows, D), bf16),
            sds((q_rows, D), bf16),
            sds((2 * D, slots), bf16),
            sds((slots, D), bf16),
            sds((q_rows, D), f32),
            sds((1, D), f32),
        ],
        [where, dc_low, y1, query_cot[0], gains, w_self, q_self, kv_self, lse_self],
        scratch=[pltpu.VMEM((q_rows, slots), f32), pltpu.VMEM((q_rows, D), bf16)],
        smem=1,
        blocks={5: s_self},
        flops=2 * slots * D * 2 * D,
        name="self_backward",
    )
    db = lax.psum_scatter(db_part, "blk", scatter_dimension=0, tiled=True)
    query_grad, dg2 = call(
        query_end_kernel,
        [sds((q_rows, D), f32), sds((1, D), f32)],
        [db, dbq, query_tokens[0], gy1, gains],
        name="query_end",
    )
    query_out = (y1 + jnp.dot(oa_low, w_out(first=w_qv, share=share, shards=shards, aligned=aligned),
                              preferred_element_type=f32)).astype(bf16)

    def outer(left, right):
        return tn(left, right).astype(bf16)

    def outer_t(left, right_t):
        return lax.dot_general(
            left, right_t, (((0,), (1,)), ((), ())), preferred_element_type=f32
        ).astype(bf16)

    def as_shares(mats):
        return jnp.concatenate(mats, axis=0).reshape(shards, share, D)

    def summed(parts):
        joined = jnp.concatenate(parts, axis=1)
        width = joined.shape[1]
        return lax.psum_scatter(
            joined.reshape(shards * width, D), everyone, scatter_dimension=0, tiled=True
        )

    up_mats = jnp.stack([outer(h_low, du_low[:, k * D : (k + 1) * D]) for k in range(4)])
    up_part = (
        up_mats.reshape(4, shards, share // 4, D).transpose(1, 0, 2, 3).reshape(shards, share, D)
    )
    down_part = outer(act_low, vis_cot).reshape(shards, share, D)
    mlp_sum = summed([up_part, down_part])

    qv_part = as_shares(
        [
            outer_t(c_all, dqat),
            outer(e_low, dkva[:, :D]),
            outer(e_low, dkva[:, D:]),
            outer(oa_low, query_cot[0]),
        ]
    )
    vq_part = as_shares(
        [
            outer(e_low, dqb),
            outer_t(c_all, dkvbt[:D]),
            outer_t(c_all, dkvbt[D:]),
            outer(o_vq, dz_vq),
        ]
    )
    cross_sum = summed([qv_part, vq_part])

    swin_part = as_shares(
        [outer(a_low, dqkv_swin[:, k * D : (k + 1) * D]) for k in range(3)]
        + [outer(o_swin, dz_swin)]
    )
    b_own = lax.dynamic_slice_in_dim(b_all, blk_here * q_rows, q_rows, 0)
    self_part = as_shares(
        [
            outer(b_own, dq_self),
            outer_t(b_all, dkvt_self[:D]),
            outer_t(b_all, dkvt_self[D:]),
            outer(o_self, dz_self),
        ]
    )
    gain_block = jnp.concatenate(
        [dg_visual[0:1], dg2, dg_visual[1:2], dg4, dg5, jnp.zeros((3, D), f32)], axis=0
    )
    gain_part = jnp.pad(
        gain_block.astype(bf16).reshape(shards, 1, gain_width),
        ((0, 0), (0, 15), (0, D - gain_width)),
    )
    last_sum = summed([swin_part, self_part, gain_part])

    def flat(value):
        return value.astype(f32).reshape(-1)

    up_grad = flat(mlp_sum[:share].reshape(4, share // 4, D).transpose(1, 0, 2))

    def back_to_grid(value):
        grid = grid_order(value, rows_here, cols_all, half)
        returned = lax.ppermute(grid[half:], "blk", up_one)
        return jnp.concatenate([returned, grid[:half]], axis=0)[None]

    return (
        back_to_grid(v3),
        query_out[None],
        back_to_grid(visual_grad),
        query_grad[None],
        flat(last_sum[:share]),
        flat(last_sum[share : 2 * share]),
        flat(cross_sum[:share]),
        flat(cross_sum[share : 2 * share]),
        up_grad,
        flat(mlp_sum[share : 2 * share]),
        flat(last_sum[2 * share, :gain_width]),
    )


def w_out(first, share, shards, aligned):
    if aligned:
        return first[3 * shards // 4 :, :share].reshape(D, D)
    return first[0, 3 * D :]


def solution(mesh):
    placed = (
        P("page", "blk", None, None),
        P("page", "blk", None),
        P("page"),
        P(("page", "blk")),
        P(("page", "blk")),
        P(("page", "blk")),
        P(("page", "blk")),
        P(("page", "blk")),
        P(("page", "blk")),
        P(("page", "blk")),
        P("page", "blk", None, None),
        P("page", "blk", None),
    )
    return jax.shard_map(
        on_device,
        mesh=mesh,
        in_specs=placed,
        out_specs=(
            P("page", "blk", None, None),
            P("page", "blk", None),
            P("page", "blk", None, None),
            P("page", "blk", None),
            P(("page", "blk")),
            P(("page", "blk")),
            P(("page", "blk")),
            P(("page", "blk")),
            P(("page", "blk")),
            P(("page", "blk")),
            P(("page", "blk")),
        ),
        check_vma=False,
    )
```

```python
import jax
import jax.numpy as jnp
from jax import lax
from jax.experimental import pallas as pl
from jax.experimental.pallas import tpu as pltpu
from jax.sharding import PartitionSpec as P

D = 768
HEADS = 12
HD = 64
FF = 3072
PAIRS = HEADS // 2
PW = 2 * HD
SCALE = HD ** (-0.5)

EPS = 1e-05
NEG = -1e30

bf16 = jnp.bfloat16
f32 = jnp.float32
VMEM_LIMIT = 56 * 1024 * 1024


def nn(left, right):
    return lax.dot_general(left, right, (((1,), (0,)), ((), ())), preferred_element_type=f32)


def nt(left, right):
    return lax.dot_general(left, right, (((1,), (1,)), ((), ())), preferred_element_type=f32)


def tn(left, right):
    return lax.dot_general(left, right, (((0,), (0,)), ((), ())), preferred_element_type=f32)


def norm_parts(rows):
    centre = jnp.mean(rows, axis=-1, keepdims=True)
    centred = rows - centre
    spread = jnp.mean(centred * centred, axis=-1, keepdims=True)
    inverse = lax.rsqrt(spread + EPS)
    return centred * inverse, inverse


def norm(rows, gain):
    return norm_parts(rows)[0] * gain


def norm_back(rows, gain, grad):
    unit, inverse = norm_parts(rows)
    grad_gain = jnp.sum(grad * unit, axis=0, keepdims=True)
    scaled = grad * gain
    first = jnp.mean(scaled, axis=-1, keepdims=True)
    second = jnp.mean(scaled * unit, axis=-1, keepdims=True)
    return inverse * (scaled - first - unit * second), grad_gain


def lane_half(half, value, dtype):
    lanes = lax.broadcasted_iota(jnp.int32, (1, PW), 1)
    return jnp.where((lanes // HD) == half, value, 0.0).astype(dtype)


def low_half(rows):
    return lax.broadcasted_iota(jnp.int32, (rows, PW), 1) < HD


def column(table, index):
    lanes = lax.broadcasted_iota(jnp.int32, table.shape, 1)
    return jnp.sum(jnp.where(lanes == index, table, 0.0), axis=-1, keepdims=True)


def pair_cols(pair, base=0):
    return pl.ds(pl.multiple_of(base + pair * PW, PW), PW)


def softmax_rows(scores):
    highest = jnp.max(scores, axis=-1, keepdims=True)
    raised = jnp.exp(scores - highest)
    totals = jnp.sum(raised, axis=-1, keepdims=True)
    return raised * (1.0 / totals), highest + jnp.log(totals)


class Stored:
    def __init__(self, arrays, lanes=(), joint=None):
        self.arrays = list(arrays)
        self.lanes = tuple(lanes)
        self.joint = joint


def stage_bits(lane):
    return (1, 2) if lane == 0 else (2, 1)


def relative(lane, core, first, second):
    bit_one, bit_two = stage_bits(lane)
    return core | (first << bit_one) | (second << bit_two)


def local_copy(source, target, sem):
    pltpu.make_async_copy(source, target, sem).start()


def fetch(where_ref, stored, refs, index, target, sem):
    if stored.joint is not None:
        first, rows = stored.joint
        count = D // rows
        for k in range(count):
            piece = refs[0].at[index * count + k, first : first + rows]
            local_copy(piece, target.at[k * rows : (k + 1) * rows], sem)
        return
    if len(refs) == 1:
        local_copy(refs[0].at[index], target, sem)
        return
    page, blk = where_ref[3], where_ref[4]
    count = len(stored.lanes)
    for number, lane in enumerate(stored.lanes):
        for core in range(2):
            for second in range(2):
                for first in range(2):
                    ref = refs[4 * number + 2 * core + second]
                    piece = ref.at[(index ^ page) + 4 * first]
                    rows = piece.shape[0]
                    owner = blk ^ relative(lane, core, first, second)
                    start = pl.multiple_of((owner * count + number) * rows, rows)
                    local_copy(piece, target.at[pl.ds(start, rows)], sem)


def fetch_up(where_ref, stored, refs, target, sem):
    if len(refs) == 1:
        local_copy(refs[0], target, sem)
        return
    page, blk = where_ref[3], where_ref[4]
    for core in range(2):
        for second in range(2):
            for first in range(2):
                ref = refs[2 * core + second]
                near = (blk ^ relative(stored.lanes[0], 0, first, second)) >> 1
                for origin in range(4):
                    piece = ref.at[(origin ^ page) + 4 * first]
                    rows = piece.shape[0] // 2
                    spot = pl.ds(pl.multiple_of((origin * 4 + near) * rows, rows), rows)
                    for k in range(2):
                        group = 2 * ((blk & 1) ^ core) + k
                        local_copy(piece.at[k * rows : (k + 1) * rows], target.at[group, spot], sem)


class Loads:
    def __init__(self, held, sems, plan):
        self.held, self.sems, self.plan, self.done = held, sems, plan, set()

    def ready(self, *places):
        for place in places:
            if place not in self.done:
                self.done.add(place)
                start, count = self.plan[place]
                span = self.held.at[start : start + count]
                pltpu.make_async_copy(span, span, self.sems.at[place]).wait()

    def __getitem__(self, place):
        self.ready(place)
        return self.held[self.plan[place][0]]

    def part(self, place, k):
        return self.held[self.plan[place][0] + k]


def call(kernel, outs, ins, scratch=(), smem=1, loads=(), slots=None, flops=0, name=None):
    def whole(value):
        zeros = (0,) * len(value.shape)
        return pl.BlockSpec(value.shape, lambda i: zeros, pipeline_mode=pl.Buffered(1))

    specs = []
    for index, value in enumerate(ins):
        if index < smem:
            specs.append(pl.BlockSpec(memory_space=pltpu.SMEM))
        else:
            specs.append(whole(value))
    single = not isinstance(outs, list)
    shapes = [outs] if single else outs
    count_in, count_out = len(ins), len(shapes)
    unique, plan, size = [], [], 0
    for stored, which in loads:
        if stored not in unique:
            unique.append(stored)
        width = 4 if which is None else 1
        plan.append((size, width))
        size += width
    arrays = [array for stored in unique for array in stored.arrays]
    gathered, slot_scratch = [], []
    if slots:
        gathered, part, own = slots
        blocks = len(gathered) if len(gathered) > 1 else gathered[0].shape[0]
        slot_scratch = [pltpu.VMEM((blocks, own, D), bf16), pltpu.SemaphoreType.DMA]
    held = [pltpu.VMEM((size, D, D), bf16), pltpu.SemaphoreType.DMA((len(plan),))] if loads else []

    def body(*refs):
        inner = list(refs[:count_in])
        at = count_in
        taken = {}
        for stored in unique:
            taken[id(stored)] = refs[at : at + len(stored.arrays)]
            at += len(stored.arrays)
        pieces = refs[at : at + len(gathered)]
        at += len(gathered)
        results = list(refs[at : at + count_out])
        rest = list(refs[at + count_out :])
        if slots:
            together, slot_sem = rest[:2]
            rest = rest[2:]
            rows = slice(part * own, (part + 1) * own)
            if len(pieces) == 1:
                local_copy(pieces[0].at[:, rows], together, slot_sem)
            for k, piece in enumerate(pieces if len(pieces) > 1 else ()):
                local_copy(piece.at[rows], together.at[inner[0][4] ^ k], slot_sem)
            inner.append(together)
        if not loads:
            kernel(*inner, *results, *rest)
            return
        kept, sems = rest[-2], rest[-1]
        for place, (stored, which) in enumerate(loads):
            mine, (start, width) = taken[id(stored)], plan[place]
            if which is None:
                fetch_up(inner[0], stored, mine, kept.at[start : start + width], sems.at[place])
            else:
                fetch(inner[0], stored, mine, which, kept.at[start], sems.at[place])
        if slots:
            pltpu.make_async_copy(together, together, slot_sem).wait()
        weights = Loads(kept, sems, plan)
        kernel(*inner, weights, *results, *rest[:-2])
        weights.ready(*range(len(plan)))

    moved = sum(v.size * v.dtype.itemsize for v in list(ins) + shapes) + size * D * D * 2
    result = pl.pallas_call(
        body,
        grid=(1,),
        out_shape=shapes,
        in_specs=specs + [pl.BlockSpec(memory_space=pl.ANY)] * (len(arrays) + len(gathered)),
        out_specs=[whole(value) for value in shapes],
        scratch_shapes=slot_scratch + list(scratch) + held,
        compiler_params=pltpu.CompilerParams(
            vmem_limit_bytes=VMEM_LIMIT, dimension_semantics=("arbitrary",)
        ),
        cost_estimate=pl.CostEstimate(flops=int(flops), bytes_accessed=int(moved), transcendentals=0),
        name=name,
    )(*ins, *arrays, *gathered)
    return result[0] if single else result


def sds(shape, dtype):
    return jax.ShapeDtypeStruct(shape, dtype)


def self_bias(bias_ref, first_row, live):
    rows, slots = bias_ref.shape
    keys = lax.broadcasted_iota(jnp.int32, (rows, slots), 1)
    places = lax.broadcasted_iota(jnp.int32, (rows, slots), 0) + first_row
    bias_ref[...] = jnp.where((keys <= places) & (keys < live), 0.0, NEG)


def self_forward_kernel(
    where_ref, g_ref, y_ref, w, b_ref, q_ref, kv_ref, lse_ref, o_ref, y1_ref, c_ref, bias_ref
):
    first_row, live = where_ref[0], where_ref[1]
    slots, own = b_ref.shape[0], q_ref.shape[0]
    tile = 256
    group = tile // own
    w.ready(0, 1)

    def project(i, carry):
        rows = pl.ds(pl.multiple_of(i * tile, tile), tile)
        part = y_ref[pl.ds(i * group, group)].reshape(tile, D)
        normed = norm(part.astype(f32), g_ref[1:2, :]).astype(bf16)
        b_ref[rows, :] = normed
        kv_ref[rows, 0:D] = nn(normed, w[0]).astype(bf16)
        kv_ref[rows, D : 2 * D] = nn(normed, w[1]).astype(bf16)
        return carry

    lax.fori_loop(0, slots // tile, project, 0)
    mine = pl.ds(pl.multiple_of(first_row, 16), own)
    q_ref[...] = nn(b_ref[mine, :], w[2]).astype(bf16)
    self_bias(bias_ref, first_row, live)
    lse_ref[...] = jnp.zeros_like(lse_ref)
    lanes = lax.broadcasted_iota(jnp.int32, lse_ref.shape, 1)
    low = low_half(own)

    def attend(pair, carry):
        queries = q_ref[:, pair_cols(pair)]
        keys = kv_ref[:, pair_cols(pair)]
        values = kv_ref[:, pair_cols(pair, D)]
        mixed = []
        table = lse_ref[...]
        for half in range(2):
            scores = nt(queries * lane_half(half, SCALE, bf16), keys) + bias_ref[...]
            chances, log_totals = softmax_rows(scores)
            mixed.append(nn(chances.astype(bf16), values))
            table = jnp.where(lanes == 2 * pair + half, log_totals, table)
        lse_ref[...] = table
        o_ref[:, pair_cols(pair)] = jnp.where(low, mixed[0], mixed[1]).astype(bf16)
        return carry

    lax.fori_loop(0, PAIRS, attend, 0)
    y1 = y_ref[where_ref[4]].astype(f32) + nn(o_ref[...], w[3])
    y1_ref[...] = y1
    c_ref[...] = norm(y1, g_ref[3:4, :]).astype(bf16)


def window_bias(rows, side, row_split, col_split):
    def flags(shape, dim):
        token = lax.broadcasted_iota(jnp.int32, shape, dim)
        row, col = token // side, token % side
        return jnp.where(row >= side // 2, row_split, 0) + jnp.where(
            col >= side // 2, 2 * col_split, 0
        )

    return jnp.where(flags((rows, rows), 0) == flags((rows, rows), 1), 0.0, NEG)


def swin_forward_kernel(
    side, where_ref, x_ref, g_ref, w, a_ref, qkv_ref, lse_ref, o_ref, v1_ref, e_ref, bias_ref
):
    is_last = where_ref[2]
    tokens = x_ref.shape[0]
    rows = side * side
    windows = tokens // rows
    x = x_ref[...].astype(f32)
    normed = norm(x, g_ref[0:1, :]).astype(bf16)
    a_ref[...] = normed
    for k in range(3):
        qkv_ref[:, k * D : (k + 1) * D] = nn(normed, w[k]).astype(bf16)
    for win in range(windows):
        bias_ref[win] = window_bias(rows, side, is_last, 1 if win == windows - 1 else 0)
    lse_ref[...] = jnp.zeros_like(lse_ref)
    lanes = lax.broadcasted_iota(jnp.int32, (rows, lse_ref.shape[1]), 1)
    low = low_half(rows)

    def attend(pair, carry):
        for win in range(windows):
            at = slice(win * rows, (win + 1) * rows)
            queries = qkv_ref[at, pair_cols(pair)]
            keys = qkv_ref[at, pair_cols(pair, D)]
            values = qkv_ref[at, pair_cols(pair, 2 * D)]
            mixed = []
            table = lse_ref[at, :]
            for half in range(2):
                scores = nt(queries * lane_half(half, SCALE, bf16), keys) + bias_ref[win]
                chances, log_totals = softmax_rows(scores)
                mixed.append(nn(chances.astype(bf16), values))
                table = jnp.where(lanes == 2 * pair + half, log_totals, table)
            lse_ref[at, :] = table
            o_ref[at, pair_cols(pair)] = jnp.where(low, mixed[0], mixed[1]).astype(bf16)
        return carry

    lax.fori_loop(0, PAIRS, attend, 0)
    v1 = x + nn(o_ref[...], w[3])
    v1_ref[...] = v1
    e_ref[...] = norm(v1, g_ref[2:3, :]).astype(bf16)


def cross_forward_kernel(
    where_ref,
    c_ref,
    e_ref,
    cot_ref,
    w,
    qa_ref,
    kvb_ref,
    doa_ref,
    kva_ref,
    qb_ref,
    stats_ref,
):
    slots, tokens = qa_ref.shape[0], e_ref.shape[0]
    tile = 256
    normed = e_ref[...]
    for k in range(2):
        kva_ref[:, k * D : (k + 1) * D] = nn(normed, w[k]).astype(bf16)
    qb_ref[...] = nn(normed, w[2]).astype(bf16)
    w.ready(3, 4, 5, 6)
    group = tile // cot_ref.shape[1]

    def project(i, carry):
        rows = pl.ds(pl.multiple_of(i * tile, tile), tile)
        part = c_ref[rows, :]
        qa_ref[rows, :] = nn(part, w[3]).astype(bf16)
        for k in range(2):
            kvb_ref[rows, k * D : (k + 1) * D] = nn(part, w[4 + k]).astype(bf16)
        cot = cot_ref[pl.ds(i * group, group)].reshape(tile, D)
        doa_ref[rows, :] = nt(cot, w[6]).astype(bf16)
        return carry

    lax.fori_loop(0, slots // tile, project, 0)
    stats_ref[...] = jnp.zeros_like(stats_ref)

    def page_stats(pair, carry):
        keys = kva_ref[:, pair_cols(pair)]
        values = kva_ref[:, pair_cols(pair, D)]
        for half in range(2):
            head = 2 * pair + half
            keys_h = keys * lane_half(half, SCALE, bf16)
            values_h = values * lane_half(half, 1.0, bf16)
            for i in range(slots // tile):
                rows = slice(i * tile, (i + 1) * tile)
                scores = nt(keys_h, qa_ref[rows, pair_cols(pair)])
                highest = jnp.max(scores, axis=0, keepdims=True)
                raised = jnp.exp(scores - highest)
                grads = nt(values_h, doa_ref[rows, pair_cols(pair)])
                stats_ref[0, pl.ds(head, 1), rows] = highest
                stats_ref[1, pl.ds(head, 1), rows] = jnp.sum(raised, axis=0, keepdims=True)
                stats_ref[2, pl.ds(head, 1), rows] = jnp.sum(raised * grads, axis=0, keepdims=True)
        return carry

    lax.fori_loop(0, PAIRS, page_stats, 0)


def vq_forward_kernel(where_ref, qb_ref, kvb_ref, lse_ref, ob_ref):
    live = where_ref[1]
    tokens, slots = qb_ref.shape[0], kvb_ref.shape[0]
    lse_ref[...] = jnp.zeros_like(lse_ref)
    lanes = lax.broadcasted_iota(jnp.int32, lse_ref.shape, 1)
    low = low_half(tokens)
    bias = jnp.where(lax.broadcasted_iota(jnp.int32, (1, slots), 1) < live, 0.0, NEG)

    def attend(pair, carry):
        queries = qb_ref[:, pair_cols(pair)]
        keys = kvb_ref[:, pair_cols(pair)]
        values = kvb_ref[:, pair_cols(pair, D)]
        mixed = []
        table = lse_ref[...]
        for half in range(2):
            scores = nt(queries * lane_half(half, SCALE, bf16), keys) + bias
            chances, log_totals = softmax_rows(scores)
            mixed.append(nn(chances.astype(bf16), values))
            table = jnp.where(lanes == 2 * pair + half, log_totals, table)
        lse_ref[...] = table
        ob_ref[:, pair_cols(pair)] = jnp.where(low, mixed[0], mixed[1]).astype(bf16)
        return carry

    lax.fori_loop(0, PAIRS, attend, 0)


GELU_A = 0.7978845608028654
GELU_B = 0.044715


def mlp_kernel(
    where_ref,
    v1_ref,
    ob_ref,
    cot_ref,
    g_ref,
    w,
    v3_ref,
    h_ref,
    act_ref,
    du_ref,
    g2_ref,
    dz_ref,
    dob_ref,
    dg_ref,
    v2_ref,
    sum_ref,
    dh_ref,
):
    v2 = v1_ref[...] + nn(ob_ref[...], w[0])
    v2_ref[...] = v2
    sum_ref[...] = v2
    h_ref[...] = norm(v2, g_ref[4:5, :]).astype(bf16)
    dh_ref[...] = jnp.zeros_like(dh_ref)
    w.ready(1, 2, 3, 4, 5)

    def chunk(k, carry):
        up, down = w.part(1, k), w.part(2, k)
        at = pl.ds(pl.multiple_of(k * D, D), D)
        u = nn(h_ref[...], up)
        squared = u * u
        bend = jnp.tanh(GELU_A * (u + GELU_B * u * squared))
        act = (0.5 * u * (1.0 + bend)).astype(bf16)
        act_ref[:, at] = act
        slope = 0.5 * (1.0 + bend) + 0.5 * u * (1.0 - bend * bend) * GELU_A * (
            1.0 + 3.0 * GELU_B * squared
        )
        du = (nt(cot_ref[...], down) * slope).astype(bf16)
        du_ref[:, at] = du
        sum_ref[...] += nn(act, down)
        dh_ref[...] += nt(du, up)
        return carry

    lax.fori_loop(0, FF // D, chunk, 0)
    v3_ref[...] = sum_ref[...].astype(bf16)
    part, dg = norm_back(v2_ref[...], g_ref[4:5, :], dh_ref[...])
    dg_ref[...] = dg
    g2 = cot_ref[...].astype(f32) + part
    g2_ref[...] = g2
    dz = g2.astype(bf16)
    dz_ref[...] = dz
    dob_ref[...] = nt(dz, w[0]).astype(bf16)


def vq_backward_kernel(
    where_ref, qb_ref, kvb_ref, dob_ref, lse_ref, dqb_ref, dkvbt_ref
):
    live = where_ref[1]
    tokens, slots = qb_ref.shape[0], kvb_ref.shape[0]
    bias = jnp.where(lax.broadcasted_iota(jnp.int32, (1, slots), 1) < live, 0.0, NEG)
    low = low_half(tokens)

    def back(pair, carry):
        queries = qb_ref[:, pair_cols(pair)]
        keys = kvb_ref[:, pair_cols(pair)]
        values = kvb_ref[:, pair_cols(pair, D)]
        grads = dob_ref[:, pair_cols(pair)]
        queries_t = (queries * SCALE).astype(f32).T.astype(bf16)
        grads_t = grads.astype(f32).T.astype(bf16)
        parts = []
        for half in range(2):
            own = slice(half * HD, (half + 1) * HD)
            scores = nt(queries * lane_half(half, SCALE, bf16), keys) + bias
            chances = jnp.exp(scores - column(lse_ref[...], 2 * pair + half))
            slopes = nt(grads * lane_half(half, 1.0, bf16), values)
            centre = jnp.sum(chances * slopes, axis=-1, keepdims=True)
            ds = (chances * (slopes - centre)).astype(bf16)
            parts.append(nn(ds, keys))
            at = pair * PW + half * HD
            dkvbt_ref[pl.ds(pl.multiple_of(at, HD), HD), :] = nn(queries_t[own], ds).astype(bf16)
            dkvbt_ref[pl.ds(pl.multiple_of(D + at, HD), HD), :] = nn(
                grads_t[own], chances.astype(bf16)
            ).astype(bf16)
        dqb_ref[:, pair_cols(pair)] = (jnp.where(low, parts[0], parts[1]) * SCALE).astype(bf16)
        return carry

    lax.fori_loop(0, PAIRS, back, 0)


def hand_out(where_ref, held, outs):
    if len(outs) == 1:
        outs[0][...] = held[...]
        return
    rows = outs[0].shape[1]
    for core, out in enumerate(outs):
        for k in range(4):
            start = pl.multiple_of((where_ref[4] ^ (2 * k + core)) * rows, rows)
            out[k] = held[pl.ds(start, rows), :]


def qv_backward_kernel(
    where_ref,
    qa_ref,
    kva_ref,
    doa_ref,
    lse_ref,
    centre_ref,
    dkvbt_ref,
    w,
    dqat_ref,
    dkva_ref,
    *rest,
):
    dc_refs, held = rest[:-1], rest[-1]
    slots, tokens = qa_ref.shape[0], kva_ref.shape[0]
    low = low_half(tokens)
    tile = 512

    def back(pair, carry):
        keys = kva_ref[:, pair_cols(pair)]
        values = kva_ref[:, pair_cols(pair, D)]
        keys_t = (keys * SCALE).astype(f32).T.astype(bf16)
        values_t = values.astype(f32).T.astype(bf16)
        for i in range(slots // tile):
            rows = slice(i * tile, (i + 1) * tile)
            queries = qa_ref[rows, pair_cols(pair)]
            grads = doa_ref[rows, pair_cols(pair)]
            dk, dv, mixed = [], [], []
            for half in range(2):
                head = 2 * pair + half
                own = slice(half * HD, (half + 1) * HD)
                scores = nt(keys * lane_half(half, SCALE, bf16), queries)
                chances = jnp.exp(scores - lse_ref[pl.ds(head, 1), rows])
                slopes = nt(values * lane_half(half, 1.0, bf16), grads)
                ds = (chances * (slopes - centre_ref[pl.ds(head, 1), rows])).astype(bf16)
                rounded = chances.astype(bf16)
                mixed.append(nn(values_t[own], rounded))
                dqat_ref[pl.ds(pl.multiple_of(head * HD, HD), HD), rows] = nn(
                    keys_t[own], ds
                ).astype(bf16)
                dk.append(nn(ds, queries))
                dv.append(nn(rounded, grads))
            held[rows, pair_cols(pair, D)] = jnp.concatenate(mixed, axis=0).T.astype(bf16)
            dk_now = jnp.where(low, dk[0], dk[1]) * SCALE
            dv_now = jnp.where(low, dv[0], dv[1])
            if i == 0:
                dk_sum, dv_sum = dk_now, dv_now
            else:
                dk_sum, dv_sum = dk_sum + dk_now, dv_sum + dv_now
        dkva_ref[:, pair_cols(pair)] = dk_sum.astype(bf16)
        dkva_ref[:, pair_cols(pair, D)] = dv_sum.astype(bf16)
        return carry

    lax.fori_loop(0, PAIRS, back, 0)
    for i in range(slots // tile):
        cols = slice(i * tile, (i + 1) * tile)
        total = nn(w[0], dqat_ref[:, cols])
        total += nn(w[1], dkvbt_ref[0:D, cols])
        total += nn(w[2], dkvbt_ref[D : 2 * D, cols])
        held[cols, 0:D] = total.T.astype(bf16)
    hand_out(where_ref, held, dc_refs)


def swin_backward_kernel(
    side,
    where_ref,
    x_ref,
    v1_ref,
    g2_ref,
    g_ref,
    dkva_ref,
    dqb_ref,
    qkv_ref,
    lse_ref,
    w,
    dz_ref,
    dqkv_ref,
    grad_ref,
    dg_ref,
    bias_ref,
    do_ref,
):
    is_last = where_ref[2]
    tokens = x_ref.shape[0]
    rows = side * side
    windows = tokens // rows
    de = nt(dkva_ref[:, 0:D], w[0])
    de += nt(dkva_ref[:, D : 2 * D], w[1])
    de += nt(dqb_ref[...], w[2])
    part, dg3 = norm_back(v1_ref[...], g_ref[2:3, :], de)
    g1 = g2_ref[...] + part
    grad_ref[...] = g1
    dz = g1.astype(bf16)
    dz_ref[...] = dz
    do_ref[...] = nt(dz, w[3]).astype(bf16)
    for win in range(windows):
        bias_ref[win] = window_bias(rows, side, is_last, 1 if win == windows - 1 else 0)
    low = low_half(rows)

    def back(pair, carry):
        for win in range(windows):
            at = slice(win * rows, (win + 1) * rows)
            queries = qkv_ref[at, pair_cols(pair)]
            keys = qkv_ref[at, pair_cols(pair, D)]
            values = qkv_ref[at, pair_cols(pair, 2 * D)]
            grads = do_ref[at, pair_cols(pair)]
            dq, dk, dv = [], [], []
            for half in range(2):
                scores = nt(queries * lane_half(half, SCALE, bf16), keys) + bias_ref[win]
                chances = jnp.exp(scores - column(lse_ref[at, :], 2 * pair + half))
                slopes = nt(grads * lane_half(half, 1.0, bf16), values)
                centre = jnp.sum(chances * slopes, axis=-1, keepdims=True)
                ds = (chances * (slopes - centre)).astype(bf16)
                dq.append(nn(ds, keys))
                dk.append(tn(ds, queries))
                dv.append(tn(chances.astype(bf16), grads))
            for k, (pieces, factor) in enumerate(((dq, SCALE), (dk, SCALE), (dv, 1.0))):
                dqkv_ref[at, pair_cols(pair, k * D)] = (
                    jnp.where(low, pieces[0], pieces[1]) * factor
                ).astype(bf16)
        return carry

    lax.fori_loop(0, PAIRS, back, 0)
    da = nt(dqkv_ref[:, 0:D], w[4])
    da += nt(dqkv_ref[:, D : 2 * D], w[5])
    da += nt(dqkv_ref[:, 2 * D : 3 * D], w[6])
    part, dg1 = norm_back(x_ref[...].astype(f32), g_ref[0:1, :], da)
    grad_ref[...] += part
    dg_ref[...] = jnp.concatenate([dg1, dg3], axis=0)


def self_backward_kernel(
    where_ref,
    dc_ref,
    y1_ref,
    cot_ref,
    g_ref,
    q_ref,
    kv_ref,
    lse_ref,
    w,
    gy1_ref,
    dz_ref,
    dq_ref,
    dkvt_ref,
    dbq_ref,
    dg_ref,
    *rest,
):
    db_refs, (bias_ref, do_ref, db_held) = rest[:-3], rest[-3:]
    first_row, live = where_ref[0], where_ref[1]
    own_rows, slots = q_ref.shape[0], kv_ref.shape[0]
    part, dg = norm_back(y1_ref[...], g_ref[3:4, :], dc_ref[...].astype(f32))
    dg_ref[...] = dg
    gy1 = cot_ref[...].astype(f32) + part
    gy1_ref[...] = gy1
    dz = gy1.astype(bf16)
    dz_ref[...] = dz
    do_ref[...] = nt(dz, w[0]).astype(bf16)
    self_bias(bias_ref, first_row, live)
    low = low_half(own_rows)

    def back(pair, carry):
        queries = q_ref[:, pair_cols(pair)]
        keys = kv_ref[:, pair_cols(pair)]
        values = kv_ref[:, pair_cols(pair, D)]
        grads = do_ref[:, pair_cols(pair)]
        queries_t = (queries * SCALE).astype(f32).T.astype(bf16)
        grads_t = grads.astype(f32).T.astype(bf16)
        parts = []
        for half in range(2):
            own = slice(half * HD, (half + 1) * HD)
            scores = nt(queries * lane_half(half, SCALE, bf16), keys) + bias_ref[...]
            chances = jnp.exp(scores - column(lse_ref[...], 2 * pair + half))
            slopes = nt(grads * lane_half(half, 1.0, bf16), values)
            centre = jnp.sum(chances * slopes, axis=-1, keepdims=True)
            ds = (chances * (slopes - centre)).astype(bf16)
            parts.append(nn(ds, keys))
            at = pair * PW + half * HD
            dkvt_ref[pl.ds(pl.multiple_of(at, HD), HD), :] = nn(queries_t[own], ds).astype(bf16)
            dkvt_ref[pl.ds(pl.multiple_of(D + at, HD), HD), :] = nn(
                grads_t[own], chances.astype(bf16)
            ).astype(bf16)
        dq_ref[:, pair_cols(pair)] = (jnp.where(low, parts[0], parts[1]) * SCALE).astype(bf16)
        return carry

    lax.fori_loop(0, PAIRS, back, 0)
    dbq_ref[...] = nt(dq_ref[...], w[1])
    tile = 256
    for i in range(slots // tile):
        cols = slice(i * tile, (i + 1) * tile)
        total = nn(w[2], dkvt_ref[0:D, cols])
        total += nn(w[3], dkvt_ref[D : 2 * D, cols])
        db_held[cols, :] = total.T.astype(bf16)
    hand_out(where_ref, db_held, db_refs)


def query_end_kernel(
    where_ref, db_ref, dbq_ref, y_ref, gy1_ref, g_ref, y1_ref, oa_ref, w, grad_ref, dg_ref, out_ref
):
    part, dg = norm_back(
        y_ref[...].astype(f32), g_ref[1:2, :], db_ref[...].astype(f32) + dbq_ref[...]
    )
    grad_ref[...] = gy1_ref[...] + part
    dg_ref[...] = dg
    out_ref[...] = (y1_ref[...] + nn(oa_ref[...], w[0])).astype(bf16)


def weight_grad_call(where, weights, name, shards=0):
    arrays, items = [], []

    def place(value):
        for index, known in enumerate(arrays):
            if known is value:
                return index
        arrays.append(value)
        return len(arrays) - 1

    for lanes, kind, entries in weights:
        for index, (left, left_at, right, right_at, form) in enumerate(entries):
            items.append((lanes, kind, index, place(left), left_at, place(right), right_at, form))
    count = len(arrays)
    rows = D // 8 // len(weights[0][0])

    def body(*refs):
        where_ref = refs[0]
        ins = refs[1 : 1 + count]
        *outs, held, sems = refs[1 + count :]
        keep, send = outs[0], outs[-1]
        page, blk = where_ref[3], where_ref[4]

        def place_natural(slot, lane, kind, index):
            out, width = outs[0], 4 * D // shards
            each = width // 2
            for k in range(2 * D // width if kind == "up" else D // width):
                if kind == "up":
                    piece = held.at[slot, k * each : (k + 1) * each]
                    first = lane * width + (index % 2) * each
                    local_copy(
                        piece, out.at[2 * k + index // 2, first : first + each], sems.at[slot]
                    )
                else:
                    piece = held.at[slot, k * width : (k + 1) * width]
                    owner = index * (D // width) + k
                    spot = slice(lane * width, (lane + 1) * width)
                    local_copy(piece, out.at[owner, spot], sems.at[slot])

        def finish(slot):
            pltpu.make_async_copy(held.at[slot], held.at[slot], sems.at[slot]).wait()

        def place_up(slot, lane, index, core, first, second):
            near = (blk ^ relative(lane, 0, first, second)) >> 1
            group, k = index // 2, index % 2
            out = send if core else keep

            @pl.when(((blk & 1) ^ core) == group)
            def _():
                half = rows // 2
                for origin in range(4):
                    spot = first * 8 + second * 4 + (origin ^ page)
                    take = pl.ds(pl.multiple_of((origin * 4 + near) * half, half), half)
                    local_copy(
                        held.at[slot, take],
                        out.at[lane, spot, k * half : (k + 1) * half],
                        sems.at[slot],
                    )

        def place_rows(slot, lanes, index, core, first, second):
            out = send if core else keep
            for number, lane in enumerate(lanes):
                owner = blk ^ relative(lane, core, first, second)
                spot = first * 8 + second * 4 + (index ^ page)
                start = pl.multiple_of((owner * len(lanes) + number) * rows, rows)
                local_copy(held.at[slot, pl.ds(start, rows)], out.at[lane, spot], sems.at[slot])

        for step, (lanes, kind, index, left, left_at, right, right_at, form) in enumerate(items):
            slot = step % 2
            if step >= 2:
                finish(slot)
            lhs = ins[left][:, left_at * D : (left_at + 1) * D]
            if form == "tt":
                rhs = ins[right][right_at * D : (right_at + 1) * D, :]
                product = nt(lhs.astype(f32).T.astype(bf16), rhs)
            else:
                product = tn(lhs, ins[right][:, right_at * D : (right_at + 1) * D])
            held[slot] = product.astype(bf16)
            if shards:
                place_natural(slot, lanes[0], kind, index)
                continue
            for core in range(2):
                for first in range(2):
                    for second in range(2):
                        if kind == "up":
                            place_up(slot, lanes[0], index, core, first, second)
                        else:
                            place_rows(slot, lanes, index, core, first, second)
        for step in range(max(0, len(items) - 2), len(items)):
            finish(step % 2)

    shapes = [sds((2, 16, rows, D), bf16)] * 2
    if shards:
        shapes = [sds((shards, len(weights) * 4 * D // shards, D), bf16)]
    moved = 2 * len(items) * D * D + sum(v.size * 2 for v in arrays)
    return pl.pallas_call(
        body,
        grid=(1,),
        out_shape=shapes,
        in_specs=[pl.BlockSpec(memory_space=pltpu.SMEM)]
        + [
            pl.BlockSpec(v.shape, lambda i: (0, 0), pipeline_mode=pl.Buffered(1)) for v in arrays
        ],
        out_specs=[pl.BlockSpec(memory_space=pl.ANY)] * len(shapes),
        scratch_shapes=[pltpu.VMEM((2, D, D), bf16), pltpu.SemaphoreType.DMA((2,))],
        compiler_params=pltpu.CompilerParams(
            vmem_limit_bytes=VMEM_LIMIT, dimension_semantics=("arbitrary",)
        ),
        cost_estimate=pl.CostEstimate(
            flops=int(len(items) * 1.6e-6 * 1.1e15), bytes_accessed=int(moved), transcendentals=0
        ),
        name=name,
    )(where, *arrays)


def window_order(grid_rows, half):
    rows, cols, _ = grid_rows.shape
    rolled = jnp.roll(grid_rows, -half, axis=1)
    shaped = rolled.reshape(rows, cols // rows, rows, D).transpose(1, 0, 2, 3)
    return shaped.reshape(rows * cols, D)


def grid_order(tokens_in, rows, cols, half):
    shaped = tokens_in.reshape(cols // rows, rows, rows, D).transpose(1, 0, 2, 3)
    return jnp.roll(shaped.reshape(rows, cols, D), half, axis=1)


def after(value, *others):
    return lax.optimization_barrier((value, others))[0]


def swapped(value, axis, flip):
    count = lax.axis_size(axis)
    return lax.ppermute(value, axis, [(i, i ^ flip) for i in range(count)])


def from_pages(value):
    pages = lax.axis_size("page")
    return [value] + [swapped(value, "page", k) for k in range(1, pages)]


def spread_first(shares):
    parts = from_pages(jnp.stack(shares))
    return [jnp.stack([part[k] for part in parts]) for k in range(2)]


def spread_second(held):
    return [
        jnp.concatenate([held[0], swapped(held[0], "blk", 2)]),
        jnp.concatenate([held[1], swapped(held[1], "blk", 4)]),
    ]


def spread_third(near):
    return [swapped(near[0], "blk", 4), swapped(near[1], "blk", 2)]


def spread_core(held):
    return [swapped(value, "blk", 1) for value in held]


def lane_arrays(near, far, near_core, far_core, lane):
    return [near[lane], far[lane], near_core[lane], far_core[lane]]


def added(left, right):
    return (left.astype(f32) + right.astype(f32)).astype(bf16)


def collect_first(keep, send, *gate):
    got = swapped(send, "blk", 1)
    keep = after(keep, *gate)
    return [[added(keep[k, i : i + 8], got[k, i : i + 8]) for i in (0, 8)] for k in range(2)]


def collect_second(held, *gate):
    got = swapped(held[0][1], "blk", 2), swapped(held[1][1], "blk", 4)
    kept = after([held[0][0], held[1][0]], *gate)
    return [[added(kept[k][i : i + 4], got[k][i : i + 4]) for i in (0, 4)] for k in range(2)]


def collect_third(held, *gate):
    got = swapped(held[0][1], "blk", 4), swapped(held[1][1], "blk", 2)
    kept = after([held[0][0], held[1][0]], *gate)
    sums = [added(kept[k], got[k]) for k in range(2)]
    return [jnp.stack([sums[k][i] for k in range(2)]) for i in range(4)]


def collect_last(held, *gate):
    total = after(held[0], *gate).astype(f32)
    for k in range(1, 4):
        total = total + swapped(held[k], "page", k).astype(f32)
    return total


def collect_blocks(parts):
    if len(parts) == 1:
        return lax.psum_scatter(parts[0], "blk", scatter_dimension=0, tiled=True)
    keep, send = parts
    got = swapped(send, "blk", 1)
    chips = [added(keep[k], got[k]) for k in range(4)]
    total = chips[0].astype(f32)
    for k in range(1, 4):
        total = total + swapped(chips[k], "blk", 2 * k).astype(f32)
    return total.astype(bf16)


def summed_everywhere(value):
    for axis in ("blk", "page"):
        flip = 1
        while flip < lax.axis_size(axis):
            value = value + swapped(value, axis, flip)
            flip *= 2
    return value


def on_device(
    visual,
    query_tokens,
    answer_len,
    attn_swin,
    attn_self,
    attn_qv,
    attn_vq,
    mlp_up,
    mlp_down,
    norm_gains,
    visual_cot,
    query_cot,
):
    everyone = ("page", "blk")
    pages = lax.axis_size("page")
    page_here = lax.axis_index("page")
    blk_count = lax.axis_size("blk")
    blk_here = lax.axis_index("blk")
    shards = pages * blk_count
    rows_here, cols_all = visual.shape[1], visual.shape[2]
    half = rows_here // 2
    tokens = rows_here * cols_all
    q_rows = query_tokens.shape[1]
    slots = q_rows * blk_count
    share = attn_swin.shape[0] // D
    staged = pages == 4 and blk_count == 8 and share % 32 == 0
    gain_width = norm_gains.shape[0]
    core_here = blk_here % 2

    where = jnp.stack(
        [
            blk_here * q_rows,
            answer_len[0],
            (blk_here == blk_count - 1).astype(jnp.int32),
            page_here,
            blk_here,
        ]
    ).astype(jnp.int32)

    def flat_share(value):
        return value.astype(bf16).reshape(share, D)

    gain_pages = jnp.concatenate(from_pages(norm_gains.astype(bf16)))[None]
    gain_rows = jnp.pad(gain_pages, ((0, 15), (0, D - pages * gain_width)))
    slot_own = jnp.concatenate([query_tokens[0], query_cot[0], gain_rows], axis=0)
    slots_joined = lax.all_gather(slot_own, "blk", axis=0)
    slot_arrays = [slots_joined]
    gain_parts = slots_joined[:, 2 * q_rows, : pages * gain_width]
    gain_parts = gain_parts.reshape(blk_count, pages, gain_width)
    gains = jnp.take(gain_parts, jnp.arange(pages) ^ page_here, axis=1)
    gains = gains.transpose(1, 0, 2).reshape(8, D).astype(f32)
    if staged:
        a_z = spread_first([flat_share(attn_self), flat_share(attn_swin)])
        a_near = spread_second(a_z)
        c_z = spread_first(after([flat_share(attn_qv), flat_share(attn_vq)], a_z))
        a_far = spread_third(a_near)
        a_near_core, a_far_core = spread_core(a_near), spread_core(a_far)
        w_self, w_swin = [
            Stored(lane_arrays(a_near, a_far, a_near_core, a_far_core, k), (k,)) for k in range(2)
        ]
        up_groups = after(mlp_up, a_near).astype(bf16)
        up_groups = up_groups.reshape(share // 4, 2, 2, D).transpose(1, 2, 0, 3)
        mine = jnp.where(core_here == 0, up_groups[0], up_groups[1])
        other = swapped(jnp.where(core_here == 0, up_groups[1], up_groups[0]), "blk", 1)
        up_share = jnp.where(
            core_here == 0,
            jnp.concatenate([mine, other], axis=1),
            jnp.concatenate([other, mine], axis=1),
        ).reshape(share, D)
        d_z = spread_first(after([up_share, flat_share(mlp_down)], c_z))
        c_near = spread_second(after(c_z, a_far))
        c_far = spread_third(c_near)
        c_near_core, c_far_core = spread_core(c_near), spread_core(c_far)
        w_qv, w_vq = [
            Stored(lane_arrays(c_near, c_far, c_near_core, c_far_core, k), (k,)) for k in range(2)
        ]
        d_near = spread_second(after(d_z, c_far))
        d_far = spread_third(d_near)
        d_near_core, d_far_core = spread_core(d_near), spread_core(d_far)
        w_up, w_down = [
            Stored(lane_arrays(d_near, d_far, d_near_core, d_far_core, k), (k,)) for k in range(2)
        ]
    else:
        up_share = (
            mlp_up.astype(bf16).reshape(share // 4, 4, D).transpose(1, 0, 2).reshape(share, D)
        )
        joined = lax.all_gather(
            jnp.concatenate(
                [flat_share(v) for v in (attn_self, attn_swin, attn_qv, attn_vq, mlp_down)]
                + [up_share],
                axis=0,
            ),
            everyone,
            axis=0,
            tiled=True,
        ).reshape(shards, -1, D)
        w_self, w_swin, w_qv, w_vq, w_down = [
            Stored([joined[:, k * share : (k + 1) * share].reshape(4, D, D)]) for k in range(5)
        ]
        up_all = joined[:, 5 * share : 6 * share].reshape(shards, 4, share // 4, D)
        w_up = Stored([up_all.transpose(1, 0, 2, 3).reshape(4, D, D)])

    down_one = [(i, (i - 1) % blk_count) for i in range(blk_count)]
    up_one = [(i, (i + 1) % blk_count) for i in range(blk_count)]
    both = jnp.concatenate([visual, visual_cot], axis=0)
    if staged:
        both = after(both, a_near)
    lent = lax.ppermute(both[:, :half], "blk", down_one)
    both = jnp.concatenate([both[:, half:], lent], axis=1)
    vis_in = window_order(both[0], half)
    vis_cot = window_order(both[1], half)

    b_all, q_self, kv_self, lse_self, o_self, y1, c_own = call(
        self_forward_kernel,
        [
            sds((slots, D), bf16),
            sds((q_rows, D), bf16),
            sds((slots, 2 * D), bf16),
            sds((q_rows, 128), f32),
            sds((q_rows, D), bf16),
            sds((q_rows, D), f32),
            sds((q_rows, D), bf16),
        ],
        [where, gains],
        slots=(slot_arrays, 0, q_rows),
        scratch=[pltpu.VMEM((q_rows, slots), f32)],
        loads=[(w_self, 1), (w_self, 2), (w_self, 0), (w_self, 3)],
        flops=15e-6 * 1.1e15,
        name="self_forward",
    )
    c_all = lax.all_gather(c_own, "blk", axis=0, tiled=True)

    def swin_forward(*refs):
        swin_forward_kernel(rows_here, *refs)

    a_low, qkv_swin, lse_swin, o_swin, v1, e_low = call(
        swin_forward,
        [
            sds((tokens, D), bf16),
            sds((tokens, 3 * D), bf16),
            sds((tokens, 128), f32),
            sds((tokens, D), bf16),
            sds((tokens, D), f32),
            sds((tokens, D), bf16),
        ],
        [where, vis_in, gains],
        scratch=[pltpu.VMEM((cols_all // rows_here, rows_here**2, rows_here**2), f32)],
        loads=[(w_swin, k) for k in range(4)],
        flops=11e-6 * 1.1e15,
        name="swin_forward",
    )

    qa, kvb, doa, kva, qb, stats = call(
        cross_forward_kernel,
        [
            sds((slots, D), bf16),
            sds((slots, 2 * D), bf16),
            sds((slots, D), bf16),
            sds((tokens, 2 * D), bf16),
            sds((tokens, D), bf16),
            sds((3, 16, slots), f32),
        ],
        [where, c_all, e_low],
        slots=(slot_arrays, 1, q_rows),
        loads=[(w_qv, 1), (w_qv, 2), (w_vq, 0), (w_qv, 0), (w_vq, 1), (w_vq, 2), (w_qv, 3)],
        flops=18e-6 * 1.1e15,
        name="cross_forward",
    )
    lse_vq, o_vq = call(
        vq_forward_kernel,
        [sds((tokens, 128), f32), sds((tokens, D), bf16)],
        [where, qb, kvb],
        flops=11e-6 * 1.1e15,
        name="vq_forward",
    )

    all_stats = lax.all_gather(stats, "blk", axis=0)
    peaks = jnp.max(all_stats[:, 0], axis=0)
    weights = jnp.exp(all_stats[:, 0] - peaks[None])
    totals = jnp.sum(all_stats[:, 1] * weights, axis=0)
    lse_qv = peaks + jnp.log(totals)
    centre_qv = jnp.sum(all_stats[:, 2] * weights, axis=0) / totals

    v3, h_low, act_low, du_low, g2, dz_vq, dob, dg5 = call(
        mlp_kernel,
        [
            sds((tokens, D), bf16),
            sds((tokens, D), bf16),
            sds((tokens, FF), bf16),
            sds((tokens, FF), bf16),
            sds((tokens, D), f32),
            sds((tokens, D), bf16),
            sds((tokens, D), bf16),
            sds((1, D), f32),
        ],
        [where, v1, o_vq, vis_cot, gains],
        scratch=[pltpu.VMEM((tokens, D), f32)] * 3,
        loads=[(w_vq, 3), (w_up, None)] + [(w_down, k) for k in range(4)],
        flops=14e-6 * 1.1e15,
        name="mlp",
    )

    up_entries = [(h_low, 0, du_low, k, "tn") for k in range(4)]
    down_entries = [(act_low, k, vis_cot, 0, "tn") for k in range(4)]
    where_vq_back = where
    if staged:
        m_keep, m_send = weight_grad_call(
            where, [((0,), "up", up_entries), ((1,), "rows", down_entries)], "mlp_grads"
        )
        where_vq_back = after(where, m_keep)

    dqb, dkvbt = call(
        vq_backward_kernel,
        [sds((tokens, D), bf16), sds((2 * D, slots), bf16)],
        [where_vq_back, qb, kvb, dob, lse_vq],
        flops=16e-6 * 1.1e15,
        name="vq_backward",
    )
    dqat, dkva, *merged_parts = call(
        qv_backward_kernel,
        [sds((D, slots), bf16), sds((tokens, 2 * D), bf16)] + [sds((slots, 2 * D), bf16)],
        [where, qa, kva, doa, lse_qv, centre_qv, dkvbt],
        scratch=[pltpu.VMEM((slots, 2 * D), bf16)],
        loads=[(w_qv, 0), (w_vq, 1), (w_vq, 2)],
        flops=23e-6 * 1.1e15,
        name="qv_backward",
    )
    merged = collect_blocks(merged_parts)
    dc, oa_low = merged[:, :D], merged[:, D:]

    def swin_backward(*refs):
        swin_backward_kernel(rows_here, *refs)

    dz_swin, dqkv_swin, visual_grad, dg_visual = call(
        swin_backward,
        [
            sds((tokens, D), bf16),
            sds((tokens, 3 * D), bf16),
            sds((tokens, D), f32),
            sds((2, D), f32),
        ],
        [where, vis_in, v1, g2, gains, dkva, dqb, qkv_swin, lse_swin],
        scratch=[
            pltpu.VMEM((cols_all // rows_here, rows_here**2, rows_here**2), f32),
            pltpu.VMEM((tokens, D), bf16),
        ],
        loads=[(w_qv, 1), (w_qv, 2), (w_vq, 0), (w_swin, 3)] + [(w_swin, k) for k in range(3)],
        flops=20e-6 * 1.1e15,
        name="swin_backward",
    )

    swin_entries = [(a_low, 0, dqkv_swin, k, "tn") for k in range(3)]
    swin_entries.append((o_swin, 0, dz_swin, 0, "tn"))
    vq_entries = [
        (e_low, 0, dqb, 0, "tn"),
        (c_all, 0, dkvbt, 0, "tt"),
        (c_all, 0, dkvbt, 1, "tt"),
        (o_vq, 0, dz_vq, 0, "tn"),
    ]
    qv_entries = [
        (c_all, 0, dqat, 0, "tt"),
        (e_low, 0, dkva, 0, "tn"),
        (e_low, 0, dkva, 1, "tn"),
        (oa_low, 0, query_cot[0], 0, "tn"),
    ]
    if staged:
        p_keep, p_send = weight_grad_call(
            where, [((0,), "rows", vq_entries), ((1,), "rows", swin_entries)], "patch_grads"
        )

    gy1, dz_self, dq_self, dkvt_self, dbq, dg4, *db_parts = call(
        self_backward_kernel,
        [
            sds((q_rows, D), f32),
            sds((q_rows, D), bf16),
            sds((q_rows, D), bf16),
            sds((2 * D, slots), bf16),
            sds((q_rows, D), f32),
            sds((1, D), f32),
        ]
        + ([sds((4, q_rows, D), bf16)] * 2 if staged else [sds((slots, D), bf16)]),
        [where, dc, y1, query_cot[0], gains, q_self, kv_self, lse_self],
        scratch=[
            pltpu.VMEM((q_rows, slots), f32),
            pltpu.VMEM((q_rows, D), bf16),
            pltpu.VMEM((slots, D), bf16),
        ],
        loads=[(w_self, 3), (w_self, 0), (w_self, 1), (w_self, 2)],
        flops=15e-6 * 1.1e15,
        name="self_backward",
    )
    b_own = lax.dynamic_slice_in_dim(b_all, blk_here * q_rows, q_rows, 0)
    self_entries = [
        (b_own, 0, dq_self, 0, "tn"),
        (b_all, 0, dkvt_self, 0, "tt"),
        (b_all, 0, dkvt_self, 1, "tt"),
        (o_self, 0, dz_self, 0, "tn"),
    ]
    db = collect_blocks(db_parts)
    where_end = where
    if staged:
        z_keep, z_send = weight_grad_call(
            where, [((0,), "rows", qv_entries), ((1,), "rows", self_entries)], "slot_grads"
        )
        m_one = collect_first(m_keep, m_send, dqb)
        m_two = collect_second(m_one, dz_swin)
        m_three = collect_third(m_two, gy1)
        mlp_sum = collect_last(m_three, z_keep)
        p_one = collect_first(p_keep, p_send, gy1)
        p_two = collect_second(p_one, z_keep)
        p_three = collect_third(p_two)
        z_one = collect_first(z_keep, z_send)
        where_end = after(where, z_keep)
    query_grad, dg2, query_out = call(
        query_end_kernel,
        [sds((q_rows, D), f32), sds((1, D), f32), sds((q_rows, D), bf16)],
        [where_end, db, dbq, query_tokens[0], gy1, gains, y1, oa_low],
        loads=[(w_qv, 3)],
        name="query_end",
    )

    gain_block = jnp.concatenate(
        [dg_visual[0:1], dg2, dg_visual[1:2], dg4, dg5, jnp.zeros((3, D), f32)], axis=0
    )
    gain_sum = summed_everywhere(gain_block)
    gain_grad = lax.dynamic_slice_in_dim(
        gain_sum.reshape(-1), (page_here * blk_count + blk_here) * gain_width, gain_width, 0
    )

    def flat(value):
        return value.astype(f32).reshape(-1)

    if staged:
        patch_sum = collect_last(p_three)
        slot_sum = collect_last(collect_third(collect_second(z_one)))
        up_sum = mlp_sum[0].reshape(2, 2, share // 4, D)
        up_mine = jnp.where(core_here == 0, up_sum[:, 0], up_sum[:, 1])
        up_other = swapped(jnp.where(core_here == 0, up_sum[:, 1], up_sum[:, 0]), "blk", 1)
        up_grad = jnp.where(
            core_here == 0,
            jnp.concatenate([up_mine, up_other], axis=0),
            jnp.concatenate([up_other, up_mine], axis=0),
        )
        up_grad = flat(up_grad.transpose(1, 0, 2))
        swin_grad, self_grad = flat(patch_sum[1]), flat(slot_sum[1])
        qv_grad, vq_grad = flat(slot_sum[0]), flat(patch_sum[0])
        down_grad = flat(mlp_sum[1])
    else:

        def outer(left, right):
            return tn(left, right).astype(bf16)

        def outer_t(left, right_t):
            return lax.dot_general(
                left, right_t, (((0,), (1,)), ((), ())), preferred_element_type=f32
            ).astype(bf16)

        def as_shares(mats):
            return jnp.concatenate(mats, axis=0).reshape(shards, share, D)

        def summed(parts):
            joined = jnp.concatenate(parts, axis=1)
            width = joined.shape[1]
            return lax.psum_scatter(
                joined.reshape(shards * width, D), everyone, scatter_dimension=0, tiled=True
            )

        up_mats = jnp.stack([outer(h_low, du_low[:, k * D : (k + 1) * D]) for k in range(4)])
        up_part = (
            up_mats.reshape(4, shards, share // 4, D)
            .transpose(1, 0, 2, 3)
            .reshape(shards, share, D)
        )
        down_part = outer(act_low, vis_cot).reshape(shards, share, D)
        mlp_sum = summed([up_part, down_part])
        qv_part = as_shares(
            [
                outer_t(c_all, dqat),
                outer(e_low, dkva[:, :D]),
                outer(e_low, dkva[:, D:]),
                outer(oa_low, query_cot[0]),
            ]
        )
        vq_part = as_shares(
            [
                outer(e_low, dqb),
                outer_t(c_all, dkvbt[:D]),
                outer_t(c_all, dkvbt[D:]),
                outer(o_vq, dz_vq),
            ]
        )
        cross_sum = summed([qv_part, vq_part])
        swin_part = as_shares(
            [outer(a_low, dqkv_swin[:, k * D : (k + 1) * D]) for k in range(3)]
            + [outer(o_swin, dz_swin)]
        )
        self_part = as_shares(
            [
                outer(b_own, dq_self),
                outer_t(b_all, dkvt_self[:D]),
                outer_t(b_all, dkvt_self[D:]),
                outer(o_self, dz_self),
            ]
        )
        last_sum = summed([swin_part, self_part])
        up_grad = flat(mlp_sum[:share].reshape(4, share // 4, D).transpose(1, 0, 2))
        down_grad = flat(mlp_sum[share:])
        qv_grad, vq_grad = flat(cross_sum[:share]), flat(cross_sum[share:])
        swin_grad, self_grad = flat(last_sum[:share]), flat(last_sum[share:])

    def back_to_grid(value):
        grid = grid_order(value, rows_here, cols_all, half)
        returned = lax.ppermute(grid[half:], "blk", up_one)
        return jnp.concatenate([returned, grid[:half]], axis=0)[None]

    return (
        back_to_grid(v3),
        query_out[None],
        back_to_grid(visual_grad),
        query_grad[None],
        swin_grad,
        self_grad,
        qv_grad,
        vq_grad,
        up_grad,
        down_grad,
        gain_grad,
    )


def solution(mesh):
    placed = (
        P("page", "blk", None, None),
        P("page", "blk", None),
        P("page"),
        P(("page", "blk")),
        P(("page", "blk")),
        P(("page", "blk")),
        P(("page", "blk")),
        P(("page", "blk")),
        P(("page", "blk")),
        P(("page", "blk")),
        P("page", "blk", None, None),
        P("page", "blk", None),
    )
    return jax.shard_map(
        on_device,
        mesh=mesh,
        in_specs=placed,
        out_specs=(
            P("page", "blk", None, None),
            P("page", "blk", None),
            P("page", "blk", None, None),
            P("page", "blk", None),
            P(("page", "blk")),
            P(("page", "blk")),
            P(("page", "blk")),
            P(("page", "blk")),
            P(("page", "blk")),
            P(("page", "blk")),
            P(("page", "blk")),
        ),
        check_vma=False,
    )
```

```python
import jax
import jax.numpy as jnp
from jax import lax
from jax.experimental import pallas as pl
from jax.experimental.pallas import tpu as pltpu
from jax.sharding import PartitionSpec as P

D = 768
HEADS = 12
HD = 64
FF = 3072
PAIRS = HEADS // 2
PW = 2 * HD
SCALE = HD ** (-0.5)

EPS = 1e-05
NEG = -1e30

bf16 = jnp.bfloat16
f32 = jnp.float32
VMEM_LIMIT = 56 * 1024 * 1024


def nn(left, right):
    return lax.dot_general(left, right, (((1,), (0,)), ((), ())), preferred_element_type=f32)


def nt(left, right):
    return lax.dot_general(left, right, (((1,), (1,)), ((), ())), preferred_element_type=f32)


def tn(left, right):
    return lax.dot_general(left, right, (((0,), (0,)), ((), ())), preferred_element_type=f32)


def norm_parts(rows):
    centre = jnp.mean(rows, axis=-1, keepdims=True)
    centred = rows - centre
    spread = jnp.mean(centred * centred, axis=-1, keepdims=True)
    inverse = lax.rsqrt(spread + EPS)
    return centred * inverse, inverse


def norm(rows, gain):
    return norm_parts(rows)[0] * gain


def norm_back(rows, gain, grad):
    unit, inverse = norm_parts(rows)
    grad_gain = jnp.sum(grad * unit, axis=0, keepdims=True)
    scaled = grad * gain
    first = jnp.mean(scaled, axis=-1, keepdims=True)
    second = jnp.mean(scaled * unit, axis=-1, keepdims=True)
    return inverse * (scaled - first - unit * second), grad_gain


def lane_half(half, value, dtype):
    lanes = lax.broadcasted_iota(jnp.int32, (1, PW), 1)
    return jnp.where((lanes // HD) == half, value, 0.0).astype(dtype)


def low_half(rows):
    return lax.broadcasted_iota(jnp.int32, (rows, PW), 1) < HD


def column(table, index):
    lanes = lax.broadcasted_iota(jnp.int32, table.shape, 1)
    return jnp.sum(jnp.where(lanes == index, table, 0.0), axis=-1, keepdims=True)


def pair_cols(pair, base=0):
    return pl.ds(pl.multiple_of(base + pair * PW, PW), PW)


def softmax_rows(scores):
    highest = jnp.max(scores, axis=-1, keepdims=True)
    raised = jnp.exp(scores - highest)
    totals = jnp.sum(raised, axis=-1, keepdims=True)
    return raised * (1.0 / totals), highest + jnp.log(totals)


class Stored:
    def __init__(self, arrays, lanes=(), joint=None):
        self.arrays = list(arrays)
        self.lanes = tuple(lanes)
        self.joint = joint


def stage_bits(lane):
    return (1, 2) if lane == 0 else (2, 1)


def relative(lane, core, first, second):
    bit_one, bit_two = stage_bits(lane)
    return core | (first << bit_one) | (second << bit_two)


def local_copy(source, target, sem):
    pltpu.make_async_copy(source, target, sem).start()


def fetch(where_ref, stored, refs, index, target, sem):
    if stored.joint is not None:
        first, rows = stored.joint
        count = D // rows
        for k in range(count):
            piece = refs[0].at[index * count + k, first : first + rows]
            local_copy(piece, target.at[k * rows : (k + 1) * rows], sem)
        return
    if len(refs) == 1:
        local_copy(refs[0].at[index], target, sem)
        return
    page, blk = where_ref[3], where_ref[4]
    count = len(stored.lanes)
    for number, lane in enumerate(stored.lanes):
        for core in range(2):
            for second in range(2):
                for first in range(2):
                    ref = refs[4 * number + 2 * core + second]
                    piece = ref.at[(index ^ page) + 4 * first]
                    rows = piece.shape[0]
                    owner = blk ^ relative(lane, core, first, second)
                    start = pl.multiple_of((owner * count + number) * rows, rows)
                    local_copy(piece, target.at[pl.ds(start, rows)], sem)


def fetch_up(where_ref, stored, refs, target, sem):
    if len(refs) == 1:
        local_copy(refs[0], target, sem)
        return
    page, blk = where_ref[3], where_ref[4]
    for core in range(2):
        for second in range(2):
            for first in range(2):
                ref = refs[2 * core + second]
                near = (blk ^ relative(stored.lanes[0], 0, first, second)) >> 1
                for origin in range(4):
                    piece = ref.at[(origin ^ page) + 4 * first]
                    rows = piece.shape[0] // 2
                    spot = pl.ds(pl.multiple_of((origin * 4 + near) * rows, rows), rows)
                    for k in range(2):
                        group = 2 * ((blk & 1) ^ core) + k
                        local_copy(piece.at[k * rows : (k + 1) * rows], target.at[group, spot], sem)


class Loads:
    def __init__(self, held, sems, plan):
        self.held, self.sems, self.plan, self.done = held, sems, plan, set()

    def ready(self, *places):
        for place in places:
            if place not in self.done:
                self.done.add(place)
                start, count = self.plan[place]
                span = self.held.at[start : start + count]
                pltpu.make_async_copy(span, span, self.sems.at[place]).wait()

    def __getitem__(self, place):
        self.ready(place)
        return self.held[self.plan[place][0]]

    def part(self, place, k):
        return self.held[self.plan[place][0] + k]


def call(kernel, outs, ins, scratch=(), smem=1, loads=(), slots=None, flops=0, name=None):
    def whole(value):
        zeros = (0,) * len(value.shape)
        return pl.BlockSpec(value.shape, lambda i: zeros, pipeline_mode=pl.Buffered(1))

    specs = []
    for index, value in enumerate(ins):
        if index < smem:
            specs.append(pl.BlockSpec(memory_space=pltpu.SMEM))
        else:
            specs.append(whole(value))
    single = not isinstance(outs, list)
    shapes = [outs] if single else outs
    count_in, count_out = len(ins), len(shapes)
    unique, plan, size = [], [], 0
    for stored, which in loads:
        if stored not in unique:
            unique.append(stored)
        width = 4 if which is None else 1
        plan.append((size, width))
        size += width
    arrays = [array for stored in unique for array in stored.arrays]
    gathered, slot_scratch = [], []
    if slots:
        gathered, part, own = slots
        blocks = len(gathered) if len(gathered) > 1 else gathered[0].shape[0]
        slot_scratch = [pltpu.VMEM((blocks, own, D), bf16), pltpu.SemaphoreType.DMA]
    held = [pltpu.VMEM((size, D, D), bf16), pltpu.SemaphoreType.DMA((len(plan),))] if loads else []

    def body(*refs):
        inner = list(refs[:count_in])
        at = count_in
        taken = {}
        for stored in unique:
            taken[id(stored)] = refs[at : at + len(stored.arrays)]
            at += len(stored.arrays)
        pieces = refs[at : at + len(gathered)]
        at += len(gathered)
        results = list(refs[at : at + count_out])
        rest = list(refs[at + count_out :])
        if slots:
            together, slot_sem = rest[:2]
            rest = rest[2:]
            rows = slice(part * own, (part + 1) * own)
            if len(pieces) == 1:
                local_copy(pieces[0].at[:, rows], together, slot_sem)
            for k, piece in enumerate(pieces if len(pieces) > 1 else ()):
                local_copy(piece.at[rows], together.at[inner[0][4] ^ k], slot_sem)
            inner.append(together)
        if not loads:
            kernel(*inner, *results, *rest)
            return
        kept, sems = rest[-2], rest[-1]
        for place, (stored, which) in enumerate(loads):
            mine, (start, width) = taken[id(stored)], plan[place]
            if which is None:
                fetch_up(inner[0], stored, mine, kept.at[start : start + width], sems.at[place])
            else:
                fetch(inner[0], stored, mine, which, kept.at[start], sems.at[place])
        if slots:
            pltpu.make_async_copy(together, together, slot_sem).wait()
        weights = Loads(kept, sems, plan)
        kernel(*inner, weights, *results, *rest[:-2])
        weights.ready(*range(len(plan)))

    moved = sum(v.size * v.dtype.itemsize for v in list(ins) + shapes) + size * D * D * 2
    result = pl.pallas_call(
        body,
        grid=(1,),
        out_shape=shapes,
        in_specs=specs + [pl.BlockSpec(memory_space=pl.ANY)] * (len(arrays) + len(gathered)),
        out_specs=[whole(value) for value in shapes],
        scratch_shapes=slot_scratch + list(scratch) + held,
        compiler_params=pltpu.CompilerParams(
            vmem_limit_bytes=VMEM_LIMIT, dimension_semantics=("arbitrary",)
        ),
        cost_estimate=pl.CostEstimate(flops=int(flops), bytes_accessed=int(moved), transcendentals=0),
        name=name,
    )(*ins, *arrays, *gathered)
    return result[0] if single else result


def sds(shape, dtype):
    return jax.ShapeDtypeStruct(shape, dtype)


def self_bias(bias_ref, first_row, live):
    rows, slots = bias_ref.shape
    keys = lax.broadcasted_iota(jnp.int32, (rows, slots), 1)
    places = lax.broadcasted_iota(jnp.int32, (rows, slots), 0) + first_row
    bias_ref[...] = jnp.where((keys <= places) & (keys < live), 0.0, NEG)


def self_forward_kernel(
    where_ref, g_ref, y_ref, w, b_ref, q_ref, kv_ref, lse_ref, o_ref, y1_ref, c_ref, bias_ref
):
    first_row, live = where_ref[0], where_ref[1]
    slots, own = b_ref.shape[0], q_ref.shape[0]
    tile = 256
    group = tile // own
    w.ready(0, 1)

    def project(i, carry):
        rows = pl.ds(pl.multiple_of(i * tile, tile), tile)
        part = y_ref[pl.ds(i * group, group)].reshape(tile, D)
        normed = norm(part.astype(f32), g_ref[1:2, :]).astype(bf16)
        b_ref[rows, :] = normed
        kv_ref[rows, 0:D] = nn(normed, w[0]).astype(bf16)
        kv_ref[rows, D : 2 * D] = nn(normed, w[1]).astype(bf16)
        return carry

    lax.fori_loop(0, slots // tile, project, 0)
    mine = pl.ds(pl.multiple_of(first_row, 16), own)
    q_ref[...] = nn(b_ref[mine, :], w[2]).astype(bf16)
    self_bias(bias_ref, first_row, live)
    lse_ref[...] = jnp.zeros_like(lse_ref)
    lanes = lax.broadcasted_iota(jnp.int32, lse_ref.shape, 1)
    low = low_half(own)

    def attend(pair, carry):
        queries = q_ref[:, pair_cols(pair)]
        keys = kv_ref[:, pair_cols(pair)]
        values = kv_ref[:, pair_cols(pair, D)]
        mixed = []
        table = lse_ref[...]
        for half in range(2):
            scores = nt(queries * lane_half(half, SCALE, bf16), keys) + bias_ref[...]
            chances, log_totals = softmax_rows(scores)
            mixed.append(nn(chances.astype(bf16), values))
            table = jnp.where(lanes == 2 * pair + half, log_totals, table)
        lse_ref[...] = table
        o_ref[:, pair_cols(pair)] = jnp.where(low, mixed[0], mixed[1]).astype(bf16)
        return carry

    lax.fori_loop(0, PAIRS, attend, 0)
    y1 = y_ref[where_ref[4]].astype(f32) + nn(o_ref[...], w[3])
    y1_ref[...] = y1
    c_ref[...] = norm(y1, g_ref[3:4, :]).astype(bf16)


def window_bias(rows, side, row_split, col_split):
    def flags(shape, dim):
        token = lax.broadcasted_iota(jnp.int32, shape, dim)
        row, col = token // side, token % side
        return jnp.where(row >= side // 2, row_split, 0) + jnp.where(
            col >= side // 2, 2 * col_split, 0
        )

    return jnp.where(flags((rows, rows), 0) == flags((rows, rows), 1), 0.0, NEG)


def swin_forward_kernel(
    side, where_ref, x_ref, g_ref, w, a_ref, qkv_ref, lse_ref, o_ref, v1_ref, e_ref, bias_ref
):
    is_last = where_ref[2]
    tokens = x_ref.shape[0]
    rows = side * side
    windows = tokens // rows
    x = x_ref[...].astype(f32)
    normed = norm(x, g_ref[0:1, :]).astype(bf16)
    a_ref[...] = normed
    for k in range(3):
        qkv_ref[:, k * D : (k + 1) * D] = nn(normed, w[k]).astype(bf16)
    for win in range(windows):
        bias_ref[win] = window_bias(rows, side, is_last, 1 if win == windows - 1 else 0)
    lse_ref[...] = jnp.zeros_like(lse_ref)
    lanes = lax.broadcasted_iota(jnp.int32, (rows, lse_ref.shape[1]), 1)
    low = low_half(rows)

    def attend(pair, carry):
        for win in range(windows):
            at = slice(win * rows, (win + 1) * rows)
            queries = qkv_ref[at, pair_cols(pair)]
            keys = qkv_ref[at, pair_cols(pair, D)]
            values = qkv_ref[at, pair_cols(pair, 2 * D)]
            mixed = []
            table = lse_ref[at, :]
            for half in range(2):
                scores = nt(queries * lane_half(half, SCALE, bf16), keys) + bias_ref[win]
                chances, log_totals = softmax_rows(scores)
                mixed.append(nn(chances.astype(bf16), values))
                table = jnp.where(lanes == 2 * pair + half, log_totals, table)
            lse_ref[at, :] = table
            o_ref[at, pair_cols(pair)] = jnp.where(low, mixed[0], mixed[1]).astype(bf16)
        return carry

    lax.fori_loop(0, PAIRS, attend, 0)
    v1 = x + nn(o_ref[...], w[3])
    v1_ref[...] = v1
    e_ref[...] = norm(v1, g_ref[2:3, :]).astype(bf16)


def cross_forward_kernel(
    where_ref,
    c_ref,
    e_ref,
    cot_ref,
    w,
    qa_ref,
    kvb_ref,
    doa_ref,
    kva_ref,
    qb_ref,
    stats_ref,
):
    slots, tokens = qa_ref.shape[0], e_ref.shape[0]
    tile = 256
    normed = e_ref[...]
    for k in range(2):
        kva_ref[:, k * D : (k + 1) * D] = nn(normed, w[k]).astype(bf16)
    qb_ref[...] = nn(normed, w[2]).astype(bf16)
    w.ready(3, 4, 5, 6)
    group = tile // cot_ref.shape[1]

    def project(i, carry):
        rows = pl.ds(pl.multiple_of(i * tile, tile), tile)
        part = c_ref[rows, :]
        qa_ref[rows, :] = nn(part, w[3]).astype(bf16)
        for k in range(2):
            kvb_ref[rows, k * D : (k + 1) * D] = nn(part, w[4 + k]).astype(bf16)
        cot = cot_ref[pl.ds(i * group, group)].reshape(tile, D)
        doa_ref[rows, :] = nt(cot, w[6]).astype(bf16)
        return carry

    lax.fori_loop(0, slots // tile, project, 0)
    stats_ref[...] = jnp.zeros_like(stats_ref)

    def page_stats(pair, carry):
        keys = kva_ref[:, pair_cols(pair)]
        values = kva_ref[:, pair_cols(pair, D)]
        for half in range(2):
            head = 2 * pair + half
            keys_h = keys * lane_half(half, SCALE, bf16)
            values_h = values * lane_half(half, 1.0, bf16)
            for i in range(slots // tile):
                rows = slice(i * tile, (i + 1) * tile)
                scores = nt(keys_h, qa_ref[rows, pair_cols(pair)])
                highest = jnp.max(scores, axis=0, keepdims=True)
                raised = jnp.exp(scores - highest)
                grads = nt(values_h, doa_ref[rows, pair_cols(pair)])
                stats_ref[0, pl.ds(head, 1), rows] = highest
                stats_ref[1, pl.ds(head, 1), rows] = jnp.sum(raised, axis=0, keepdims=True)
                stats_ref[2, pl.ds(head, 1), rows] = jnp.sum(raised * grads, axis=0, keepdims=True)
        return carry

    lax.fori_loop(0, PAIRS, page_stats, 0)


def vq_forward_kernel(where_ref, qb_ref, kvb_ref, lse_ref, ob_ref):
    live = where_ref[1]
    tokens, slots = qb_ref.shape[0], kvb_ref.shape[0]
    lse_ref[...] = jnp.zeros_like(lse_ref)
    lanes = lax.broadcasted_iota(jnp.int32, lse_ref.shape, 1)
    low = low_half(tokens)
    bias = jnp.where(lax.broadcasted_iota(jnp.int32, (1, slots), 1) < live, 0.0, NEG)

    def attend(pair, carry):
        queries = qb_ref[:, pair_cols(pair)]
        keys = kvb_ref[:, pair_cols(pair)]
        values = kvb_ref[:, pair_cols(pair, D)]
        mixed = []
        table = lse_ref[...]
        for half in range(2):
            scores = nt(queries * lane_half(half, SCALE, bf16), keys) + bias
            chances, log_totals = softmax_rows(scores)
            mixed.append(nn(chances.astype(bf16), values))
            table = jnp.where(lanes == 2 * pair + half, log_totals, table)
        lse_ref[...] = table
        ob_ref[:, pair_cols(pair)] = jnp.where(low, mixed[0], mixed[1]).astype(bf16)
        return carry

    lax.fori_loop(0, PAIRS, attend, 0)


GELU_A = 0.7978845608028654
GELU_B = 0.044715


def mlp_kernel(
    where_ref,
    v1_ref,
    ob_ref,
    cot_ref,
    g_ref,
    w,
    v3_ref,
    h_ref,
    act_ref,
    du_ref,
    g2_ref,
    dz_ref,
    dob_ref,
    dg_ref,
    v2_ref,
    sum_ref,
    dh_ref,
):
    v2 = v1_ref[...] + nn(ob_ref[...], w[0])
    v2_ref[...] = v2
    sum_ref[...] = v2
    h_ref[...] = norm(v2, g_ref[4:5, :]).astype(bf16)
    dh_ref[...] = jnp.zeros_like(dh_ref)
    w.ready(1, 2, 3, 4, 5)

    def chunk(k, carry):
        up, down = w.part(1, k), w.part(2, k)
        at = pl.ds(pl.multiple_of(k * D, D), D)
        u = nn(h_ref[...], up)
        squared = u * u
        bend = jnp.tanh(GELU_A * (u + GELU_B * u * squared))
        act = (0.5 * u * (1.0 + bend)).astype(bf16)
        act_ref[:, at] = act
        slope = 0.5 * (1.0 + bend) + 0.5 * u * (1.0 - bend * bend) * GELU_A * (
            1.0 + 3.0 * GELU_B * squared
        )
        du = (nt(cot_ref[...], down) * slope).astype(bf16)
        du_ref[:, at] = du
        sum_ref[...] += nn(act, down)
        dh_ref[...] += nt(du, up)
        return carry

    lax.fori_loop(0, FF // D, chunk, 0)
    v3_ref[...] = sum_ref[...].astype(bf16)
    part, dg = norm_back(v2_ref[...], g_ref[4:5, :], dh_ref[...])
    dg_ref[...] = dg
    g2 = cot_ref[...].astype(f32) + part
    g2_ref[...] = g2
    dz = g2.astype(bf16)
    dz_ref[...] = dz
    dob_ref[...] = nt(dz, w[0]).astype(bf16)


def vq_backward_kernel(
    where_ref, qb_ref, kvb_ref, dob_ref, lse_ref, dqb_ref, dkvbt_ref
):
    live = where_ref[1]
    tokens, slots = qb_ref.shape[0], kvb_ref.shape[0]
    bias = jnp.where(lax.broadcasted_iota(jnp.int32, (1, slots), 1) < live, 0.0, NEG)
    low = low_half(tokens)

    def back(pair, carry):
        queries = qb_ref[:, pair_cols(pair)]
        keys = kvb_ref[:, pair_cols(pair)]
        values = kvb_ref[:, pair_cols(pair, D)]
        grads = dob_ref[:, pair_cols(pair)]
        queries_t = (queries * SCALE).astype(f32).T.astype(bf16)
        grads_t = grads.astype(f32).T.astype(bf16)
        parts = []
        for half in range(2):
            own = slice(half * HD, (half + 1) * HD)
            scores = nt(queries * lane_half(half, SCALE, bf16), keys) + bias
            chances = jnp.exp(scores - column(lse_ref[...], 2 * pair + half))
            slopes = nt(grads * lane_half(half, 1.0, bf16), values)
            centre = jnp.sum(chances * slopes, axis=-1, keepdims=True)
            ds = (chances * (slopes - centre)).astype(bf16)
            parts.append(nn(ds, keys))
            at = pair * PW + half * HD
            dkvbt_ref[pl.ds(pl.multiple_of(at, HD), HD), :] = nn(queries_t[own], ds).astype(bf16)
            dkvbt_ref[pl.ds(pl.multiple_of(D + at, HD), HD), :] = nn(
                grads_t[own], chances.astype(bf16)
            ).astype(bf16)
        dqb_ref[:, pair_cols(pair)] = (jnp.where(low, parts[0], parts[1]) * SCALE).astype(bf16)
        return carry

    lax.fori_loop(0, PAIRS, back, 0)


def hand_out(where_ref, held, outs):
    if len(outs) == 1:
        outs[0][...] = held[...]
        return
    rows = outs[0].shape[1]
    for core, out in enumerate(outs):
        for k in range(4):
            start = pl.multiple_of((where_ref[4] ^ (2 * k + core)) * rows, rows)
            out[k] = held[pl.ds(start, rows), :]


def qv_backward_kernel(
    where_ref,
    qa_ref,
    kva_ref,
    doa_ref,
    lse_ref,
    centre_ref,
    dkvbt_ref,
    w,
    dqat_ref,
    dkva_ref,
    *rest,
):
    dc_refs, held = rest[:-1], rest[-1]
    slots, tokens = qa_ref.shape[0], kva_ref.shape[0]
    low = low_half(tokens)
    tile = 512

    def back(pair, carry):
        keys = kva_ref[:, pair_cols(pair)]
        values = kva_ref[:, pair_cols(pair, D)]
        keys_t = (keys * SCALE).astype(f32).T.astype(bf16)
        values_t = values.astype(f32).T.astype(bf16)
        for i in range(slots // tile):
            rows = slice(i * tile, (i + 1) * tile)
            queries = qa_ref[rows, pair_cols(pair)]
            grads = doa_ref[rows, pair_cols(pair)]
            dk, dv, mixed = [], [], []
            for half in range(2):
                head = 2 * pair + half
                own = slice(half * HD, (half + 1) * HD)
                scores = nt(keys * lane_half(half, SCALE, bf16), queries)
                chances = jnp.exp(scores - lse_ref[pl.ds(head, 1), rows])
                slopes = nt(values * lane_half(half, 1.0, bf16), grads)
                ds = (chances * (slopes - centre_ref[pl.ds(head, 1), rows])).astype(bf16)
                rounded = chances.astype(bf16)
                mixed.append(nn(values_t[own], rounded))
                dqat_ref[pl.ds(pl.multiple_of(head * HD, HD), HD), rows] = nn(
                    keys_t[own], ds
                ).astype(bf16)
                dk.append(nn(ds, queries))
                dv.append(nn(rounded, grads))
            held[rows, pair_cols(pair, D)] = jnp.concatenate(mixed, axis=0).T.astype(bf16)
            dk_now = jnp.where(low, dk[0], dk[1]) * SCALE
            dv_now = jnp.where(low, dv[0], dv[1])
            if i == 0:
                dk_sum, dv_sum = dk_now, dv_now
            else:
                dk_sum, dv_sum = dk_sum + dk_now, dv_sum + dv_now
        dkva_ref[:, pair_cols(pair)] = dk_sum.astype(bf16)
        dkva_ref[:, pair_cols(pair, D)] = dv_sum.astype(bf16)
        return carry

    lax.fori_loop(0, PAIRS, back, 0)
    for i in range(slots // tile):
        cols = slice(i * tile, (i + 1) * tile)
        total = nn(w[0], dqat_ref[:, cols])
        total += nn(w[1], dkvbt_ref[0:D, cols])
        total += nn(w[2], dkvbt_ref[D : 2 * D, cols])
        held[cols, 0:D] = total.T.astype(bf16)
    hand_out(where_ref, held, dc_refs)


def swin_backward_kernel(
    side,
    where_ref,
    x_ref,
    v1_ref,
    g2_ref,
    g_ref,
    dkva_ref,
    dqb_ref,
    qkv_ref,
    lse_ref,
    w,
    dz_ref,
    dqkv_ref,
    grad_ref,
    dg_ref,
    bias_ref,
    do_ref,
):
    is_last = where_ref[2]
    tokens = x_ref.shape[0]
    rows = side * side
    windows = tokens // rows
    de = nt(dkva_ref[:, 0:D], w[0])
    de += nt(dkva_ref[:, D : 2 * D], w[1])
    de += nt(dqb_ref[...], w[2])
    part, dg3 = norm_back(v1_ref[...], g_ref[2:3, :], de)
    g1 = g2_ref[...] + part
    grad_ref[...] = g1
    dz = g1.astype(bf16)
    dz_ref[...] = dz
    do_ref[...] = nt(dz, w[3]).astype(bf16)
    for win in range(windows):
        bias_ref[win] = window_bias(rows, side, is_last, 1 if win == windows - 1 else 0)
    low = low_half(rows)

    def back(pair, carry):
        for win in range(windows):
            at = slice(win * rows, (win + 1) * rows)
            queries = qkv_ref[at, pair_cols(pair)]
            keys = qkv_ref[at, pair_cols(pair, D)]
            values = qkv_ref[at, pair_cols(pair, 2 * D)]
            grads = do_ref[at, pair_cols(pair)]
            dq, dk, dv = [], [], []
            for half in range(2):
                scores = nt(queries * lane_half(half, SCALE, bf16), keys) + bias_ref[win]
                chances = jnp.exp(scores - column(lse_ref[at, :], 2 * pair + half))
                slopes = nt(grads * lane_half(half, 1.0, bf16), values)
                centre = jnp.sum(chances * slopes, axis=-1, keepdims=True)
                ds = (chances * (slopes - centre)).astype(bf16)
                dq.append(nn(ds, keys))
                dk.append(tn(ds, queries))
                dv.append(tn(chances.astype(bf16), grads))
            for k, (pieces, factor) in enumerate(((dq, SCALE), (dk, SCALE), (dv, 1.0))):
                dqkv_ref[at, pair_cols(pair, k * D)] = (
                    jnp.where(low, pieces[0], pieces[1]) * factor
                ).astype(bf16)
        return carry

    lax.fori_loop(0, PAIRS, back, 0)
    da = nt(dqkv_ref[:, 0:D], w[4])
    da += nt(dqkv_ref[:, D : 2 * D], w[5])
    da += nt(dqkv_ref[:, 2 * D : 3 * D], w[6])
    part, dg1 = norm_back(x_ref[...].astype(f32), g_ref[0:1, :], da)
    grad_ref[...] += part
    dg_ref[...] = jnp.concatenate([dg1, dg3], axis=0)


def self_backward_kernel(
    where_ref,
    dc_ref,
    y1_ref,
    cot_ref,
    g_ref,
    q_ref,
    kv_ref,
    lse_ref,
    y_ref,
    w,
    gy1_ref,
    dz_ref,
    dq_ref,
    dkvt_ref,
    dbq_ref,
    dg_ref,
    *rest,
):
    db_refs, (bias_ref, do_ref, db_held) = rest[:-3], rest[-3:]
    group = 256 // q_ref.shape[0]
    first_row, live = where_ref[0], where_ref[1]
    own_rows, slots = q_ref.shape[0], kv_ref.shape[0]
    part, dg = norm_back(y1_ref[...], g_ref[3:4, :], dc_ref[...].astype(f32))
    gy1 = cot_ref[...].astype(f32) + part
    gy1_ref[...] = gy1
    dz = gy1.astype(bf16)
    dz_ref[...] = dz
    do_ref[...] = nt(dz, w[0]).astype(bf16)
    self_bias(bias_ref, first_row, live)
    low = low_half(own_rows)

    def back(pair, carry):
        queries = q_ref[:, pair_cols(pair)]
        keys = kv_ref[:, pair_cols(pair)]
        values = kv_ref[:, pair_cols(pair, D)]
        grads = do_ref[:, pair_cols(pair)]
        queries_t = (queries * SCALE).astype(f32).T.astype(bf16)
        grads_t = grads.astype(f32).T.astype(bf16)
        parts = []
        for half in range(2):
            own = slice(half * HD, (half + 1) * HD)
            scores = nt(queries * lane_half(half, SCALE, bf16), keys) + bias_ref[...]
            chances = jnp.exp(scores - column(lse_ref[...], 2 * pair + half))
            slopes = nt(grads * lane_half(half, 1.0, bf16), values)
            centre = jnp.sum(chances * slopes, axis=-1, keepdims=True)
            ds = (chances * (slopes - centre)).astype(bf16)
            parts.append(nn(ds, keys))
            at = pair * PW + half * HD
            dkvt_ref[pl.ds(pl.multiple_of(at, HD), HD), :] = nn(queries_t[own], ds).astype(bf16)
            dkvt_ref[pl.ds(pl.multiple_of(D + at, HD), HD), :] = nn(
                grads_t[own], chances.astype(bf16)
            ).astype(bf16)
        dq_ref[:, pair_cols(pair)] = (jnp.where(low, parts[0], parts[1]) * SCALE).astype(bf16)
        return carry

    lax.fori_loop(0, PAIRS, back, 0)
    dbq = nt(dq_ref[...], w[1])
    dbq_ref[...] = dbq
    unit = norm_parts(y_ref[where_ref[4]].astype(f32))[0]
    dg2 = jnp.sum(dbq * unit, axis=0, keepdims=True)
    tile = 256
    for i in range(slots // tile):
        cols = slice(i * tile, (i + 1) * tile)
        total = nn(w[2], dkvt_ref[0:D, cols])
        total += nn(w[3], dkvt_ref[D : 2 * D, cols])
        back = total.T
        db_held[cols, :] = back.astype(bf16)
        part = y_ref[i * group : (i + 1) * group].reshape(tile, D)
        unit = norm_parts(part.astype(f32))[0]
        dg2 += jnp.sum(back * unit, axis=0, keepdims=True)
    dg_ref[...] = jnp.concatenate([dg2, dg], axis=0)
    hand_out(where_ref, db_held, db_refs)


def query_end_kernel(
    where_ref, db_ref, dbq_ref, y_ref, gy1_ref, g_ref, y1_ref, oa_ref, w, grad_ref, out_ref
):
    part, _ = norm_back(
        y_ref[...].astype(f32), g_ref[1:2, :], db_ref[...].astype(f32) + dbq_ref[...]
    )
    grad_ref[...] = gy1_ref[...] + part
    out_ref[...] = (y1_ref[...] + nn(oa_ref[...], w[0])).astype(bf16)


def weight_grad_call(where, weights, name, shards=0):
    arrays, items = [], []

    def place(value):
        for index, known in enumerate(arrays):
            if known is value:
                return index
        arrays.append(value)
        return len(arrays) - 1

    for lanes, kind, entries in weights:
        for index, (left, left_at, right, right_at, form) in enumerate(entries):
            items.append((lanes, kind, index, place(left), left_at, place(right), right_at, form))
    count = len(arrays)
    rows = D // 8 // len(weights[0][0])

    def body(*refs):
        where_ref = refs[0]
        ins = refs[1 : 1 + count]
        *outs, held, sems = refs[1 + count :]
        keep, send = outs[0], outs[-1]
        page, blk = where_ref[3], where_ref[4]

        def place_natural(slot, lane, kind, index):
            out, width = outs[0], 4 * D // shards
            each = width // 2
            for k in range(2 * D // width if kind == "up" else D // width):
                if kind == "up":
                    piece = held.at[slot, k * each : (k + 1) * each]
                    first = lane * width + (index % 2) * each
                    local_copy(
                        piece, out.at[2 * k + index // 2, first : first + each], sems.at[slot]
                    )
                else:
                    piece = held.at[slot, k * width : (k + 1) * width]
                    owner = index * (D // width) + k
                    spot = slice(lane * width, (lane + 1) * width)
                    local_copy(piece, out.at[owner, spot], sems.at[slot])

        def finish(slot):
            pltpu.make_async_copy(held.at[slot], held.at[slot], sems.at[slot]).wait()

        def place_up(slot, lane, index, core, first, second):
            near = (blk ^ relative(lane, 0, first, second)) >> 1
            group, k = index // 2, index % 2
            out = send if core else keep

            @pl.when(((blk & 1) ^ core) == group)
            def _():
                half = rows // 2
                for origin in range(4):
                    spot = first * 8 + second * 4 + (origin ^ page)
                    take = pl.ds(pl.multiple_of((origin * 4 + near) * half, half), half)
                    local_copy(
                        held.at[slot, take],
                        out.at[lane, spot, k * half : (k + 1) * half],
                        sems.at[slot],
                    )

        def place_rows(slot, lanes, index, core, first, second):
            out = send if core else keep
            for number, lane in enumerate(lanes):
                owner = blk ^ relative(lane, core, first, second)
                spot = first * 8 + second * 4 + (index ^ page)
                start = pl.multiple_of((owner * len(lanes) + number) * rows, rows)
                local_copy(held.at[slot, pl.ds(start, rows)], out.at[lane, spot], sems.at[slot])

        for step, (lanes, kind, index, left, left_at, right, right_at, form) in enumerate(items):
            slot = step % 2
            if step >= 2:
                finish(slot)
            lhs = ins[left][:, left_at * D : (left_at + 1) * D]
            if form == "tt":
                rhs = ins[right][right_at * D : (right_at + 1) * D, :]
                product = nt(lhs.astype(f32).T.astype(bf16), rhs)
            else:
                product = tn(lhs, ins[right][:, right_at * D : (right_at + 1) * D])
            held[slot] = product.astype(bf16)
            if shards:
                place_natural(slot, lanes[0], kind, index)
                continue
            for core in range(2):
                for first in range(2):
                    for second in range(2):
                        if kind == "up":
                            place_up(slot, lanes[0], index, core, first, second)
                        else:
                            place_rows(slot, lanes, index, core, first, second)
        for step in range(max(0, len(items) - 2), len(items)):
            finish(step % 2)

    shapes = [sds((2, 16, rows, D), bf16)] * 2
    if shards:
        shapes = [sds((shards, len(weights) * 4 * D // shards, D), bf16)]
    moved = 2 * len(items) * D * D + sum(v.size * 2 for v in arrays)
    return pl.pallas_call(
        body,
        grid=(1,),
        out_shape=shapes,
        in_specs=[pl.BlockSpec(memory_space=pltpu.SMEM)]
        + [
            pl.BlockSpec(v.shape, lambda i: (0, 0), pipeline_mode=pl.Buffered(1)) for v in arrays
        ],
        out_specs=[pl.BlockSpec(memory_space=pl.ANY)] * len(shapes),
        scratch_shapes=[pltpu.VMEM((2, D, D), bf16), pltpu.SemaphoreType.DMA((2,))],
        compiler_params=pltpu.CompilerParams(
            vmem_limit_bytes=VMEM_LIMIT, dimension_semantics=("arbitrary",)
        ),
        cost_estimate=pl.CostEstimate(
            flops=int(len(items) * 1.6e-6 * 1.1e15), bytes_accessed=int(moved), transcendentals=0
        ),
        name=name,
    )(where, *arrays)


def window_order(grid_rows, half):
    rows, cols, _ = grid_rows.shape
    rolled = jnp.roll(grid_rows, -half, axis=1)
    shaped = rolled.reshape(rows, cols // rows, rows, D).transpose(1, 0, 2, 3)
    return shaped.reshape(rows * cols, D)


def grid_order(tokens_in, rows, cols, half):
    shaped = tokens_in.reshape(cols // rows, rows, rows, D).transpose(1, 0, 2, 3)
    return jnp.roll(shaped.reshape(rows, cols, D), half, axis=1)


def after(value, *others):
    return lax.optimization_barrier((value, others))[0]


def swapped(value, axis, flip):
    count = lax.axis_size(axis)
    return lax.ppermute(value, axis, [(i, i ^ flip) for i in range(count)])


def from_pages(value):
    pages = lax.axis_size("page")
    return [value] + [swapped(value, "page", k) for k in range(1, pages)]


def spread_first(shares):
    parts = from_pages(jnp.stack(shares))
    return [jnp.stack([part[k] for part in parts]) for k in range(2)]


def spread_second(held, *gate):
    got = swapped(held[0], "blk", 2), swapped(held[1], "blk", 4)
    held = after(held, *gate)
    return [jnp.concatenate([held[k], got[k]]) for k in range(2)]


def spread_third(near):
    return [swapped(near[0], "blk", 4), swapped(near[1], "blk", 2)]


def spread_core(held):
    return [swapped(value, "blk", 1) for value in held]


def lane_arrays(near, far, near_core, far_core, lane):
    return [near[lane], far[lane], near_core[lane], far_core[lane]]


def added(left, right):
    return (left.astype(f32) + right.astype(f32)).astype(bf16)


def collect_first(keep, send, *gate):
    got = swapped(send, "blk", 1)
    keep = after(keep, *gate)
    return [[added(keep[k, i : i + 8], got[k, i : i + 8]) for i in (0, 8)] for k in range(2)]


def collect_second(held, *gate):
    got = swapped(held[0][1], "blk", 2), swapped(held[1][1], "blk", 4)
    kept = after([held[0][0], held[1][0]], *gate)
    return [[added(kept[k][i : i + 4], got[k][i : i + 4]) for i in (0, 4)] for k in range(2)]


def collect_third(held, *gate):
    got = swapped(held[0][1], "blk", 4), swapped(held[1][1], "blk", 2)
    kept = after([held[0][0], held[1][0]], *gate)
    sums = [added(kept[k], got[k]) for k in range(2)]
    return [jnp.stack([sums[k][i] for k in range(2)]) for i in range(4)]


def collect_last(held, *gate):
    total = after(held[0], *gate).astype(f32)
    for k in range(1, 4):
        total = total + swapped(held[k], "page", k).astype(f32)
    return total


def blocks_in_chip(parts, gate):
    keep, send = parts
    got = swapped(send, "blk", 1)
    keep = after(keep, gate)
    return [added(keep[k], got[k]) for k in range(4)]


def blocks_over_chips(chips, gate):
    total = after(chips[0], gate).astype(f32)
    for k in range(1, 4):
        total = total + swapped(chips[k], "blk", 2 * k).astype(f32)
    return total


def scattered_blocks(part):
    return lax.psum_scatter(part, "blk", scatter_dimension=0, tiled=True)


def on_device(
    visual,
    query_tokens,
    answer_len,
    attn_swin,
    attn_self,
    attn_qv,
    attn_vq,
    mlp_up,
    mlp_down,
    norm_gains,
    visual_cot,
    query_cot,
):
    everyone = ("page", "blk")
    pages = lax.axis_size("page")
    page_here = lax.axis_index("page")
    blk_count = lax.axis_size("blk")
    blk_here = lax.axis_index("blk")
    shards = pages * blk_count
    rows_here, cols_all = visual.shape[1], visual.shape[2]
    half = rows_here // 2
    tokens = rows_here * cols_all
    q_rows = query_tokens.shape[1]
    slots = q_rows * blk_count
    share = attn_swin.shape[0] // D
    staged = pages == 4 and blk_count == 8 and share % 32 == 0
    gain_width = norm_gains.shape[0]
    core_here = blk_here % 2

    where = jnp.stack(
        [
            blk_here * q_rows,
            answer_len[0],
            (blk_here == blk_count - 1).astype(jnp.int32),
            page_here,
            blk_here,
        ]
    ).astype(jnp.int32)

    def flat_share(value):
        return value.astype(bf16).reshape(share, D)

    gain_rows = jnp.pad(norm_gains.astype(bf16)[None], ((0, 15), (0, D - gain_width)))
    slot_own = jnp.concatenate([query_tokens[0], query_cot[0], gain_rows], axis=0)
    slots_joined = lax.all_gather(slot_own, "blk", axis=0)
    slot_arrays = [slots_joined]
    gain_parts = jnp.stack(from_pages(slots_joined[:, 2 * q_rows, :gain_width].reshape(-1)))
    gains = jnp.take(gain_parts, jnp.arange(pages) ^ page_here, axis=0)
    gains = gains.reshape(8, D).astype(f32)
    if staged:
        a_z = spread_first([flat_share(attn_self), flat_share(attn_swin)])
        a_near = spread_second(a_z)
        c_z = spread_first(after([flat_share(attn_qv), flat_share(attn_vq)], a_z))
        a_far = spread_third(a_near)
        a_near_core, a_far_core = spread_core(a_near), spread_core(a_far)
        w_self, w_swin = [
            Stored(lane_arrays(a_near, a_far, a_near_core, a_far_core, k), (k,)) for k in range(2)
        ]
        up_groups = after(mlp_up, a_near).astype(bf16)
        up_groups = up_groups.reshape(share // 4, 2, 2, D).transpose(1, 2, 0, 3)
        mine = jnp.where(core_here == 0, up_groups[0], up_groups[1])
        other = swapped(jnp.where(core_here == 0, up_groups[1], up_groups[0]), "blk", 1)
        up_share = jnp.where(
            core_here == 0,
            jnp.concatenate([mine, other], axis=1),
            jnp.concatenate([other, mine], axis=1),
        ).reshape(share, D)
        d_z = spread_first(after([up_share, flat_share(mlp_down)], c_z))
        c_near = spread_second(after(c_z, a_far, gains))
        c_far = spread_third(c_near)
    else:
        up_share = (
            mlp_up.astype(bf16).reshape(share // 4, 4, D).transpose(1, 0, 2).reshape(share, D)
        )
        joined = lax.all_gather(
            jnp.concatenate(
                [flat_share(v) for v in (attn_self, attn_swin, attn_qv, attn_vq, mlp_down)]
                + [up_share],
                axis=0,
            ),
            everyone,
            axis=0,
            tiled=True,
        ).reshape(shards, -1, D)
        w_self, w_swin, w_qv, w_vq, w_down = [
            Stored([joined[:, k * share : (k + 1) * share].reshape(4, D, D)]) for k in range(5)
        ]
        up_all = joined[:, 5 * share : 6 * share].reshape(shards, 4, share // 4, D)
        w_up = Stored([up_all.transpose(1, 0, 2, 3).reshape(4, D, D)])

    down_one = [(i, (i - 1) % blk_count) for i in range(blk_count)]
    up_one = [(i, (i + 1) % blk_count) for i in range(blk_count)]
    both = jnp.concatenate([visual, visual_cot], axis=0)
    if staged:
        both = after(both, a_near)
    lent = lax.ppermute(both[:, :half], "blk", down_one)
    both = jnp.concatenate([both[:, half:], lent], axis=1)
    vis_in = window_order(both[0], half)
    vis_cot = window_order(both[1], half)

    where_self = where_swin = where_cross = where_vq = where
    if staged:
        where_self = after(where, vis_in, vis_cot)
    b_all, q_self, kv_self, lse_self, o_self, y1, c_own = call(
        self_forward_kernel,
        [
            sds((slots, D), bf16),
            sds((q_rows, D), bf16),
            sds((slots, 2 * D), bf16),
            sds((q_rows, 128), f32),
            sds((q_rows, D), bf16),
            sds((q_rows, D), f32),
            sds((q_rows, D), bf16),
        ],
        [where_self, gains],
        slots=(slot_arrays, 0, q_rows),
        scratch=[pltpu.VMEM((q_rows, slots), f32)],
        loads=[(w_self, 1), (w_self, 2), (w_self, 0), (w_self, 3)],
        flops=15e-6 * 1.1e15,
        name="self_forward",
    )
    if staged:
        c_far = after(c_far, c_own)
        c_near_core, c_far_core = spread_core(c_near), spread_core(c_far)
        w_qv, w_vq = [
            Stored(lane_arrays(c_near, c_far, c_near_core, c_far_core, k), (k,)) for k in range(2)
        ]
        where_swin = after(where, c_far)
        d_z = after(d_z, c_far)
    c_all = lax.all_gather(c_own, "blk", axis=0, tiled=True)

    def swin_forward(*refs):
        swin_forward_kernel(rows_here, *refs)

    a_low, qkv_swin, lse_swin, o_swin, v1, e_low = call(
        swin_forward,
        [
            sds((tokens, D), bf16),
            sds((tokens, 3 * D), bf16),
            sds((tokens, 128), f32),
            sds((tokens, D), bf16),
            sds((tokens, D), f32),
            sds((tokens, D), bf16),
        ],
        [where_swin, vis_in, gains],
        scratch=[pltpu.VMEM((cols_all // rows_here, rows_here**2, rows_here**2), f32)],
        loads=[(w_swin, k) for k in range(4)],
        flops=11e-6 * 1.1e15,
        name="swin_forward",
    )

    if staged:
        d_near = spread_second(d_z, e_low)
        d_far = spread_third(d_near)
        where_cross = after(where, d_near)
    qa, kvb, doa, kva, qb, stats = call(
        cross_forward_kernel,
        [
            sds((slots, D), bf16),
            sds((slots, 2 * D), bf16),
            sds((slots, D), bf16),
            sds((tokens, 2 * D), bf16),
            sds((tokens, D), bf16),
            sds((3, 16, slots), f32),
        ],
        [where_cross, c_all, e_low],
        slots=(slot_arrays, 1, q_rows),
        loads=[(w_qv, 1), (w_qv, 2), (w_vq, 0), (w_qv, 0), (w_vq, 1), (w_vq, 2), (w_qv, 3)],
        flops=18e-6 * 1.1e15,
        name="cross_forward",
    )
    if staged:
        d_far = after(d_far, qb)
        d_near_core, d_far_core = spread_core(d_near), spread_core(d_far)
        w_up, w_down = [
            Stored(lane_arrays(d_near, d_far, d_near_core, d_far_core, k), (k,)) for k in range(2)
        ]
        where_vq = after(where, d_far)
    lse_vq, o_vq = call(
        vq_forward_kernel,
        [sds((tokens, 128), f32), sds((tokens, D), bf16)],
        [where_vq, qb, kvb],
        flops=11e-6 * 1.1e15,
        name="vq_forward",
    )

    all_stats = lax.all_gather(stats, "blk", axis=0)
    peaks = jnp.max(all_stats[:, 0], axis=0)
    weights = jnp.exp(all_stats[:, 0] - peaks[None])
    totals = jnp.sum(all_stats[:, 1] * weights, axis=0)
    lse_qv = peaks + jnp.log(totals)
    centre_qv = jnp.sum(all_stats[:, 2] * weights, axis=0) / totals

    v3, h_low, act_low, du_low, g2, dz_vq, dob, dg5 = call(
        mlp_kernel,
        [
            sds((tokens, D), bf16),
            sds((tokens, D), bf16),
            sds((tokens, FF), bf16),
            sds((tokens, FF), bf16),
            sds((tokens, D), f32),
            sds((tokens, D), bf16),
            sds((tokens, D), bf16),
            sds((1, D), f32),
        ],
        [where, v1, o_vq, vis_cot, gains],
        scratch=[pltpu.VMEM((tokens, D), f32)] * 3,
        loads=[(w_vq, 3), (w_up, None)] + [(w_down, k) for k in range(4)],
        flops=14e-6 * 1.1e15,
        name="mlp",
    )

    def back_to_grid(value):
        grid = grid_order(value, rows_here, cols_all, half)
        returned = lax.ppermute(grid[half:], "blk", up_one)
        return jnp.concatenate([returned, grid[:half]], axis=0)[None]

    def flat(value):
        return value.astype(f32).reshape(-1)

    def gains_over_pages(db_all):
        gain_sum = db_all[q_rows, : pages * gain_width].reshape(pages, gain_width).astype(f32)
        kept = jnp.take(gain_sum, page_here, axis=0)
        for k in range(1, pages):
            kept = kept + swapped(jnp.take(gain_sum, page_here ^ k, axis=0), "page", k)
        return kept

    def late_sums(db_all, mlp_sum):
        up_sum = mlp_sum[0].reshape(2, 2, share // 4, D)
        mine = jnp.where(core_here == 0, up_sum[:, 0], up_sum[:, 1])
        other = swapped(jnp.where(core_here == 0, up_sum[:, 1], up_sum[:, 0]), "blk", 1)
        joined_up = jnp.where(
            core_here == 0,
            jnp.concatenate([mine, other], axis=0),
            jnp.concatenate([other, mine], axis=0),
        )
        return gains_over_pages(db_all), flat(joined_up.transpose(1, 0, 2))

    up_entries = [(h_low, 0, du_low, k, "tn") for k in range(4)]
    down_entries = [(act_low, k, vis_cot, 0, "tn") for k in range(4)]
    where_vq_back = where
    if staged:
        m_keep, m_send = weight_grad_call(
            after(where, lse_qv, centre_qv), [((0,), "up", up_entries), ((1,), "rows", down_entries)], "mlp_grads"
        )
        where_vq_back = after(where, m_keep)

    dqb, dkvbt = call(
        vq_backward_kernel,
        [sds((tokens, D), bf16), sds((2 * D, slots), bf16)],
        [where_vq_back, qb, kvb, dob, lse_vq],
        flops=16e-6 * 1.1e15,
        name="vq_backward",
    )
    where_swin_back = where_self_back = where_qv_back = where
    if staged:
        visual_out = back_to_grid(after(v3, m_keep))
        where_qv_back = after(where, visual_out)
        m_one = collect_first(m_keep, m_send, dqb)
        where_qv_back = after(where, visual_out, m_one)
    dqat, dkva, *merged_parts = call(
        qv_backward_kernel,
        [sds((D, slots), bf16), sds((tokens, 2 * D), bf16)] + [sds((slots, 2 * D), bf16)],
        [where_qv_back, qa, kva, doa, lse_qv, centre_qv, dkvbt],
        scratch=[pltpu.VMEM((slots, 2 * D), bf16)],
        loads=[(w_qv, 0), (w_vq, 1), (w_vq, 2)],
        flops=23e-6 * 1.1e15,
        name="qv_backward",
    )
    merged = scattered_blocks(merged_parts[0])
    if staged:
        m_two = collect_second(m_one, dqat)
        where_swin_back = after(where, m_two)
    dc, oa_low = merged[:, :D], merged[:, D:]

    def swin_backward(*refs):
        swin_backward_kernel(rows_here, *refs)

    dz_swin, dqkv_swin, visual_grad, dg_visual = call(
        swin_backward,
        [
            sds((tokens, D), bf16),
            sds((tokens, 3 * D), bf16),
            sds((tokens, D), f32),
            sds((2, D), f32),
        ],
        [where_swin_back, vis_in, v1, g2, gains, dkva, dqb, qkv_swin, lse_swin],
        scratch=[
            pltpu.VMEM((cols_all // rows_here, rows_here**2, rows_here**2), f32),
            pltpu.VMEM((tokens, D), bf16),
        ],
        loads=[(w_qv, 1), (w_qv, 2), (w_vq, 0), (w_swin, 3)] + [(w_swin, k) for k in range(3)],
        flops=20e-6 * 1.1e15,
        name="swin_backward",
    )

    swin_entries = [(a_low, 0, dqkv_swin, k, "tn") for k in range(3)]
    swin_entries.append((o_swin, 0, dz_swin, 0, "tn"))
    vq_entries = [
        (e_low, 0, dqb, 0, "tn"),
        (c_all, 0, dkvbt, 0, "tt"),
        (c_all, 0, dkvbt, 1, "tt"),
        (o_vq, 0, dz_vq, 0, "tn"),
    ]
    qv_entries = [
        (c_all, 0, dqat, 0, "tt"),
        (e_low, 0, dkva, 0, "tn"),
        (e_low, 0, dkva, 1, "tn"),
        (oa_low, 0, query_cot[0], 0, "tn"),
    ]
    if staged:
        m_three = collect_third(m_two, dz_swin)
        p_keep, p_send = weight_grad_call(
            after(where, m_three), [((0,), "rows", vq_entries), ((1,), "rows", swin_entries)], "patch_grads"
        )
        p_one = collect_first(p_keep, p_send)
        where_self_back = after(where, p_one)

    gy1, dz_self, dq_self, dkvt_self, dbq, dg_slots, *db_parts = call(
        self_backward_kernel,
        [
            sds((q_rows, D), f32),
            sds((q_rows, D), bf16),
            sds((q_rows, D), bf16),
            sds((2 * D, slots), bf16),
            sds((q_rows, D), f32),
            sds((2, D), f32),
        ]
        + ([sds((4, q_rows, D), bf16)] * 2 if staged else [sds((slots, D), bf16)]),
        [where_self_back, dc, y1, query_cot[0], gains, q_self, kv_self, lse_self],
        slots=(slot_arrays, 0, q_rows),
        scratch=[
            pltpu.VMEM((q_rows, slots), f32),
            pltpu.VMEM((q_rows, D), bf16),
            pltpu.VMEM((slots, D), bf16),
        ],
        loads=[(w_self, 3), (w_self, 0), (w_self, 1), (w_self, 2)],
        flops=15e-6 * 1.1e15,
        name="self_backward",
    )
    b_own = lax.dynamic_slice_in_dim(b_all, blk_here * q_rows, q_rows, 0)
    self_entries = [
        (b_own, 0, dq_self, 0, "tn"),
        (b_all, 0, dkvt_self, 0, "tt"),
        (b_all, 0, dkvt_self, 1, "tt"),
        (o_self, 0, dz_self, 0, "tn"),
    ]
    gain_block = jnp.concatenate(
        [dg_visual[0:1], dg_slots[0:1], dg_visual[1:2], dg_slots[1:2], dg5, jnp.zeros((3, D), f32)],
        axis=0,
    )
    gain_block = gain_block.astype(bf16).reshape(pages, blk_count, gain_width).transpose(1, 0, 2)
    gain_block = gain_block.reshape(blk_count, 1, pages * gain_width)
    gain_block = jnp.pad(gain_block, ((0, 0), (0, 15), (0, D - pages * gain_width)))
    if staged:
        order = (jnp.arange(8).reshape(4, 2) * 1).transpose(1, 0) ^ blk_here
        db_parts = [
            jnp.concatenate([db_parts[core], gain_block[order[core]]], axis=1) for core in range(2)
        ]
    else:
        whole_part = db_parts[0].reshape(blk_count, q_rows, D)
        whole_part = jnp.concatenate([whole_part, gain_block], axis=1)
        db_all = scattered_blocks(whole_part.reshape(blk_count * (q_rows + 16), D)).astype(f32)
    where_end = where
    if staged:
        p_two = collect_second(p_one, gy1)
        mlp_sum = collect_last(m_three, gy1)
        z_keep, z_send = weight_grad_call(
            after(where, p_two, mlp_sum), [((0,), "rows", qv_entries), ((1,), "rows", self_entries)], "slot_grads"
        )
        db_chips = blocks_in_chip(db_parts, z_keep)
        z_one = collect_first(z_keep, z_send)
        db_all = blocks_over_chips(db_chips, z_one)
        p_three = collect_third(p_two, z_keep)
        z_two = collect_second(after(z_one, p_three, db_all))
        patch_sum = collect_last(p_three)
        z_two, db_all, mlp_sum = after((z_two, db_all, mlp_sum), patch_sum)
        z_three = collect_third(z_two)
        gain_grad, up_grad = late_sums(db_all, mlp_sum)
        z_three = after(z_three, gain_grad, up_grad)
        visual_grad = back_to_grid(after(visual_grad, z_three))
        where_end = after(where, z_three, visual_grad)
    db = db_all[:q_rows]
    query_grad, query_out = call(
        query_end_kernel,
        [sds((q_rows, D), f32), sds((q_rows, D), bf16)],
        [where_end, db, dbq, query_tokens[0], gy1, gains, y1, oa_low],
        loads=[(w_qv, 3)],
        name="query_end",
    )

    if staged:
        slot_sum = collect_last(z_three)
        swin_grad, self_grad = flat(patch_sum[1]), flat(slot_sum[1])
        qv_grad, vq_grad = flat(slot_sum[0]), flat(patch_sum[0])
        down_grad = flat(mlp_sum[1])
    else:
        visual_out, visual_grad = back_to_grid(v3), back_to_grid(visual_grad)
        gain_grad = gains_over_pages(db_all)

        def outer(left, right):
            return tn(left, right).astype(bf16)

        def outer_t(left, right_t):
            return lax.dot_general(
                left, right_t, (((0,), (1,)), ((), ())), preferred_element_type=f32
            ).astype(bf16)

        def as_shares(mats):
            return jnp.concatenate(mats, axis=0).reshape(shards, share, D)

        def summed(parts):
            joined = jnp.concatenate(parts, axis=1)
            width = joined.shape[1]
            return lax.psum_scatter(
                joined.reshape(shards * width, D), everyone, scatter_dimension=0, tiled=True
            )

        up_mats = jnp.stack([outer(h_low, du_low[:, k * D : (k + 1) * D]) for k in range(4)])
        up_part = (
            up_mats.reshape(4, shards, share // 4, D)
            .transpose(1, 0, 2, 3)
            .reshape(shards, share, D)
        )
        down_part = outer(act_low, vis_cot).reshape(shards, share, D)
        mlp_sum = summed([up_part, down_part])
        qv_part = as_shares(
            [
                outer_t(c_all, dqat),
                outer(e_low, dkva[:, :D]),
                outer(e_low, dkva[:, D:]),
                outer(oa_low, query_cot[0]),
            ]
        )
        vq_part = as_shares(
            [
                outer(e_low, dqb),
                outer_t(c_all, dkvbt[:D]),
                outer_t(c_all, dkvbt[D:]),
                outer(o_vq, dz_vq),
            ]
        )
        cross_sum = summed([qv_part, vq_part])
        swin_part = as_shares(
            [outer(a_low, dqkv_swin[:, k * D : (k + 1) * D]) for k in range(3)]
            + [outer(o_swin, dz_swin)]
        )
        self_part = as_shares(
            [
                outer(b_own, dq_self),
                outer_t(b_all, dkvt_self[:D]),
                outer_t(b_all, dkvt_self[D:]),
                outer(o_self, dz_self),
            ]
        )
        last_sum = summed([swin_part, self_part])
        up_grad = flat(mlp_sum[:share].reshape(4, share // 4, D).transpose(1, 0, 2))
        down_grad = flat(mlp_sum[share:])
        qv_grad, vq_grad = flat(cross_sum[:share]), flat(cross_sum[share:])
        swin_grad, self_grad = flat(last_sum[:share]), flat(last_sum[share:])

    return (
        visual_out,
        query_out[None],
        visual_grad,
        query_grad[None],
        swin_grad,
        self_grad,
        qv_grad,
        vq_grad,
        up_grad,
        down_grad,
        gain_grad,
    )


def solution(mesh):
    placed = (
        P("page", "blk", None, None),
        P("page", "blk", None),
        P("page"),
        P(("page", "blk")),
        P(("page", "blk")),
        P(("page", "blk")),
        P(("page", "blk")),
        P(("page", "blk")),
        P(("page", "blk")),
        P(("page", "blk")),
        P("page", "blk", None, None),
        P("page", "blk", None),
    )
    return jax.shard_map(
        on_device,
        mesh=mesh,
        in_specs=placed,
        out_specs=(
            P("page", "blk", None, None),
            P("page", "blk", None),
            P("page", "blk", None, None),
            P("page", "blk", None),
            P(("page", "blk")),
            P(("page", "blk")),
            P(("page", "blk")),
            P(("page", "blk")),
            P(("page", "blk")),
            P(("page", "blk")),
            P(("page", "blk")),
        ),
        check_vma=False,
    )
```

```python
import jax
import jax.numpy as jnp
from jax import lax
from jax.experimental import pallas as pl
from jax.experimental.pallas import tpu as pltpu
from jax.sharding import PartitionSpec as P

D = 768
HEADS = 12
HD = 64
FF = 3072
PAIRS = HEADS // 2
PW = 2 * HD
SCALE = HD ** (-0.5)

EPS = 1e-05
NEG = -1e30

bf16 = jnp.bfloat16
f32 = jnp.float32
VMEM_LIMIT = 56 * 1024 * 1024


def nn(left, right):
    return lax.dot_general(left, right, (((1,), (0,)), ((), ())), preferred_element_type=f32)


def nt(left, right):
    return lax.dot_general(left, right, (((1,), (1,)), ((), ())), preferred_element_type=f32)


def tn(left, right):
    return lax.dot_general(left, right, (((0,), (0,)), ((), ())), preferred_element_type=f32)


def norm_parts(rows):
    centre = jnp.mean(rows, axis=-1, keepdims=True)
    centred = rows - centre
    spread = jnp.mean(centred * centred, axis=-1, keepdims=True)
    inverse = lax.rsqrt(spread + EPS)
    return centred * inverse, inverse


def norm(rows, gain):
    return norm_parts(rows)[0] * gain


def norm_back(rows, gain, grad):
    unit, inverse = norm_parts(rows)
    grad_gain = jnp.sum(grad * unit, axis=0, keepdims=True)
    scaled = grad * gain
    first = jnp.mean(scaled, axis=-1, keepdims=True)
    second = jnp.mean(scaled * unit, axis=-1, keepdims=True)
    return inverse * (scaled - first - unit * second), grad_gain


def lane_half(half, value, dtype):
    lanes = lax.broadcasted_iota(jnp.int32, (1, PW), 1)
    return jnp.where((lanes // HD) == half, value, 0.0).astype(dtype)


def low_half(rows):
    return lax.broadcasted_iota(jnp.int32, (rows, PW), 1) < HD


def column(table, index):
    lanes = lax.broadcasted_iota(jnp.int32, table.shape, 1)
    return jnp.sum(jnp.where(lanes == index, table, 0.0), axis=-1, keepdims=True)


def pair_cols(pair, base=0):
    return pl.ds(pl.multiple_of(base + pair * PW, PW), PW)


def softmax_rows(scores):
    highest = jnp.max(scores, axis=-1, keepdims=True)
    raised = jnp.exp(scores - highest)
    totals = jnp.sum(raised, axis=-1, keepdims=True)
    return raised * (1.0 / totals), highest + jnp.log(totals)


class Stored:
    def __init__(self, arrays, lanes=(), joint=None):
        self.arrays = list(arrays)
        self.lanes = tuple(lanes)
        self.joint = joint


def stage_bits(lane):
    return (1, 2) if lane == 0 else (2, 1)


def relative(lane, core, first, second):
    bit_one, bit_two = stage_bits(lane)
    return core | (first << bit_one) | (second << bit_two)


def local_copy(source, target, sem):
    pltpu.make_async_copy(source, target, sem).start()


def fetch(where_ref, stored, refs, index, target, sem):
    if stored.joint is not None:
        first, rows = stored.joint
        count = D // rows
        for k in range(count):
            piece = refs[0].at[index * count + k, first : first + rows]
            local_copy(piece, target.at[k * rows : (k + 1) * rows], sem)
        return
    if len(refs) == 1:
        local_copy(refs[0].at[index], target, sem)
        return
    page, blk = where_ref[3], where_ref[4]
    count = len(stored.lanes)
    for number, lane in enumerate(stored.lanes):
        for core in range(2):
            for second in range(2):
                for first in range(2):
                    ref = refs[4 * number + 2 * core + second]
                    piece = ref.at[(index ^ page) + 4 * first]
                    rows = piece.shape[0]
                    owner = blk ^ relative(lane, core, first, second)
                    start = pl.multiple_of((owner * count + number) * rows, rows)
                    local_copy(piece, target.at[pl.ds(start, rows)], sem)


def fetch_up(where_ref, stored, refs, target, sem):
    if len(refs) == 1:
        local_copy(refs[0], target, sem)
        return
    page, blk = where_ref[3], where_ref[4]
    for core in range(2):
        for second in range(2):
            for first in range(2):
                ref = refs[2 * core + second]
                near = (blk ^ relative(stored.lanes[0], 0, first, second)) >> 1
                for origin in range(4):
                    piece = ref.at[(origin ^ page) + 4 * first]
                    rows = piece.shape[0] // 2
                    spot = pl.ds(pl.multiple_of((origin * 4 + near) * rows, rows), rows)
                    for k in range(2):
                        group = 2 * ((blk & 1) ^ core) + k
                        local_copy(piece.at[k * rows : (k + 1) * rows], target.at[group, spot], sem)


class Loads:
    def __init__(self, held, sems, plan):
        self.held, self.sems, self.plan, self.done = held, sems, plan, set()

    def ready(self, *places):
        for place in places:
            if place not in self.done:
                self.done.add(place)
                start, count = self.plan[place]
                span = self.held.at[start : start + count]
                pltpu.make_async_copy(span, span, self.sems.at[place]).wait()

    def __getitem__(self, place):
        self.ready(place)
        return self.held[self.plan[place][0]]

    def part(self, place, k):
        return self.held[self.plan[place][0] + k]


def call(kernel, outs, ins, scratch=(), smem=1, loads=(), slots=None, flops=0, name=None):
    def whole(value):
        zeros = (0,) * len(value.shape)
        return pl.BlockSpec(value.shape, lambda i: zeros, pipeline_mode=pl.Buffered(1))

    specs = []
    for index, value in enumerate(ins):
        if index < smem:
            specs.append(pl.BlockSpec(memory_space=pltpu.SMEM))
        else:
            specs.append(whole(value))
    single = not isinstance(outs, list)
    shapes = [outs] if single else outs
    count_in, count_out = len(ins), len(shapes)
    unique, plan, size = [], [], 0
    for stored, which in loads:
        if stored not in unique:
            unique.append(stored)
        width = 4 if which is None else 1
        plan.append((size, width))
        size += width
    arrays = [array for stored in unique for array in stored.arrays]
    gathered, slot_scratch = [], []
    if slots:
        gathered, part, own = slots
        blocks = len(gathered) if len(gathered) > 1 else gathered[0].shape[0]
        slot_scratch = [pltpu.VMEM((blocks, own, D), bf16), pltpu.SemaphoreType.DMA]
    held = [pltpu.VMEM((size, D, D), bf16), pltpu.SemaphoreType.DMA((len(plan),))] if loads else []

    def body(*refs):
        inner = list(refs[:count_in])
        at = count_in
        taken = {}
        for stored in unique:
            taken[id(stored)] = refs[at : at + len(stored.arrays)]
            at += len(stored.arrays)
        pieces = refs[at : at + len(gathered)]
        at += len(gathered)
        results = list(refs[at : at + count_out])
        rest = list(refs[at + count_out :])
        if slots:
            together, slot_sem = rest[:2]
            rest = rest[2:]
            rows = slice(part * own, (part + 1) * own)
            if len(pieces) == 1:
                local_copy(pieces[0].at[:, rows], together, slot_sem)
            for k, piece in enumerate(pieces if len(pieces) > 1 else ()):
                local_copy(piece.at[rows], together.at[inner[0][4] ^ k], slot_sem)
            inner.append(together)
        if not loads:
            kernel(*inner, *results, *rest)
            return
        kept, sems = rest[-2], rest[-1]
        for place, (stored, which) in enumerate(loads):
            mine, (start, width) = taken[id(stored)], plan[place]
            if which is None:
                fetch_up(inner[0], stored, mine, kept.at[start : start + width], sems.at[place])
            else:
                fetch(inner[0], stored, mine, which, kept.at[start], sems.at[place])
        if slots:
            pltpu.make_async_copy(together, together, slot_sem).wait()
        weights = Loads(kept, sems, plan)
        kernel(*inner, weights, *results, *rest[:-2])
        weights.ready(*range(len(plan)))

    moved = sum(v.size * v.dtype.itemsize for v in list(ins) + shapes) + size * D * D * 2
    result = pl.pallas_call(
        body,
        grid=(1,),
        out_shape=shapes,
        in_specs=specs + [pl.BlockSpec(memory_space=pl.ANY)] * (len(arrays) + len(gathered)),
        out_specs=[whole(value) for value in shapes],
        scratch_shapes=slot_scratch + list(scratch) + held,
        compiler_params=pltpu.CompilerParams(
            vmem_limit_bytes=VMEM_LIMIT, dimension_semantics=("arbitrary",)
        ),
        cost_estimate=pl.CostEstimate(flops=int(flops), bytes_accessed=int(moved), transcendentals=0),
        name=name,
    )(*ins, *arrays, *gathered)
    return result[0] if single else result


def sds(shape, dtype):
    return jax.ShapeDtypeStruct(shape, dtype)


def self_bias(bias_ref, first_row, live):
    rows, slots = bias_ref.shape
    keys = lax.broadcasted_iota(jnp.int32, (rows, slots), 1)
    places = lax.broadcasted_iota(jnp.int32, (rows, slots), 0) + first_row
    bias_ref[...] = jnp.where((keys <= places) & (keys < live), 0.0, NEG)


def self_forward_kernel(
    where_ref, g_ref, y_ref, w, b_ref, q_ref, kv_ref, lse_ref, o_ref, y1_ref, c_ref, bias_ref
):
    first_row, live = where_ref[0], where_ref[1]
    slots, own = b_ref.shape[0], q_ref.shape[0]
    tile = 256
    group = tile // own
    w.ready(0, 1)

    def project(i, carry):
        rows = pl.ds(pl.multiple_of(i * tile, tile), tile)
        part = y_ref[pl.ds(i * group, group)].reshape(tile, D)
        normed = norm(part.astype(f32), g_ref[1:2, :]).astype(bf16)
        b_ref[rows, :] = normed
        kv_ref[rows, 0:D] = nn(normed, w[0]).astype(bf16)
        kv_ref[rows, D : 2 * D] = nn(normed, w[1]).astype(bf16)
        return carry

    lax.fori_loop(0, slots // tile, project, 0)
    mine = pl.ds(pl.multiple_of(first_row, 16), own)
    q_ref[...] = nn(b_ref[mine, :], w[2]).astype(bf16)
    self_bias(bias_ref, first_row, live)
    lse_ref[...] = jnp.zeros_like(lse_ref)
    lanes = lax.broadcasted_iota(jnp.int32, lse_ref.shape, 1)
    low = low_half(own)

    def attend(pair, carry):
        queries = q_ref[:, pair_cols(pair)]
        keys = kv_ref[:, pair_cols(pair)]
        values = kv_ref[:, pair_cols(pair, D)]
        mixed = []
        table = lse_ref[...]
        for half in range(2):
            scores = nt(queries * lane_half(half, SCALE, bf16), keys) + bias_ref[...]
            chances, log_totals = softmax_rows(scores)
            mixed.append(nn(chances.astype(bf16), values))
            table = jnp.where(lanes == 2 * pair + half, log_totals, table)
        lse_ref[...] = table
        o_ref[:, pair_cols(pair)] = jnp.where(low, mixed[0], mixed[1]).astype(bf16)
        return carry

    lax.fori_loop(0, PAIRS, attend, 0)
    y1 = y_ref[where_ref[4]].astype(f32) + nn(o_ref[...], w[3])
    y1_ref[...] = y1
    c_ref[...] = norm(y1, g_ref[3:4, :]).astype(bf16)


def window_bias(rows, side, row_split, col_split):
    def flags(shape, dim):
        token = lax.broadcasted_iota(jnp.int32, shape, dim)
        row, col = token // side, token % side
        return jnp.where(row >= side // 2, row_split, 0) + jnp.where(
            col >= side // 2, 2 * col_split, 0
        )

    return jnp.where(flags((rows, rows), 0) == flags((rows, rows), 1), 0.0, NEG)


def swin_forward_kernel(
    side, where_ref, x_ref, g_ref, w, a_ref, qkv_ref, lse_ref, o_ref, v1_ref, e_ref, bias_ref
):
    is_last = where_ref[2]
    tokens = x_ref.shape[0]
    rows = side * side
    windows = tokens // rows
    x = x_ref[...].astype(f32)
    normed = norm(x, g_ref[0:1, :]).astype(bf16)
    a_ref[...] = normed
    for k in range(3):
        qkv_ref[:, k * D : (k + 1) * D] = nn(normed, w[k]).astype(bf16)
    for win in range(windows):
        bias_ref[win] = window_bias(rows, side, is_last, 1 if win == windows - 1 else 0)
    lse_ref[...] = jnp.zeros_like(lse_ref)
    lanes = lax.broadcasted_iota(jnp.int32, (rows, lse_ref.shape[1]), 1)
    low = low_half(rows)

    def attend(pair, carry):
        for win in range(windows):
            at = slice(win * rows, (win + 1) * rows)
            queries = qkv_ref[at, pair_cols(pair)]
            keys = qkv_ref[at, pair_cols(pair, D)]
            values = qkv_ref[at, pair_cols(pair, 2 * D)]
            mixed = []
            table = lse_ref[at, :]
            for half in range(2):
                scores = nt(queries * lane_half(half, SCALE, bf16), keys) + bias_ref[win]
                chances, log_totals = softmax_rows(scores)
                mixed.append(nn(chances.astype(bf16), values))
                table = jnp.where(lanes == 2 * pair + half, log_totals, table)
            lse_ref[at, :] = table
            o_ref[at, pair_cols(pair)] = jnp.where(low, mixed[0], mixed[1]).astype(bf16)
        return carry

    lax.fori_loop(0, PAIRS, attend, 0)
    v1 = x + nn(o_ref[...], w[3])
    v1_ref[...] = v1
    e_ref[...] = norm(v1, g_ref[2:3, :]).astype(bf16)


def cross_forward_kernel(
    where_ref,
    c_ref,
    e_ref,
    cot_ref,
    w,
    qa_ref,
    kvb_ref,
    doa_ref,
    kva_ref,
    qb_ref,
    stats_ref,
):
    slots, tokens = qa_ref.shape[0], e_ref.shape[0]
    tile = 256
    normed = e_ref[...]
    for k in range(2):
        kva_ref[:, k * D : (k + 1) * D] = nn(normed, w[k]).astype(bf16)
    qb_ref[...] = nn(normed, w[2]).astype(bf16)
    w.ready(3, 4, 5, 6)
    group = tile // cot_ref.shape[1]

    def project(i, carry):
        rows = pl.ds(pl.multiple_of(i * tile, tile), tile)
        part = c_ref[rows, :]
        qa_ref[rows, :] = nn(part, w[3]).astype(bf16)
        for k in range(2):
            kvb_ref[rows, k * D : (k + 1) * D] = nn(part, w[4 + k]).astype(bf16)
        cot = cot_ref[pl.ds(i * group, group)].reshape(tile, D)
        doa_ref[rows, :] = nt(cot, w[6]).astype(bf16)
        return carry

    lax.fori_loop(0, slots // tile, project, 0)
    stats_ref[...] = jnp.zeros_like(stats_ref)

    def page_stats(pair, carry):
        keys = kva_ref[:, pair_cols(pair)]
        values = kva_ref[:, pair_cols(pair, D)]
        for half in range(2):
            head = 2 * pair + half
            keys_h = keys * lane_half(half, SCALE, bf16)
            values_h = values * lane_half(half, 1.0, bf16)
            for i in range(slots // tile):
                rows = slice(i * tile, (i + 1) * tile)
                scores = nt(keys_h, qa_ref[rows, pair_cols(pair)])
                highest = jnp.max(scores, axis=0, keepdims=True)
                raised = jnp.exp(scores - highest)
                grads = nt(values_h, doa_ref[rows, pair_cols(pair)])
                stats_ref[0, pl.ds(head, 1), rows] = highest
                stats_ref[1, pl.ds(head, 1), rows] = jnp.sum(raised, axis=0, keepdims=True)
                stats_ref[2, pl.ds(head, 1), rows] = jnp.sum(raised * grads, axis=0, keepdims=True)
        return carry

    lax.fori_loop(0, PAIRS, page_stats, 0)


def vq_forward_kernel(where_ref, qb_ref, kvb_ref, lse_ref, ob_ref):
    live = where_ref[1]
    tokens, slots = qb_ref.shape[0], kvb_ref.shape[0]
    lse_ref[...] = jnp.zeros_like(lse_ref)
    lanes = lax.broadcasted_iota(jnp.int32, lse_ref.shape, 1)
    low = low_half(tokens)
    bias = jnp.where(lax.broadcasted_iota(jnp.int32, (1, slots), 1) < live, 0.0, NEG)

    def attend(pair, carry):
        queries = qb_ref[:, pair_cols(pair)]
        keys = kvb_ref[:, pair_cols(pair)]
        values = kvb_ref[:, pair_cols(pair, D)]
        mixed = []
        table = lse_ref[...]
        for half in range(2):
            scores = nt(queries * lane_half(half, SCALE, bf16), keys) + bias
            chances, log_totals = softmax_rows(scores)
            mixed.append(nn(chances.astype(bf16), values))
            table = jnp.where(lanes == 2 * pair + half, log_totals, table)
        lse_ref[...] = table
        ob_ref[:, pair_cols(pair)] = jnp.where(low, mixed[0], mixed[1]).astype(bf16)
        return carry

    lax.fori_loop(0, PAIRS, attend, 0)


GELU_A = 0.7978845608028654
GELU_B = 0.044715


def mlp_kernel(
    where_ref,
    v1_ref,
    ob_ref,
    cot_ref,
    g_ref,
    w,
    v3_ref,
    h_ref,
    act_ref,
    du_ref,
    g2_ref,
    dz_ref,
    dob_ref,
    dg_ref,
    v2_ref,
    sum_ref,
    dh_ref,
):
    v2 = v1_ref[...] + nn(ob_ref[...], w[0])
    v2_ref[...] = v2
    sum_ref[...] = v2
    h_ref[...] = norm(v2, g_ref[4:5, :]).astype(bf16)
    dh_ref[...] = jnp.zeros_like(dh_ref)
    w.ready(1, 2, 3, 4, 5)

    def chunk(k, carry):
        up, down = w.part(1, k), w.part(2, k)
        at = pl.ds(pl.multiple_of(k * D, D), D)
        u = nn(h_ref[...], up)
        squared = u * u
        bend = jnp.tanh(GELU_A * (u + GELU_B * u * squared))
        act = (0.5 * u * (1.0 + bend)).astype(bf16)
        act_ref[:, at] = act
        slope = 0.5 * (1.0 + bend) + 0.5 * u * (1.0 - bend * bend) * GELU_A * (
            1.0 + 3.0 * GELU_B * squared
        )
        du = (nt(cot_ref[...], down) * slope).astype(bf16)
        du_ref[:, at] = du
        sum_ref[...] += nn(act, down)
        dh_ref[...] += nt(du, up)
        return carry

    lax.fori_loop(0, FF // D, chunk, 0)
    v3_ref[...] = sum_ref[...].astype(bf16)
    part, dg = norm_back(v2_ref[...], g_ref[4:5, :], dh_ref[...])
    dg_ref[...] = dg
    g2 = cot_ref[...].astype(f32) + part
    g2_ref[...] = g2
    dz = g2.astype(bf16)
    dz_ref[...] = dz
    dob_ref[...] = nt(dz, w[0]).astype(bf16)


def vq_backward_kernel(
    where_ref, qb_ref, kvb_ref, dob_ref, lse_ref, dqb_ref, dkvbt_ref
):
    live = where_ref[1]
    tokens, slots = qb_ref.shape[0], kvb_ref.shape[0]
    bias = jnp.where(lax.broadcasted_iota(jnp.int32, (1, slots), 1) < live, 0.0, NEG)
    low = low_half(tokens)

    def back(pair, carry):
        queries = qb_ref[:, pair_cols(pair)]
        keys = kvb_ref[:, pair_cols(pair)]
        values = kvb_ref[:, pair_cols(pair, D)]
        grads = dob_ref[:, pair_cols(pair)]
        queries_t = (queries * SCALE).astype(f32).T.astype(bf16)
        grads_t = grads.astype(f32).T.astype(bf16)
        parts = []
        for half in range(2):
            own = slice(half * HD, (half + 1) * HD)
            scores = nt(queries * lane_half(half, SCALE, bf16), keys) + bias
            chances = jnp.exp(scores - column(lse_ref[...], 2 * pair + half))
            slopes = nt(grads * lane_half(half, 1.0, bf16), values)
            centre = jnp.sum(chances * slopes, axis=-1, keepdims=True)
            ds = (chances * (slopes - centre)).astype(bf16)
            parts.append(nn(ds, keys))
            at = pair * PW + half * HD
            dkvbt_ref[pl.ds(pl.multiple_of(at, HD), HD), :] = nn(queries_t[own], ds).astype(bf16)
            dkvbt_ref[pl.ds(pl.multiple_of(D + at, HD), HD), :] = nn(
                grads_t[own], chances.astype(bf16)
            ).astype(bf16)
        dqb_ref[:, pair_cols(pair)] = (jnp.where(low, parts[0], parts[1]) * SCALE).astype(bf16)
        return carry

    lax.fori_loop(0, PAIRS, back, 0)


def hand_out(where_ref, held, outs):
    if len(outs) == 1:
        outs[0][...] = held[...]
        return
    rows = outs[0].shape[1]
    for core, out in enumerate(outs):
        for k in range(4):
            start = pl.multiple_of((where_ref[4] ^ (2 * k + core)) * rows, rows)
            out[k] = held[pl.ds(start, rows), :]


def qv_backward_kernel(
    where_ref,
    qa_ref,
    kva_ref,
    doa_ref,
    lse_ref,
    centre_ref,
    dkvbt_ref,
    w,
    dqat_ref,
    dkva_ref,
    *rest,
):
    dc_refs, held = rest[:-1], rest[-1]
    slots, tokens = qa_ref.shape[0], kva_ref.shape[0]
    low = low_half(tokens)
    tile = 512

    def back(pair, carry):
        keys = kva_ref[:, pair_cols(pair)]
        values = kva_ref[:, pair_cols(pair, D)]
        keys_t = (keys * SCALE).astype(f32).T.astype(bf16)
        values_t = values.astype(f32).T.astype(bf16)
        for i in range(slots // tile):
            rows = slice(i * tile, (i + 1) * tile)
            queries = qa_ref[rows, pair_cols(pair)]
            grads = doa_ref[rows, pair_cols(pair)]
            dk, dv, mixed = [], [], []
            for half in range(2):
                head = 2 * pair + half
                own = slice(half * HD, (half + 1) * HD)
                scores = nt(keys * lane_half(half, SCALE, bf16), queries)
                chances = jnp.exp(scores - lse_ref[pl.ds(head, 1), rows])
                slopes = nt(values * lane_half(half, 1.0, bf16), grads)
                ds = (chances * (slopes - centre_ref[pl.ds(head, 1), rows])).astype(bf16)
                rounded = chances.astype(bf16)
                mixed.append(nn(values_t[own], rounded))
                dqat_ref[pl.ds(pl.multiple_of(head * HD, HD), HD), rows] = nn(
                    keys_t[own], ds
                ).astype(bf16)
                dk.append(nn(ds, queries))
                dv.append(nn(rounded, grads))
            held[rows, pair_cols(pair, D)] = jnp.concatenate(mixed, axis=0).T.astype(bf16)
            dk_now = jnp.where(low, dk[0], dk[1]) * SCALE
            dv_now = jnp.where(low, dv[0], dv[1])
            if i == 0:
                dk_sum, dv_sum = dk_now, dv_now
            else:
                dk_sum, dv_sum = dk_sum + dk_now, dv_sum + dv_now
        dkva_ref[:, pair_cols(pair)] = dk_sum.astype(bf16)
        dkva_ref[:, pair_cols(pair, D)] = dv_sum.astype(bf16)
        return carry

    lax.fori_loop(0, PAIRS, back, 0)
    for i in range(slots // tile):
        cols = slice(i * tile, (i + 1) * tile)
        total = nn(w[0], dqat_ref[:, cols])
        total += nn(w[1], dkvbt_ref[0:D, cols])
        total += nn(w[2], dkvbt_ref[D : 2 * D, cols])
        held[cols, 0:D] = total.T.astype(bf16)
    hand_out(where_ref, held, dc_refs)


def swin_backward_kernel(
    side,
    where_ref,
    x_ref,
    v1_ref,
    g2_ref,
    g_ref,
    dkva_ref,
    dqb_ref,
    qkv_ref,
    lse_ref,
    w,
    dz_ref,
    dqkv_ref,
    grad_ref,
    dg_ref,
    bias_ref,
    do_ref,
):
    is_last = where_ref[2]
    tokens = x_ref.shape[0]
    rows = side * side
    windows = tokens // rows
    de = nt(dkva_ref[:, 0:D], w[0])
    de += nt(dkva_ref[:, D : 2 * D], w[1])
    de += nt(dqb_ref[...], w[2])
    part, dg3 = norm_back(v1_ref[...], g_ref[2:3, :], de)
    g1 = g2_ref[...] + part
    grad_ref[...] = g1
    dz = g1.astype(bf16)
    dz_ref[...] = dz
    do_ref[...] = nt(dz, w[3]).astype(bf16)
    for win in range(windows):
        bias_ref[win] = window_bias(rows, side, is_last, 1 if win == windows - 1 else 0)
    low = low_half(rows)

    def back(pair, carry):
        for win in range(windows):
            at = slice(win * rows, (win + 1) * rows)
            queries = qkv_ref[at, pair_cols(pair)]
            keys = qkv_ref[at, pair_cols(pair, D)]
            values = qkv_ref[at, pair_cols(pair, 2 * D)]
            grads = do_ref[at, pair_cols(pair)]
            dq, dk, dv = [], [], []
            for half in range(2):
                scores = nt(queries * lane_half(half, SCALE, bf16), keys) + bias_ref[win]
                chances = jnp.exp(scores - column(lse_ref[at, :], 2 * pair + half))
                slopes = nt(grads * lane_half(half, 1.0, bf16), values)
                centre = jnp.sum(chances * slopes, axis=-1, keepdims=True)
                ds = (chances * (slopes - centre)).astype(bf16)
                dq.append(nn(ds, keys))
                dk.append(tn(ds, queries))
                dv.append(tn(chances.astype(bf16), grads))
            for k, (pieces, factor) in enumerate(((dq, SCALE), (dk, SCALE), (dv, 1.0))):
                dqkv_ref[at, pair_cols(pair, k * D)] = (
                    jnp.where(low, pieces[0], pieces[1]) * factor
                ).astype(bf16)
        return carry

    lax.fori_loop(0, PAIRS, back, 0)
    da = nt(dqkv_ref[:, 0:D], w[4])
    da += nt(dqkv_ref[:, D : 2 * D], w[5])
    da += nt(dqkv_ref[:, 2 * D : 3 * D], w[6])
    part, dg1 = norm_back(x_ref[...].astype(f32), g_ref[0:1, :], da)
    grad_ref[...] += part
    dg_ref[...] = jnp.concatenate([dg1, dg3], axis=0)


def self_backward_kernel(
    where_ref,
    dc_ref,
    y1_ref,
    cot_ref,
    g_ref,
    q_ref,
    kv_ref,
    lse_ref,
    y_ref,
    w,
    gy1_ref,
    dz_ref,
    dq_ref,
    dkvt_ref,
    dbq_ref,
    dg_ref,
    *rest,
):
    db_refs, (bias_ref, do_ref, db_held) = rest[:-3], rest[-3:]
    group = 256 // q_ref.shape[0]
    first_row, live = where_ref[0], where_ref[1]
    own_rows, slots = q_ref.shape[0], kv_ref.shape[0]
    part, dg = norm_back(y1_ref[...], g_ref[3:4, :], dc_ref[...].astype(f32))
    gy1 = cot_ref[...].astype(f32) + part
    gy1_ref[...] = gy1
    dz = gy1.astype(bf16)
    dz_ref[...] = dz
    do_ref[...] = nt(dz, w[0]).astype(bf16)
    self_bias(bias_ref, first_row, live)
    low = low_half(own_rows)

    def back(pair, carry):
        queries = q_ref[:, pair_cols(pair)]
        keys = kv_ref[:, pair_cols(pair)]
        values = kv_ref[:, pair_cols(pair, D)]
        grads = do_ref[:, pair_cols(pair)]
        queries_t = (queries * SCALE).astype(f32).T.astype(bf16)
        grads_t = grads.astype(f32).T.astype(bf16)
        parts = []
        for half in range(2):
            own = slice(half * HD, (half + 1) * HD)
            scores = nt(queries * lane_half(half, SCALE, bf16), keys) + bias_ref[...]
            chances = jnp.exp(scores - column(lse_ref[...], 2 * pair + half))
            slopes = nt(grads * lane_half(half, 1.0, bf16), values)
            centre = jnp.sum(chances * slopes, axis=-1, keepdims=True)
            ds = (chances * (slopes - centre)).astype(bf16)
            parts.append(nn(ds, keys))
            at = pair * PW + half * HD
            dkvt_ref[pl.ds(pl.multiple_of(at, HD), HD), :] = nn(queries_t[own], ds).astype(bf16)
            dkvt_ref[pl.ds(pl.multiple_of(D + at, HD), HD), :] = nn(
                grads_t[own], chances.astype(bf16)
            ).astype(bf16)
        dq_ref[:, pair_cols(pair)] = (jnp.where(low, parts[0], parts[1]) * SCALE).astype(bf16)
        return carry

    lax.fori_loop(0, PAIRS, back, 0)
    dbq = nt(dq_ref[...], w[1])
    dbq_ref[...] = dbq
    unit = norm_parts(y_ref[where_ref[4]].astype(f32))[0]
    dg2 = jnp.sum(dbq * unit, axis=0, keepdims=True)
    tile = 256
    for i in range(slots // tile):
        cols = slice(i * tile, (i + 1) * tile)
        total = nn(w[2], dkvt_ref[0:D, cols])
        total += nn(w[3], dkvt_ref[D : 2 * D, cols])
        back = total.T
        db_held[cols, :] = back.astype(bf16)
        part = y_ref[i * group : (i + 1) * group].reshape(tile, D)
        unit = norm_parts(part.astype(f32))[0]
        dg2 += jnp.sum(back * unit, axis=0, keepdims=True)
    dg_ref[...] = jnp.concatenate([dg2, dg], axis=0)
    hand_out(where_ref, db_held, db_refs)


def query_end_kernel(
    where_ref, db_ref, dbq_ref, y_ref, gy1_ref, g_ref, y1_ref, oa_ref, w, grad_ref, out_ref
):
    part, _ = norm_back(
        y_ref[...].astype(f32), g_ref[1:2, :], db_ref[...].astype(f32) + dbq_ref[...]
    )
    grad_ref[...] = gy1_ref[...] + part
    out_ref[...] = (y1_ref[...] + nn(oa_ref[...], w[0])).astype(bf16)


def weight_grad_call(where, weights, name, shards=0):
    arrays, items = [], []

    def place(value):
        for index, known in enumerate(arrays):
            if known is value:
                return index
        arrays.append(value)
        return len(arrays) - 1

    for lanes, kind, entries in weights:
        for index, (left, left_at, right, right_at, form) in enumerate(entries):
            items.append((lanes, kind, index, place(left), left_at, place(right), right_at, form))
    count = len(arrays)
    rows = D // 8 // len(weights[0][0])

    def body(*refs):
        where_ref = refs[0]
        ins = refs[1 : 1 + count]
        *outs, held, sems = refs[1 + count :]
        keep, send = outs[0], outs[-1]
        page, blk = where_ref[3], where_ref[4]

        def place_natural(slot, lane, kind, index):
            out, width = outs[0], 4 * D // shards
            each = width // 2
            for k in range(2 * D // width if kind == "up" else D // width):
                if kind == "up":
                    piece = held.at[slot, k * each : (k + 1) * each]
                    first = lane * width + (index % 2) * each
                    local_copy(
                        piece, out.at[2 * k + index // 2, first : first + each], sems.at[slot]
                    )
                else:
                    piece = held.at[slot, k * width : (k + 1) * width]
                    owner = index * (D // width) + k
                    spot = slice(lane * width, (lane + 1) * width)
                    local_copy(piece, out.at[owner, spot], sems.at[slot])

        def finish(slot):
            pltpu.make_async_copy(held.at[slot], held.at[slot], sems.at[slot]).wait()

        def place_up(slot, lane, index, core, first, second):
            near = (blk ^ relative(lane, 0, first, second)) >> 1
            group, k = index // 2, index % 2
            out = send if core else keep

            @pl.when(((blk & 1) ^ core) == group)
            def _():
                half = rows // 2
                for origin in range(4):
                    spot = first * 8 + second * 4 + (origin ^ page)
                    take = pl.ds(pl.multiple_of((origin * 4 + near) * half, half), half)
                    local_copy(
                        held.at[slot, take],
                        out.at[lane, spot, k * half : (k + 1) * half],
                        sems.at[slot],
                    )

        def place_rows(slot, lanes, index, core, first, second):
            out = send if core else keep
            for number, lane in enumerate(lanes):
                owner = blk ^ relative(lane, core, first, second)
                spot = first * 8 + second * 4 + (index ^ page)
                start = pl.multiple_of((owner * len(lanes) + number) * rows, rows)
                local_copy(held.at[slot, pl.ds(start, rows)], out.at[lane, spot], sems.at[slot])

        for step, (lanes, kind, index, left, left_at, right, right_at, form) in enumerate(items):
            slot = step % 2
            if step >= 2:
                finish(slot)
            lhs = ins[left][:, left_at * D : (left_at + 1) * D]
            if form == "tt":
                rhs = ins[right][right_at * D : (right_at + 1) * D, :]
                product = nt(lhs.astype(f32).T.astype(bf16), rhs)
            else:
                product = tn(lhs, ins[right][:, right_at * D : (right_at + 1) * D])
            held[slot] = product.astype(bf16)
            if shards:
                place_natural(slot, lanes[0], kind, index)
                continue
            for core in range(2):
                for first in range(2):
                    for second in range(2):
                        if kind == "up":
                            place_up(slot, lanes[0], index, core, first, second)
                        else:
                            place_rows(slot, lanes, index, core, first, second)
        for step in range(max(0, len(items) - 2), len(items)):
            finish(step % 2)

    shapes = [sds((2, 16, rows, D), bf16)] * 2
    if shards:
        shapes = [sds((shards, len(weights) * 4 * D // shards, D), bf16)]
    moved = 2 * len(items) * D * D + sum(v.size * 2 for v in arrays)
    return pl.pallas_call(
        body,
        grid=(1,),
        out_shape=shapes,
        in_specs=[pl.BlockSpec(memory_space=pltpu.SMEM)]
        + [
            pl.BlockSpec(v.shape, lambda i: (0, 0), pipeline_mode=pl.Buffered(1)) for v in arrays
        ],
        out_specs=[pl.BlockSpec(memory_space=pl.ANY)] * len(shapes),
        scratch_shapes=[pltpu.VMEM((2, D, D), bf16), pltpu.SemaphoreType.DMA((2,))],
        compiler_params=pltpu.CompilerParams(
            vmem_limit_bytes=VMEM_LIMIT, dimension_semantics=("arbitrary",)
        ),
        cost_estimate=pl.CostEstimate(
            flops=int(len(items) * 1.6e-6 * 1.1e15), bytes_accessed=int(moved), transcendentals=0
        ),
        name=name,
    )(where, *arrays)


def window_order(grid_rows, half):
    rows, cols, _ = grid_rows.shape
    rolled = jnp.roll(grid_rows, -half, axis=1)
    shaped = rolled.reshape(rows, cols // rows, rows, D).transpose(1, 0, 2, 3)
    return shaped.reshape(rows * cols, D)


def grid_order(tokens_in, rows, cols, half):
    shaped = tokens_in.reshape(cols // rows, rows, rows, D).transpose(1, 0, 2, 3)
    return jnp.roll(shaped.reshape(rows, cols, D), half, axis=1)


def after(value, *others):
    return lax.optimization_barrier((value, others))[0]


def swapped(value, axis, flip):
    count = lax.axis_size(axis)
    return lax.ppermute(value, axis, [(i, i ^ flip) for i in range(count)])


def from_pages(value):
    pages = lax.axis_size("page")
    return [value] + [swapped(value, "page", k) for k in range(1, pages)]


def spread_first(shares):
    parts = from_pages(jnp.stack(shares))
    return [jnp.stack([part[k] for part in parts]) for k in range(2)]


def spread_second(held, *gate):
    got = swapped(held[0], "blk", 2), swapped(held[1], "blk", 4)
    held, got = after((held, got), *gate)
    return [jnp.concatenate([held[k], got[k]]) for k in range(2)]


def spread_third(near):
    return [swapped(near[0], "blk", 4), swapped(near[1], "blk", 2)]


def spread_core(held):
    return [swapped(value, "blk", 1) for value in held]


def lane_arrays(near, far, near_core, far_core, lane):
    return [near[lane], far[lane], near_core[lane], far_core[lane]]


def added(left, right):
    return (left.astype(f32) + right.astype(f32)).astype(bf16)


def collect_first(keep, send, *gate):
    got = swapped(send, "blk", 1)
    keep = after(keep, *gate)
    return [[added(keep[k, i : i + 8], got[k, i : i + 8]) for i in (0, 8)] for k in range(2)]


def collect_second(held, *gate):
    got = swapped(held[0][1], "blk", 2), swapped(held[1][1], "blk", 4)
    kept = after([held[0][0], held[1][0]], *gate)
    return [[added(kept[k][i : i + 4], got[k][i : i + 4]) for i in (0, 4)] for k in range(2)]


def collect_third(held, *gate):
    got = swapped(held[0][1], "blk", 4), swapped(held[1][1], "blk", 2)
    kept = after([held[0][0], held[1][0]], *gate)
    sums = [added(kept[k], got[k]) for k in range(2)]
    return [jnp.stack([sums[k][i] for k in range(2)]) for i in range(4)]


def collect_last(held, *gate):
    total = after(held[0], *gate).astype(f32)
    for k in range(1, 4):
        total = total + swapped(held[k], "page", k).astype(f32)
    return total


def blocks_in_chip(parts, gate):
    keep, send = parts
    got = swapped(send, "blk", 1)
    keep = after(keep, gate)
    return [added(keep[k], got[k]) for k in range(4)]


def blocks_over_chips(chips, gate):
    total = after(chips[0], gate).astype(f32)
    for k in range(1, 4):
        total = total + swapped(chips[k], "blk", 2 * k).astype(f32)
    return total


def scattered_blocks(part):
    return lax.psum_scatter(part, "blk", scatter_dimension=0, tiled=True)


def on_device(
    visual,
    query_tokens,
    answer_len,
    attn_swin,
    attn_self,
    attn_qv,
    attn_vq,
    mlp_up,
    mlp_down,
    norm_gains,
    visual_cot,
    query_cot,
):
    everyone = ("page", "blk")
    pages = lax.axis_size("page")
    page_here = lax.axis_index("page")
    blk_count = lax.axis_size("blk")
    blk_here = lax.axis_index("blk")
    shards = pages * blk_count
    rows_here, cols_all = visual.shape[1], visual.shape[2]
    half = rows_here // 2
    tokens = rows_here * cols_all
    q_rows = query_tokens.shape[1]
    slots = q_rows * blk_count
    share = attn_swin.shape[0] // D
    staged = pages == 4 and blk_count == 8 and share % 32 == 0
    gain_width = norm_gains.shape[0]
    core_here = blk_here % 2

    where = jnp.stack(
        [
            blk_here * q_rows,
            answer_len[0],
            (blk_here == blk_count - 1).astype(jnp.int32),
            page_here,
            blk_here,
        ]
    ).astype(jnp.int32)

    def flat_share(value):
        return value.astype(bf16).reshape(share, D)

    gain_rows = jnp.pad(norm_gains.astype(bf16)[None], ((0, 15), (0, D - gain_width)))
    slot_own = jnp.concatenate([query_tokens[0], query_cot[0], gain_rows], axis=0)
    slots_joined = lax.all_gather(slot_own, "blk", axis=0)
    slot_arrays = [slots_joined]
    gain_parts = jnp.stack(from_pages(slots_joined[:, 2 * q_rows, :gain_width].reshape(-1)))
    gains = jnp.take(gain_parts, jnp.arange(pages) ^ page_here, axis=0)
    gains = gains.reshape(8, D).astype(f32)
    if staged:
        a_z = spread_first([flat_share(attn_self), flat_share(attn_swin)])
        a_near = spread_second(a_z)
        c_z = spread_first(after([flat_share(attn_qv), flat_share(attn_vq)], a_z))
        a_far = spread_third(a_near)
        a_near_core, a_far_core = spread_core(a_near), spread_core(a_far)
        w_self, w_swin = [
            Stored(lane_arrays(a_near, a_far, a_near_core, a_far_core, k), (k,)) for k in range(2)
        ]
        up_groups = after(mlp_up, a_near).astype(bf16)
        up_groups = up_groups.reshape(share // 4, 2, 2, D).transpose(1, 2, 0, 3)
        mine = jnp.where(core_here == 0, up_groups[0], up_groups[1])
        other = swapped(jnp.where(core_here == 0, up_groups[1], up_groups[0]), "blk", 1)
        up_share = jnp.where(
            core_here == 0,
            jnp.concatenate([mine, other], axis=1),
            jnp.concatenate([other, mine], axis=1),
        ).reshape(share, D)
        d_z = spread_first(after([up_share, flat_share(mlp_down)], c_z))
        c_near = spread_second(after(c_z, a_far, gains))
        c_far = spread_third(c_near)
    else:
        up_share = (
            mlp_up.astype(bf16).reshape(share // 4, 4, D).transpose(1, 0, 2).reshape(share, D)
        )
        joined = lax.all_gather(
            jnp.concatenate(
                [flat_share(v) for v in (attn_self, attn_swin, attn_qv, attn_vq, mlp_down)]
                + [up_share],
                axis=0,
            ),
            everyone,
            axis=0,
            tiled=True,
        ).reshape(shards, -1, D)
        w_self, w_swin, w_qv, w_vq, w_down = [
            Stored([joined[:, k * share : (k + 1) * share].reshape(4, D, D)]) for k in range(5)
        ]
        up_all = joined[:, 5 * share : 6 * share].reshape(shards, 4, share // 4, D)
        w_up = Stored([up_all.transpose(1, 0, 2, 3).reshape(4, D, D)])

    down_one = [(i, (i - 1) % blk_count) for i in range(blk_count)]
    up_one = [(i, (i + 1) % blk_count) for i in range(blk_count)]
    both = jnp.concatenate([visual, visual_cot], axis=0)
    if staged:
        both = after(both, a_near)
    lent = lax.ppermute(both[:, :half], "blk", down_one)
    both = jnp.concatenate([both[:, half:], lent], axis=1)
    vis_in = window_order(both[0], half)
    vis_cot = window_order(both[1], half)

    where_self = where_swin = where_cross = where_vq = where
    if staged:
        where_self = after(where, vis_in, vis_cot, a_near_core, a_far_core)
    b_all, q_self, kv_self, lse_self, o_self, y1, c_own = call(
        self_forward_kernel,
        [
            sds((slots, D), bf16),
            sds((q_rows, D), bf16),
            sds((slots, 2 * D), bf16),
            sds((q_rows, 128), f32),
            sds((q_rows, D), bf16),
            sds((q_rows, D), f32),
            sds((q_rows, D), bf16),
        ],
        [where_self, gains],
        slots=(slot_arrays, 0, q_rows),
        scratch=[pltpu.VMEM((q_rows, slots), f32)],
        loads=[(w_self, 1), (w_self, 2), (w_self, 0), (w_self, 3)],
        flops=15e-6 * 1.1e15,
        name="self_forward",
    )
    if staged:
        c_near_core = spread_core(c_near)
        c_far, c_near_core = after((c_far, c_near_core), c_own)
        c_far_core = spread_core(c_far)
        w_qv, w_vq = [
            Stored(lane_arrays(c_near, c_far, c_near_core, c_far_core, k), (k,)) for k in range(2)
        ]
        where_swin = after(where, c_far, c_near_core)
        d_z = after(d_z, c_far)
    c_all = lax.all_gather(c_own, "blk", axis=0, tiled=True)

    def swin_forward(*refs):
        swin_forward_kernel(rows_here, *refs)

    a_low, qkv_swin, lse_swin, o_swin, v1, e_low = call(
        swin_forward,
        [
            sds((tokens, D), bf16),
            sds((tokens, 3 * D), bf16),
            sds((tokens, 128), f32),
            sds((tokens, D), bf16),
            sds((tokens, D), f32),
            sds((tokens, D), bf16),
        ],
        [where_swin, vis_in, gains],
        scratch=[pltpu.VMEM((cols_all // rows_here, rows_here**2, rows_here**2), f32)],
        loads=[(w_swin, k) for k in range(4)],
        flops=11e-6 * 1.1e15,
        name="swin_forward",
    )

    if staged:
        d_near = spread_second(d_z, e_low)
        d_far = spread_third(d_near)
        where_cross = after(where, d_near)
    qa, kvb, doa, kva, qb, stats = call(
        cross_forward_kernel,
        [
            sds((slots, D), bf16),
            sds((slots, 2 * D), bf16),
            sds((slots, D), bf16),
            sds((tokens, 2 * D), bf16),
            sds((tokens, D), bf16),
            sds((3, 16, slots), f32),
        ],
        [where_cross, c_all, e_low],
        slots=(slot_arrays, 1, q_rows),
        loads=[(w_qv, 1), (w_qv, 2), (w_vq, 0), (w_qv, 0), (w_vq, 1), (w_vq, 2), (w_qv, 3)],
        flops=18e-6 * 1.1e15,
        name="cross_forward",
    )
    if staged:
        d_far = after(d_far, qb)
        d_near_core, d_far_core = spread_core(d_near), spread_core(d_far)
        w_up, w_down = [
            Stored(lane_arrays(d_near, d_far, d_near_core, d_far_core, k), (k,)) for k in range(2)
        ]
        where_vq = after(where, d_far)
    lse_vq, o_vq = call(
        vq_forward_kernel,
        [sds((tokens, 128), f32), sds((tokens, D), bf16)],
        [where_vq, qb, kvb],
        flops=11e-6 * 1.1e15,
        name="vq_forward",
    )

    all_stats = lax.all_gather(stats, "blk", axis=0)
    peaks = jnp.max(all_stats[:, 0], axis=0)
    weights = jnp.exp(all_stats[:, 0] - peaks[None])
    totals = jnp.sum(all_stats[:, 1] * weights, axis=0)
    lse_qv = peaks + jnp.log(totals)
    centre_qv = jnp.sum(all_stats[:, 2] * weights, axis=0) / totals

    v3, h_low, act_low, du_low, g2, dz_vq, dob, dg5 = call(
        mlp_kernel,
        [
            sds((tokens, D), bf16),
            sds((tokens, D), bf16),
            sds((tokens, FF), bf16),
            sds((tokens, FF), bf16),
            sds((tokens, D), f32),
            sds((tokens, D), bf16),
            sds((tokens, D), bf16),
            sds((1, D), f32),
        ],
        [where, v1, o_vq, vis_cot, gains],
        scratch=[pltpu.VMEM((tokens, D), f32)] * 3,
        loads=[(w_vq, 3), (w_up, None)] + [(w_down, k) for k in range(4)],
        flops=14e-6 * 1.1e15,
        name="mlp",
    )

    def back_to_grid(value, *gate):
        grid = grid_order(value, rows_here, cols_all, half)
        returned = lax.ppermute(grid[half:], "blk", up_one)
        returned, grid = after((returned, grid), *gate)
        return jnp.concatenate([returned, grid[:half]], axis=0)[None]

    def flat(value):
        return value.astype(f32).reshape(-1)

    def gains_over_pages(db_all):
        gain_sum = db_all[q_rows, : pages * gain_width].reshape(pages, gain_width).astype(f32)
        kept = jnp.take(gain_sum, page_here, axis=0)
        for k in range(1, pages):
            kept = kept + swapped(jnp.take(gain_sum, page_here ^ k, axis=0), "page", k)
        return kept

    def with_gains(held, db_all):
        gain_sum = db_all[q_rows, : pages * gain_width].reshape(pages, gain_width)
        joined = []
        for k in range(pages):
            row = jnp.take(gain_sum, page_here ^ k, axis=0)[None, None]
            row = jnp.pad(row, ((0, 1), (0, 7), (0, D - gain_width)))
            joined.append(jnp.concatenate([held[k], row], axis=1))
        return joined

    def up_over_core(mlp_sum):
        up_sum = mlp_sum[0].reshape(2, 2, share // 4, D)
        mine = jnp.where(core_here == 0, up_sum[:, 0], up_sum[:, 1])
        other = swapped(jnp.where(core_here == 0, up_sum[:, 1], up_sum[:, 0]), "blk", 1)
        joined_up = jnp.where(
            core_here == 0,
            jnp.concatenate([mine, other], axis=0),
            jnp.concatenate([other, mine], axis=0),
        )
        return flat(joined_up.transpose(1, 0, 2))

    up_entries = [(h_low, 0, du_low, k, "tn") for k in range(4)]
    down_entries = [(act_low, k, vis_cot, 0, "tn") for k in range(4)]
    where_vq_back = where
    if staged:
        m_keep, m_send = weight_grad_call(
            after(where, lse_qv, centre_qv), [((0,), "up", up_entries), ((1,), "rows", down_entries)], "mlp_grads"
        )
        where_vq_back = after(where, m_keep)

    dqb, dkvbt = call(
        vq_backward_kernel,
        [sds((tokens, D), bf16), sds((2 * D, slots), bf16)],
        [where_vq_back, qb, kvb, dob, lse_vq],
        flops=16e-6 * 1.1e15,
        name="vq_backward",
    )
    where_swin_back = where_self_back = where_qv_back = where
    if staged:
        visual_out = back_to_grid(after(v3, m_keep))
        where_qv_back = after(where, visual_out)
        m_one = collect_first(m_keep, m_send, dqb)
        where_qv_back = after(where, visual_out, m_one)
    dqat, dkva, *merged_parts = call(
        qv_backward_kernel,
        [sds((D, slots), bf16), sds((tokens, 2 * D), bf16)] + [sds((slots, 2 * D), bf16)],
        [where_qv_back, qa, kva, doa, lse_qv, centre_qv, dkvbt],
        scratch=[pltpu.VMEM((slots, 2 * D), bf16)],
        loads=[(w_qv, 0), (w_vq, 1), (w_vq, 2)],
        flops=23e-6 * 1.1e15,
        name="qv_backward",
    )
    merged = scattered_blocks(merged_parts[0])
    if staged:
        m_two = collect_second(m_one, dqat)
        where_swin_back = after(where, m_two)
    dc, oa_low = merged[:, :D], merged[:, D:]

    def swin_backward(*refs):
        swin_backward_kernel(rows_here, *refs)

    dz_swin, dqkv_swin, visual_grad, dg_visual = call(
        swin_backward,
        [
            sds((tokens, D), bf16),
            sds((tokens, 3 * D), bf16),
            sds((tokens, D), f32),
            sds((2, D), f32),
        ],
        [where_swin_back, vis_in, v1, g2, gains, dkva, dqb, qkv_swin, lse_swin],
        scratch=[
            pltpu.VMEM((cols_all // rows_here, rows_here**2, rows_here**2), f32),
            pltpu.VMEM((tokens, D), bf16),
        ],
        loads=[(w_qv, 1), (w_qv, 2), (w_vq, 0), (w_swin, 3)] + [(w_swin, k) for k in range(3)],
        flops=20e-6 * 1.1e15,
        name="swin_backward",
    )

    swin_entries = [(a_low, 0, dqkv_swin, k, "tn") for k in range(3)]
    swin_entries.append((o_swin, 0, dz_swin, 0, "tn"))
    vq_entries = [
        (e_low, 0, dqb, 0, "tn"),
        (c_all, 0, dkvbt, 0, "tt"),
        (c_all, 0, dkvbt, 1, "tt"),
        (o_vq, 0, dz_vq, 0, "tn"),
    ]
    qv_entries = [
        (c_all, 0, dqat, 0, "tt"),
        (e_low, 0, dkva, 0, "tn"),
        (e_low, 0, dkva, 1, "tn"),
        (oa_low, 0, query_cot[0], 0, "tn"),
    ]
    if staged:
        m_three = collect_third(m_two, dz_swin)
        p_keep, p_send = weight_grad_call(
            after(where, m_three), [((0,), "rows", vq_entries), ((1,), "rows", swin_entries)], "patch_grads"
        )
        p_one = collect_first(p_keep, p_send)
        where_self_back = after(where, p_one)

    gy1, dz_self, dq_self, dkvt_self, dbq, dg_slots, db_part = call(
        self_backward_kernel,
        [
            sds((q_rows, D), f32),
            sds((q_rows, D), bf16),
            sds((q_rows, D), bf16),
            sds((2 * D, slots), bf16),
            sds((q_rows, D), f32),
            sds((2, D), f32),
        ]
        + [sds((slots, D), bf16)],
        [where_self_back, dc, y1, query_cot[0], gains, q_self, kv_self, lse_self],
        slots=(slot_arrays, 0, q_rows),
        scratch=[
            pltpu.VMEM((q_rows, slots), f32),
            pltpu.VMEM((q_rows, D), bf16),
            pltpu.VMEM((slots, D), bf16),
        ],
        loads=[(w_self, 3), (w_self, 0), (w_self, 1), (w_self, 2)],
        flops=15e-6 * 1.1e15,
        name="self_backward",
    )
    b_own = lax.dynamic_slice_in_dim(b_all, blk_here * q_rows, q_rows, 0)
    self_entries = [
        (b_own, 0, dq_self, 0, "tn"),
        (b_all, 0, dkvt_self, 0, "tt"),
        (b_all, 0, dkvt_self, 1, "tt"),
        (o_self, 0, dz_self, 0, "tn"),
    ]
    gain_block = jnp.concatenate(
        [dg_visual[0:1], dg_slots[0:1], dg_visual[1:2], dg_slots[1:2], dg5, jnp.zeros((3, D), f32)],
        axis=0,
    )
    gain_block = gain_block.astype(bf16).reshape(pages, blk_count, gain_width).transpose(1, 0, 2)
    gain_block = gain_block.reshape(blk_count, 1, pages * gain_width)
    gain_block = jnp.pad(gain_block, ((0, 0), (0, 15), (0, D - pages * gain_width)))
    whole_part = jnp.concatenate([db_part.reshape(blk_count, q_rows, D), gain_block], axis=1)
    db_all = scattered_blocks(whole_part.reshape(blk_count * (q_rows + 16), D))
    where_end = where
    if staged:
        p_two = collect_second(p_one, gy1)
        mlp_sum = collect_last(m_three, gy1)
        z_keep, z_send = weight_grad_call(
            after(where, p_two, mlp_sum), [((0,), "rows", qv_entries), ((1,), "rows", self_entries)], "slot_grads"
        )
        visual_grad = back_to_grid(visual_grad, z_keep)
        z_keep, z_send = after((z_keep, z_send), visual_grad)
        z_one = collect_first(z_keep, z_send)
        p_three = collect_third(p_two, z_one)
        z_two = collect_second(after(z_one, p_three))
        patch_sum = collect_last(after(p_three, z_one))
        db_all = after(db_all, patch_sum)
        up_grad = up_over_core(mlp_sum)
        z_two = after(z_two, patch_sum, up_grad)
        z_three = with_gains(collect_third(z_two), db_all)
        where_end = after(where, z_three)
    db = db_all[:q_rows]
    query_grad, query_out = call(
        query_end_kernel,
        [sds((q_rows, D), f32), sds((q_rows, D), bf16)],
        [where_end, db, dbq, query_tokens[0], gy1, gains, y1, oa_low],
        loads=[(w_qv, 3)],
        name="query_end",
    )

    if staged:
        slot_sum = collect_last(z_three)
        gain_grad, slot_sum = slot_sum[0, share, :gain_width], slot_sum[:, :share]
        swin_grad, self_grad = flat(patch_sum[1]), flat(slot_sum[1])
        qv_grad, vq_grad = flat(slot_sum[0]), flat(patch_sum[0])
        down_grad = flat(mlp_sum[1])
    else:
        visual_out, visual_grad = back_to_grid(v3), back_to_grid(visual_grad)
        gain_grad = gains_over_pages(db_all)

        def outer(left, right):
            return tn(left, right).astype(bf16)

        def outer_t(left, right_t):
            return lax.dot_general(
                left, right_t, (((0,), (1,)), ((), ())), preferred_element_type=f32
            ).astype(bf16)

        def as_shares(mats):
            return jnp.concatenate(mats, axis=0).reshape(shards, share, D)

        def summed(parts):
            joined = jnp.concatenate(parts, axis=1)
            width = joined.shape[1]
            return lax.psum_scatter(
                joined.reshape(shards * width, D), everyone, scatter_dimension=0, tiled=True
            )

        up_mats = jnp.stack([outer(h_low, du_low[:, k * D : (k + 1) * D]) for k in range(4)])
        up_part = (
            up_mats.reshape(4, shards, share // 4, D)
            .transpose(1, 0, 2, 3)
            .reshape(shards, share, D)
        )
        down_part = outer(act_low, vis_cot).reshape(shards, share, D)
        mlp_sum = summed([up_part, down_part])
        qv_part = as_shares(
            [
                outer_t(c_all, dqat),
                outer(e_low, dkva[:, :D]),
                outer(e_low, dkva[:, D:]),
                outer(oa_low, query_cot[0]),
            ]
        )
        vq_part = as_shares(
            [
                outer(e_low, dqb),
                outer_t(c_all, dkvbt[:D]),
                outer_t(c_all, dkvbt[D:]),
                outer(o_vq, dz_vq),
            ]
        )
        cross_sum = summed([qv_part, vq_part])
        swin_part = as_shares(
            [outer(a_low, dqkv_swin[:, k * D : (k + 1) * D]) for k in range(3)]
            + [outer(o_swin, dz_swin)]
        )
        self_part = as_shares(
            [
                outer(b_own, dq_self),
                outer_t(b_all, dkvt_self[:D]),
                outer_t(b_all, dkvt_self[D:]),
                outer(o_self, dz_self),
            ]
        )
        last_sum = summed([swin_part, self_part])
        up_grad = flat(mlp_sum[:share].reshape(4, share // 4, D).transpose(1, 0, 2))
        down_grad = flat(mlp_sum[share:])
        qv_grad, vq_grad = flat(cross_sum[:share]), flat(cross_sum[share:])
        swin_grad, self_grad = flat(last_sum[:share]), flat(last_sum[share:])

    return (
        visual_out,
        query_out[None],
        visual_grad,
        query_grad[None],
        swin_grad,
        self_grad,
        qv_grad,
        vq_grad,
        up_grad,
        down_grad,
        gain_grad,
    )


def solution(mesh):
    placed = (
        P("page", "blk", None, None),
        P("page", "blk", None),
        P("page"),
        P(("page", "blk")),
        P(("page", "blk")),
        P(("page", "blk")),
        P(("page", "blk")),
        P(("page", "blk")),
        P(("page", "blk")),
        P(("page", "blk")),
        P("page", "blk", None, None),
        P("page", "blk", None),
    )
    return jax.shard_map(
        on_device,
        mesh=mesh,
        in_specs=placed,
        out_specs=(
            P("page", "blk", None, None),
            P("page", "blk", None),
            P("page", "blk", None, None),
            P("page", "blk", None),
            P(("page", "blk")),
            P(("page", "blk")),
            P(("page", "blk")),
            P(("page", "blk")),
            P(("page", "blk")),
            P(("page", "blk")),
            P(("page", "blk")),
        ),
        check_vma=False,
    )
```

```python
import jax
import jax.numpy as jnp
from jax import lax
from jax.experimental import pallas as pl
from jax.experimental.pallas import tpu as pltpu
from jax.sharding import PartitionSpec as P

D = 768
HEADS = 12
HD = 64
FF = 3072
PAIRS = HEADS // 2
PW = 2 * HD
SCALE = HD ** (-0.5)

EPS = 1e-05
NEG = -1e30

bf16 = jnp.bfloat16
f32 = jnp.float32
VMEM_LIMIT = 56 * 1024 * 1024


def nn(left, right):
    return lax.dot_general(left, right, (((1,), (0,)), ((), ())), preferred_element_type=f32)


def nt(left, right):
    return lax.dot_general(left, right, (((1,), (1,)), ((), ())), preferred_element_type=f32)


def tn(left, right):
    return lax.dot_general(left, right, (((0,), (0,)), ((), ())), preferred_element_type=f32)


def norm_parts(rows):
    centre = jnp.mean(rows, axis=-1, keepdims=True)
    centred = rows - centre
    spread = jnp.mean(centred * centred, axis=-1, keepdims=True)
    inverse = lax.rsqrt(spread + EPS)
    return centred * inverse, inverse


def norm(rows, gain):
    return norm_parts(rows)[0] * gain


def norm_back(rows, gain, grad):
    unit, inverse = norm_parts(rows)
    grad_gain = jnp.sum(grad * unit, axis=0, keepdims=True)
    scaled = grad * gain
    first = jnp.mean(scaled, axis=-1, keepdims=True)
    second = jnp.mean(scaled * unit, axis=-1, keepdims=True)
    return inverse * (scaled - first - unit * second), grad_gain


def lane_half(half, value, dtype):
    lanes = lax.broadcasted_iota(jnp.int32, (1, PW), 1)
    return jnp.where((lanes // HD) == half, value, 0.0).astype(dtype)


def low_half(rows):
    return lax.broadcasted_iota(jnp.int32, (rows, PW), 1) < HD


def column(table, index):
    lanes = lax.broadcasted_iota(jnp.int32, table.shape, 1)
    return jnp.sum(jnp.where(lanes == index, table, 0.0), axis=-1, keepdims=True)


def pair_cols(pair, base=0):
    return pl.ds(pl.multiple_of(base + pair * PW, PW), PW)


def softmax_rows(scores):
    highest = jnp.max(scores, axis=-1, keepdims=True)
    raised = jnp.exp(scores - highest)
    totals = jnp.sum(raised, axis=-1, keepdims=True)
    return raised * (1.0 / totals), highest + jnp.log(totals)


class Stored:
    def __init__(self, arrays, lanes=(), joint=None):
        self.arrays = list(arrays)
        self.lanes = tuple(lanes)
        self.joint = joint


def stage_bits(lane):
    return (1, 2) if lane == 0 else (2, 1)


def relative(lane, core, first, second):
    bit_one, bit_two = stage_bits(lane)
    return core | (first << bit_one) | (second << bit_two)


def local_copy(source, target, sem):
    pltpu.make_async_copy(source, target, sem).start()


def fetch(where_ref, stored, refs, index, target, sem):
    if stored.joint is not None:
        first, rows = stored.joint
        count = D // rows
        for k in range(count):
            piece = refs[0].at[index * count + k, first : first + rows]
            local_copy(piece, target.at[k * rows : (k + 1) * rows], sem)
        return
    if len(refs) == 1:
        local_copy(refs[0].at[index], target, sem)
        return
    page, blk = where_ref[3], where_ref[4]
    count = len(stored.lanes)
    for number, lane in enumerate(stored.lanes):
        for core in range(2):
            for second in range(2):
                for first in range(2):
                    ref = refs[4 * number + 2 * core + second]
                    piece = ref.at[(index ^ page) + 4 * first]
                    rows = piece.shape[0]
                    owner = blk ^ relative(lane, core, first, second)
                    start = pl.multiple_of((owner * count + number) * rows, rows)
                    local_copy(piece, target.at[pl.ds(start, rows)], sem)


def fetch_up(where_ref, stored, refs, target, sem):
    if len(refs) == 1:
        local_copy(refs[0], target, sem)
        return
    page, blk = where_ref[3], where_ref[4]
    for core in range(2):
        for second in range(2):
            for first in range(2):
                ref = refs[2 * core + second]
                near = (blk ^ relative(stored.lanes[0], 0, first, second)) >> 1
                for origin in range(4):
                    piece = ref.at[(origin ^ page) + 4 * first]
                    rows = piece.shape[0] // 2
                    spot = pl.ds(pl.multiple_of((origin * 4 + near) * rows, rows), rows)
                    for k in range(2):
                        group = 2 * ((blk & 1) ^ core) + k
                        local_copy(piece.at[k * rows : (k + 1) * rows], target.at[group, spot], sem)


class Loads:
    def __init__(self, held, sems, plan):
        self.held, self.sems, self.plan, self.done = held, sems, plan, set()

    def ready(self, *places):
        for place in places:
            if place not in self.done:
                self.done.add(place)
                start, count = self.plan[place]
                span = self.held.at[start : start + count]
                pltpu.make_async_copy(span, span, self.sems.at[place]).wait()

    def __getitem__(self, place):
        self.ready(place)
        return self.held[self.plan[place][0]]

    def part(self, place, k):
        return self.held[self.plan[place][0] + k]


def call(kernel, outs, ins, scratch=(), smem=1, loads=(), slots=None, flops=0, name=None):
    def whole(value):
        zeros = (0,) * len(value.shape)
        return pl.BlockSpec(value.shape, lambda i: zeros, pipeline_mode=pl.Buffered(1))

    specs = []
    for index, value in enumerate(ins):
        if index < smem:
            specs.append(pl.BlockSpec(memory_space=pltpu.SMEM))
        else:
            specs.append(whole(value))
    single = not isinstance(outs, list)
    shapes = [outs] if single else outs
    count_in, count_out = len(ins), len(shapes)
    unique, plan, size = [], [], 0
    for stored, which in loads:
        if stored not in unique:
            unique.append(stored)
        width = 4 if which is None else 1
        plan.append((size, width))
        size += width
    arrays = [array for stored in unique for array in stored.arrays]
    gathered, slot_scratch = [], []
    if slots:
        gathered, part, own = slots
        blocks = len(gathered) if len(gathered) > 1 else gathered[0].shape[0]
        slot_scratch = [pltpu.VMEM((blocks, own, D), bf16), pltpu.SemaphoreType.DMA]
    held = [pltpu.VMEM((size, D, D), bf16), pltpu.SemaphoreType.DMA((len(plan),))] if loads else []

    def body(*refs):
        inner = list(refs[:count_in])
        at = count_in
        taken = {}
        for stored in unique:
            taken[id(stored)] = refs[at : at + len(stored.arrays)]
            at += len(stored.arrays)
        pieces = refs[at : at + len(gathered)]
        at += len(gathered)
        results = list(refs[at : at + count_out])
        rest = list(refs[at + count_out :])
        if slots:
            together, slot_sem = rest[:2]
            rest = rest[2:]
            rows = slice(part * own, (part + 1) * own)
            if len(pieces) == 1:
                local_copy(pieces[0].at[:, rows], together, slot_sem)
            for k, piece in enumerate(pieces if len(pieces) > 1 else ()):
                local_copy(piece.at[rows], together.at[inner[0][4] ^ k], slot_sem)
            inner.append(together)
        if not loads:
            kernel(*inner, *results, *rest)
            return
        kept, sems = rest[-2], rest[-1]
        for place, (stored, which) in enumerate(loads):
            mine, (start, width) = taken[id(stored)], plan[place]
            if which is None:
                fetch_up(inner[0], stored, mine, kept.at[start : start + width], sems.at[place])
            else:
                fetch(inner[0], stored, mine, which, kept.at[start], sems.at[place])
        if slots:
            pltpu.make_async_copy(together, together, slot_sem).wait()
        weights = Loads(kept, sems, plan)
        kernel(*inner, weights, *results, *rest[:-2])
        weights.ready(*range(len(plan)))

    moved = sum(v.size * v.dtype.itemsize for v in list(ins) + shapes) + size * D * D * 2
    result = pl.pallas_call(
        body,
        grid=(1,),
        out_shape=shapes,
        in_specs=specs + [pl.BlockSpec(memory_space=pl.ANY)] * (len(arrays) + len(gathered)),
        out_specs=[whole(value) for value in shapes],
        scratch_shapes=slot_scratch + list(scratch) + held,
        compiler_params=pltpu.CompilerParams(
            vmem_limit_bytes=VMEM_LIMIT, dimension_semantics=("arbitrary",)
        ),
        cost_estimate=pl.CostEstimate(flops=int(flops), bytes_accessed=int(moved), transcendentals=0),
        name=name,
    )(*ins, *arrays, *gathered)
    return result[0] if single else result


def sds(shape, dtype):
    return jax.ShapeDtypeStruct(shape, dtype)


def self_bias(bias_ref, first_row, live):
    rows, slots = bias_ref.shape
    keys = lax.broadcasted_iota(jnp.int32, (rows, slots), 1)
    places = lax.broadcasted_iota(jnp.int32, (rows, slots), 0) + first_row
    bias_ref[...] = jnp.where((keys <= places) & (keys < live), 0.0, NEG)


def self_forward_kernel(
    where_ref, g_ref, y_ref, w, b_ref, q_ref, kv_ref, lse_ref, o_ref, y1_ref, c_ref, bias_ref
):
    first_row, live = where_ref[0], where_ref[1]
    slots, own = b_ref.shape[0], q_ref.shape[0]
    tile = 256
    group = tile // own
    w.ready(0, 1)

    def project(i, carry):
        rows = pl.ds(pl.multiple_of(i * tile, tile), tile)
        part = y_ref[pl.ds(i * group, group)].reshape(tile, D)
        normed = norm(part.astype(f32), g_ref[1:2, :]).astype(bf16)
        b_ref[rows, :] = normed
        kv_ref[rows, 0:D] = nn(normed, w[0]).astype(bf16)
        kv_ref[rows, D : 2 * D] = nn(normed, w[1]).astype(bf16)
        return carry

    lax.fori_loop(0, slots // tile, project, 0)
    mine = pl.ds(pl.multiple_of(first_row, 16), own)
    q_ref[...] = nn(b_ref[mine, :], w[2]).astype(bf16)
    self_bias(bias_ref, first_row, live)
    lse_ref[...] = jnp.zeros_like(lse_ref)
    lanes = lax.broadcasted_iota(jnp.int32, lse_ref.shape, 1)
    low = low_half(own)

    def attend(pair, carry):
        queries = q_ref[:, pair_cols(pair)]
        keys = kv_ref[:, pair_cols(pair)]
        values = kv_ref[:, pair_cols(pair, D)]
        mixed = []
        table = lse_ref[...]
        for half in range(2):
            scores = nt(queries * lane_half(half, SCALE, bf16), keys) + bias_ref[...]
            chances, log_totals = softmax_rows(scores)
            mixed.append(nn(chances.astype(bf16), values))
            table = jnp.where(lanes == 2 * pair + half, log_totals, table)
        lse_ref[...] = table
        o_ref[:, pair_cols(pair)] = jnp.where(low, mixed[0], mixed[1]).astype(bf16)
        return carry

    lax.fori_loop(0, PAIRS, attend, 0)
    y1 = y_ref[where_ref[4]].astype(f32) + nn(o_ref[...], w[3])
    y1_ref[...] = y1
    c_ref[...] = norm(y1, g_ref[3:4, :]).astype(bf16)


def window_bias(rows, side, row_split, col_split):
    def flags(shape, dim):
        token = lax.broadcasted_iota(jnp.int32, shape, dim)
        row, col = token // side, token % side
        return jnp.where(row >= side // 2, row_split, 0) + jnp.where(
            col >= side // 2, 2 * col_split, 0
        )

    return jnp.where(flags((rows, rows), 0) == flags((rows, rows), 1), 0.0, NEG)


def swin_forward_kernel(
    side, where_ref, x_ref, g_ref, w, a_ref, qkv_ref, lse_ref, o_ref, v1_ref, e_ref, bias_ref
):
    is_last = where_ref[2]
    tokens = x_ref.shape[0]
    rows = side * side
    windows = tokens // rows
    x = x_ref[...].astype(f32)
    normed = norm(x, g_ref[0:1, :]).astype(bf16)
    a_ref[...] = normed
    for k in range(3):
        qkv_ref[:, k * D : (k + 1) * D] = nn(normed, w[k]).astype(bf16)
    for win in range(windows):
        bias_ref[win] = window_bias(rows, side, is_last, 1 if win == windows - 1 else 0)
    lse_ref[...] = jnp.zeros_like(lse_ref)
    lanes = lax.broadcasted_iota(jnp.int32, (rows, lse_ref.shape[1]), 1)
    low = low_half(rows)

    def attend(pair, carry):
        for win in range(windows):
            at = slice(win * rows, (win + 1) * rows)
            queries = qkv_ref[at, pair_cols(pair)]
            keys = qkv_ref[at, pair_cols(pair, D)]
            values = qkv_ref[at, pair_cols(pair, 2 * D)]
            mixed = []
            table = lse_ref[at, :]
            for half in range(2):
                scores = nt(queries * lane_half(half, SCALE, bf16), keys) + bias_ref[win]
                chances, log_totals = softmax_rows(scores)
                mixed.append(nn(chances.astype(bf16), values))
                table = jnp.where(lanes == 2 * pair + half, log_totals, table)
            lse_ref[at, :] = table
            o_ref[at, pair_cols(pair)] = jnp.where(low, mixed[0], mixed[1]).astype(bf16)
        return carry

    lax.fori_loop(0, PAIRS, attend, 0)
    v1 = x + nn(o_ref[...], w[3])
    v1_ref[...] = v1
    e_ref[...] = norm(v1, g_ref[2:3, :]).astype(bf16)


def cross_forward_kernel(
    where_ref,
    c_ref,
    e_ref,
    cot_ref,
    w,
    qa_ref,
    kvb_ref,
    doa_ref,
    kva_ref,
    qb_ref,
    stats_ref,
):
    slots, tokens = qa_ref.shape[0], e_ref.shape[0]
    tile = 256
    normed = e_ref[...]
    for k in range(2):
        kva_ref[:, k * D : (k + 1) * D] = nn(normed, w[k]).astype(bf16)
    qb_ref[...] = nn(normed, w[2]).astype(bf16)
    w.ready(3, 4, 5, 6)
    group = tile // cot_ref.shape[1]

    def project(i, carry):
        rows = pl.ds(pl.multiple_of(i * tile, tile), tile)
        part = c_ref[rows, :]
        qa_ref[rows, :] = nn(part, w[3]).astype(bf16)
        for k in range(2):
            kvb_ref[rows, k * D : (k + 1) * D] = nn(part, w[4 + k]).astype(bf16)
        cot = cot_ref[pl.ds(i * group, group)].reshape(tile, D)
        doa_ref[rows, :] = nt(cot, w[6]).astype(bf16)
        return carry

    lax.fori_loop(0, slots // tile, project, 0)
    stats_ref[...] = jnp.zeros_like(stats_ref)

    def page_stats(pair, carry):
        keys = kva_ref[:, pair_cols(pair)]
        values = kva_ref[:, pair_cols(pair, D)]
        for half in range(2):
            head = 2 * pair + half
            keys_h = keys * lane_half(half, SCALE, bf16)
            values_h = values * lane_half(half, 1.0, bf16)
            for i in range(slots // tile):
                rows = slice(i * tile, (i + 1) * tile)
                scores = nt(keys_h, qa_ref[rows, pair_cols(pair)])
                highest = jnp.max(scores, axis=0, keepdims=True)
                raised = jnp.exp(scores - highest)
                grads = nt(values_h, doa_ref[rows, pair_cols(pair)])
                stats_ref[0, pl.ds(head, 1), rows] = highest
                stats_ref[1, pl.ds(head, 1), rows] = jnp.sum(raised, axis=0, keepdims=True)
                stats_ref[2, pl.ds(head, 1), rows] = jnp.sum(raised * grads, axis=0, keepdims=True)
        return carry

    lax.fori_loop(0, PAIRS, page_stats, 0)


def vq_forward_kernel(where_ref, qb_ref, kvb_ref, lse_ref, ob_ref):
    live = where_ref[1]
    tokens, slots = qb_ref.shape[0], kvb_ref.shape[0]
    lse_ref[...] = jnp.zeros_like(lse_ref)
    lanes = lax.broadcasted_iota(jnp.int32, lse_ref.shape, 1)
    low = low_half(tokens)
    bias = jnp.where(lax.broadcasted_iota(jnp.int32, (1, slots), 1) < live, 0.0, NEG)

    def attend(pair, carry):
        queries = qb_ref[:, pair_cols(pair)]
        keys = kvb_ref[:, pair_cols(pair)]
        values = kvb_ref[:, pair_cols(pair, D)]
        mixed = []
        table = lse_ref[...]
        for half in range(2):
            scores = nt(queries * lane_half(half, SCALE, bf16), keys) + bias
            chances, log_totals = softmax_rows(scores)
            mixed.append(nn(chances.astype(bf16), values))
            table = jnp.where(lanes == 2 * pair + half, log_totals, table)
        lse_ref[...] = table
        ob_ref[:, pair_cols(pair)] = jnp.where(low, mixed[0], mixed[1]).astype(bf16)
        return carry

    lax.fori_loop(0, PAIRS, attend, 0)


GELU_A = 0.7978845608028654
GELU_B = 0.044715


def mlp_kernel(
    where_ref,
    v1_ref,
    ob_ref,
    cot_ref,
    g_ref,
    w,
    v3_ref,
    h_ref,
    act_ref,
    du_ref,
    g2_ref,
    dz_ref,
    dob_ref,
    dg_ref,
    v2_ref,
    sum_ref,
    dh_ref,
):
    v2 = v1_ref[...] + nn(ob_ref[...], w[0])
    v2_ref[...] = v2
    sum_ref[...] = v2
    h_ref[...] = norm(v2, g_ref[4:5, :]).astype(bf16)
    dh_ref[...] = jnp.zeros_like(dh_ref)
    w.ready(1, 2, 3, 4, 5)

    def chunk(k, carry):
        up, down = w.part(1, k), w.part(2, k)
        at = pl.ds(pl.multiple_of(k * D, D), D)
        u = nn(h_ref[...], up)
        squared = u * u
        bend = jnp.tanh(GELU_A * (u + GELU_B * u * squared))
        act = (0.5 * u * (1.0 + bend)).astype(bf16)
        act_ref[:, at] = act
        slope = 0.5 * (1.0 + bend) + 0.5 * u * (1.0 - bend * bend) * GELU_A * (
            1.0 + 3.0 * GELU_B * squared
        )
        du = (nt(cot_ref[...], down) * slope).astype(bf16)
        du_ref[:, at] = du
        sum_ref[...] += nn(act, down)
        dh_ref[...] += nt(du, up)
        return carry

    lax.fori_loop(0, FF // D, chunk, 0)
    v3_ref[...] = sum_ref[...].astype(bf16)
    part, dg = norm_back(v2_ref[...], g_ref[4:5, :], dh_ref[...])
    dg_ref[...] = dg
    g2 = cot_ref[...].astype(f32) + part
    g2_ref[...] = g2
    dz = g2.astype(bf16)
    dz_ref[...] = dz
    dob_ref[...] = nt(dz, w[0]).astype(bf16)


def vq_backward_kernel(
    where_ref, qb_ref, kvb_ref, dob_ref, lse_ref, dqb_ref, dkvbt_ref
):
    live = where_ref[1]
    tokens, slots = qb_ref.shape[0], kvb_ref.shape[0]
    bias = jnp.where(lax.broadcasted_iota(jnp.int32, (1, slots), 1) < live, 0.0, NEG)
    low = low_half(tokens)

    def back(pair, carry):
        queries = qb_ref[:, pair_cols(pair)]
        keys = kvb_ref[:, pair_cols(pair)]
        values = kvb_ref[:, pair_cols(pair, D)]
        grads = dob_ref[:, pair_cols(pair)]
        queries_t = (queries * SCALE).astype(f32).T.astype(bf16)
        grads_t = grads.astype(f32).T.astype(bf16)
        parts = []
        for half in range(2):
            own = slice(half * HD, (half + 1) * HD)
            scores = nt(queries * lane_half(half, SCALE, bf16), keys) + bias
            chances = jnp.exp(scores - column(lse_ref[...], 2 * pair + half))
            slopes = nt(grads * lane_half(half, 1.0, bf16), values)
            centre = jnp.sum(chances * slopes, axis=-1, keepdims=True)
            ds = (chances * (slopes - centre)).astype(bf16)
            parts.append(nn(ds, keys))
            at = pair * PW + half * HD
            dkvbt_ref[pl.ds(pl.multiple_of(at, HD), HD), :] = nn(queries_t[own], ds).astype(bf16)
            dkvbt_ref[pl.ds(pl.multiple_of(D + at, HD), HD), :] = nn(
                grads_t[own], chances.astype(bf16)
            ).astype(bf16)
        dqb_ref[:, pair_cols(pair)] = (jnp.where(low, parts[0], parts[1]) * SCALE).astype(bf16)
        return carry

    lax.fori_loop(0, PAIRS, back, 0)


def hand_out(where_ref, held, outs):
    if len(outs) == 1:
        outs[0][...] = held[...]
        return
    rows = outs[0].shape[1]
    for core, out in enumerate(outs):
        for k in range(4):
            start = pl.multiple_of((where_ref[4] ^ (2 * k + core)) * rows, rows)
            out[k] = held[pl.ds(start, rows), :]


def qv_backward_kernel(
    where_ref,
    qa_ref,
    kva_ref,
    doa_ref,
    lse_ref,
    centre_ref,
    dkvbt_ref,
    w,
    dqat_ref,
    dkva_ref,
    *rest,
):
    dc_refs, held = rest[:-1], rest[-1]
    slots, tokens = qa_ref.shape[0], kva_ref.shape[0]
    low = low_half(tokens)
    tile = 512

    def back(pair, carry):
        keys = kva_ref[:, pair_cols(pair)]
        values = kva_ref[:, pair_cols(pair, D)]
        keys_t = (keys * SCALE).astype(f32).T.astype(bf16)
        values_t = values.astype(f32).T.astype(bf16)
        for i in range(slots // tile):
            rows = slice(i * tile, (i + 1) * tile)
            queries = qa_ref[rows, pair_cols(pair)]
            grads = doa_ref[rows, pair_cols(pair)]
            dk, dv, mixed = [], [], []
            for half in range(2):
                head = 2 * pair + half
                own = slice(half * HD, (half + 1) * HD)
                scores = nt(keys * lane_half(half, SCALE, bf16), queries)
                chances = jnp.exp(scores - lse_ref[pl.ds(head, 1), rows])
                slopes = nt(values * lane_half(half, 1.0, bf16), grads)
                ds = (chances * (slopes - centre_ref[pl.ds(head, 1), rows])).astype(bf16)
                rounded = chances.astype(bf16)
                mixed.append(nn(values_t[own], rounded))
                dqat_ref[pl.ds(pl.multiple_of(head * HD, HD), HD), rows] = nn(
                    keys_t[own], ds
                ).astype(bf16)
                dk.append(nn(ds, queries))
                dv.append(nn(rounded, grads))
            held[rows, pair_cols(pair, D)] = jnp.concatenate(mixed, axis=0).T.astype(bf16)
            dk_now = jnp.where(low, dk[0], dk[1]) * SCALE
            dv_now = jnp.where(low, dv[0], dv[1])
            if i == 0:
                dk_sum, dv_sum = dk_now, dv_now
            else:
                dk_sum, dv_sum = dk_sum + dk_now, dv_sum + dv_now
        dkva_ref[:, pair_cols(pair)] = dk_sum.astype(bf16)
        dkva_ref[:, pair_cols(pair, D)] = dv_sum.astype(bf16)
        return carry

    lax.fori_loop(0, PAIRS, back, 0)
    for i in range(slots // tile):
        cols = slice(i * tile, (i + 1) * tile)
        total = nn(w[0], dqat_ref[:, cols])
        total += nn(w[1], dkvbt_ref[0:D, cols])
        total += nn(w[2], dkvbt_ref[D : 2 * D, cols])
        held[cols, 0:D] = total.T.astype(bf16)
    hand_out(where_ref, held, dc_refs)


def swin_backward_kernel(
    side,
    where_ref,
    x_ref,
    v1_ref,
    g2_ref,
    g_ref,
    dkva_ref,
    dqb_ref,
    qkv_ref,
    lse_ref,
    w,
    dz_ref,
    dqkv_ref,
    grad_ref,
    dg_ref,
    bias_ref,
    do_ref,
):
    is_last = where_ref[2]
    tokens = x_ref.shape[0]
    rows = side * side
    windows = tokens // rows
    de = nt(dkva_ref[:, 0:D], w[0])
    de += nt(dkva_ref[:, D : 2 * D], w[1])
    de += nt(dqb_ref[...], w[2])
    part, dg3 = norm_back(v1_ref[...], g_ref[2:3, :], de)
    g1 = g2_ref[...] + part
    grad_ref[...] = g1
    dz = g1.astype(bf16)
    dz_ref[...] = dz
    do_ref[...] = nt(dz, w[3]).astype(bf16)
    for win in range(windows):
        bias_ref[win] = window_bias(rows, side, is_last, 1 if win == windows - 1 else 0)
    low = low_half(rows)

    def back(pair, carry):
        for win in range(windows):
            at = slice(win * rows, (win + 1) * rows)
            queries = qkv_ref[at, pair_cols(pair)]
            keys = qkv_ref[at, pair_cols(pair, D)]
            values = qkv_ref[at, pair_cols(pair, 2 * D)]
            grads = do_ref[at, pair_cols(pair)]
            dq, dk, dv = [], [], []
            for half in range(2):
                scores = nt(queries * lane_half(half, SCALE, bf16), keys) + bias_ref[win]
                chances = jnp.exp(scores - column(lse_ref[at, :], 2 * pair + half))
                slopes = nt(grads * lane_half(half, 1.0, bf16), values)
                centre = jnp.sum(chances * slopes, axis=-1, keepdims=True)
                ds = (chances * (slopes - centre)).astype(bf16)
                dq.append(nn(ds, keys))
                dk.append(tn(ds, queries))
                dv.append(tn(chances.astype(bf16), grads))
            for k, (pieces, factor) in enumerate(((dq, SCALE), (dk, SCALE), (dv, 1.0))):
                dqkv_ref[at, pair_cols(pair, k * D)] = (
                    jnp.where(low, pieces[0], pieces[1]) * factor
                ).astype(bf16)
        return carry

    lax.fori_loop(0, PAIRS, back, 0)
    da = nt(dqkv_ref[:, 0:D], w[4])
    da += nt(dqkv_ref[:, D : 2 * D], w[5])
    da += nt(dqkv_ref[:, 2 * D : 3 * D], w[6])
    part, dg1 = norm_back(x_ref[...].astype(f32), g_ref[0:1, :], da)
    grad_ref[...] += part
    dg_ref[...] = jnp.concatenate([dg1, dg3], axis=0)


def self_backward_kernel(
    where_ref,
    dc_ref,
    y1_ref,
    cot_ref,
    g_ref,
    q_ref,
    kv_ref,
    lse_ref,
    y_ref,
    w,
    gy1_ref,
    dz_ref,
    dq_ref,
    dkvt_ref,
    dbq_ref,
    dg_ref,
    *rest,
):
    db_refs, (bias_ref, do_ref, db_held) = rest[:-3], rest[-3:]
    group = 256 // q_ref.shape[0]
    first_row, live = where_ref[0], where_ref[1]
    own_rows, slots = q_ref.shape[0], kv_ref.shape[0]
    part, dg = norm_back(y1_ref[...], g_ref[3:4, :], dc_ref[...].astype(f32))
    gy1 = cot_ref[...].astype(f32) + part
    gy1_ref[...] = gy1
    dz = gy1.astype(bf16)
    dz_ref[...] = dz
    do_ref[...] = nt(dz, w[0]).astype(bf16)
    self_bias(bias_ref, first_row, live)
    low = low_half(own_rows)

    def back(pair, carry):
        queries = q_ref[:, pair_cols(pair)]
        keys = kv_ref[:, pair_cols(pair)]
        values = kv_ref[:, pair_cols(pair, D)]
        grads = do_ref[:, pair_cols(pair)]
        queries_t = (queries * SCALE).astype(f32).T.astype(bf16)
        grads_t = grads.astype(f32).T.astype(bf16)
        parts = []
        for half in range(2):
            own = slice(half * HD, (half + 1) * HD)
            scores = nt(queries * lane_half(half, SCALE, bf16), keys) + bias_ref[...]
            chances = jnp.exp(scores - column(lse_ref[...], 2 * pair + half))
            slopes = nt(grads * lane_half(half, 1.0, bf16), values)
            centre = jnp.sum(chances * slopes, axis=-1, keepdims=True)
            ds = (chances * (slopes - centre)).astype(bf16)
            parts.append(nn(ds, keys))
            at = pair * PW + half * HD
            dkvt_ref[pl.ds(pl.multiple_of(at, HD), HD), :] = nn(queries_t[own], ds).astype(bf16)
            dkvt_ref[pl.ds(pl.multiple_of(D + at, HD), HD), :] = nn(
                grads_t[own], chances.astype(bf16)
            ).astype(bf16)
        dq_ref[:, pair_cols(pair)] = (jnp.where(low, parts[0], parts[1]) * SCALE).astype(bf16)
        return carry

    lax.fori_loop(0, PAIRS, back, 0)
    dbq = nt(dq_ref[...], w[1])
    dbq_ref[...] = dbq
    unit = norm_parts(y_ref[where_ref[4]].astype(f32))[0]
    dg2 = jnp.sum(dbq * unit, axis=0, keepdims=True)
    tile = 256
    for i in range(slots // tile):
        cols = slice(i * tile, (i + 1) * tile)
        total = nn(w[2], dkvt_ref[0:D, cols])
        total += nn(w[3], dkvt_ref[D : 2 * D, cols])
        back = total.T
        db_held[cols, :] = back.astype(bf16)
        part = y_ref[i * group : (i + 1) * group].reshape(tile, D)
        unit = norm_parts(part.astype(f32))[0]
        dg2 += jnp.sum(back * unit, axis=0, keepdims=True)
    dg_ref[...] = jnp.concatenate([dg2, dg], axis=0)
    hand_out(where_ref, db_held, db_refs)


def query_end_kernel(
    where_ref, db_ref, dbq_ref, y_ref, gy1_ref, g_ref, y1_ref, oa_ref, w, grad_ref, out_ref
):
    part, _ = norm_back(
        y_ref[...].astype(f32), g_ref[1:2, :], db_ref[...].astype(f32) + dbq_ref[...]
    )
    grad_ref[...] = gy1_ref[...] + part
    out_ref[...] = (y1_ref[...] + nn(oa_ref[...], w[0])).astype(bf16)


def weight_grad_call(where, weights, name, shards=0):
    arrays, items = [], []

    def place(value):
        for index, known in enumerate(arrays):
            if known is value:
                return index
        arrays.append(value)
        return len(arrays) - 1

    for lanes, kind, entries in weights:
        for index, (left, left_at, right, right_at, form) in enumerate(entries):
            items.append((lanes, kind, index, place(left), left_at, place(right), right_at, form))
    count = len(arrays)
    rows = D // 8 // len(weights[0][0])

    def body(*refs):
        where_ref = refs[0]
        ins = refs[1 : 1 + count]
        *outs, held, sems, flipped = refs[1 + count :]
        turned = None
        keep, send = outs[0], outs[-1]
        page, blk = where_ref[3], where_ref[4]

        def place_natural(slot, lane, kind, index):
            out, width = outs[0], 4 * D // shards
            each = width // 2
            for k in range(2 * D // width if kind == "up" else D // width):
                if kind == "up":
                    piece = held.at[slot, k * each : (k + 1) * each]
                    first = lane * width + (index % 2) * each
                    local_copy(
                        piece, out.at[2 * k + index // 2, first : first + each], sems.at[slot]
                    )
                else:
                    piece = held.at[slot, k * width : (k + 1) * width]
                    owner = index * (D // width) + k
                    spot = slice(lane * width, (lane + 1) * width)
                    local_copy(piece, out.at[owner, spot], sems.at[slot])

        def finish(slot):
            pltpu.make_async_copy(held.at[slot], held.at[slot], sems.at[slot]).wait()

        def place_up(slot, lane, index, core, first, second):
            near = (blk ^ relative(lane, 0, first, second)) >> 1
            group, k = index // 2, index % 2
            out = send if core else keep

            @pl.when(((blk & 1) ^ core) == group)
            def _():
                half = rows // 2
                for origin in range(4):
                    spot = first * 8 + second * 4 + (origin ^ page)
                    take = pl.ds(pl.multiple_of((origin * 4 + near) * half, half), half)
                    local_copy(
                        held.at[slot, take],
                        out.at[lane, spot, k * half : (k + 1) * half],
                        sems.at[slot],
                    )

        def place_rows(slot, lanes, index, core, first, second):
            out = send if core else keep
            for number, lane in enumerate(lanes):
                owner = blk ^ relative(lane, core, first, second)
                spot = first * 8 + second * 4 + (index ^ page)
                start = pl.multiple_of((owner * len(lanes) + number) * rows, rows)
                local_copy(held.at[slot, pl.ds(start, rows)], out.at[lane, spot], sems.at[slot])

        for step, (lanes, kind, index, left, left_at, right, right_at, form) in enumerate(items):
            slot = step % 2
            if step >= 2:
                finish(slot)
            lhs = ins[left][:, left_at * D : (left_at + 1) * D]
            if form == "tt":
                rhs = ins[right][right_at * D : (right_at + 1) * D, :]
                if turned != (left, left_at):
                    turned = (left, left_at)
                    flipped[...] = lhs.T
                product = nt(flipped[...], rhs)
            else:
                product = tn(lhs, ins[right][:, right_at * D : (right_at + 1) * D])
            held[slot] = product.astype(bf16)
            if shards:
                place_natural(slot, lanes[0], kind, index)
                continue
            for core in range(2):
                for first in range(2):
                    for second in range(2):
                        if kind == "up":
                            place_up(slot, lanes[0], index, core, first, second)
                        else:
                            place_rows(slot, lanes, index, core, first, second)
        for step in range(max(0, len(items) - 2), len(items)):
            finish(step % 2)

    shapes = [sds((2, 16, rows, D), bf16)] * 2
    if shards:
        shapes = [sds((shards, len(weights) * 4 * D // shards, D), bf16)]
    turned_rows = max([128] + [arrays[item[3]].shape[0] for item in items if item[7] == "tt"])
    moved = 2 * len(items) * D * D + sum(v.size * 2 for v in arrays)
    return pl.pallas_call(
        body,
        grid=(1,),
        out_shape=shapes,
        in_specs=[pl.BlockSpec(memory_space=pltpu.SMEM)]
        + [
            pl.BlockSpec(v.shape, lambda i: (0, 0), pipeline_mode=pl.Buffered(1)) for v in arrays
        ],
        out_specs=[pl.BlockSpec(memory_space=pl.ANY)] * len(shapes),
        scratch_shapes=[
            pltpu.VMEM((2, D, D), bf16),
            pltpu.SemaphoreType.DMA((2,)),
            pltpu.VMEM((D, turned_rows), bf16),
        ],
        compiler_params=pltpu.CompilerParams(
            vmem_limit_bytes=VMEM_LIMIT, dimension_semantics=("arbitrary",)
        ),
        cost_estimate=pl.CostEstimate(
            flops=int(len(items) * 1.6e-6 * 1.1e15), bytes_accessed=int(moved), transcendentals=0
        ),
        name=name,
    )(where, *arrays)


def window_order(grid_rows, half):
    rows, cols, _ = grid_rows.shape
    rolled = jnp.roll(grid_rows, -half, axis=1)
    shaped = rolled.reshape(rows, cols // rows, rows, D).transpose(1, 0, 2, 3)
    return shaped.reshape(rows * cols, D)


def grid_order(tokens_in, rows, cols, half):
    shaped = tokens_in.reshape(cols // rows, rows, rows, D).transpose(1, 0, 2, 3)
    return jnp.roll(shaped.reshape(rows, cols, D), half, axis=1)


def after(value, *others):
    return lax.optimization_barrier((value, others))[0]


def swapped(value, axis, flip):
    count = lax.axis_size(axis)
    return lax.ppermute(value, axis, [(i, i ^ flip) for i in range(count)])


def from_pages(value):
    pages = lax.axis_size("page")
    return [value] + [swapped(value, "page", k) for k in range(1, pages)]


def spread_first(shares):
    parts = from_pages(jnp.stack(shares))
    return [jnp.stack([part[k] for part in parts]) for k in range(2)]


def spread_second(held, *gate):
    got = swapped(held[0], "blk", 2), swapped(held[1], "blk", 4)
    held, got = after((held, got), *gate)
    return [jnp.concatenate([held[k], got[k]]) for k in range(2)]


def spread_third(near):
    return [swapped(near[0], "blk", 4), swapped(near[1], "blk", 2)]


def spread_core(held):
    return [swapped(value, "blk", 1) for value in held]


def lane_arrays(near, far, near_core, far_core, lane):
    return [near[lane], far[lane], near_core[lane], far_core[lane]]


def added(left, right):
    return (left.astype(f32) + right.astype(f32)).astype(bf16)


def collect_first(keep, send, *gate):
    got = swapped(send, "blk", 1)
    keep = after(keep, *gate)
    return [[added(keep[k, i : i + 8], got[k, i : i + 8]) for i in (0, 8)] for k in range(2)]


def collect_second(held, *gate):
    got = swapped(held[0][1], "blk", 2), swapped(held[1][1], "blk", 4)
    kept = after([held[0][0], held[1][0]], *gate)
    return [[added(kept[k][i : i + 4], got[k][i : i + 4]) for i in (0, 4)] for k in range(2)]


def collect_third(held, *gate):
    got = swapped(held[0][1], "blk", 4), swapped(held[1][1], "blk", 2)
    kept = after([held[0][0], held[1][0]], *gate)
    sums = [added(kept[k], got[k]) for k in range(2)]
    return [jnp.stack([sums[k][i] for k in range(2)]) for i in range(4)]


def collect_last(held, *gate):
    total = after(held[0], *gate).astype(f32)
    for k in range(1, 4):
        total = total + swapped(held[k], "page", k).astype(f32)
    return total


def blocks_in_chip(parts, gate):
    keep, send = parts
    got = swapped(send, "blk", 1)
    keep = after(keep, gate)
    return [added(keep[k], got[k]) for k in range(4)]


def blocks_over_chips(chips, gate):
    total = after(chips[0], gate).astype(f32)
    for k in range(1, 4):
        total = total + swapped(chips[k], "blk", 2 * k).astype(f32)
    return total


def scattered_blocks(part):
    return lax.psum_scatter(part, "blk", scatter_dimension=0, tiled=True)


def on_device(
    visual,
    query_tokens,
    answer_len,
    attn_swin,
    attn_self,
    attn_qv,
    attn_vq,
    mlp_up,
    mlp_down,
    norm_gains,
    visual_cot,
    query_cot,
):
    everyone = ("page", "blk")
    pages = lax.axis_size("page")
    page_here = lax.axis_index("page")
    blk_count = lax.axis_size("blk")
    blk_here = lax.axis_index("blk")
    shards = pages * blk_count
    rows_here, cols_all = visual.shape[1], visual.shape[2]
    half = rows_here // 2
    tokens = rows_here * cols_all
    q_rows = query_tokens.shape[1]
    slots = q_rows * blk_count
    share = attn_swin.shape[0] // D
    staged = pages == 4 and blk_count == 8 and share % 32 == 0
    gain_width = norm_gains.shape[0]
    core_here = blk_here % 2

    where = jnp.stack(
        [
            blk_here * q_rows,
            answer_len[0],
            (blk_here == blk_count - 1).astype(jnp.int32),
            page_here,
            blk_here,
        ]
    ).astype(jnp.int32)

    down_one = [(i, (i - 1) % blk_count) for i in range(blk_count)]
    up_one = [(i, (i + 1) % blk_count) for i in range(blk_count)]
    both = jnp.concatenate([visual, visual_cot], axis=0)
    lent = lax.ppermute(both[:, :half], "blk", down_one)
    both = jnp.concatenate([both[:, half:], lent], axis=1)
    vis_in = window_order(both[0], half)
    vis_cot = window_order(both[1], half)

    def flat_share(value):
        return value.astype(bf16).reshape(share, D)

    gain_rows = jnp.pad(norm_gains.astype(bf16)[None], ((0, 15), (0, D - gain_width)))
    slot_own = jnp.concatenate([query_tokens[0], query_cot[0], gain_rows], axis=0)
    slots_joined = lax.all_gather(slot_own, "blk", axis=0)
    slot_arrays = [slots_joined]
    gain_parts = jnp.stack(from_pages(slots_joined[:, 2 * q_rows, :gain_width].reshape(-1)))
    gains = jnp.take(gain_parts, jnp.arange(pages) ^ page_here, axis=0)
    gains = gains.reshape(8, D).astype(f32)
    if staged:
        a_z = spread_first([flat_share(attn_self), flat_share(attn_swin)])
        a_z = after(a_z, vis_in, vis_cot)
        a_near = spread_second(a_z)
        c_z = spread_first(after([flat_share(attn_qv), flat_share(attn_vq)], a_z))
        a_far = spread_third(a_near)
        a_near_core, a_far_core = spread_core(a_near), spread_core(a_far)
        w_self, w_swin = [
            Stored(lane_arrays(a_near, a_far, a_near_core, a_far_core, k), (k,)) for k in range(2)
        ]
        up_groups = after(mlp_up, a_near).astype(bf16)
        up_groups = up_groups.reshape(share // 4, 2, 2, D).transpose(1, 2, 0, 3)
        mine = jnp.where(core_here == 0, up_groups[0], up_groups[1])
        other = swapped(jnp.where(core_here == 0, up_groups[1], up_groups[0]), "blk", 1)
        up_share = jnp.where(
            core_here == 0,
            jnp.concatenate([mine, other], axis=1),
            jnp.concatenate([other, mine], axis=1),
        ).reshape(share, D)
        d_z = spread_first(after([up_share, flat_share(mlp_down)], c_z))
        c_near = spread_second(after(c_z, a_far, gains))
        c_far = spread_third(c_near)
    else:
        up_share = (
            mlp_up.astype(bf16).reshape(share // 4, 4, D).transpose(1, 0, 2).reshape(share, D)
        )
        joined = lax.all_gather(
            jnp.concatenate(
                [flat_share(v) for v in (attn_self, attn_swin, attn_qv, attn_vq, mlp_down)]
                + [up_share],
                axis=0,
            ),
            everyone,
            axis=0,
            tiled=True,
        ).reshape(shards, -1, D)
        w_self, w_swin, w_qv, w_vq, w_down = [
            Stored([joined[:, k * share : (k + 1) * share].reshape(4, D, D)]) for k in range(5)
        ]
        up_all = joined[:, 5 * share : 6 * share].reshape(shards, 4, share // 4, D)
        w_up = Stored([up_all.transpose(1, 0, 2, 3).reshape(4, D, D)])

    where_self = where_swin = where_cross = where_vq = where
    if staged:
        where_self = after(where, vis_in, vis_cot, a_near_core, a_far_core)
    b_all, q_self, kv_self, lse_self, o_self, y1, c_own = call(
        self_forward_kernel,
        [
            sds((slots, D), bf16),
            sds((q_rows, D), bf16),
            sds((slots, 2 * D), bf16),
            sds((q_rows, 128), f32),
            sds((q_rows, D), bf16),
            sds((q_rows, D), f32),
            sds((q_rows, D), bf16),
        ],
        [where_self, gains],
        slots=(slot_arrays, 0, q_rows),
        scratch=[pltpu.VMEM((q_rows, slots), f32)],
        loads=[(w_self, 1), (w_self, 2), (w_self, 0), (w_self, 3)],
        flops=15e-6 * 1.1e15,
        name="self_forward",
    )
    if staged:
        c_near_core = spread_core(c_near)
        c_far, c_near_core = after((c_far, c_near_core), c_own)
        c_far_core = spread_core(c_far)
        w_qv, w_vq = [
            Stored(lane_arrays(c_near, c_far, c_near_core, c_far_core, k), (k,)) for k in range(2)
        ]
        where_swin = after(where, c_far, c_near_core)
        d_z = after(d_z, c_far)
    c_all = lax.all_gather(c_own, "blk", axis=0, tiled=True)

    def swin_forward(*refs):
        swin_forward_kernel(rows_here, *refs)

    a_low, qkv_swin, lse_swin, o_swin, v1, e_low = call(
        swin_forward,
        [
            sds((tokens, D), bf16),
            sds((tokens, 3 * D), bf16),
            sds((tokens, 128), f32),
            sds((tokens, D), bf16),
            sds((tokens, D), f32),
            sds((tokens, D), bf16),
        ],
        [where_swin, vis_in, gains],
        scratch=[pltpu.VMEM((cols_all // rows_here, rows_here**2, rows_here**2), f32)],
        loads=[(w_swin, k) for k in range(4)],
        flops=11e-6 * 1.1e15,
        name="swin_forward",
    )

    if staged:
        d_near = spread_second(d_z, e_low)
        d_far = spread_third(d_near)
        where_cross = after(where, d_near)
    qa, kvb, doa, kva, qb, stats = call(
        cross_forward_kernel,
        [
            sds((slots, D), bf16),
            sds((slots, 2 * D), bf16),
            sds((slots, D), bf16),
            sds((tokens, 2 * D), bf16),
            sds((tokens, D), bf16),
            sds((3, 16, slots), f32),
        ],
        [where_cross, c_all, e_low],
        slots=(slot_arrays, 1, q_rows),
        loads=[(w_qv, 1), (w_qv, 2), (w_vq, 0), (w_qv, 0), (w_vq, 1), (w_vq, 2), (w_qv, 3)],
        flops=18e-6 * 1.1e15,
        name="cross_forward",
    )
    if staged:
        d_far = after(d_far, qb)
        d_near_core, d_far_core = spread_core(d_near), spread_core(d_far)
        w_up, w_down = [
            Stored(lane_arrays(d_near, d_far, d_near_core, d_far_core, k), (k,)) for k in range(2)
        ]
        where_vq = after(where, d_far)
    lse_vq, o_vq = call(
        vq_forward_kernel,
        [sds((tokens, 128), f32), sds((tokens, D), bf16)],
        [where_vq, qb, kvb],
        flops=11e-6 * 1.1e15,
        name="vq_forward",
    )

    all_stats = lax.all_gather(stats, "blk", axis=0)
    peaks = jnp.max(all_stats[:, 0], axis=0)
    weights = jnp.exp(all_stats[:, 0] - peaks[None])
    totals = jnp.sum(all_stats[:, 1] * weights, axis=0)
    lse_qv = peaks + jnp.log(totals)
    centre_qv = jnp.sum(all_stats[:, 2] * weights, axis=0) / totals

    v3, h_low, act_low, du_low, g2, dz_vq, dob, dg5 = call(
        mlp_kernel,
        [
            sds((tokens, D), bf16),
            sds((tokens, D), bf16),
            sds((tokens, FF), bf16),
            sds((tokens, FF), bf16),
            sds((tokens, D), f32),
            sds((tokens, D), bf16),
            sds((tokens, D), bf16),
            sds((1, D), f32),
        ],
        [where, v1, o_vq, vis_cot, gains],
        scratch=[pltpu.VMEM((tokens, D), f32)] * 3,
        loads=[(w_vq, 3), (w_up, None)] + [(w_down, k) for k in range(4)],
        flops=14e-6 * 1.1e15,
        name="mlp",
    )

    def back_to_grid(value, *gate):
        grid = grid_order(value, rows_here, cols_all, half)
        returned = lax.ppermute(grid[half:], "blk", up_one)
        returned, grid = after((returned, grid), *gate)
        return jnp.concatenate([returned, grid[:half]], axis=0)[None]

    def flat(value):
        return value.astype(f32).reshape(-1)

    def gains_over_pages(db_all):
        gain_sum = db_all[q_rows, : pages * gain_width].reshape(pages, gain_width).astype(f32)
        kept = jnp.take(gain_sum, page_here, axis=0)
        for k in range(1, pages):
            kept = kept + swapped(jnp.take(gain_sum, page_here ^ k, axis=0), "page", k)
        return kept

    def with_gains(held, db_all):
        gain_sum = db_all[q_rows, : pages * gain_width].reshape(pages, gain_width)
        joined = []
        for k in range(pages):
            row = jnp.take(gain_sum, page_here ^ k, axis=0)[None, None]
            row = jnp.pad(row, ((0, 1), (0, 7), (0, D - gain_width)))
            joined.append(jnp.concatenate([held[k], row], axis=1))
        return joined

    def up_over_core(mlp_sum):
        up_sum = mlp_sum[0].reshape(2, 2, share // 4, D)
        mine = jnp.where(core_here == 0, up_sum[:, 0], up_sum[:, 1])
        other = swapped(jnp.where(core_here == 0, up_sum[:, 1], up_sum[:, 0]), "blk", 1)
        joined_up = jnp.where(
            core_here == 0,
            jnp.concatenate([mine, other], axis=0),
            jnp.concatenate([other, mine], axis=0),
        )
        return flat(joined_up.transpose(1, 0, 2))

    up_entries = [(h_low, 0, du_low, k, "tn") for k in range(4)]
    down_entries = [(act_low, k, vis_cot, 0, "tn") for k in range(4)]
    where_vq_back = where
    if staged:
        m_keep, m_send = weight_grad_call(
            after(where, lse_qv, centre_qv), [((0,), "up", up_entries), ((1,), "rows", down_entries)], "mlp_grads"
        )
        where_vq_back = after(where, m_keep)

    dqb, dkvbt = call(
        vq_backward_kernel,
        [sds((tokens, D), bf16), sds((2 * D, slots), bf16)],
        [where_vq_back, qb, kvb, dob, lse_vq],
        flops=16e-6 * 1.1e15,
        name="vq_backward",
    )
    where_swin_back = where_self_back = where_qv_back = where
    if staged:
        visual_out = back_to_grid(after(v3, m_keep))
        where_qv_back = after(where, visual_out)
        m_one = collect_first(m_keep, m_send, dqb)
        where_qv_back = after(where, visual_out, m_one)
    dqat, dkva, *merged_parts = call(
        qv_backward_kernel,
        [sds((D, slots), bf16), sds((tokens, 2 * D), bf16)] + [sds((slots, 2 * D), bf16)],
        [where_qv_back, qa, kva, doa, lse_qv, centre_qv, dkvbt],
        scratch=[pltpu.VMEM((slots, 2 * D), bf16)],
        loads=[(w_qv, 0), (w_vq, 1), (w_vq, 2)],
        flops=23e-6 * 1.1e15,
        name="qv_backward",
    )
    merged = scattered_blocks(merged_parts[0])
    if staged:
        m_two = collect_second(m_one, dqat)
        where_swin_back = after(where, m_two)
    dc, oa_low = merged[:, :D], merged[:, D:]

    def swin_backward(*refs):
        swin_backward_kernel(rows_here, *refs)

    dz_swin, dqkv_swin, visual_grad, dg_visual = call(
        swin_backward,
        [
            sds((tokens, D), bf16),
            sds((tokens, 3 * D), bf16),
            sds((tokens, D), f32),
            sds((2, D), f32),
        ],
        [where_swin_back, vis_in, v1, g2, gains, dkva, dqb, qkv_swin, lse_swin],
        scratch=[
            pltpu.VMEM((cols_all // rows_here, rows_here**2, rows_here**2), f32),
            pltpu.VMEM((tokens, D), bf16),
        ],
        loads=[(w_qv, 1), (w_qv, 2), (w_vq, 0), (w_swin, 3)] + [(w_swin, k) for k in range(3)],
        flops=20e-6 * 1.1e15,
        name="swin_backward",
    )

    swin_entries = [(a_low, 0, dqkv_swin, k, "tn") for k in range(3)]
    swin_entries.append((o_swin, 0, dz_swin, 0, "tn"))
    vq_entries = [
        (e_low, 0, dqb, 0, "tn"),
        (c_all, 0, dkvbt, 0, "tt"),
        (c_all, 0, dkvbt, 1, "tt"),
        (o_vq, 0, dz_vq, 0, "tn"),
    ]
    qv_entries = [
        (c_all, 0, dqat, 0, "tt"),
        (e_low, 0, dkva, 0, "tn"),
        (e_low, 0, dkva, 1, "tn"),
        (oa_low, 0, query_cot[0], 0, "tn"),
    ]
    if staged:
        m_three = collect_third(m_two, dz_swin)
        p_keep, p_send = weight_grad_call(
            after(where, m_three), [((0,), "rows", vq_entries), ((1,), "rows", swin_entries)], "patch_grads"
        )
        p_one = collect_first(p_keep, p_send)
        where_self_back = after(where, p_one)

    gy1, dz_self, dq_self, dkvt_self, dbq, dg_slots, db_part = call(
        self_backward_kernel,
        [
            sds((q_rows, D), f32),
            sds((q_rows, D), bf16),
            sds((q_rows, D), bf16),
            sds((2 * D, slots), bf16),
            sds((q_rows, D), f32),
            sds((2, D), f32),
        ]
        + [sds((slots, D), bf16)],
        [where_self_back, dc, y1, query_cot[0], gains, q_self, kv_self, lse_self],
        slots=(slot_arrays, 0, q_rows),
        scratch=[
            pltpu.VMEM((q_rows, slots), f32),
            pltpu.VMEM((q_rows, D), bf16),
            pltpu.VMEM((slots, D), bf16),
        ],
        loads=[(w_self, 3), (w_self, 0), (w_self, 1), (w_self, 2)],
        flops=15e-6 * 1.1e15,
        name="self_backward",
    )
    b_own = lax.dynamic_slice_in_dim(b_all, blk_here * q_rows, q_rows, 0)
    self_entries = [
        (b_own, 0, dq_self, 0, "tn"),
        (b_all, 0, dkvt_self, 0, "tt"),
        (b_all, 0, dkvt_self, 1, "tt"),
        (o_self, 0, dz_self, 0, "tn"),
    ]
    gain_block = jnp.concatenate(
        [dg_visual[0:1], dg_slots[0:1], dg_visual[1:2], dg_slots[1:2], dg5, jnp.zeros((3, D), f32)],
        axis=0,
    )
    gain_block = gain_block.astype(bf16).reshape(pages, blk_count, gain_width).transpose(1, 0, 2)
    gain_block = gain_block.reshape(blk_count, 1, pages * gain_width)
    gain_block = jnp.pad(gain_block, ((0, 0), (0, 15), (0, D - pages * gain_width)))
    whole_part = jnp.concatenate([db_part.reshape(blk_count, q_rows, D), gain_block], axis=1)
    db_all = scattered_blocks(whole_part.reshape(blk_count * (q_rows + 16), D))
    where_end = where
    if staged:
        p_two = collect_second(p_one, gy1)
        mlp_sum = collect_last(m_three, gy1)
        z_keep, z_send = weight_grad_call(
            after(where, p_two, mlp_sum), [((0,), "rows", qv_entries), ((1,), "rows", self_entries)], "slot_grads"
        )
        visual_grad = back_to_grid(visual_grad, z_keep)
        z_keep, z_send = after((z_keep, z_send), visual_grad)
        z_one = collect_first(z_keep, z_send)
        p_three = collect_third(p_two, z_one)
        z_two = collect_second(after(z_one, p_three))
        patch_sum = collect_last(after(p_three, z_one))
        db_all = after(db_all, patch_sum)
        up_grad = up_over_core(mlp_sum)
        z_two = after(z_two, patch_sum, up_grad)
        z_three = with_gains(collect_third(z_two), db_all)
        where_end = after(where, z_three)
    db = db_all[:q_rows]
    query_grad, query_out = call(
        query_end_kernel,
        [sds((q_rows, D), f32), sds((q_rows, D), bf16)],
        [where_end, db, dbq, query_tokens[0], gy1, gains, y1, oa_low],
        loads=[(w_qv, 3)],
        name="query_end",
    )

    if staged:
        slot_sum = collect_last(z_three)
        gain_grad, slot_sum = slot_sum[0, share, :gain_width], slot_sum[:, :share]
        swin_grad, self_grad = flat(patch_sum[1]), flat(slot_sum[1])
        qv_grad, vq_grad = flat(slot_sum[0]), flat(patch_sum[0])
        down_grad = flat(mlp_sum[1])
    else:
        visual_out, visual_grad = back_to_grid(v3), back_to_grid(visual_grad)
        gain_grad = gains_over_pages(db_all)

        def outer(left, right):
            return tn(left, right).astype(bf16)

        def outer_t(left, right_t):
            return lax.dot_general(
                left, right_t, (((0,), (1,)), ((), ())), preferred_element_type=f32
            ).astype(bf16)

        def as_shares(mats):
            return jnp.concatenate(mats, axis=0).reshape(shards, share, D)

        def summed(parts):
            joined = jnp.concatenate(parts, axis=1)
            width = joined.shape[1]
            return lax.psum_scatter(
                joined.reshape(shards * width, D), everyone, scatter_dimension=0, tiled=True
            )

        up_mats = jnp.stack([outer(h_low, du_low[:, k * D : (k + 1) * D]) for k in range(4)])
        up_part = (
            up_mats.reshape(4, shards, share // 4, D)
            .transpose(1, 0, 2, 3)
            .reshape(shards, share, D)
        )
        down_part = outer(act_low, vis_cot).reshape(shards, share, D)
        mlp_sum = summed([up_part, down_part])
        qv_part = as_shares(
            [
                outer_t(c_all, dqat),
                outer(e_low, dkva[:, :D]),
                outer(e_low, dkva[:, D:]),
                outer(oa_low, query_cot[0]),
            ]
        )
        vq_part = as_shares(
            [
                outer(e_low, dqb),
                outer_t(c_all, dkvbt[:D]),
                outer_t(c_all, dkvbt[D:]),
                outer(o_vq, dz_vq),
            ]
        )
        cross_sum = summed([qv_part, vq_part])
        swin_part = as_shares(
            [outer(a_low, dqkv_swin[:, k * D : (k + 1) * D]) for k in range(3)]
            + [outer(o_swin, dz_swin)]
        )
        self_part = as_shares(
            [
                outer(b_own, dq_self),
                outer_t(b_all, dkvt_self[:D]),
                outer_t(b_all, dkvt_self[D:]),
                outer(o_self, dz_self),
            ]
        )
        last_sum = summed([swin_part, self_part])
        up_grad = flat(mlp_sum[:share].reshape(4, share // 4, D).transpose(1, 0, 2))
        down_grad = flat(mlp_sum[share:])
        qv_grad, vq_grad = flat(cross_sum[:share]), flat(cross_sum[share:])
        swin_grad, self_grad = flat(last_sum[:share]), flat(last_sum[share:])

    return (
        visual_out,
        query_out[None],
        visual_grad,
        query_grad[None],
        swin_grad,
        self_grad,
        qv_grad,
        vq_grad,
        up_grad,
        down_grad,
        gain_grad,
    )


def solution(mesh):
    placed = (
        P("page", "blk", None, None),
        P("page", "blk", None),
        P("page"),
        P(("page", "blk")),
        P(("page", "blk")),
        P(("page", "blk")),
        P(("page", "blk")),
        P(("page", "blk")),
        P(("page", "blk")),
        P(("page", "blk")),
        P("page", "blk", None, None),
        P("page", "blk", None),
    )
    return jax.shard_map(
        on_device,
        mesh=mesh,
        in_specs=placed,
        out_specs=(
            P("page", "blk", None, None),
            P("page", "blk", None),
            P("page", "blk", None, None),
            P("page", "blk", None),
            P(("page", "blk")),
            P(("page", "blk")),
            P(("page", "blk")),
            P(("page", "blk")),
            P(("page", "blk")),
            P(("page", "blk")),
            P(("page", "blk")),
        ),
        check_vma=False,
    )
```

```python
import jax
import jax.numpy as jnp
from jax import lax
from jax.experimental import pallas as pl
from jax.experimental.pallas import tpu as pltpu
from jax.sharding import PartitionSpec as P

D = 768
HEADS = 12
HD = 64
FF = 3072
PAIRS = HEADS // 2
PW = 2 * HD
SCALE = HD ** (-0.5)

EPS = 1e-05
NEG = -1e30

bf16 = jnp.bfloat16
f32 = jnp.float32
VMEM_LIMIT = 56 * 1024 * 1024


def nn(left, right):
    return lax.dot_general(left, right, (((1,), (0,)), ((), ())), preferred_element_type=f32)


def nt(left, right):
    return lax.dot_general(left, right, (((1,), (1,)), ((), ())), preferred_element_type=f32)


def tn(left, right):
    return lax.dot_general(left, right, (((0,), (0,)), ((), ())), preferred_element_type=f32)


def norm_parts(rows):
    centre = jnp.mean(rows, axis=-1, keepdims=True)
    centred = rows - centre
    spread = jnp.mean(centred * centred, axis=-1, keepdims=True)
    inverse = lax.rsqrt(spread + EPS)
    return centred * inverse, inverse


def norm(rows, gain):
    return norm_parts(rows)[0] * gain


def norm_back(rows, gain, grad):
    unit, inverse = norm_parts(rows)
    grad_gain = jnp.sum(grad * unit, axis=0, keepdims=True)
    scaled = grad * gain
    first = jnp.mean(scaled, axis=-1, keepdims=True)
    second = jnp.mean(scaled * unit, axis=-1, keepdims=True)
    return inverse * (scaled - first - unit * second), grad_gain


def lane_half(half, value, dtype):
    lanes = lax.broadcasted_iota(jnp.int32, (1, PW), 1)
    return jnp.where((lanes // HD) == half, value, 0.0).astype(dtype)


def low_half(rows):
    return lax.broadcasted_iota(jnp.int32, (rows, PW), 1) < HD


def column(table, index):
    lanes = lax.broadcasted_iota(jnp.int32, table.shape, 1)
    return jnp.sum(jnp.where(lanes == index, table, 0.0), axis=-1, keepdims=True)


def pair_cols(pair, base=0):
    return pl.ds(pl.multiple_of(base + pair * PW, PW), PW)


def softmax_rows(scores):
    highest = jnp.max(scores, axis=-1, keepdims=True)
    raised = jnp.exp(scores - highest)
    totals = jnp.sum(raised, axis=-1, keepdims=True)
    return raised * (1.0 / totals), highest + jnp.log(totals)


class Stored:
    def __init__(self, arrays, lanes=(), joint=None):
        self.arrays = list(arrays)
        self.lanes = tuple(lanes)
        self.joint = joint


def stage_bits(lane):
    return (1, 2) if lane == 0 else (2, 1)


def relative(lane, core, first, second):
    bit_one, bit_two = stage_bits(lane)
    return core | (first << bit_one) | (second << bit_two)


def local_copy(source, target, sem):
    pltpu.make_async_copy(source, target, sem).start()


def fetch(where_ref, stored, refs, index, target, sem):
    if stored.joint is not None:
        first, rows = stored.joint
        count = D // rows
        for k in range(count):
            piece = refs[0].at[index * count + k, first : first + rows]
            local_copy(piece, target.at[k * rows : (k + 1) * rows], sem)
        return
    if len(refs) == 1:
        local_copy(refs[0].at[index], target, sem)
        return
    page, blk = where_ref[3], where_ref[4]
    count = len(stored.lanes)
    for number, lane in enumerate(stored.lanes):
        for core in range(2):
            for second in range(2):
                for first in range(2):
                    ref = refs[4 * number + 2 * core + second]
                    piece = ref.at[(index ^ page) + 4 * first]
                    rows = piece.shape[0]
                    owner = blk ^ relative(lane, core, first, second)
                    start = pl.multiple_of((owner * count + number) * rows, rows)
                    local_copy(piece, target.at[pl.ds(start, rows)], sem)


def fetch_up(where_ref, stored, refs, target, sem):
    if len(refs) == 1:
        local_copy(refs[0], target, sem)
        return
    page, blk = where_ref[3], where_ref[4]
    for core in range(2):
        for second in range(2):
            for first in range(2):
                ref = refs[2 * core + second]
                near = (blk ^ relative(stored.lanes[0], 0, first, second)) >> 1
                for origin in range(4):
                    piece = ref.at[(origin ^ page) + 4 * first]
                    rows = piece.shape[0] // 2
                    spot = pl.ds(pl.multiple_of((origin * 4 + near) * rows, rows), rows)
                    for k in range(2):
                        group = 2 * ((blk & 1) ^ core) + k
                        local_copy(piece.at[k * rows : (k + 1) * rows], target.at[group, spot], sem)


class Loads:
    def __init__(self, held, sems, plan):
        self.held, self.sems, self.plan, self.done = held, sems, plan, set()

    def ready(self, *places):
        for place in places:
            if place not in self.done:
                self.done.add(place)
                start, count = self.plan[place]
                span = self.held.at[start : start + count]
                pltpu.make_async_copy(span, span, self.sems.at[place]).wait()

    def __getitem__(self, place):
        self.ready(place)
        return self.held[self.plan[place][0]]

    def part(self, place, k):
        return self.held[self.plan[place][0] + k]


def call(kernel, outs, ins, scratch=(), smem=1, loads=(), slots=None, flops=0, name=None):
    def whole(value):
        zeros = (0,) * len(value.shape)
        return pl.BlockSpec(value.shape, lambda i: zeros, pipeline_mode=pl.Buffered(1))

    specs = []
    for index, value in enumerate(ins):
        if index < smem:
            specs.append(pl.BlockSpec(memory_space=pltpu.SMEM))
        else:
            specs.append(whole(value))
    single = not isinstance(outs, list)
    shapes = [outs] if single else outs
    count_in, count_out = len(ins), len(shapes)
    unique, plan, size = [], [], 0
    for stored, which in loads:
        if stored not in unique:
            unique.append(stored)
        width = 4 if which is None else 1
        plan.append((size, width))
        size += width
    arrays = [array for stored in unique for array in stored.arrays]
    gathered, slot_scratch = [], []
    if slots:
        gathered, part, own = slots
        blocks = len(gathered) if len(gathered) > 1 else gathered[0].shape[0]
        slot_scratch = [pltpu.VMEM((blocks, own, D), bf16), pltpu.SemaphoreType.DMA]
    held = [pltpu.VMEM((size, D, D), bf16), pltpu.SemaphoreType.DMA((len(plan),))] if loads else []

    def body(*refs):
        inner = list(refs[:count_in])
        at = count_in
        taken = {}
        for stored in unique:
            taken[id(stored)] = refs[at : at + len(stored.arrays)]
            at += len(stored.arrays)
        pieces = refs[at : at + len(gathered)]
        at += len(gathered)
        results = list(refs[at : at + count_out])
        rest = list(refs[at + count_out :])
        if slots:
            together, slot_sem = rest[:2]
            rest = rest[2:]
            rows = slice(part * own, (part + 1) * own)
            if len(pieces) == 1:
                local_copy(pieces[0].at[:, rows], together, slot_sem)
            for k, piece in enumerate(pieces if len(pieces) > 1 else ()):
                local_copy(piece.at[rows], together.at[inner[0][4] ^ k], slot_sem)
            inner.append(together)
        if not loads:
            kernel(*inner, *results, *rest)
            return
        kept, sems = rest[-2], rest[-1]
        for place, (stored, which) in enumerate(loads):
            mine, (start, width) = taken[id(stored)], plan[place]
            if which is None:
                fetch_up(inner[0], stored, mine, kept.at[start : start + width], sems.at[place])
            else:
                fetch(inner[0], stored, mine, which, kept.at[start], sems.at[place])
        if slots:
            pltpu.make_async_copy(together, together, slot_sem).wait()
        weights = Loads(kept, sems, plan)
        kernel(*inner, weights, *results, *rest[:-2])
        weights.ready(*range(len(plan)))

    moved = sum(v.size * v.dtype.itemsize for v in list(ins) + shapes) + size * D * D * 2
    result = pl.pallas_call(
        body,
        grid=(1,),
        out_shape=shapes,
        in_specs=specs + [pl.BlockSpec(memory_space=pl.ANY)] * (len(arrays) + len(gathered)),
        out_specs=[whole(value) for value in shapes],
        scratch_shapes=slot_scratch + list(scratch) + held,
        compiler_params=pltpu.CompilerParams(
            vmem_limit_bytes=VMEM_LIMIT, dimension_semantics=("arbitrary",)
        ),
        cost_estimate=pl.CostEstimate(flops=int(flops), bytes_accessed=int(moved), transcendentals=0),
        name=name,
    )(*ins, *arrays, *gathered)
    return result[0] if single else result


def sds(shape, dtype):
    return jax.ShapeDtypeStruct(shape, dtype)


def self_bias(bias_ref, first_row, live):
    rows, slots = bias_ref.shape
    keys = lax.broadcasted_iota(jnp.int32, (rows, slots), 1)
    places = lax.broadcasted_iota(jnp.int32, (rows, slots), 0) + first_row
    bias_ref[...] = jnp.where((keys <= places) & (keys < live), 0.0, NEG)


def self_forward_kernel(
    where_ref, g_ref, y_ref, w, b_ref, q_ref, kv_ref, lse_ref, o_ref, y1_ref, c_ref, bias_ref
):
    first_row, live = where_ref[0], where_ref[1]
    slots, own = b_ref.shape[0], q_ref.shape[0]
    tile = 256
    group = tile // own
    w.ready(0, 1)

    def project(i, carry):
        rows = pl.ds(pl.multiple_of(i * tile, tile), tile)
        part = y_ref[pl.ds(i * group, group)].reshape(tile, D)
        normed = norm(part.astype(f32), g_ref[1:2, :]).astype(bf16)
        b_ref[rows, :] = normed
        kv_ref[rows, 0:D] = nn(normed, w[0]).astype(bf16)
        kv_ref[rows, D : 2 * D] = nn(normed, w[1]).astype(bf16)
        return carry

    lax.fori_loop(0, slots // tile, project, 0)
    mine = pl.ds(pl.multiple_of(first_row, 16), own)
    q_ref[...] = nn(b_ref[mine, :], w[2]).astype(bf16)
    self_bias(bias_ref, first_row, live)
    lse_ref[...] = jnp.zeros_like(lse_ref)
    lanes = lax.broadcasted_iota(jnp.int32, lse_ref.shape, 1)
    low = low_half(own)

    def attend(pair, carry):
        queries = q_ref[:, pair_cols(pair)]
        keys = kv_ref[:, pair_cols(pair)]
        values = kv_ref[:, pair_cols(pair, D)]
        mixed = []
        table = lse_ref[...]
        for half in range(2):
            scores = nt(queries * lane_half(half, SCALE, bf16), keys) + bias_ref[...]
            chances, log_totals = softmax_rows(scores)
            mixed.append(nn(chances.astype(bf16), values))
            table = jnp.where(lanes == 2 * pair + half, log_totals, table)
        lse_ref[...] = table
        o_ref[:, pair_cols(pair)] = jnp.where(low, mixed[0], mixed[1]).astype(bf16)
        return carry

    lax.fori_loop(0, PAIRS, attend, 0)
    y1 = y_ref[where_ref[4]].astype(f32) + nn(o_ref[...], w[3])
    y1_ref[...] = y1
    c_ref[...] = norm(y1, g_ref[3:4, :]).astype(bf16)


def window_bias(rows, side, row_split, col_split):
    def flags(shape, dim):
        token = lax.broadcasted_iota(jnp.int32, shape, dim)
        row, col = token // side, token % side
        return jnp.where(row >= side // 2, row_split, 0) + jnp.where(
            col >= side // 2, 2 * col_split, 0
        )

    return jnp.where(flags((rows, rows), 0) == flags((rows, rows), 1), 0.0, NEG)


def swin_forward_kernel(
    side, where_ref, x_ref, g_ref, w, a_ref, qkv_ref, lse_ref, o_ref, v1_ref, e_ref, bias_ref
):
    is_last = where_ref[2]
    tokens = x_ref.shape[0]
    rows = side * side
    windows = tokens // rows
    x = x_ref[...].astype(f32)
    normed = norm(x, g_ref[0:1, :]).astype(bf16)
    a_ref[...] = normed
    for k in range(3):
        qkv_ref[:, k * D : (k + 1) * D] = nn(normed, w[k]).astype(bf16)
    for win in range(windows):
        bias_ref[win] = window_bias(rows, side, is_last, 1 if win == windows - 1 else 0)
    lse_ref[...] = jnp.zeros_like(lse_ref)
    lanes = lax.broadcasted_iota(jnp.int32, (rows, lse_ref.shape[1]), 1)
    low = low_half(rows)

    def attend(pair, carry):
        for win in range(windows):
            at = slice(win * rows, (win + 1) * rows)
            queries = qkv_ref[at, pair_cols(pair)]
            keys = qkv_ref[at, pair_cols(pair, D)]
            values = qkv_ref[at, pair_cols(pair, 2 * D)]
            mixed = []
            table = lse_ref[at, :]
            for half in range(2):
                scores = nt(queries * lane_half(half, SCALE, bf16), keys) + bias_ref[win]
                chances, log_totals = softmax_rows(scores)
                mixed.append(nn(chances.astype(bf16), values))
                table = jnp.where(lanes == 2 * pair + half, log_totals, table)
            lse_ref[at, :] = table
            o_ref[at, pair_cols(pair)] = jnp.where(low, mixed[0], mixed[1]).astype(bf16)
        return carry

    lax.fori_loop(0, PAIRS, attend, 0)
    v1 = x + nn(o_ref[...], w[3])
    v1_ref[...] = v1
    e_ref[...] = norm(v1, g_ref[2:3, :]).astype(bf16)


def cross_forward_kernel(
    where_ref,
    c_ref,
    e_ref,
    cot_ref,
    w,
    qa_ref,
    kvb_ref,
    doa_ref,
    kva_ref,
    qb_ref,
    stats_ref,
):
    slots, tokens = qa_ref.shape[0], e_ref.shape[0]
    tile = 256
    normed = e_ref[...]
    for k in range(2):
        kva_ref[:, k * D : (k + 1) * D] = nn(normed, w[k]).astype(bf16)
    qb_ref[...] = nn(normed, w[2]).astype(bf16)
    w.ready(3, 4, 5, 6)
    group = tile // cot_ref.shape[1]

    def project(i, carry):
        rows = pl.ds(pl.multiple_of(i * tile, tile), tile)
        part = c_ref[rows, :]
        qa_ref[rows, :] = nn(part, w[3]).astype(bf16)
        for k in range(2):
            kvb_ref[rows, k * D : (k + 1) * D] = nn(part, w[4 + k]).astype(bf16)
        cot = cot_ref[pl.ds(i * group, group)].reshape(tile, D)
        doa_ref[rows, :] = nt(cot, w[6]).astype(bf16)
        return carry

    lax.fori_loop(0, slots // tile, project, 0)
    stats_ref[...] = jnp.zeros_like(stats_ref)

    def page_stats(pair, carry):
        keys = kva_ref[:, pair_cols(pair)]
        values = kva_ref[:, pair_cols(pair, D)]
        for half in range(2):
            head = 2 * pair + half
            keys_h = keys * lane_half(half, SCALE, bf16)
            values_h = values * lane_half(half, 1.0, bf16)
            for i in range(slots // tile):
                rows = slice(i * tile, (i + 1) * tile)
                scores = nt(keys_h, qa_ref[rows, pair_cols(pair)])
                highest = jnp.max(scores, axis=0, keepdims=True)
                raised = jnp.exp(scores - highest)
                grads = nt(values_h, doa_ref[rows, pair_cols(pair)])
                stats_ref[0, pl.ds(head, 1), rows] = highest
                stats_ref[1, pl.ds(head, 1), rows] = jnp.sum(raised, axis=0, keepdims=True)
                stats_ref[2, pl.ds(head, 1), rows] = jnp.sum(raised * grads, axis=0, keepdims=True)
        return carry

    lax.fori_loop(0, PAIRS, page_stats, 0)


def vq_forward_kernel(where_ref, qb_ref, kvb_ref, lse_ref, ob_ref):
    live = where_ref[1]
    tokens, slots = qb_ref.shape[0], kvb_ref.shape[0]
    lse_ref[...] = jnp.zeros_like(lse_ref)
    lanes = lax.broadcasted_iota(jnp.int32, lse_ref.shape, 1)
    low = low_half(tokens)
    bias = jnp.where(lax.broadcasted_iota(jnp.int32, (1, slots), 1) < live, 0.0, NEG)

    def attend(pair, carry):
        queries = qb_ref[:, pair_cols(pair)]
        keys = kvb_ref[:, pair_cols(pair)]
        values = kvb_ref[:, pair_cols(pair, D)]
        mixed = []
        table = lse_ref[...]
        for half in range(2):
            scores = nt(queries * lane_half(half, SCALE, bf16), keys) + bias
            chances, log_totals = softmax_rows(scores)
            mixed.append(nn(chances.astype(bf16), values))
            table = jnp.where(lanes == 2 * pair + half, log_totals, table)
        lse_ref[...] = table
        ob_ref[:, pair_cols(pair)] = jnp.where(low, mixed[0], mixed[1]).astype(bf16)
        return carry

    lax.fori_loop(0, PAIRS, attend, 0)


GELU_A = 0.7978845608028654
GELU_B = 0.044715


def mlp_kernel(
    where_ref,
    v1_ref,
    ob_ref,
    cot_ref,
    g_ref,
    w,
    v3_ref,
    h_ref,
    act_ref,
    du_ref,
    g2_ref,
    dz_ref,
    dob_ref,
    dg_ref,
    v2_ref,
    sum_ref,
    dh_ref,
):
    v2 = v1_ref[...] + nn(ob_ref[...], w[0])
    v2_ref[...] = v2
    sum_ref[...] = v2
    h_ref[...] = norm(v2, g_ref[4:5, :]).astype(bf16)
    dh_ref[...] = jnp.zeros_like(dh_ref)
    w.ready(1, 2, 3, 4, 5)

    def chunk(k, carry):
        up, down = w.part(1, k), w.part(2, k)
        at = pl.ds(pl.multiple_of(k * D, D), D)
        u = nn(h_ref[...], up)
        squared = u * u
        bend = jnp.tanh(GELU_A * (u + GELU_B * u * squared))
        act = (0.5 * u * (1.0 + bend)).astype(bf16)
        act_ref[:, at] = act
        slope = 0.5 * (1.0 + bend) + 0.5 * u * (1.0 - bend * bend) * GELU_A * (
            1.0 + 3.0 * GELU_B * squared
        )
        du = (nt(cot_ref[...], down) * slope).astype(bf16)
        du_ref[:, at] = du
        sum_ref[...] += nn(act, down)
        dh_ref[...] += nt(du, up)
        return carry

    lax.fori_loop(0, FF // D, chunk, 0)
    v3_ref[...] = sum_ref[...].astype(bf16)
    part, dg = norm_back(v2_ref[...], g_ref[4:5, :], dh_ref[...])
    dg_ref[...] = dg
    g2 = cot_ref[...].astype(f32) + part
    g2_ref[...] = g2
    dz = g2.astype(bf16)
    dz_ref[...] = dz
    dob_ref[...] = nt(dz, w[0]).astype(bf16)


def vq_backward_kernel(
    where_ref, qb_ref, kvb_ref, dob_ref, lse_ref, dqb_ref, dkvbt_ref
):
    live = where_ref[1]
    tokens, slots = qb_ref.shape[0], kvb_ref.shape[0]
    bias = jnp.where(lax.broadcasted_iota(jnp.int32, (1, slots), 1) < live, 0.0, NEG)
    low = low_half(tokens)

    def back(pair, carry):
        queries = qb_ref[:, pair_cols(pair)]
        keys = kvb_ref[:, pair_cols(pair)]
        values = kvb_ref[:, pair_cols(pair, D)]
        grads = dob_ref[:, pair_cols(pair)]
        queries_t = (queries * SCALE).astype(f32).T.astype(bf16)
        grads_t = grads.astype(f32).T.astype(bf16)
        parts = []
        for half in range(2):
            own = slice(half * HD, (half + 1) * HD)
            scores = nt(queries * lane_half(half, SCALE, bf16), keys) + bias
            chances = jnp.exp(scores - column(lse_ref[...], 2 * pair + half))
            slopes = nt(grads * lane_half(half, 1.0, bf16), values)
            centre = jnp.sum(chances * slopes, axis=-1, keepdims=True)
            ds = (chances * (slopes - centre)).astype(bf16)
            parts.append(nn(ds, keys))
            at = pair * PW + half * HD
            dkvbt_ref[pl.ds(pl.multiple_of(at, HD), HD), :] = nn(queries_t[own], ds).astype(bf16)
            dkvbt_ref[pl.ds(pl.multiple_of(D + at, HD), HD), :] = nn(
                grads_t[own], chances.astype(bf16)
            ).astype(bf16)
        dqb_ref[:, pair_cols(pair)] = (jnp.where(low, parts[0], parts[1]) * SCALE).astype(bf16)
        return carry

    lax.fori_loop(0, PAIRS, back, 0)


def hand_out(where_ref, held, outs):
    if len(outs) == 1:
        outs[0][...] = held[...]
        return
    rows = outs[0].shape[1]
    for core, out in enumerate(outs):
        for k in range(4):
            start = pl.multiple_of((where_ref[4] ^ (2 * k + core)) * rows, rows)
            out[k] = held[pl.ds(start, rows), :]


def qv_backward_kernel(
    where_ref,
    qa_ref,
    kva_ref,
    doa_ref,
    lse_ref,
    centre_ref,
    dkvbt_ref,
    w,
    dqat_ref,
    dkva_ref,
    *rest,
):
    dc_refs, held = rest[:-1], rest[-1]
    slots, tokens = qa_ref.shape[0], kva_ref.shape[0]
    low = low_half(tokens)
    tile = 512

    def back(pair, carry):
        keys = kva_ref[:, pair_cols(pair)]
        values = kva_ref[:, pair_cols(pair, D)]
        keys_t = (keys * SCALE).astype(f32).T.astype(bf16)
        values_t = values.astype(f32).T.astype(bf16)
        for i in range(slots // tile):
            rows = slice(i * tile, (i + 1) * tile)
            queries = qa_ref[rows, pair_cols(pair)]
            grads = doa_ref[rows, pair_cols(pair)]
            dk, dv, mixed = [], [], []
            for half in range(2):
                head = 2 * pair + half
                own = slice(half * HD, (half + 1) * HD)
                scores = nt(keys * lane_half(half, SCALE, bf16), queries)
                chances = jnp.exp(scores - lse_ref[pl.ds(head, 1), rows])
                slopes = nt(values * lane_half(half, 1.0, bf16), grads)
                ds = (chances * (slopes - centre_ref[pl.ds(head, 1), rows])).astype(bf16)
                rounded = chances.astype(bf16)
                mixed.append(nn(values_t[own], rounded))
                dqat_ref[pl.ds(pl.multiple_of(head * HD, HD), HD), rows] = nn(
                    keys_t[own], ds
                ).astype(bf16)
                dk.append(nn(ds, queries))
                dv.append(nn(rounded, grads))
            held[rows, pair_cols(pair, D)] = jnp.concatenate(mixed, axis=0).T.astype(bf16)
            dk_now = jnp.where(low, dk[0], dk[1]) * SCALE
            dv_now = jnp.where(low, dv[0], dv[1])
            if i == 0:
                dk_sum, dv_sum = dk_now, dv_now
            else:
                dk_sum, dv_sum = dk_sum + dk_now, dv_sum + dv_now
        dkva_ref[:, pair_cols(pair)] = dk_sum.astype(bf16)
        dkva_ref[:, pair_cols(pair, D)] = dv_sum.astype(bf16)
        return carry

    lax.fori_loop(0, PAIRS, back, 0)
    for i in range(slots // tile):
        cols = slice(i * tile, (i + 1) * tile)
        total = nn(w[0], dqat_ref[:, cols])
        total += nn(w[1], dkvbt_ref[0:D, cols])
        total += nn(w[2], dkvbt_ref[D : 2 * D, cols])
        held[cols, 0:D] = total.T.astype(bf16)
    hand_out(where_ref, held, dc_refs)


def swin_backward_kernel(
    side,
    where_ref,
    x_ref,
    v1_ref,
    g2_ref,
    g_ref,
    dkva_ref,
    dqb_ref,
    qkv_ref,
    lse_ref,
    w,
    dz_ref,
    dqkv_ref,
    grad_ref,
    dg_ref,
    bias_ref,
    do_ref,
):
    is_last = where_ref[2]
    tokens = x_ref.shape[0]
    rows = side * side
    windows = tokens // rows
    de = nt(dkva_ref[:, 0:D], w[0])
    de += nt(dkva_ref[:, D : 2 * D], w[1])
    de += nt(dqb_ref[...], w[2])
    part, dg3 = norm_back(v1_ref[...], g_ref[2:3, :], de)
    g1 = g2_ref[...] + part
    grad_ref[...] = g1
    dz = g1.astype(bf16)
    dz_ref[...] = dz
    do_ref[...] = nt(dz, w[3]).astype(bf16)
    for win in range(windows):
        bias_ref[win] = window_bias(rows, side, is_last, 1 if win == windows - 1 else 0)
    low = low_half(rows)

    def back(pair, carry):
        for win in range(windows):
            at = slice(win * rows, (win + 1) * rows)
            queries = qkv_ref[at, pair_cols(pair)]
            keys = qkv_ref[at, pair_cols(pair, D)]
            values = qkv_ref[at, pair_cols(pair, 2 * D)]
            grads = do_ref[at, pair_cols(pair)]
            dq, dk, dv = [], [], []
            for half in range(2):
                scores = nt(queries * lane_half(half, SCALE, bf16), keys) + bias_ref[win]
                chances = jnp.exp(scores - column(lse_ref[at, :], 2 * pair + half))
                slopes = nt(grads * lane_half(half, 1.0, bf16), values)
                centre = jnp.sum(chances * slopes, axis=-1, keepdims=True)
                ds = (chances * (slopes - centre)).astype(bf16)
                dq.append(nn(ds, keys))
                dk.append(tn(ds, queries))
                dv.append(tn(chances.astype(bf16), grads))
            for k, (pieces, factor) in enumerate(((dq, SCALE), (dk, SCALE), (dv, 1.0))):
                dqkv_ref[at, pair_cols(pair, k * D)] = (
                    jnp.where(low, pieces[0], pieces[1]) * factor
                ).astype(bf16)
        return carry

    lax.fori_loop(0, PAIRS, back, 0)
    da = nt(dqkv_ref[:, 0:D], w[4])
    da += nt(dqkv_ref[:, D : 2 * D], w[5])
    da += nt(dqkv_ref[:, 2 * D : 3 * D], w[6])
    part, dg1 = norm_back(x_ref[...].astype(f32), g_ref[0:1, :], da)
    grad_ref[...] += part
    dg_ref[...] = jnp.concatenate([dg1, dg3], axis=0)


def self_backward_kernel(
    where_ref,
    dc_ref,
    y1_ref,
    cot_ref,
    g_ref,
    q_ref,
    kv_ref,
    lse_ref,
    y_ref,
    w,
    gy1_ref,
    dz_ref,
    dq_ref,
    dkvt_ref,
    dbq_ref,
    dg_ref,
    *rest,
):
    db_refs, (bias_ref, do_ref, db_held) = rest[:-3], rest[-3:]
    group = 256 // q_ref.shape[0]
    first_row, live = where_ref[0], where_ref[1]
    own_rows, slots = q_ref.shape[0], kv_ref.shape[0]
    part, dg = norm_back(y1_ref[...], g_ref[3:4, :], dc_ref[...].astype(f32))
    gy1 = cot_ref[...].astype(f32) + part
    gy1_ref[...] = gy1
    dz = gy1.astype(bf16)
    dz_ref[...] = dz
    do_ref[...] = nt(dz, w[0]).astype(bf16)
    self_bias(bias_ref, first_row, live)
    low = low_half(own_rows)

    def back(pair, carry):
        queries = q_ref[:, pair_cols(pair)]
        keys = kv_ref[:, pair_cols(pair)]
        values = kv_ref[:, pair_cols(pair, D)]
        grads = do_ref[:, pair_cols(pair)]
        queries_t = (queries * SCALE).astype(f32).T.astype(bf16)
        grads_t = grads.astype(f32).T.astype(bf16)
        parts = []
        for half in range(2):
            own = slice(half * HD, (half + 1) * HD)
            scores = nt(queries * lane_half(half, SCALE, bf16), keys) + bias_ref[...]
            chances = jnp.exp(scores - column(lse_ref[...], 2 * pair + half))
            slopes = nt(grads * lane_half(half, 1.0, bf16), values)
            centre = jnp.sum(chances * slopes, axis=-1, keepdims=True)
            ds = (chances * (slopes - centre)).astype(bf16)
            parts.append(nn(ds, keys))
            at = pair * PW + half * HD
            dkvt_ref[pl.ds(pl.multiple_of(at, HD), HD), :] = nn(queries_t[own], ds).astype(bf16)
            dkvt_ref[pl.ds(pl.multiple_of(D + at, HD), HD), :] = nn(
                grads_t[own], chances.astype(bf16)
            ).astype(bf16)
        dq_ref[:, pair_cols(pair)] = (jnp.where(low, parts[0], parts[1]) * SCALE).astype(bf16)
        return carry

    lax.fori_loop(0, PAIRS, back, 0)
    dbq = nt(dq_ref[...], w[1])
    dbq_ref[...] = dbq
    unit = norm_parts(y_ref[where_ref[4]].astype(f32))[0]
    dg2 = jnp.sum(dbq * unit, axis=0, keepdims=True)
    tile = 256
    for i in range(slots // tile):
        cols = slice(i * tile, (i + 1) * tile)
        total = nn(w[2], dkvt_ref[0:D, cols])
        total += nn(w[3], dkvt_ref[D : 2 * D, cols])
        back = total.T
        db_held[cols, :] = back.astype(bf16)
        part = y_ref[i * group : (i + 1) * group].reshape(tile, D)
        unit = norm_parts(part.astype(f32))[0]
        dg2 += jnp.sum(back * unit, axis=0, keepdims=True)
    dg_ref[...] = jnp.concatenate([dg2, dg], axis=0)
    hand_out(where_ref, db_held, db_refs)


def query_end_kernel(
    where_ref, db_ref, dbq_ref, y_ref, gy1_ref, g_ref, y1_ref, oa_ref, w, grad_ref, out_ref
):
    part, _ = norm_back(
        y_ref[...].astype(f32), g_ref[1:2, :], db_ref[...].astype(f32) + dbq_ref[...]
    )
    grad_ref[...] = gy1_ref[...] + part
    out_ref[...] = (y1_ref[...] + nn(oa_ref[...], w[0])).astype(bf16)


def weight_grad_call(where, weights, name, shards=0):
    arrays, items = [], []

    def place(value):
        for index, known in enumerate(arrays):
            if known is value:
                return index
        arrays.append(value)
        return len(arrays) - 1

    for lanes, kind, entries in weights:
        for index, (left, left_at, right, right_at, form) in enumerate(entries):
            items.append((lanes, kind, index, place(left), left_at, place(right), right_at, form))
    count = len(arrays)
    rows = D // 8 // len(weights[0][0])

    def body(*refs):
        where_ref = refs[0]
        ins = refs[1 : 1 + count]
        *outs, held, sems, flipped = refs[1 + count :]
        turned = None
        keep, send = outs[0], outs[-1]
        page, blk = where_ref[3], where_ref[4]

        def place_natural(slot, lane, kind, index):
            out, width = outs[0], 4 * D // shards
            each = width // 2
            for k in range(2 * D // width if kind == "up" else D // width):
                if kind == "up":
                    piece = held.at[slot, k * each : (k + 1) * each]
                    first = lane * width + (index % 2) * each
                    local_copy(
                        piece, out.at[2 * k + index // 2, first : first + each], sems.at[slot]
                    )
                else:
                    piece = held.at[slot, k * width : (k + 1) * width]
                    owner = index * (D // width) + k
                    spot = slice(lane * width, (lane + 1) * width)
                    local_copy(piece, out.at[owner, spot], sems.at[slot])

        def finish(slot):
            pltpu.make_async_copy(held.at[slot], held.at[slot], sems.at[slot]).wait()

        def place_up(slot, lane, index, core, first, second):
            near = (blk ^ relative(lane, 0, first, second)) >> 1
            group, k = index // 2, index % 2
            out = send if core else keep

            @pl.when(((blk & 1) ^ core) == group)
            def _():
                half = rows // 2
                for origin in range(4):
                    spot = first * 8 + second * 4 + (origin ^ page)
                    take = pl.ds(pl.multiple_of((origin * 4 + near) * half, half), half)
                    local_copy(
                        held.at[slot, take],
                        out.at[lane, spot, k * half : (k + 1) * half],
                        sems.at[slot],
                    )

        def place_rows(slot, lanes, index, core, first, second):
            out = send if core else keep
            for number, lane in enumerate(lanes):
                owner = blk ^ relative(lane, core, first, second)
                spot = first * 8 + second * 4 + (index ^ page)
                start = pl.multiple_of((owner * len(lanes) + number) * rows, rows)
                local_copy(held.at[slot, pl.ds(start, rows)], out.at[lane, spot], sems.at[slot])

        for step, (lanes, kind, index, left, left_at, right, right_at, form) in enumerate(items):
            slot = step % 2
            if step >= 2:
                finish(slot)
            lhs = ins[left][:, left_at * D : (left_at + 1) * D]
            if form == "tt":
                rhs = ins[right][right_at * D : (right_at + 1) * D, :]
                if turned != (left, left_at):
                    turned = (left, left_at)
                    flipped[...] = lhs.T
                product = nt(flipped[...], rhs)
            else:
                product = tn(lhs, ins[right][:, right_at * D : (right_at + 1) * D])
            held[slot] = product.astype(bf16)
            if shards:
                place_natural(slot, lanes[0], kind, index)
                continue
            for core in range(2):
                for first in range(2):
                    for second in range(2):
                        if kind == "up":
                            place_up(slot, lanes[0], index, core, first, second)
                        else:
                            place_rows(slot, lanes, index, core, first, second)
        for step in range(max(0, len(items) - 2), len(items)):
            finish(step % 2)

    shapes = [sds((2, 16, rows, D), bf16)] * 2
    if shards:
        shapes = [sds((shards, len(weights) * 4 * D // shards, D), bf16)]
    turned_rows = max([128] + [arrays[item[3]].shape[0] for item in items if item[7] == "tt"])
    moved = 2 * len(items) * D * D + sum(v.size * 2 for v in arrays)
    return pl.pallas_call(
        body,
        grid=(1,),
        out_shape=shapes,
        in_specs=[pl.BlockSpec(memory_space=pltpu.SMEM)]
        + [
            pl.BlockSpec(v.shape, lambda i: (0, 0), pipeline_mode=pl.Buffered(1)) for v in arrays
        ],
        out_specs=[pl.BlockSpec(memory_space=pl.ANY)] * len(shapes),
        scratch_shapes=[
            pltpu.VMEM((2, D, D), bf16),
            pltpu.SemaphoreType.DMA((2,)),
            pltpu.VMEM((D, turned_rows), bf16),
        ],
        compiler_params=pltpu.CompilerParams(
            vmem_limit_bytes=VMEM_LIMIT, dimension_semantics=("arbitrary",)
        ),
        cost_estimate=pl.CostEstimate(
            flops=int(len(items) * 1.6e-6 * 1.1e15), bytes_accessed=int(moved), transcendentals=0
        ),
        name=name,
    )(where, *arrays)


def window_order(grid_rows, half):
    rows, cols, _ = grid_rows.shape
    rolled = jnp.roll(grid_rows, -half, axis=1)
    shaped = rolled.reshape(rows, cols // rows, rows, D).transpose(1, 0, 2, 3)
    return shaped.reshape(rows * cols, D)


def grid_order(tokens_in, rows, cols, half):
    shaped = tokens_in.reshape(cols // rows, rows, rows, D).transpose(1, 0, 2, 3)
    return jnp.roll(shaped.reshape(rows, cols, D), half, axis=1)


def after(value, *others):
    return lax.optimization_barrier((value, others))[0]


def swapped(value, axis, flip):
    count = lax.axis_size(axis)
    return lax.ppermute(value, axis, [(i, i ^ flip) for i in range(count)])


def from_pages(value):
    pages = lax.axis_size("page")
    return [value] + [swapped(value, "page", k) for k in range(1, pages)]


def spread_first(shares):
    parts = from_pages(jnp.stack(shares))
    return [jnp.stack([part[k] for part in parts]) for k in range(2)]


def spread_second(held, *gate):
    got = swapped(held[0], "blk", 2), swapped(held[1], "blk", 4)
    held, got = after((held, got), *gate)
    return [jnp.concatenate([held[k], got[k]]) for k in range(2)]


def spread_third(near):
    return [swapped(near[0], "blk", 4), swapped(near[1], "blk", 2)]


def spread_core(held):
    return [swapped(value, "blk", 1) for value in held]


def lane_arrays(near, far, near_core, far_core, lane):
    return [near[lane], far[lane], near_core[lane], far_core[lane]]


def added(left, right):
    return (left.astype(f32) + right.astype(f32)).astype(bf16)


def collect_first(keep, send, *gate):
    got = swapped(send, "blk", 1)
    keep = after(keep, *gate)
    return [[added(keep[k, i : i + 8], got[k, i : i + 8]) for i in (0, 8)] for k in range(2)]


def collect_second(held, *gate):
    got = swapped(held[0][1], "blk", 2), swapped(held[1][1], "blk", 4)
    kept = after([held[0][0], held[1][0]], *gate)
    return [[added(kept[k][i : i + 4], got[k][i : i + 4]) for i in (0, 4)] for k in range(2)]


def collect_third(held, *gate):
    got = swapped(held[0][1], "blk", 4), swapped(held[1][1], "blk", 2)
    kept = after([held[0][0], held[1][0]], *gate)
    sums = [added(kept[k], got[k]) for k in range(2)]
    return [jnp.stack([sums[k][i] for k in range(2)]) for i in range(4)]


def collect_last(held, *gate):
    total = after(held[0], *gate).astype(f32)
    for k in range(1, 4):
        total = total + swapped(held[k], "page", k).astype(f32)
    return total


def blocks_in_chip(parts, gate):
    keep, send = parts
    got = swapped(send, "blk", 1)
    keep = after(keep, gate)
    return [added(keep[k], got[k]) for k in range(4)]


def blocks_over_chips(chips, gate):
    total = after(chips[0], gate).astype(f32)
    for k in range(1, 4):
        total = total + swapped(chips[k], "blk", 2 * k).astype(f32)
    return total


def scattered_blocks(part):
    return lax.psum_scatter(part, "blk", scatter_dimension=0, tiled=True)


def on_device(
    visual,
    query_tokens,
    answer_len,
    attn_swin,
    attn_self,
    attn_qv,
    attn_vq,
    mlp_up,
    mlp_down,
    norm_gains,
    visual_cot,
    query_cot,
):
    everyone = ("page", "blk")
    pages = lax.axis_size("page")
    page_here = lax.axis_index("page")
    blk_count = lax.axis_size("blk")
    blk_here = lax.axis_index("blk")
    shards = pages * blk_count
    rows_here, cols_all = visual.shape[1], visual.shape[2]
    half = rows_here // 2
    tokens = rows_here * cols_all
    q_rows = query_tokens.shape[1]
    slots = q_rows * blk_count
    share = attn_swin.shape[0] // D
    staged = pages == 4 and blk_count == 8 and share % 32 == 0
    gain_width = norm_gains.shape[0]
    core_here = blk_here % 2

    where = jnp.stack(
        [
            blk_here * q_rows,
            answer_len[0],
            (blk_here == blk_count - 1).astype(jnp.int32),
            page_here,
            blk_here,
        ]
    ).astype(jnp.int32)

    down_one = [(i, (i - 1) % blk_count) for i in range(blk_count)]
    up_one = [(i, (i + 1) % blk_count) for i in range(blk_count)]
    both = jnp.concatenate([visual, visual_cot], axis=0)
    lent = lax.ppermute(both[:, :half], "blk", down_one)
    both = jnp.concatenate([both[:, half:], lent], axis=1)
    vis_in = window_order(both[0], half)
    vis_cot = window_order(both[1], half)

    def flat_share(value):
        return value.astype(bf16).reshape(share, D)

    gain_rows = jnp.pad(norm_gains.astype(bf16)[None], ((0, 15), (0, D - gain_width)))
    slot_own = jnp.concatenate([query_tokens[0], query_cot[0], gain_rows], axis=0)
    slots_joined = lax.all_gather(slot_own, "blk", axis=0)
    slot_arrays = [slots_joined]
    gain_parts = jnp.stack(from_pages(slots_joined[:, 2 * q_rows, :gain_width].reshape(-1)))
    gains = jnp.take(gain_parts, jnp.arange(pages) ^ page_here, axis=0)
    gains = gains.reshape(8, D).astype(f32)
    if staged:
        a_z = spread_first([flat_share(attn_self), flat_share(attn_swin)])
        a_z = after(a_z, vis_in, vis_cot)
        a_near = spread_second(a_z)
        c_z = spread_first(after([flat_share(attn_qv), flat_share(attn_vq)], a_z))
        a_far = spread_third(a_near)
        a_near_core, a_far_core = spread_core(a_near), spread_core(a_far)
        w_self, w_swin = [
            Stored(lane_arrays(a_near, a_far, a_near_core, a_far_core, k), (k,)) for k in range(2)
        ]
        up_groups = after(mlp_up, a_near).astype(bf16)
        up_groups = up_groups.reshape(share // 4, 2, 2, D).transpose(1, 2, 0, 3)
        mine = jnp.where(core_here == 0, up_groups[0], up_groups[1])
        other = swapped(jnp.where(core_here == 0, up_groups[1], up_groups[0]), "blk", 1)
        up_share = jnp.where(
            core_here == 0,
            jnp.concatenate([mine, other], axis=1),
            jnp.concatenate([other, mine], axis=1),
        ).reshape(share, D)
        d_z = spread_first(after([up_share, flat_share(mlp_down)], c_z))
        c_near = spread_second(after(c_z, a_far, gains))
        c_far = spread_third(c_near)
    else:
        up_share = (
            mlp_up.astype(bf16).reshape(share // 4, 4, D).transpose(1, 0, 2).reshape(share, D)
        )
        joined = lax.all_gather(
            jnp.concatenate(
                [flat_share(v) for v in (attn_self, attn_swin, attn_qv, attn_vq, mlp_down)]
                + [up_share],
                axis=0,
            ),
            everyone,
            axis=0,
            tiled=True,
        ).reshape(shards, -1, D)
        w_self, w_swin, w_qv, w_vq, w_down = [
            Stored([joined[:, k * share : (k + 1) * share].reshape(4, D, D)]) for k in range(5)
        ]
        up_all = joined[:, 5 * share : 6 * share].reshape(shards, 4, share // 4, D)
        w_up = Stored([up_all.transpose(1, 0, 2, 3).reshape(4, D, D)])

    where_self = where_swin = where_cross = where_vq = where
    if staged:
        where_self = after(where, vis_in, vis_cot, a_near_core, a_far_core)
    b_all, q_self, kv_self, lse_self, o_self, y1, c_own = call(
        self_forward_kernel,
        [
            sds((slots, D), bf16),
            sds((q_rows, D), bf16),
            sds((slots, 2 * D), bf16),
            sds((q_rows, 128), f32),
            sds((q_rows, D), bf16),
            sds((q_rows, D), f32),
            sds((q_rows, D), bf16),
        ],
        [where_self, gains],
        slots=(slot_arrays, 0, q_rows),
        scratch=[pltpu.VMEM((q_rows, slots), f32)],
        loads=[(w_self, 1), (w_self, 2), (w_self, 0), (w_self, 3)],
        flops=15e-6 * 1.1e15,
        name="self_forward",
    )
    if staged:
        c_near_core = spread_core(c_near)
        c_far, c_near_core = after((c_far, c_near_core), c_own)
        c_far_core = spread_core(c_far)
        w_qv, w_vq = [
            Stored(lane_arrays(c_near, c_far, c_near_core, c_far_core, k), (k,)) for k in range(2)
        ]
        where_swin = after(where, c_far, c_near_core)
        d_z = after(d_z, c_far)
    c_all = lax.all_gather(c_own, "blk", axis=0, tiled=True)

    def swin_forward(*refs):
        swin_forward_kernel(rows_here, *refs)

    a_low, qkv_swin, lse_swin, o_swin, v1, e_low = call(
        swin_forward,
        [
            sds((tokens, D), bf16),
            sds((tokens, 3 * D), bf16),
            sds((tokens, 128), f32),
            sds((tokens, D), bf16),
            sds((tokens, D), f32),
            sds((tokens, D), bf16),
        ],
        [where_swin, vis_in, gains],
        scratch=[pltpu.VMEM((cols_all // rows_here, rows_here**2, rows_here**2), f32)],
        loads=[(w_swin, k) for k in range(4)],
        flops=11e-6 * 1.1e15,
        name="swin_forward",
    )

    if staged:
        d_near = spread_second(d_z, e_low)
        d_far = spread_third(d_near)
        where_cross = after(where, d_near)
    qa, kvb, doa, kva, qb, stats = call(
        cross_forward_kernel,
        [
            sds((slots, D), bf16),
            sds((slots, 2 * D), bf16),
            sds((slots, D), bf16),
            sds((tokens, 2 * D), bf16),
            sds((tokens, D), bf16),
            sds((3, 16, slots), f32),
        ],
        [where_cross, c_all, e_low],
        slots=(slot_arrays, 1, q_rows),
        loads=[(w_qv, 1), (w_qv, 2), (w_vq, 0), (w_qv, 0), (w_vq, 1), (w_vq, 2), (w_qv, 3)],
        flops=18e-6 * 1.1e15,
        name="cross_forward",
    )
    if staged:
        d_far = after(d_far, qb)
        d_near_core, d_far_core = spread_core(d_near), spread_core(d_far)
        w_up, w_down = [
            Stored(lane_arrays(d_near, d_far, d_near_core, d_far_core, k), (k,)) for k in range(2)
        ]
        where_vq = after(where, d_far)
    lse_vq, o_vq = call(
        vq_forward_kernel,
        [sds((tokens, 128), f32), sds((tokens, D), bf16)],
        [where_vq, qb, kvb],
        flops=11e-6 * 1.1e15,
        name="vq_forward",
    )

    all_stats = lax.all_gather(stats, "blk", axis=0)
    peaks = jnp.max(all_stats[:, 0], axis=0)
    weights = jnp.exp(all_stats[:, 0] - peaks[None])
    totals = jnp.sum(all_stats[:, 1] * weights, axis=0)
    lse_qv = peaks + jnp.log(totals)
    centre_qv = jnp.sum(all_stats[:, 2] * weights, axis=0) / totals

    v3, h_low, act_low, du_low, g2, dz_vq, dob, dg5 = call(
        mlp_kernel,
        [
            sds((tokens, D), bf16),
            sds((tokens, D), bf16),
            sds((tokens, FF), bf16),
            sds((tokens, FF), bf16),
            sds((tokens, D), f32),
            sds((tokens, D), bf16),
            sds((tokens, D), bf16),
            sds((1, D), f32),
        ],
        [where, v1, o_vq, vis_cot, gains],
        scratch=[pltpu.VMEM((tokens, D), f32)] * 3,
        loads=[(w_vq, 3), (w_up, None)] + [(w_down, k) for k in range(4)],
        flops=14e-6 * 1.1e15,
        name="mlp",
    )

    def back_to_grid(value, *gate):
        grid = grid_order(value, rows_here, cols_all, half)
        returned = lax.ppermute(grid[half:].astype(bf16), "blk", up_one)
        returned, grid = after((returned, grid), *gate)
        returned = returned.astype(grid.dtype)
        return jnp.concatenate([returned, grid[:half]], axis=0)[None]

    def flat(value):
        return value.astype(f32).reshape(-1)

    def gains_over_pages(db_all):
        gain_sum = db_all[q_rows, : pages * gain_width].reshape(pages, gain_width).astype(f32)
        kept = jnp.take(gain_sum, page_here, axis=0)
        for k in range(1, pages):
            kept = kept + swapped(jnp.take(gain_sum, page_here ^ k, axis=0), "page", k)
        return kept

    def with_gains(held, db_all):
        gain_sum = db_all[q_rows, : pages * gain_width].reshape(pages, gain_width)
        joined = []
        for k in range(pages):
            row = jnp.take(gain_sum, page_here ^ k, axis=0)[None, None]
            row = jnp.pad(row, ((0, 1), (0, 7), (0, D - gain_width)))
            joined.append(jnp.concatenate([held[k], row], axis=1))
        return joined

    def up_over_core(mlp_sum):
        up_sum = mlp_sum[0].reshape(2, 2, share // 4, D)
        mine = jnp.where(core_here == 0, up_sum[:, 0], up_sum[:, 1])
        other = swapped(jnp.where(core_here == 0, up_sum[:, 1], up_sum[:, 0]), "blk", 1)
        joined_up = jnp.where(
            core_here == 0,
            jnp.concatenate([mine, other], axis=0),
            jnp.concatenate([other, mine], axis=0),
        )
        return flat(joined_up.transpose(1, 0, 2))

    up_entries = [(h_low, 0, du_low, k, "tn") for k in range(4)]
    down_entries = [(act_low, k, vis_cot, 0, "tn") for k in range(4)]
    where_vq_back = where
    if staged:
        m_keep, m_send = weight_grad_call(
            after(where, lse_qv, centre_qv), [((0,), "up", up_entries), ((1,), "rows", down_entries)], "mlp_grads"
        )
        where_vq_back = after(where, m_keep)

    dqb, dkvbt = call(
        vq_backward_kernel,
        [sds((tokens, D), bf16), sds((2 * D, slots), bf16)],
        [where_vq_back, qb, kvb, dob, lse_vq],
        flops=16e-6 * 1.1e15,
        name="vq_backward",
    )
    where_swin_back = where_self_back = where_qv_back = where
    if staged:
        visual_out = back_to_grid(after(v3, m_keep))
        where_qv_back = after(where, visual_out)
        m_one = collect_first(m_keep, m_send, dqb)
        where_qv_back = after(where, visual_out, m_one)
    dqat, dkva, *merged_parts = call(
        qv_backward_kernel,
        [sds((D, slots), bf16), sds((tokens, 2 * D), bf16)] + [sds((slots, 2 * D), bf16)],
        [where_qv_back, qa, kva, doa, lse_qv, centre_qv, dkvbt],
        scratch=[pltpu.VMEM((slots, 2 * D), bf16)],
        loads=[(w_qv, 0), (w_vq, 1), (w_vq, 2)],
        flops=23e-6 * 1.1e15,
        name="qv_backward",
    )
    merged = scattered_blocks(merged_parts[0])
    if staged:
        m_two = collect_second(m_one, dqat)
        where_swin_back = after(where, m_two)
    dc, oa_low = merged[:, :D], merged[:, D:]

    def swin_backward(*refs):
        swin_backward_kernel(rows_here, *refs)

    dz_swin, dqkv_swin, visual_grad, dg_visual = call(
        swin_backward,
        [
            sds((tokens, D), bf16),
            sds((tokens, 3 * D), bf16),
            sds((tokens, D), f32),
            sds((2, D), f32),
        ],
        [where_swin_back, vis_in, v1, g2, gains, dkva, dqb, qkv_swin, lse_swin],
        scratch=[
            pltpu.VMEM((cols_all // rows_here, rows_here**2, rows_here**2), f32),
            pltpu.VMEM((tokens, D), bf16),
        ],
        loads=[(w_qv, 1), (w_qv, 2), (w_vq, 0), (w_swin, 3)] + [(w_swin, k) for k in range(3)],
        flops=20e-6 * 1.1e15,
        name="swin_backward",
    )

    swin_entries = [(a_low, 0, dqkv_swin, k, "tn") for k in range(3)]
    swin_entries.append((o_swin, 0, dz_swin, 0, "tn"))
    vq_entries = [
        (e_low, 0, dqb, 0, "tn"),
        (c_all, 0, dkvbt, 0, "tt"),
        (c_all, 0, dkvbt, 1, "tt"),
        (o_vq, 0, dz_vq, 0, "tn"),
    ]
    qv_entries = [
        (c_all, 0, dqat, 0, "tt"),
        (e_low, 0, dkva, 0, "tn"),
        (e_low, 0, dkva, 1, "tn"),
        (oa_low, 0, query_cot[0], 0, "tn"),
    ]
    if staged:
        m_three = collect_third(m_two, dz_swin)
        p_keep, p_send = weight_grad_call(
            after(where, m_three), [((0,), "rows", vq_entries), ((1,), "rows", swin_entries)], "patch_grads"
        )
        p_one = collect_first(p_keep, p_send)
        where_self_back = after(where, p_one)

    gy1, dz_self, dq_self, dkvt_self, dbq, dg_slots, db_part = call(
        self_backward_kernel,
        [
            sds((q_rows, D), f32),
            sds((q_rows, D), bf16),
            sds((q_rows, D), bf16),
            sds((2 * D, slots), bf16),
            sds((q_rows, D), f32),
            sds((2, D), f32),
        ]
        + [sds((slots, D), bf16)],
        [where_self_back, dc, y1, query_cot[0], gains, q_self, kv_self, lse_self],
        slots=(slot_arrays, 0, q_rows),
        scratch=[
            pltpu.VMEM((q_rows, slots), f32),
            pltpu.VMEM((q_rows, D), bf16),
            pltpu.VMEM((slots, D), bf16),
        ],
        loads=[(w_self, 3), (w_self, 0), (w_self, 1), (w_self, 2)],
        flops=15e-6 * 1.1e15,
        name="self_backward",
    )
    b_own = lax.dynamic_slice_in_dim(b_all, blk_here * q_rows, q_rows, 0)
    self_entries = [
        (b_own, 0, dq_self, 0, "tn"),
        (b_all, 0, dkvt_self, 0, "tt"),
        (b_all, 0, dkvt_self, 1, "tt"),
        (o_self, 0, dz_self, 0, "tn"),
    ]
    gain_block = jnp.concatenate(
        [dg_visual[0:1], dg_slots[0:1], dg_visual[1:2], dg_slots[1:2], dg5, jnp.zeros((3, D), f32)],
        axis=0,
    )
    gain_block = gain_block.astype(bf16).reshape(pages, blk_count, gain_width).transpose(1, 0, 2)
    gain_block = gain_block.reshape(blk_count, 1, pages * gain_width)
    gain_block = jnp.pad(gain_block, ((0, 0), (0, 15), (0, D - pages * gain_width)))
    whole_part = jnp.concatenate([db_part.reshape(blk_count, q_rows, D), gain_block], axis=1)
    db_all = scattered_blocks(whole_part.reshape(blk_count * (q_rows + 16), D))
    where_end = where
    if staged:
        p_two = collect_second(p_one, gy1)
        mlp_sum = collect_last(m_three, gy1)
        z_keep, z_send = weight_grad_call(
            after(where, p_two, mlp_sum), [((0,), "rows", qv_entries), ((1,), "rows", self_entries)], "slot_grads"
        )
        visual_grad = back_to_grid(visual_grad, z_keep)
        z_keep, z_send = after((z_keep, z_send), visual_grad)
        z_one = collect_first(z_keep, z_send)
        p_three = collect_third(p_two, z_one)
        z_two = collect_second(after(z_one, p_three))
        patch_sum = collect_last(after(p_three, z_one))
        db_all = after(db_all, patch_sum)
        up_grad = up_over_core(mlp_sum)
        z_two = after(z_two, patch_sum, up_grad)
        z_three = with_gains(collect_third(z_two), db_all)
        where_end = after(where, z_three)
    db = db_all[:q_rows]
    query_grad, query_out = call(
        query_end_kernel,
        [sds((q_rows, D), f32), sds((q_rows, D), bf16)],
        [where_end, db, dbq, query_tokens[0], gy1, gains, y1, oa_low],
        loads=[(w_qv, 3)],
        name="query_end",
    )

    if staged:
        slot_sum = collect_last(z_three)
        gain_grad, slot_sum = slot_sum[0, share, :gain_width], slot_sum[:, :share]
        swin_grad, self_grad = flat(patch_sum[1]), flat(slot_sum[1])
        qv_grad, vq_grad = flat(slot_sum[0]), flat(patch_sum[0])
        down_grad = flat(mlp_sum[1])
    else:
        visual_out, visual_grad = back_to_grid(v3), back_to_grid(visual_grad)
        gain_grad = gains_over_pages(db_all)

        def outer(left, right):
            return tn(left, right).astype(bf16)

        def outer_t(left, right_t):
            return lax.dot_general(
                left, right_t, (((0,), (1,)), ((), ())), preferred_element_type=f32
            ).astype(bf16)

        def as_shares(mats):
            return jnp.concatenate(mats, axis=0).reshape(shards, share, D)

        def summed(parts):
            joined = jnp.concatenate(parts, axis=1)
            width = joined.shape[1]
            return lax.psum_scatter(
                joined.reshape(shards * width, D), everyone, scatter_dimension=0, tiled=True
            )

        up_mats = jnp.stack([outer(h_low, du_low[:, k * D : (k + 1) * D]) for k in range(4)])
        up_part = (
            up_mats.reshape(4, shards, share // 4, D)
            .transpose(1, 0, 2, 3)
            .reshape(shards, share, D)
        )
        down_part = outer(act_low, vis_cot).reshape(shards, share, D)
        mlp_sum = summed([up_part, down_part])
        qv_part = as_shares(
            [
                outer_t(c_all, dqat),
                outer(e_low, dkva[:, :D]),
                outer(e_low, dkva[:, D:]),
                outer(oa_low, query_cot[0]),
            ]
        )
        vq_part = as_shares(
            [
                outer(e_low, dqb),
                outer_t(c_all, dkvbt[:D]),
                outer_t(c_all, dkvbt[D:]),
                outer(o_vq, dz_vq),
            ]
        )
        cross_sum = summed([qv_part, vq_part])
        swin_part = as_shares(
            [outer(a_low, dqkv_swin[:, k * D : (k + 1) * D]) for k in range(3)]
            + [outer(o_swin, dz_swin)]
        )
        self_part = as_shares(
            [
                outer(b_own, dq_self),
                outer_t(b_all, dkvt_self[:D]),
                outer_t(b_all, dkvt_self[D:]),
                outer(o_self, dz_self),
            ]
        )
        last_sum = summed([swin_part, self_part])
        up_grad = flat(mlp_sum[:share].reshape(4, share // 4, D).transpose(1, 0, 2))
        down_grad = flat(mlp_sum[share:])
        qv_grad, vq_grad = flat(cross_sum[:share]), flat(cross_sum[share:])
        swin_grad, self_grad = flat(last_sum[:share]), flat(last_sum[share:])

    return (
        visual_out,
        query_out[None],
        visual_grad,
        query_grad[None],
        swin_grad,
        self_grad,
        qv_grad,
        vq_grad,
        up_grad,
        down_grad,
        gain_grad,
    )


def solution(mesh):
    placed = (
        P("page", "blk", None, None),
        P("page", "blk", None),
        P("page"),
        P(("page", "blk")),
        P(("page", "blk")),
        P(("page", "blk")),
        P(("page", "blk")),
        P(("page", "blk")),
        P(("page", "blk")),
        P(("page", "blk")),
        P("page", "blk", None, None),
        P("page", "blk", None),
    )
    return jax.shard_map(
        on_device,
        mesh=mesh,
        in_specs=placed,
        out_specs=(
            P("page", "blk", None, None),
            P("page", "blk", None),
            P("page", "blk", None, None),
            P("page", "blk", None),
            P(("page", "blk")),
            P(("page", "blk")),
            P(("page", "blk")),
            P(("page", "blk")),
            P(("page", "blk")),
            P(("page", "blk")),
            P(("page", "blk")),
        ),
        check_vma=False,
    )
```

```python
import jax
import jax.numpy as jnp
from jax import lax
from jax.experimental import pallas as pl
from jax.experimental.pallas import tpu as pltpu
from jax.sharding import PartitionSpec as P

D = 768
HEADS = 12
HD = 64
FF = 3072
PAIRS = HEADS // 2
PW = 2 * HD
SCALE = HD ** (-0.5)

EPS = 1e-05
NEG = -1e30

bf16 = jnp.bfloat16
f32 = jnp.float32
VMEM_LIMIT = 56 * 1024 * 1024


def nn(left, right):
    return lax.dot_general(left, right, (((1,), (0,)), ((), ())), preferred_element_type=f32)


def nt(left, right):
    return lax.dot_general(left, right, (((1,), (1,)), ((), ())), preferred_element_type=f32)


def tn(left, right):
    return lax.dot_general(left, right, (((0,), (0,)), ((), ())), preferred_element_type=f32)


def norm_parts(rows):
    centre = jnp.mean(rows, axis=-1, keepdims=True)
    centred = rows - centre
    spread = jnp.mean(centred * centred, axis=-1, keepdims=True)
    inverse = lax.rsqrt(spread + EPS)
    return centred * inverse, inverse


def norm(rows, gain):
    return norm_parts(rows)[0] * gain


def norm_back(rows, gain, grad):
    unit, inverse = norm_parts(rows)
    grad_gain = jnp.sum(grad * unit, axis=0, keepdims=True)
    scaled = grad * gain
    first = jnp.mean(scaled, axis=-1, keepdims=True)
    second = jnp.mean(scaled * unit, axis=-1, keepdims=True)
    return inverse * (scaled - first - unit * second), grad_gain


def lane_half(half, value, dtype):
    lanes = lax.broadcasted_iota(jnp.int32, (1, PW), 1)
    return jnp.where((lanes // HD) == half, value, 0.0).astype(dtype)


def low_half(rows):
    return lax.broadcasted_iota(jnp.int32, (rows, PW), 1) < HD


def column(table, index):
    lanes = lax.broadcasted_iota(jnp.int32, table.shape, 1)
    return jnp.sum(jnp.where(lanes == index, table, 0.0), axis=-1, keepdims=True)


def pair_cols(pair, base=0):
    return pl.ds(pl.multiple_of(base + pair * PW, PW), PW)


def softmax_rows(scores):
    highest = jnp.max(scores, axis=-1, keepdims=True)
    raised = jnp.exp(scores - highest)
    totals = jnp.sum(raised, axis=-1, keepdims=True)
    return raised * (1.0 / totals), highest + jnp.log(totals)


class Stored:
    def __init__(self, arrays, lanes=(), joint=None):
        self.arrays = list(arrays)
        self.lanes = tuple(lanes)
        self.joint = joint


def stage_bits(lane):
    return (1, 2) if lane == 0 else (2, 1)


def relative(lane, core, first, second):
    bit_one, bit_two = stage_bits(lane)
    return core | (first << bit_one) | (second << bit_two)


def local_copy(source, target, sem):
    pltpu.make_async_copy(source, target, sem).start()


def fetch(where_ref, stored, refs, index, target, sem):
    if stored.joint is not None:
        first, rows = stored.joint
        count = D // rows
        for k in range(count):
            piece = refs[0].at[index * count + k, first : first + rows]
            local_copy(piece, target.at[k * rows : (k + 1) * rows], sem)
        return
    if len(refs) == 1:
        local_copy(refs[0].at[index], target, sem)
        return
    page, blk = where_ref[3], where_ref[4]
    count = len(stored.lanes)
    for number, lane in enumerate(stored.lanes):
        for core in range(2):
            for second in range(2):
                for first in range(2):
                    ref = refs[4 * number + 2 * core + second]
                    piece = ref.at[(index ^ page) + 4 * first]
                    rows = piece.shape[0]
                    owner = blk ^ relative(lane, core, first, second)
                    start = pl.multiple_of((owner * count + number) * rows, rows)
                    local_copy(piece, target.at[pl.ds(start, rows)], sem)


def fetch_up(where_ref, stored, refs, target, sem):
    if len(refs) == 1:
        local_copy(refs[0], target, sem)
        return
    page, blk = where_ref[3], where_ref[4]
    for core in range(2):
        for second in range(2):
            for first in range(2):
                ref = refs[2 * core + second]
                near = (blk ^ relative(stored.lanes[0], 0, first, second)) >> 1
                for origin in range(4):
                    piece = ref.at[(origin ^ page) + 4 * first]
                    rows = piece.shape[0] // 2
                    spot = pl.ds(pl.multiple_of((origin * 4 + near) * rows, rows), rows)
                    for k in range(2):
                        group = 2 * ((blk & 1) ^ core) + k
                        local_copy(piece.at[k * rows : (k + 1) * rows], target.at[group, spot], sem)


class Loads:
    def __init__(self, held, sems, plan):
        self.held, self.sems, self.plan, self.done = held, sems, plan, set()

    def ready(self, *places):
        for place in places:
            if place not in self.done:
                self.done.add(place)
                start, count = self.plan[place]
                span = self.held.at[start : start + count]
                pltpu.make_async_copy(span, span, self.sems.at[place]).wait()

    def __getitem__(self, place):
        self.ready(place)
        return self.held[self.plan[place][0]]

    def part(self, place, k):
        return self.held[self.plan[place][0] + k]


def call(kernel, outs, ins, scratch=(), smem=1, loads=(), slots=None, flops=0, name=None):
    def whole(value):
        zeros = (0,) * len(value.shape)
        return pl.BlockSpec(value.shape, lambda i: zeros, pipeline_mode=pl.Buffered(1))

    specs = []
    for index, value in enumerate(ins):
        if index < smem:
            specs.append(pl.BlockSpec(memory_space=pltpu.SMEM))
        else:
            specs.append(whole(value))
    single = not isinstance(outs, list)
    shapes = [outs] if single else outs
    count_in, count_out = len(ins), len(shapes)
    unique, plan, size = [], [], 0
    for stored, which in loads:
        if stored not in unique:
            unique.append(stored)
        width = 4 if which is None else 1
        plan.append((size, width))
        size += width
    arrays = [array for stored in unique for array in stored.arrays]
    gathered, slot_scratch = [], []
    if slots:
        gathered, part, own = slots
        blocks = len(gathered) if len(gathered) > 1 else gathered[0].shape[0]
        slot_scratch = [pltpu.VMEM((blocks, own, D), bf16), pltpu.SemaphoreType.DMA]
    held = [pltpu.VMEM((size, D, D), bf16), pltpu.SemaphoreType.DMA((len(plan),))] if loads else []

    def body(*refs):
        inner = list(refs[:count_in])
        at = count_in
        taken = {}
        for stored in unique:
            taken[id(stored)] = refs[at : at + len(stored.arrays)]
            at += len(stored.arrays)
        pieces = refs[at : at + len(gathered)]
        at += len(gathered)
        results = list(refs[at : at + count_out])
        rest = list(refs[at + count_out :])
        if slots:
            together, slot_sem = rest[:2]
            rest = rest[2:]
            rows = slice(part * own, (part + 1) * own)
            if len(pieces) == 1:
                local_copy(pieces[0].at[:, rows], together, slot_sem)
            for k, piece in enumerate(pieces if len(pieces) > 1 else ()):
                local_copy(piece.at[rows], together.at[inner[0][4] ^ k], slot_sem)
            inner.append(together)
        if not loads:
            kernel(*inner, *results, *rest)
            return
        kept, sems = rest[-2], rest[-1]
        for place, (stored, which) in enumerate(loads):
            mine, (start, width) = taken[id(stored)], plan[place]
            if which is None:
                fetch_up(inner[0], stored, mine, kept.at[start : start + width], sems.at[place])
            else:
                fetch(inner[0], stored, mine, which, kept.at[start], sems.at[place])
        if slots:
            pltpu.make_async_copy(together, together, slot_sem).wait()
        weights = Loads(kept, sems, plan)
        kernel(*inner, weights, *results, *rest[:-2])
        weights.ready(*range(len(plan)))

    moved = sum(v.size * v.dtype.itemsize for v in list(ins) + shapes) + size * D * D * 2
    result = pl.pallas_call(
        body,
        grid=(1,),
        out_shape=shapes,
        in_specs=specs + [pl.BlockSpec(memory_space=pl.ANY)] * (len(arrays) + len(gathered)),
        out_specs=[whole(value) for value in shapes],
        scratch_shapes=slot_scratch + list(scratch) + held,
        compiler_params=pltpu.CompilerParams(
            vmem_limit_bytes=VMEM_LIMIT, dimension_semantics=("arbitrary",)
        ),
        cost_estimate=pl.CostEstimate(flops=int(flops), bytes_accessed=int(moved), transcendentals=0),
        name=name,
    )(*ins, *arrays, *gathered)
    return result[0] if single else result


def sds(shape, dtype):
    return jax.ShapeDtypeStruct(shape, dtype)


def self_bias(bias_ref, first_row, live):
    rows, slots = bias_ref.shape
    keys = lax.broadcasted_iota(jnp.int32, (rows, slots), 1)
    places = lax.broadcasted_iota(jnp.int32, (rows, slots), 0) + first_row
    bias_ref[...] = jnp.where((keys <= places) & (keys < live), 0.0, NEG)


def self_forward_kernel(
    where_ref, g_ref, y_ref, w, b_ref, q_ref, kv_ref, lse_ref, o_ref, y1_ref, c_ref, bias_ref
):
    first_row, live = where_ref[0], where_ref[1]
    slots, own = b_ref.shape[0], q_ref.shape[0]
    tile = 256
    group = tile // own
    w.ready(0, 1)

    def project(i, carry):
        rows = pl.ds(pl.multiple_of(i * tile, tile), tile)
        part = y_ref[pl.ds(i * group, group)].reshape(tile, D)
        normed = norm(part.astype(f32), g_ref[1:2, :]).astype(bf16)
        b_ref[rows, :] = normed
        kv_ref[rows, 0:D] = nn(normed, w[0]).astype(bf16)
        kv_ref[rows, D : 2 * D] = nn(normed, w[1]).astype(bf16)
        return carry

    lax.fori_loop(0, slots // tile, project, 0)
    mine = pl.ds(pl.multiple_of(first_row, 16), own)
    q_ref[...] = nn(b_ref[mine, :], w[2]).astype(bf16)
    self_bias(bias_ref, first_row, live)
    lse_ref[...] = jnp.zeros_like(lse_ref)
    lanes = lax.broadcasted_iota(jnp.int32, lse_ref.shape, 1)
    low = low_half(own)

    def attend(pair, carry):
        queries = q_ref[:, pair_cols(pair)]
        keys = kv_ref[:, pair_cols(pair)]
        values = kv_ref[:, pair_cols(pair, D)]
        mixed = []
        table = lse_ref[...]
        for half in range(2):
            scores = nt(queries * lane_half(half, SCALE, bf16), keys) + bias_ref[...]
            chances, log_totals = softmax_rows(scores)
            mixed.append(nn(chances.astype(bf16), values))
            table = jnp.where(lanes == 2 * pair + half, log_totals, table)
        lse_ref[...] = table
        o_ref[:, pair_cols(pair)] = jnp.where(low, mixed[0], mixed[1]).astype(bf16)
        return carry

    lax.fori_loop(0, PAIRS, attend, 0)
    y1 = y_ref[where_ref[4]].astype(f32) + nn(o_ref[...], w[3])
    y1_ref[...] = y1
    c_ref[...] = norm(y1, g_ref[3:4, :]).astype(bf16)


def window_bias(rows, side, row_split, col_split):
    def flags(shape, dim):
        token = lax.broadcasted_iota(jnp.int32, shape, dim)
        row, col = token // side, token % side
        return jnp.where(row >= side // 2, row_split, 0) + jnp.where(
            col >= side // 2, 2 * col_split, 0
        )

    return jnp.where(flags((rows, rows), 0) == flags((rows, rows), 1), 0.0, NEG)


def swin_forward_kernel(
    side, where_ref, x_ref, g_ref, w, a_ref, qkv_ref, lse_ref, o_ref, v1_ref, e_ref, bias_ref
):
    is_last = where_ref[2]
    tokens = x_ref.shape[0]
    rows = side * side
    windows = tokens // rows
    x = x_ref[...].astype(f32)
    normed = norm(x, g_ref[0:1, :]).astype(bf16)
    a_ref[...] = normed
    for k in range(3):
        qkv_ref[:, k * D : (k + 1) * D] = nn(normed, w[k]).astype(bf16)
    for win in range(windows):
        bias_ref[win] = window_bias(rows, side, is_last, 1 if win == windows - 1 else 0)
    lse_ref[...] = jnp.zeros_like(lse_ref)
    lanes = lax.broadcasted_iota(jnp.int32, (rows, lse_ref.shape[1]), 1)
    low = low_half(rows)

    def attend(pair, carry):
        for win in range(windows):
            at = slice(win * rows, (win + 1) * rows)
            queries = qkv_ref[at, pair_cols(pair)]
            keys = qkv_ref[at, pair_cols(pair, D)]
            values = qkv_ref[at, pair_cols(pair, 2 * D)]
            mixed = []
            table = lse_ref[at, :]
            for half in range(2):
                scores = nt(queries * lane_half(half, SCALE, bf16), keys) + bias_ref[win]
                chances, log_totals = softmax_rows(scores)
                mixed.append(nn(chances.astype(bf16), values))
                table = jnp.where(lanes == 2 * pair + half, log_totals, table)
            lse_ref[at, :] = table
            o_ref[at, pair_cols(pair)] = jnp.where(low, mixed[0], mixed[1]).astype(bf16)
        return carry

    lax.fori_loop(0, PAIRS, attend, 0)
    v1 = x + nn(o_ref[...], w[3])
    v1_ref[...] = v1
    e_ref[...] = norm(v1, g_ref[2:3, :]).astype(bf16)


def cross_forward_kernel(
    where_ref,
    c_ref,
    e_ref,
    cot_ref,
    w,
    qa_ref,
    kvb_ref,
    doa_ref,
    kva_ref,
    qb_ref,
    stats_ref,
):
    slots, tokens = qa_ref.shape[0], e_ref.shape[0]
    tile = 256
    normed = e_ref[...]
    for k in range(2):
        kva_ref[:, k * D : (k + 1) * D] = nn(normed, w[k]).astype(bf16)
    qb_ref[...] = nn(normed, w[2]).astype(bf16)
    w.ready(3, 4, 5, 6)
    group = tile // cot_ref.shape[1]

    def project(i, carry):
        rows = pl.ds(pl.multiple_of(i * tile, tile), tile)
        part = c_ref[rows, :]
        qa_ref[rows, :] = nn(part, w[3]).astype(bf16)
        for k in range(2):
            kvb_ref[rows, k * D : (k + 1) * D] = nn(part, w[4 + k]).astype(bf16)
        cot = cot_ref[pl.ds(i * group, group)].reshape(tile, D)
        doa_ref[rows, :] = nt(cot, w[6]).astype(bf16)
        return carry

    lax.fori_loop(0, slots // tile, project, 0)
    stats_ref[...] = jnp.zeros_like(stats_ref)

    def page_stats(pair, carry):
        keys = kva_ref[:, pair_cols(pair)]
        values = kva_ref[:, pair_cols(pair, D)]
        for half in range(2):
            head = 2 * pair + half
            keys_h = keys * lane_half(half, SCALE, bf16)
            values_h = values * lane_half(half, 1.0, bf16)
            for i in range(slots // tile):
                rows = slice(i * tile, (i + 1) * tile)
                scores = nt(keys_h, qa_ref[rows, pair_cols(pair)])
                highest = jnp.max(scores, axis=0, keepdims=True)
                raised = jnp.exp(scores - highest)
                grads = nt(values_h, doa_ref[rows, pair_cols(pair)])
                stats_ref[0, pl.ds(head, 1), rows] = highest
                stats_ref[1, pl.ds(head, 1), rows] = jnp.sum(raised, axis=0, keepdims=True)
                stats_ref[2, pl.ds(head, 1), rows] = jnp.sum(raised * grads, axis=0, keepdims=True)
        return carry

    lax.fori_loop(0, PAIRS, page_stats, 0)


def vq_forward_kernel(where_ref, qb_ref, kvb_ref, lse_ref, ob_ref):
    live = where_ref[1]
    tokens, slots = qb_ref.shape[0], kvb_ref.shape[0]
    lse_ref[...] = jnp.zeros_like(lse_ref)
    lanes = lax.broadcasted_iota(jnp.int32, lse_ref.shape, 1)
    low = low_half(tokens)
    bias = jnp.where(lax.broadcasted_iota(jnp.int32, (1, slots), 1) < live, 0.0, NEG)

    def attend(pair, carry):
        queries = qb_ref[:, pair_cols(pair)]
        keys = kvb_ref[:, pair_cols(pair)]
        values = kvb_ref[:, pair_cols(pair, D)]
        mixed = []
        table = lse_ref[...]
        for half in range(2):
            scores = nt(queries * lane_half(half, SCALE, bf16), keys) + bias
            chances, log_totals = softmax_rows(scores)
            mixed.append(nn(chances.astype(bf16), values))
            table = jnp.where(lanes == 2 * pair + half, log_totals, table)
        lse_ref[...] = table
        ob_ref[:, pair_cols(pair)] = jnp.where(low, mixed[0], mixed[1]).astype(bf16)
        return carry

    lax.fori_loop(0, PAIRS, attend, 0)


GELU_A = 0.7978845608028654
GELU_B = 0.044715


def mlp_kernel(
    where_ref,
    v1_ref,
    ob_ref,
    cot_ref,
    g_ref,
    w,
    v3_ref,
    h_ref,
    act_ref,
    du_ref,
    g2_ref,
    dz_ref,
    dob_ref,
    dg_ref,
    v2_ref,
    sum_ref,
    dh_ref,
):
    v2 = v1_ref[...] + nn(ob_ref[...], w[0])
    v2_ref[...] = v2
    sum_ref[...] = v2
    h_ref[...] = norm(v2, g_ref[4:5, :]).astype(bf16)
    dh_ref[...] = jnp.zeros_like(dh_ref)
    w.ready(1, 2, 3, 4, 5)

    def chunk(k, carry):
        up, down = w.part(1, k), w.part(2, k)
        at = pl.ds(pl.multiple_of(k * D, D), D)
        u = nn(h_ref[...], up)
        squared = u * u
        bend = jnp.tanh(GELU_A * (u + GELU_B * u * squared))
        act = (0.5 * u * (1.0 + bend)).astype(bf16)
        act_ref[:, at] = act
        slope = 0.5 * (1.0 + bend) + 0.5 * u * (1.0 - bend * bend) * GELU_A * (
            1.0 + 3.0 * GELU_B * squared
        )
        du = (nt(cot_ref[...], down) * slope).astype(bf16)
        du_ref[:, at] = du
        sum_ref[...] += nn(act, down)
        dh_ref[...] += nt(du, up)
        return carry

    lax.fori_loop(0, FF // D, chunk, 0)
    v3_ref[...] = sum_ref[...].astype(bf16)
    part, dg = norm_back(v2_ref[...], g_ref[4:5, :], dh_ref[...])
    dg_ref[...] = dg
    g2 = cot_ref[...].astype(f32) + part
    g2_ref[...] = g2
    dz = g2.astype(bf16)
    dz_ref[...] = dz
    dob_ref[...] = nt(dz, w[0]).astype(bf16)


def vq_backward_kernel(
    where_ref, qb_ref, kvb_ref, dob_ref, lse_ref, dqb_ref, dkvbt_ref
):
    live = where_ref[1]
    tokens, slots = qb_ref.shape[0], kvb_ref.shape[0]
    bias = jnp.where(lax.broadcasted_iota(jnp.int32, (1, slots), 1) < live, 0.0, NEG)
    low = low_half(tokens)

    def back(pair, carry):
        queries = qb_ref[:, pair_cols(pair)]
        keys = kvb_ref[:, pair_cols(pair)]
        values = kvb_ref[:, pair_cols(pair, D)]
        grads = dob_ref[:, pair_cols(pair)]
        queries_t = (queries * SCALE).astype(f32).T.astype(bf16)
        grads_t = grads.astype(f32).T.astype(bf16)
        parts = []
        for half in range(2):
            own = slice(half * HD, (half + 1) * HD)
            scores = nt(queries * lane_half(half, SCALE, bf16), keys) + bias
            chances = jnp.exp(scores - column(lse_ref[...], 2 * pair + half))
            slopes = nt(grads * lane_half(half, 1.0, bf16), values)
            centre = jnp.sum(chances * slopes, axis=-1, keepdims=True)
            ds = (chances * (slopes - centre)).astype(bf16)
            parts.append(nn(ds, keys))
            at = pair * PW + half * HD
            dkvbt_ref[pl.ds(pl.multiple_of(at, HD), HD), :] = nn(queries_t[own], ds).astype(bf16)
            dkvbt_ref[pl.ds(pl.multiple_of(D + at, HD), HD), :] = nn(
                grads_t[own], chances.astype(bf16)
            ).astype(bf16)
        dqb_ref[:, pair_cols(pair)] = (jnp.where(low, parts[0], parts[1]) * SCALE).astype(bf16)
        return carry

    lax.fori_loop(0, PAIRS, back, 0)


def hand_out(where_ref, held, outs):
    if len(outs) == 1:
        outs[0][...] = held[...]
        return
    rows = outs[0].shape[1]
    for core, out in enumerate(outs):
        for k in range(4):
            start = pl.multiple_of((where_ref[4] ^ (2 * k + core)) * rows, rows)
            out[k] = held[pl.ds(start, rows), :]


def qv_backward_kernel(
    where_ref,
    qa_ref,
    kva_ref,
    doa_ref,
    lse_ref,
    centre_ref,
    dkvbt_ref,
    w,
    dqat_ref,
    dkva_ref,
    *rest,
):
    dc_refs, held = rest[:-1], rest[-1]
    slots, tokens = qa_ref.shape[0], kva_ref.shape[0]
    low = low_half(tokens)
    tile = 512

    def back(pair, carry):
        keys = kva_ref[:, pair_cols(pair)]
        values = kva_ref[:, pair_cols(pair, D)]
        keys_t = (keys * SCALE).astype(f32).T.astype(bf16)
        values_t = values.astype(f32).T.astype(bf16)
        for i in range(slots // tile):
            rows = slice(i * tile, (i + 1) * tile)
            queries = qa_ref[rows, pair_cols(pair)]
            grads = doa_ref[rows, pair_cols(pair)]
            dk, dv, mixed = [], [], []
            for half in range(2):
                head = 2 * pair + half
                own = slice(half * HD, (half + 1) * HD)
                scores = nt(keys * lane_half(half, SCALE, bf16), queries)
                chances = jnp.exp(scores - lse_ref[pl.ds(head, 1), rows])
                slopes = nt(values * lane_half(half, 1.0, bf16), grads)
                ds = (chances * (slopes - centre_ref[pl.ds(head, 1), rows])).astype(bf16)
                rounded = chances.astype(bf16)
                mixed.append(nn(values_t[own], rounded))
                dqat_ref[pl.ds(pl.multiple_of(head * HD, HD), HD), rows] = nn(
                    keys_t[own], ds
                ).astype(bf16)
                dk.append(nn(ds, queries))
                dv.append(nn(rounded, grads))
            held[rows, pair_cols(pair, D)] = jnp.concatenate(mixed, axis=0).T.astype(bf16)
            dk_now = jnp.where(low, dk[0], dk[1]) * SCALE
            dv_now = jnp.where(low, dv[0], dv[1])
            if i == 0:
                dk_sum, dv_sum = dk_now, dv_now
            else:
                dk_sum, dv_sum = dk_sum + dk_now, dv_sum + dv_now
        dkva_ref[:, pair_cols(pair)] = dk_sum.astype(bf16)
        dkva_ref[:, pair_cols(pair, D)] = dv_sum.astype(bf16)
        return carry

    lax.fori_loop(0, PAIRS, back, 0)
    for i in range(slots // tile):
        cols = slice(i * tile, (i + 1) * tile)
        total = nn(w[0], dqat_ref[:, cols])
        total += nn(w[1], dkvbt_ref[0:D, cols])
        total += nn(w[2], dkvbt_ref[D : 2 * D, cols])
        held[cols, 0:D] = total.T.astype(bf16)
    hand_out(where_ref, held, dc_refs)


def swin_backward_kernel(
    side,
    where_ref,
    x_ref,
    v1_ref,
    g2_ref,
    g_ref,
    dkva_ref,
    dqb_ref,
    qkv_ref,
    lse_ref,
    w,
    dz_ref,
    dqkv_ref,
    grad_ref,
    dg_ref,
    bias_ref,
    do_ref,
):
    is_last = where_ref[2]
    tokens = x_ref.shape[0]
    rows = side * side
    windows = tokens // rows
    de = nt(dkva_ref[:, 0:D], w[0])
    de += nt(dkva_ref[:, D : 2 * D], w[1])
    de += nt(dqb_ref[...], w[2])
    part, dg3 = norm_back(v1_ref[...], g_ref[2:3, :], de)
    g1 = g2_ref[...] + part
    grad_ref[...] = g1
    dz = g1.astype(bf16)
    dz_ref[...] = dz
    do_ref[...] = nt(dz, w[3]).astype(bf16)
    for win in range(windows):
        bias_ref[win] = window_bias(rows, side, is_last, 1 if win == windows - 1 else 0)
    low = low_half(rows)

    def back(pair, carry):
        for win in range(windows):
            at = slice(win * rows, (win + 1) * rows)
            queries = qkv_ref[at, pair_cols(pair)]
            keys = qkv_ref[at, pair_cols(pair, D)]
            values = qkv_ref[at, pair_cols(pair, 2 * D)]
            grads = do_ref[at, pair_cols(pair)]
            dq, dk, dv = [], [], []
            for half in range(2):
                scores = nt(queries * lane_half(half, SCALE, bf16), keys) + bias_ref[win]
                chances = jnp.exp(scores - column(lse_ref[at, :], 2 * pair + half))
                slopes = nt(grads * lane_half(half, 1.0, bf16), values)
                centre = jnp.sum(chances * slopes, axis=-1, keepdims=True)
                ds = (chances * (slopes - centre)).astype(bf16)
                dq.append(nn(ds, keys))
                dk.append(tn(ds, queries))
                dv.append(tn(chances.astype(bf16), grads))
            for k, (pieces, factor) in enumerate(((dq, SCALE), (dk, SCALE), (dv, 1.0))):
                dqkv_ref[at, pair_cols(pair, k * D)] = (
                    jnp.where(low, pieces[0], pieces[1]) * factor
                ).astype(bf16)
        return carry

    lax.fori_loop(0, PAIRS, back, 0)
    da = nt(dqkv_ref[:, 0:D], w[4])
    da += nt(dqkv_ref[:, D : 2 * D], w[5])
    da += nt(dqkv_ref[:, 2 * D : 3 * D], w[6])
    part, dg1 = norm_back(x_ref[...].astype(f32), g_ref[0:1, :], da)
    grad_ref[...] += part
    dg_ref[...] = jnp.concatenate([dg1, dg3], axis=0)


def self_backward_kernel(
    where_ref,
    dc_ref,
    y1_ref,
    cot_ref,
    g_ref,
    q_ref,
    kv_ref,
    lse_ref,
    y_ref,
    w,
    gy1_ref,
    dz_ref,
    dq_ref,
    dkvt_ref,
    dbq_ref,
    dg_ref,
    *rest,
):
    db_refs, (bias_ref, do_ref, db_held) = rest[:-3], rest[-3:]
    group = 256 // q_ref.shape[0]
    first_row, live = where_ref[0], where_ref[1]
    own_rows, slots = q_ref.shape[0], kv_ref.shape[0]
    part, dg = norm_back(y1_ref[...], g_ref[3:4, :], dc_ref[...].astype(f32))
    gy1 = cot_ref[...].astype(f32) + part
    gy1_ref[...] = gy1
    dz = gy1.astype(bf16)
    dz_ref[...] = dz
    do_ref[...] = nt(dz, w[0]).astype(bf16)
    self_bias(bias_ref, first_row, live)
    low = low_half(own_rows)

    def back(pair, carry):
        queries = q_ref[:, pair_cols(pair)]
        keys = kv_ref[:, pair_cols(pair)]
        values = kv_ref[:, pair_cols(pair, D)]
        grads = do_ref[:, pair_cols(pair)]
        queries_t = (queries * SCALE).astype(f32).T.astype(bf16)
        grads_t = grads.astype(f32).T.astype(bf16)
        parts = []
        for half in range(2):
            own = slice(half * HD, (half + 1) * HD)
            scores = nt(queries * lane_half(half, SCALE, bf16), keys) + bias_ref[...]
            chances = jnp.exp(scores - column(lse_ref[...], 2 * pair + half))
            slopes = nt(grads * lane_half(half, 1.0, bf16), values)
            centre = jnp.sum(chances * slopes, axis=-1, keepdims=True)
            ds = (chances * (slopes - centre)).astype(bf16)
            parts.append(nn(ds, keys))
            at = pair * PW + half * HD
            dkvt_ref[pl.ds(pl.multiple_of(at, HD), HD), :] = nn(queries_t[own], ds).astype(bf16)
            dkvt_ref[pl.ds(pl.multiple_of(D + at, HD), HD), :] = nn(
                grads_t[own], chances.astype(bf16)
            ).astype(bf16)
        dq_ref[:, pair_cols(pair)] = (jnp.where(low, parts[0], parts[1]) * SCALE).astype(bf16)
        return carry

    lax.fori_loop(0, PAIRS, back, 0)
    dbq = nt(dq_ref[...], w[1])
    dbq_ref[...] = dbq
    unit = norm_parts(y_ref[where_ref[4]].astype(f32))[0]
    dg2 = jnp.sum(dbq * unit, axis=0, keepdims=True)
    tile = 256
    for i in range(slots // tile):
        cols = slice(i * tile, (i + 1) * tile)
        total = nn(w[2], dkvt_ref[0:D, cols])
        total += nn(w[3], dkvt_ref[D : 2 * D, cols])
        back = total.T
        db_held[cols, :] = back.astype(bf16)
        part = y_ref[i * group : (i + 1) * group].reshape(tile, D)
        unit = norm_parts(part.astype(f32))[0]
        dg2 += jnp.sum(back * unit, axis=0, keepdims=True)
    dg_ref[...] = jnp.concatenate([dg2, dg], axis=0)
    hand_out(where_ref, db_held, db_refs)


def query_end_kernel(
    where_ref, db_ref, dbq_ref, y_ref, gy1_ref, g_ref, y1_ref, oa_ref, w, grad_ref, out_ref
):
    part, _ = norm_back(
        y_ref[...].astype(f32), g_ref[1:2, :], db_ref[...].astype(f32) + dbq_ref[...]
    )
    grad_ref[...] = gy1_ref[...] + part
    out_ref[...] = (y1_ref[...] + nn(oa_ref[...], w[0])).astype(bf16)


def weight_grad_call(where, weights, name, shards=0):
    arrays, items = [], []

    def place(value):
        for index, known in enumerate(arrays):
            if known is value:
                return index
        arrays.append(value)
        return len(arrays) - 1

    for lanes, kind, entries in weights:
        for index, (left, left_at, right, right_at, form) in enumerate(entries):
            items.append((lanes, kind, index, place(left), left_at, place(right), right_at, form))
    count = len(arrays)
    rows = D // 8 // len(weights[0][0])

    def body(*refs):
        where_ref = refs[0]
        ins = refs[1 : 1 + count]
        *outs, held, sems, flipped = refs[1 + count :]
        turned = None
        keep, send = outs[0], outs[-1]
        page, blk = where_ref[3], where_ref[4]

        def place_natural(slot, lane, kind, index):
            out, width = outs[0], 4 * D // shards
            each = width // 2
            for k in range(2 * D // width if kind == "up" else D // width):
                if kind == "up":
                    piece = held.at[slot, k * each : (k + 1) * each]
                    first = lane * width + (index % 2) * each
                    local_copy(
                        piece, out.at[2 * k + index // 2, first : first + each], sems.at[slot]
                    )
                else:
                    piece = held.at[slot, k * width : (k + 1) * width]
                    owner = index * (D // width) + k
                    spot = slice(lane * width, (lane + 1) * width)
                    local_copy(piece, out.at[owner, spot], sems.at[slot])

        def finish(slot):
            pltpu.make_async_copy(held.at[slot], held.at[slot], sems.at[slot]).wait()

        def place_up(slot, lane, index, core, first, second):
            near = (blk ^ relative(lane, 0, first, second)) >> 1
            group, k = index // 2, index % 2
            out = send if core else keep

            @pl.when(((blk & 1) ^ core) == group)
            def _():
                half = rows // 2
                for origin in range(4):
                    spot = first * 8 + second * 4 + (origin ^ page)
                    take = pl.ds(pl.multiple_of((origin * 4 + near) * half, half), half)
                    local_copy(
                        held.at[slot, take],
                        out.at[lane, spot, k * half : (k + 1) * half],
                        sems.at[slot],
                    )

        def place_rows(slot, lanes, index, core, first, second):
            out = send if core else keep
            for number, lane in enumerate(lanes):
                owner = blk ^ relative(lane, core, first, second)
                spot = first * 8 + second * 4 + (index ^ page)
                start = pl.multiple_of((owner * len(lanes) + number) * rows, rows)
                local_copy(held.at[slot, pl.ds(start, rows)], out.at[lane, spot], sems.at[slot])

        for step, (lanes, kind, index, left, left_at, right, right_at, form) in enumerate(items):
            slot = step % 2
            if step >= 2:
                finish(slot)
            lhs = ins[left][:, left_at * D : (left_at + 1) * D]
            if form == "tt":
                rhs = ins[right][right_at * D : (right_at + 1) * D, :]
                if turned != (left, left_at):
                    turned = (left, left_at)
                    flipped[...] = lhs.T
                product = nt(flipped[...], rhs)
            else:
                product = tn(lhs, ins[right][:, right_at * D : (right_at + 1) * D])
            held[slot] = product.astype(bf16)
            if shards:
                place_natural(slot, lanes[0], kind, index)
                continue
            for core in range(2):
                for first in range(2):
                    for second in range(2):
                        if kind == "up":
                            place_up(slot, lanes[0], index, core, first, second)
                        else:
                            place_rows(slot, lanes, index, core, first, second)
        for step in range(max(0, len(items) - 2), len(items)):
            finish(step % 2)

    shapes = [sds((2, 16, rows, D), bf16)] * 2
    if shards:
        shapes = [sds((shards, len(weights) * 4 * D // shards, D), bf16)]
    turned_rows = max([128] + [arrays[item[3]].shape[0] for item in items if item[7] == "tt"])
    moved = 2 * len(items) * D * D + sum(v.size * 2 for v in arrays)
    return pl.pallas_call(
        body,
        grid=(1,),
        out_shape=shapes,
        in_specs=[pl.BlockSpec(memory_space=pltpu.SMEM)]
        + [
            pl.BlockSpec(v.shape, lambda i: (0, 0), pipeline_mode=pl.Buffered(1)) for v in arrays
        ],
        out_specs=[pl.BlockSpec(memory_space=pl.ANY)] * len(shapes),
        scratch_shapes=[
            pltpu.VMEM((2, D, D), bf16),
            pltpu.SemaphoreType.DMA((2,)),
            pltpu.VMEM((D, turned_rows), bf16),
        ],
        compiler_params=pltpu.CompilerParams(
            vmem_limit_bytes=VMEM_LIMIT, dimension_semantics=("arbitrary",)
        ),
        cost_estimate=pl.CostEstimate(
            flops=int(len(items) * 1.6e-6 * 1.1e15), bytes_accessed=int(moved), transcendentals=0
        ),
        name=name,
    )(where, *arrays)


def window_order(grid_rows, half):
    rows, cols, _ = grid_rows.shape
    rolled = jnp.roll(grid_rows, -half, axis=1)
    shaped = rolled.reshape(rows, cols // rows, rows, D).transpose(1, 0, 2, 3)
    return shaped.reshape(rows * cols, D)


def grid_order(tokens_in, rows, cols, half):
    shaped = tokens_in.reshape(cols // rows, rows, rows, D).transpose(1, 0, 2, 3)
    return jnp.roll(shaped.reshape(rows, cols, D), half, axis=1)


def after(value, *others):
    return lax.optimization_barrier((value, others))[0]


def swapped(value, axis, flip):
    count = lax.axis_size(axis)
    return lax.ppermute(value, axis, [(i, i ^ flip) for i in range(count)])


def from_pages(value):
    pages = lax.axis_size("page")
    return [value] + [swapped(value, "page", k) for k in range(1, pages)]


def spread_first(shares):
    parts = from_pages(jnp.stack(shares))
    return [jnp.stack([part[k] for part in parts]) for k in range(2)]


def spread_second(held, *gate):
    got = swapped(held[0], "blk", 2), swapped(held[1], "blk", 4)
    held, got = after((held, got), *gate)
    return [jnp.concatenate([held[k], got[k]]) for k in range(2)]


def spread_third(near):
    return [swapped(near[0], "blk", 4), swapped(near[1], "blk", 2)]


def spread_core(held):
    return [swapped(value, "blk", 1) for value in held]


def lane_arrays(near, far, near_core, far_core, lane):
    return [near[lane], far[lane], near_core[lane], far_core[lane]]


def added(left, right):
    return (left.astype(f32) + right.astype(f32)).astype(bf16)


def collect_first(keep, send, *gate):
    got = swapped(send, "blk", 1)
    keep = after(keep, *gate)
    return [[added(keep[k, i : i + 8], got[k, i : i + 8]) for i in (0, 8)] for k in range(2)]


def collect_second(held, *gate):
    got = swapped(held[0][1], "blk", 2), swapped(held[1][1], "blk", 4)
    kept = after([held[0][0], held[1][0]], *gate)
    return [[added(kept[k][i : i + 4], got[k][i : i + 4]) for i in (0, 4)] for k in range(2)]


def collect_third(held, *gate):
    got = swapped(held[0][1], "blk", 4), swapped(held[1][1], "blk", 2)
    kept = after([held[0][0], held[1][0]], *gate)
    sums = [added(kept[k], got[k]) for k in range(2)]
    return [jnp.stack([sums[k][i] for k in range(2)]) for i in range(4)]


def collect_last(held, *gate):
    total = after(held[0], *gate).astype(f32)
    for k in range(1, 4):
        total = total + swapped(held[k], "page", k).astype(f32)
    return total


def blocks_in_chip(parts, gate):
    keep, send = parts
    got = swapped(send, "blk", 1)
    keep = after(keep, gate)
    return [added(keep[k], got[k]) for k in range(4)]


def blocks_over_chips(chips, gate):
    total = after(chips[0], gate).astype(f32)
    for k in range(1, 4):
        total = total + swapped(chips[k], "blk", 2 * k).astype(f32)
    return total


def scattered_blocks(part):
    return lax.psum_scatter(part, "blk", scatter_dimension=0, tiled=True)


def on_device(
    visual,
    query_tokens,
    answer_len,
    attn_swin,
    attn_self,
    attn_qv,
    attn_vq,
    mlp_up,
    mlp_down,
    norm_gains,
    visual_cot,
    query_cot,
):
    everyone = ("page", "blk")
    pages = lax.axis_size("page")
    page_here = lax.axis_index("page")
    blk_count = lax.axis_size("blk")
    blk_here = lax.axis_index("blk")
    shards = pages * blk_count
    rows_here, cols_all = visual.shape[1], visual.shape[2]
    half = rows_here // 2
    tokens = rows_here * cols_all
    q_rows = query_tokens.shape[1]
    slots = q_rows * blk_count
    share = attn_swin.shape[0] // D
    staged = pages == 4 and blk_count == 8 and share % 32 == 0
    gain_width = norm_gains.shape[0]
    core_here = blk_here % 2

    where = jnp.stack(
        [
            blk_here * q_rows,
            answer_len[0],
            (blk_here == blk_count - 1).astype(jnp.int32),
            page_here,
            blk_here,
        ]
    ).astype(jnp.int32)

    down_one = [(i, (i - 1) % blk_count) for i in range(blk_count)]
    up_one = [(i, (i + 1) % blk_count) for i in range(blk_count)]
    both = jnp.concatenate([visual, visual_cot], axis=0)
    lent = lax.ppermute(both[:, :half], "blk", down_one)
    both = jnp.concatenate([both[:, half:], lent], axis=1)
    vis_in = window_order(both[0], half)
    vis_cot = window_order(both[1], half)

    def flat_share(value):
        return value.astype(bf16).reshape(share, D)

    gain_rows = jnp.pad(norm_gains.astype(bf16)[None], ((0, 15), (0, D - gain_width)))
    slot_own = jnp.concatenate([query_tokens[0], query_cot[0], gain_rows], axis=0)
    slots_joined = lax.all_gather(slot_own, "blk", axis=0)
    slot_arrays = [slots_joined]
    gain_parts = jnp.stack(from_pages(slots_joined[:, 2 * q_rows, :gain_width].reshape(-1)))
    gains = jnp.take(gain_parts, jnp.arange(pages) ^ page_here, axis=0)
    gains = gains.reshape(8, D).astype(f32)
    if staged:
        a_z = spread_first([flat_share(attn_self), flat_share(attn_swin)])
        a_z = after(a_z, vis_in, vis_cot)
        a_near = spread_second(a_z)
        c_z = spread_first(after([flat_share(attn_qv), flat_share(attn_vq)], a_z))
        a_far = spread_third(a_near)
        a_near_core, a_far_core = spread_core(a_near), spread_core(a_far)
        w_self, w_swin = [
            Stored(lane_arrays(a_near, a_far, a_near_core, a_far_core, k), (k,)) for k in range(2)
        ]
        up_groups = after(mlp_up, a_near).astype(bf16)
        up_groups = up_groups.reshape(share // 4, 2, 2, D).transpose(1, 2, 0, 3)
        mine = jnp.where(core_here == 0, up_groups[0], up_groups[1])
        other = swapped(jnp.where(core_here == 0, up_groups[1], up_groups[0]), "blk", 1)
        up_share = jnp.where(
            core_here == 0,
            jnp.concatenate([mine, other], axis=1),
            jnp.concatenate([other, mine], axis=1),
        ).reshape(share, D)
        d_z = spread_first(after([up_share, flat_share(mlp_down)], c_z))
        c_near = spread_second(after(c_z, a_far, gains))
        c_far = spread_third(c_near)
    else:
        up_share = (
            mlp_up.astype(bf16).reshape(share // 4, 4, D).transpose(1, 0, 2).reshape(share, D)
        )
        joined = lax.all_gather(
            jnp.concatenate(
                [flat_share(v) for v in (attn_self, attn_swin, attn_qv, attn_vq, mlp_down)]
                + [up_share],
                axis=0,
            ),
            everyone,
            axis=0,
            tiled=True,
        ).reshape(shards, -1, D)
        w_self, w_swin, w_qv, w_vq, w_down = [
            Stored([joined[:, k * share : (k + 1) * share].reshape(4, D, D)]) for k in range(5)
        ]
        up_all = joined[:, 5 * share : 6 * share].reshape(shards, 4, share // 4, D)
        w_up = Stored([up_all.transpose(1, 0, 2, 3).reshape(4, D, D)])

    where_self = where_swin = where_cross = where_vq = where
    if staged:
        where_self = after(where, vis_in, vis_cot, a_near_core, a_far_core)
    b_all, q_self, kv_self, lse_self, o_self, y1, c_own = call(
        self_forward_kernel,
        [
            sds((slots, D), bf16),
            sds((q_rows, D), bf16),
            sds((slots, 2 * D), bf16),
            sds((q_rows, 128), f32),
            sds((q_rows, D), bf16),
            sds((q_rows, D), f32),
            sds((q_rows, D), bf16),
        ],
        [where_self, gains],
        slots=(slot_arrays, 0, q_rows),
        scratch=[pltpu.VMEM((q_rows, slots), f32)],
        loads=[(w_self, 1), (w_self, 2), (w_self, 0), (w_self, 3)],
        flops=15e-6 * 1.1e15,
        name="self_forward",
    )
    if staged:
        c_near_core = spread_core(c_near)
        c_far, c_near_core = after((c_far, c_near_core), c_own)
        c_far_core = spread_core(c_far)
        w_qv, w_vq = [
            Stored(lane_arrays(c_near, c_far, c_near_core, c_far_core, k), (k,)) for k in range(2)
        ]
        where_swin = after(where, c_far, c_near_core)
        d_z = after(d_z, c_far)
    c_all = lax.all_gather(c_own, "blk", axis=0, tiled=True)

    def swin_forward(*refs):
        swin_forward_kernel(rows_here, *refs)

    a_low, qkv_swin, lse_swin, o_swin, v1, e_low = call(
        swin_forward,
        [
            sds((tokens, D), bf16),
            sds((tokens, 3 * D), bf16),
            sds((tokens, 128), f32),
            sds((tokens, D), bf16),
            sds((tokens, D), f32),
            sds((tokens, D), bf16),
        ],
        [where_swin, vis_in, gains],
        scratch=[pltpu.VMEM((cols_all // rows_here, rows_here**2, rows_here**2), f32)],
        loads=[(w_swin, k) for k in range(4)],
        flops=11e-6 * 1.1e15,
        name="swin_forward",
    )

    if staged:
        d_near = spread_second(d_z, e_low)
        d_far = spread_third(d_near)
        where_cross = after(where, d_near)
    qa, kvb, doa, kva, qb, stats = call(
        cross_forward_kernel,
        [
            sds((slots, D), bf16),
            sds((slots, 2 * D), bf16),
            sds((slots, D), bf16),
            sds((tokens, 2 * D), bf16),
            sds((tokens, D), bf16),
            sds((3, 16, slots), f32),
        ],
        [where_cross, c_all, e_low],
        slots=(slot_arrays, 1, q_rows),
        loads=[(w_qv, 1), (w_qv, 2), (w_vq, 0), (w_qv, 0), (w_vq, 1), (w_vq, 2), (w_qv, 3)],
        flops=18e-6 * 1.1e15,
        name="cross_forward",
    )
    if staged:
        d_far = after(d_far, qb)
        d_near_core, d_far_core = spread_core(d_near), spread_core(d_far)
        w_up, w_down = [
            Stored(lane_arrays(d_near, d_far, d_near_core, d_far_core, k), (k,)) for k in range(2)
        ]
        where_vq = after(where, d_far)
    lse_vq, o_vq = call(
        vq_forward_kernel,
        [sds((tokens, 128), f32), sds((tokens, D), bf16)],
        [where_vq, qb, kvb],
        flops=11e-6 * 1.1e15,
        name="vq_forward",
    )

    all_stats = lax.all_gather(stats, "blk", axis=0)
    peaks = jnp.max(all_stats[:, 0], axis=0)
    weights = jnp.exp(all_stats[:, 0] - peaks[None])
    totals = jnp.sum(all_stats[:, 1] * weights, axis=0)
    lse_qv = peaks + jnp.log(totals)
    centre_qv = jnp.sum(all_stats[:, 2] * weights, axis=0) / totals

    v3, h_low, act_low, du_low, g2, dz_vq, dob, dg5 = call(
        mlp_kernel,
        [
            sds((tokens, D), bf16),
            sds((tokens, D), bf16),
            sds((tokens, FF), bf16),
            sds((tokens, FF), bf16),
            sds((tokens, D), f32),
            sds((tokens, D), bf16),
            sds((tokens, D), bf16),
            sds((1, D), f32),
        ],
        [where, v1, o_vq, vis_cot, gains],
        scratch=[pltpu.VMEM((tokens, D), f32)] * 3,
        loads=[(w_vq, 3), (w_up, None)] + [(w_down, k) for k in range(4)],
        flops=14e-6 * 1.1e15,
        name="mlp",
    )

    def back_to_grid(value, *gate):
        grid = grid_order(value, rows_here, cols_all, half)
        returned = lax.ppermute(grid[half:].astype(bf16), "blk", up_one)
        returned, grid = after((returned, grid), *gate)
        returned = returned.astype(grid.dtype)
        return jnp.concatenate([returned, grid[:half]], axis=0)[None]

    def flat(value):
        return value.astype(f32).reshape(-1)

    def gains_over_pages(db_all):
        gain_sum = db_all[q_rows, : pages * gain_width].reshape(pages, gain_width).astype(f32)
        kept = jnp.take(gain_sum, page_here, axis=0)
        for k in range(1, pages):
            kept = kept + swapped(jnp.take(gain_sum, page_here ^ k, axis=0), "page", k)
        return kept

    def with_gains(held, db_all):
        gain_sum = db_all[q_rows, : pages * gain_width].reshape(pages, gain_width)
        joined = []
        for k in range(pages):
            row = jnp.take(gain_sum, page_here ^ k, axis=0)[None, None]
            row = jnp.pad(row, ((0, 1), (0, 7), (0, D - gain_width)))
            joined.append(jnp.concatenate([held[k], row], axis=1))
        return joined

    def up_over_core(mlp_sum):
        up_sum = mlp_sum[0].reshape(2, 2, share // 4, D)
        mine = jnp.where(core_here == 0, up_sum[:, 0], up_sum[:, 1])
        other = swapped(jnp.where(core_here == 0, up_sum[:, 1], up_sum[:, 0]), "blk", 1)
        joined_up = jnp.where(
            core_here == 0,
            jnp.concatenate([mine, other], axis=0),
            jnp.concatenate([other, mine], axis=0),
        )
        return flat(joined_up.transpose(1, 0, 2))

    up_entries = [(h_low, 0, du_low, k, "tn") for k in range(4)]
    down_entries = [(act_low, k, vis_cot, 0, "tn") for k in range(4)]
    where_vq_back = where
    if staged:
        m_keep, m_send = weight_grad_call(
            after(where, lse_qv, centre_qv), [((0,), "up", up_entries), ((1,), "rows", down_entries)], "mlp_grads"
        )
        where_vq_back = after(where, m_keep)

    dqb, dkvbt = call(
        vq_backward_kernel,
        [sds((tokens, D), bf16), sds((2 * D, slots), bf16)],
        [where_vq_back, qb, kvb, dob, lse_vq],
        flops=16e-6 * 1.1e15,
        name="vq_backward",
    )
    where_swin_back = where_self_back = where_qv_back = where
    if staged:
        visual_out = back_to_grid(after(v3, m_keep))
        where_qv_back = after(where, visual_out)
        m_one = collect_first(m_keep, m_send, dqb)
        where_qv_back = after(where, visual_out, m_one)
    dqat, dkva, *merged_parts = call(
        qv_backward_kernel,
        [sds((D, slots), bf16), sds((tokens, 2 * D), bf16)] + [sds((slots, 2 * D), bf16)],
        [where_qv_back, qa, kva, doa, lse_qv, centre_qv, dkvbt],
        scratch=[pltpu.VMEM((slots, 2 * D), bf16)],
        loads=[(w_qv, 0), (w_vq, 1), (w_vq, 2)],
        flops=23e-6 * 1.1e15,
        name="qv_backward",
    )
    merged = scattered_blocks(merged_parts[0])
    if staged:
        m_two = collect_second(m_one, dqat)
        where_swin_back = after(where, m_two)
    dc, oa_low = merged[:, :D], merged[:, D:]

    def swin_backward(*refs):
        swin_backward_kernel(rows_here, *refs)

    dz_swin, dqkv_swin, visual_grad, dg_visual = call(
        swin_backward,
        [
            sds((tokens, D), bf16),
            sds((tokens, 3 * D), bf16),
            sds((tokens, D), f32),
            sds((2, D), f32),
        ],
        [where_swin_back, vis_in, v1, g2, gains, dkva, dqb, qkv_swin, lse_swin],
        scratch=[
            pltpu.VMEM((cols_all // rows_here, rows_here**2, rows_here**2), f32),
            pltpu.VMEM((tokens, D), bf16),
        ],
        loads=[(w_qv, 1), (w_qv, 2), (w_vq, 0), (w_swin, 3)] + [(w_swin, k) for k in range(3)],
        flops=20e-6 * 1.1e15,
        name="swin_backward",
    )

    swin_entries = [(a_low, 0, dqkv_swin, k, "tn") for k in range(3)]
    swin_entries.append((o_swin, 0, dz_swin, 0, "tn"))
    vq_entries = [
        (e_low, 0, dqb, 0, "tn"),
        (c_all, 0, dkvbt, 0, "tt"),
        (c_all, 0, dkvbt, 1, "tt"),
        (o_vq, 0, dz_vq, 0, "tn"),
    ]
    qv_entries = [
        (c_all, 0, dqat, 0, "tt"),
        (e_low, 0, dkva, 0, "tn"),
        (e_low, 0, dkva, 1, "tn"),
        (oa_low, 0, query_cot[0], 0, "tn"),
    ]
    if staged:
        m_three = collect_third(m_two, dz_swin)
        p_keep, p_send = weight_grad_call(
            after(where, m_three), [((0,), "rows", vq_entries), ((1,), "rows", swin_entries)], "patch_grads"
        )
        p_one = collect_first(p_keep, p_send)
        where_self_back = after(where, p_one)

    gy1, dz_self, dq_self, dkvt_self, dbq, dg_slots, db_part = call(
        self_backward_kernel,
        [
            sds((q_rows, D), f32),
            sds((q_rows, D), bf16),
            sds((q_rows, D), bf16),
            sds((2 * D, slots), bf16),
            sds((q_rows, D), f32),
            sds((2, D), f32),
        ]
        + [sds((slots, D), bf16)],
        [where_self_back, dc, y1, query_cot[0], gains, q_self, kv_self, lse_self],
        slots=(slot_arrays, 0, q_rows),
        scratch=[
            pltpu.VMEM((q_rows, slots), f32),
            pltpu.VMEM((q_rows, D), bf16),
            pltpu.VMEM((slots, D), bf16),
        ],
        loads=[(w_self, 3), (w_self, 0), (w_self, 1), (w_self, 2)],
        flops=15e-6 * 1.1e15,
        name="self_backward",
    )
    b_own = lax.dynamic_slice_in_dim(b_all, blk_here * q_rows, q_rows, 0)
    self_entries = [
        (b_own, 0, dq_self, 0, "tn"),
        (b_all, 0, dkvt_self, 0, "tt"),
        (b_all, 0, dkvt_self, 1, "tt"),
        (o_self, 0, dz_self, 0, "tn"),
    ]
    gain_block = jnp.concatenate(
        [dg_visual[0:1], dg_slots[0:1], dg_visual[1:2], dg_slots[1:2], dg5, jnp.zeros((3, D), f32)],
        axis=0,
    )
    gain_block = gain_block.astype(bf16).reshape(pages, blk_count, gain_width).transpose(1, 0, 2)
    gain_block = gain_block.reshape(blk_count, 1, pages * gain_width)
    gain_block = jnp.pad(gain_block, ((0, 0), (0, 7), (0, D - pages * gain_width)))
    whole_part = jnp.concatenate([db_part.reshape(blk_count, q_rows, D), gain_block], axis=1)
    db_all = scattered_blocks(whole_part.reshape(blk_count * (q_rows + 8), D))
    where_end = where
    if staged:
        p_two = collect_second(p_one, gy1)
        mlp_sum = collect_last(m_three, gy1)
        z_keep, z_send = weight_grad_call(
            after(where, p_two, mlp_sum), [((0,), "rows", qv_entries), ((1,), "rows", self_entries)], "slot_grads"
        )
        visual_grad = back_to_grid(visual_grad, z_keep)
        z_keep, z_send = after((z_keep, z_send), visual_grad)
        z_one = collect_first(z_keep, z_send)
        p_three = collect_third(p_two, z_one)
        z_two = collect_second(after(z_one, p_three))
        patch_sum = collect_last(after(p_three, z_one))
        db_all = after(db_all, patch_sum)
        up_grad = up_over_core(mlp_sum)
        z_two = after(z_two, patch_sum, up_grad)
        z_three = with_gains(collect_third(z_two), db_all)
        where_end = after(where, z_three)
    db = db_all[:q_rows]
    query_grad, query_out = call(
        query_end_kernel,
        [sds((q_rows, D), f32), sds((q_rows, D), bf16)],
        [where_end, db, dbq, query_tokens[0], gy1, gains, y1, oa_low],
        loads=[(w_qv, 3)],
        name="query_end",
    )

    if staged:
        slot_sum = collect_last(z_three)
        gain_grad, slot_sum = slot_sum[0, share, :gain_width], slot_sum[:, :share]
        swin_grad, self_grad = flat(patch_sum[1]), flat(slot_sum[1])
        qv_grad, vq_grad = flat(slot_sum[0]), flat(patch_sum[0])
        down_grad = flat(mlp_sum[1])
    else:
        visual_out, visual_grad = back_to_grid(v3), back_to_grid(visual_grad)
        gain_grad = gains_over_pages(db_all)

        def outer(left, right):
            return tn(left, right).astype(bf16)

        def outer_t(left, right_t):
            return lax.dot_general(
                left, right_t, (((0,), (1,)), ((), ())), preferred_element_type=f32
            ).astype(bf16)

        def as_shares(mats):
            return jnp.concatenate(mats, axis=0).reshape(shards, share, D)

        def summed(parts):
            joined = jnp.concatenate(parts, axis=1)
            width = joined.shape[1]
            return lax.psum_scatter(
                joined.reshape(shards * width, D), everyone, scatter_dimension=0, tiled=True
            )

        up_mats = jnp.stack([outer(h_low, du_low[:, k * D : (k + 1) * D]) for k in range(4)])
        up_part = (
            up_mats.reshape(4, shards, share // 4, D)
            .transpose(1, 0, 2, 3)
            .reshape(shards, share, D)
        )
        down_part = outer(act_low, vis_cot).reshape(shards, share, D)
        mlp_sum = summed([up_part, down_part])
        qv_part = as_shares(
            [
                outer_t(c_all, dqat),
                outer(e_low, dkva[:, :D]),
                outer(e_low, dkva[:, D:]),
                outer(oa_low, query_cot[0]),
            ]
        )
        vq_part = as_shares(
            [
                outer(e_low, dqb),
                outer_t(c_all, dkvbt[:D]),
                outer_t(c_all, dkvbt[D:]),
                outer(o_vq, dz_vq),
            ]
        )
        cross_sum = summed([qv_part, vq_part])
        swin_part = as_shares(
            [outer(a_low, dqkv_swin[:, k * D : (k + 1) * D]) for k in range(3)]
            + [outer(o_swin, dz_swin)]
        )
        self_part = as_shares(
            [
                outer(b_own, dq_self),
                outer_t(b_all, dkvt_self[:D]),
                outer_t(b_all, dkvt_self[D:]),
                outer(o_self, dz_self),
            ]
        )
        last_sum = summed([swin_part, self_part])
        up_grad = flat(mlp_sum[:share].reshape(4, share // 4, D).transpose(1, 0, 2))
        down_grad = flat(mlp_sum[share:])
        qv_grad, vq_grad = flat(cross_sum[:share]), flat(cross_sum[share:])
        swin_grad, self_grad = flat(last_sum[:share]), flat(last_sum[share:])

    return (
        visual_out,
        query_out[None],
        visual_grad,
        query_grad[None],
        swin_grad,
        self_grad,
        qv_grad,
        vq_grad,
        up_grad,
        down_grad,
        gain_grad,
    )


def solution(mesh):
    placed = (
        P("page", "blk", None, None),
        P("page", "blk", None),
        P("page"),
        P(("page", "blk")),
        P(("page", "blk")),
        P(("page", "blk")),
        P(("page", "blk")),
        P(("page", "blk")),
        P(("page", "blk")),
        P(("page", "blk")),
        P("page", "blk", None, None),
        P("page", "blk", None),
    )
    return jax.shard_map(
        on_device,
        mesh=mesh,
        in_specs=placed,
        out_specs=(
            P("page", "blk", None, None),
            P("page", "blk", None),
            P("page", "blk", None, None),
            P("page", "blk", None),
            P(("page", "blk")),
            P(("page", "blk")),
            P(("page", "blk")),
            P(("page", "blk")),
            P(("page", "blk")),
            P(("page", "blk")),
            P(("page", "blk")),
        ),
        check_vma=False,
    )
```
